32 devices in a mesh: stream: 4 (over y, x), span: 8 (over z, core).
Axes of the slice: x: 2, y: 2, z: 4, core: 2. Of those that a mesh axis runs over, the one named last changes fastest.
Arguments:
- tokens: bfloat16 [4, 2048, 1024], P('stream', 'span'), may hold values from -6 to 6
- cotangent: bfloat16 [4, 2048, 1024], P('stream', 'span'), may hold values from -6 to 6
- doc_stretches: int32 [4, 3], P('stream'), may hold values from 1 to 29, 32 in all within a row
- w_qkv: bfloat16 [1024, 3072], P('span'), may hold values from -0.1875 to 0.1875
- conv_weight: bfloat16 [4, 3072], P(None, 'span'), may hold values from -3 to 3
- w_beta: bfloat16 [1024, 8], P('span'), may hold values from -0.1875 to 0.1875
- beta_bias: float32 [8], replicated, as said below
- norm_attn: bfloat16 [1024], P('span'), may hold values from 0.099609375 to 1.8984375
- norm_head: bfloat16 [128], P('span'), may hold values from 0.099609375 to 1.8984375
- w_out: bfloat16 [1024, 1024], P('span'), may hold values from -0.1875 to 0.1875
- norm_ffn: bfloat16 [1024], P('span'), may hold values from 0.099609375 to 1.8984375
- w_gate: bfloat16 [1024, 2816], P('span'), may hold values from -0.1875 to 0.1875
- w_up: bfloat16 [1024, 2816], P('span'), may hold values from -0.1875 to 0.1875
- w_down: bfloat16 [2816, 1024], P('span'), may hold values from -0.109375 to 0.109375
Outputs:
- out: bfloat16 [4, 2048, 1024], P('stream', 'span')
- grad_tokens: float32 [4, 2048, 1024], P('stream', 'span')
- grad_qkv: float32 [1024, 3072], P('span')
- grad_conv: float32 [4, 3072], P(None, 'span')
- grad_w_beta: float32 [1024, 8], P('span')
- grad_beta_bias: float32 [8], replicated
- grad_norm_attn: float32 [1024], P('span')
- grad_norm_head: float32 [128], P('span')
- grad_out: float32 [1024, 1024], P('span')
- grad_norm_ffn: float32 [1024], P('span')
- grad_gate: float32 [1024, 2816], P('span')
- grad_up: float32 [1024, 2816], P('span')
- grad_down: float32 [2816, 1024], P('span')
The draws below stay inside these ranges and needn't reach their ends.
Inputs may be any that keep to these rules, and one draw needn't show every extreme that they name: `doc_stretches`: each stream's documents in stretches of 64 tokens, in order; they sum to 32 and one of them has 29 stretches. `beta_bias`: one offset per head.
All inputs are finite; a program needn't handle non-finite values.
Results may differ from the reference program's by a relative error of at most 0.019.
Values may be sent and summed in bfloat16 or wider, within the bound.
A program may use at most 320 MiB of HBM per device.

```python
import math
import jax
import jax.numpy as jnp
import numpy as np
from jax import lax

D = 1024
H = 8
DH = 128
FF = 2816
CONV = 4
STRETCH = 64
NDOC = 3
STREAMS = 4
STREAM_TOK = 2048
STREAM_CH = 32
LONGEST = 29


def draw_beta_bias(key, part):
    key = jax.random.fold_in(key, 7)
    reach = jax.random.uniform(key, (H,), jnp.float32, 0.0, 4.8)
    return reach - 0.7 + math.log(DH / STREAM_TOK)


def block_levels(key, dims, shards, smallest, top_value):
    def one(axis_at, shards_of):
        draws = jax.random.uniform(jax.random.fold_in(jax.random.fold_in(key, 6), axis_at), (shards_of,), jnp.float32, smallest / len(shards), top_value / len(shards))
        return jnp.repeat(jnp.exp(draws), dims[axis_at] // shards_of).reshape((-1,) + (1,) * (len(dims) - axis_at - 1))

    gain = one(*shards[0])
    for cut in shards[1:]:
        gain = gain * one(*cut)
    return gain


def split_up(amount, total, most, slope):
    loads = [(1 << 20) // math.isqrt(standing ** slope) + 1 for standing in range(2, amount + 1)]
    surplus, given = total - most - (amount - 1), [1] * (amount - 1)
    while surplus > 0:
        movable = [i for i in range(amount - 1) if given[i] < most]
        whole, budget = sum([loads[i] for i in movable]), surplus
        for i in movable:
            extra = min(most - given[i], max(1, budget * loads[i] // whole), surplus)
            given[i] = given[i] + extra
            surplus = surplus - extra
    return np.array([most] + given)


def ragged_sizes(own_key, amount, total, limit, slope):
    if amount == 2:
        one = jax.random.randint(own_key, (), max(1, total - limit), min(limit, total - 1) + 1)
        return jnp.stack([one, total - one])
    sizes = jnp.asarray(split_up(amount, total, limit, slope), jnp.int32)
    couples = (amount - 1) // 2
    donor, sink = sizes[1:1 + 2 * couples:2], sizes[2:2 + 2 * couples:2]
    room = jnp.minimum(donor - 1, limit - sink)
    shifted = jax.random.randint(jax.random.fold_in(own_key, 1), (couples,), 0, 1 << 20) % (room + 1)
    sizes = sizes.at[1:1 + 2 * couples:2].set(donor - shifted).at[2:2 + 2 * couples:2].set(sink + shifted)
    return sizes[jax.random.permutation(jax.random.fold_in(own_key, 2), amount)]


def normal_values(rng, shape, spread, bound, split=(), kind=jnp.bfloat16):
    values = spread * jax.random.normal(rng, shape, jnp.float32)
    if split:
        values = values * block_levels(rng, shape, split, -0.22, 0.18)
    return jnp.clip(values, -bound, bound).astype(kind)


def setup_inputs(seed: int = 0) -> dict:
    splits = jax.random.split(jax.random.key(seed), 15)
    return {
        "tokens": normal_values(splits[0], (STREAMS, STREAM_TOK, D), 1.0, 6.0, ((0, 4), (1, 8))),
        "cotangent": normal_values(splits[1], (STREAMS, STREAM_TOK, D), 1.0, 6.0, ((0, 4), (1, 8))),
        "doc_stretches": jax.vmap(lambda own: ragged_sizes(own, NDOC, STREAM_CH, LONGEST, 0))(jax.random.split(splits[2], STREAMS)).reshape((STREAMS, NDOC)).astype(jnp.int32),
        "w_qkv": normal_values(splits[3], (D, 3 * D), D ** -0.5, 0.1875, ((0, 8),)),
        "conv_weight": normal_values(splits[4], (CONV, 3 * D), 0.5, 3.0, ((1, 8),)),
        "w_beta": normal_values(splits[5], (D, H), D ** -0.5, 0.1875, ((0, 8),)),
        "beta_bias": draw_beta_bias(jax.random.fold_in(splits[14], 71), 0),
        "norm_attn": jnp.clip(1.0 + 0.18 * jax.random.normal(splits[7], (D,), jnp.float32), 0.099609375, 1.8984375).astype(jnp.bfloat16),
        "norm_head": jnp.clip(1.0 + 0.18 * jax.random.normal(splits[8], (DH,), jnp.float32), 0.099609375, 1.8984375).astype(jnp.bfloat16),
        "w_out": normal_values(splits[9], (D, D), D ** -0.5, 0.1875, ((0, 8),)),
        "norm_ffn": jnp.clip(1.0 + 0.18 * jax.random.normal(splits[10], (D,), jnp.float32), 0.099609375, 1.8984375).astype(jnp.bfloat16),
        "w_gate": normal_values(splits[11], (D, FF), D ** -0.5, 0.1875, ((0, 8),)),
        "w_up": normal_values(splits[12], (D, FF), D ** -0.5, 0.1875, ((0, 8),)),
        "w_down": normal_values(splits[13], (FF, D), FF ** -0.5, 0.109375, ((0, 8),)),
    }


@jax.custom_vjp
def low(v):
    return lax.optimization_barrier(v.astype(jnp.bfloat16)).astype(jnp.float32)

@jax.custom_vjp
def low_back(v):
    return v

def low_keep(v):
    return (low(v), None)

def low_pass(kept, grad):
    return (grad,)

def back_keep(v):
    return (v, None)

def back_low(kept, grad):
    return (low(grad),)
low.defvjp(low_keep, low_pass)
low_back.defvjp(back_keep, back_low)
EPSILON = 1e-06
PRECISE = lax.Precision.HIGHEST

def matrix(first_op, second_op):
    return jnp.dot(first_op, second_op, precision=PRECISE, preferred_element_type=jnp.float32)

def rms_scale(values, gain_vec):
    return values * lax.rsqrt(lax.optimization_barrier(jnp.mean(values * values, -1, keepdims=True)) + EPSILON) * gain_vec

def unit_rows(values):
    return values * lax.rsqrt(lax.optimization_barrier(jnp.sum(values * values, -1, keepdims=True)) + EPSILON)

def delta_rule(queries, keys_in, values_in, strength, starts):
    token_total = queries.shape[0]
    blocks = token_total // STRETCH

    def token_step(memory, pieces):
        query_row, key_row, value_row, beta_row, reset_flag = pieces
        memory = memory * (1.0 - reset_flag)
        predicted = jnp.einsum('hab,hb->ha', memory, key_row, precision=PRECISE)
        update = beta_row[:, None] * (value_row - predicted)
        memory = memory + jnp.einsum('ha,hb->hab', update, key_row, precision=PRECISE)
        return (memory, jnp.einsum('hab,hb->ha', memory, query_row, precision=PRECISE))

    def block_step(memory, pieces):
        return lax.scan(token_step, memory, pieces)
    pieces = tuple((array_in.reshape((blocks, STRETCH) + array_in.shape[1:]) for array_in in (queries, keys_in, values_in, strength, starts)))
    initial = jnp.zeros((H, DH, DH), jnp.float32)
    _, readout = lax.scan(jax.checkpoint(block_step), initial, pieces)
    return readout.reshape(token_total, H, DH)

def feed_forward(middle, norm_ffn, w_gate, w_up, w_down):
    token_total = middle.shape[0]
    block_rows = math.gcd(token_total, 4096)

    def one_block(row_block):
        normed_ffn = low(rms_scale(row_block, norm_ffn))
        gate = low_back(matrix(normed_ffn, w_gate))
        up_part = low_back(matrix(normed_ffn, w_up))
        hidden = low(jax.nn.silu(gate) * up_part)
        return row_block + low_back(matrix(hidden, w_down))
    blocks = middle.reshape(token_total // block_rows, block_rows, D)
    return lax.map(jax.checkpoint(one_block), blocks).reshape(token_total, D)

def stream_forward(inputs_f, starts, w_qkv, conv_weight, w_beta, beta_bias, norm_attn, norm_head, w_out, norm_ffn, w_gate, w_up, w_down):
    token_total = inputs_f.shape[0]
    normed = low(rms_scale(inputs_f, norm_attn))
    projected = low(low_back(matrix(normed, w_qkv)))
    strength = jax.nn.sigmoid(low_back(matrix(normed, w_beta)) + beta_bias)
    indices = jnp.arange(token_total, dtype=jnp.int32)
    latest = lax.cummax(jnp.where(starts > 0.5, indices, 0).astype(jnp.int32), axis=0)
    distance = indices - latest
    mixed = jnp.zeros_like(projected)
    for tap_index in range(CONV):
        earlier = jnp.pad(projected, ((tap_index, 0), (0, 0)))[:token_total]
        allowed = (distance >= tap_index).astype(jnp.float32)[:, None]
        mixed = mixed + conv_weight[tap_index] * allowed * earlier
    active = jax.nn.silu(mixed)
    queries = low(unit_rows(active[:, :D].reshape(token_total, H, DH)))
    keys_in = low(unit_rows(active[:, D:2 * D].reshape(token_total, H, DH)))
    values_in = low(active[:, 2 * D:].reshape(token_total, H, DH))
    readout = delta_rule(queries, keys_in, values_in, strength, starts)
    normal_heads = low(rms_scale(readout, norm_head).reshape(token_total, D))
    middle = inputs_f + low_back(matrix(normal_heads, w_out))
    return feed_forward(middle, norm_ffn, w_gate, w_up, w_down)

def reference(tokens, cotangent, doc_stretches, w_qkv, conv_weight, w_beta, beta_bias, norm_attn, norm_head, w_out, norm_ffn, w_gate, w_up, w_down):
    weights = tuple((array_in.astype(jnp.float32) for array_in in (w_qkv, conv_weight, w_beta, beta_bias, norm_attn, norm_head, w_out, norm_ffn, w_gate, w_up, w_down)))
    stretch_ids = jnp.arange(STREAM_CH, dtype=jnp.int32)
    token_ids = jnp.arange(STREAM_TOK, dtype=jnp.int32)
    outputs = []
    input_grads = []
    totals = None
    for stream_index in range(STREAMS):
        lengths = doc_stretches[stream_index].astype(jnp.int32)
        begins = (jnp.cumsum(lengths) - lengths).astype(jnp.int32)
        stretch_flag = jnp.any(stretch_ids[:, None] == begins[None, :], axis=1)
        starts = ((token_ids % STRETCH == 0) & stretch_flag[token_ids // STRETCH]).astype(jnp.float32)

        def closed(inputs_f, *params):
            return stream_forward(inputs_f, starts, *params)
        result, pullback = jax.vjp(closed, tokens[stream_index].astype(jnp.float32), *weights)
        gradients = pullback(cotangent[stream_index].astype(jnp.float32))
        outputs.append(result)
        input_grads.append(gradients[0])
        if totals is None:
            totals = list(gradients[1:])
        else:
            totals = [first_op + second_op for first_op, second_op in zip(totals, gradients[1:])]
    return (jnp.stack(outputs).astype(jnp.bfloat16), jnp.stack(input_grads), totals[0], totals[1], totals[2], totals[3], totals[4], totals[5], totals[6], totals[7], totals[8], totals[9], totals[10])
```

```python
import functools

import jax
import jax.numpy as jnp
from jax import lax
from jax.experimental import pallas as pl
from jax.experimental.pallas import tpu as pltpu
from jax.sharding import PartitionSpec as P

STRETCH = 64
HALO = 16
EPSILON = 1e-06
F32 = jnp.float32
BF16 = jnp.bfloat16
AXES = ("stream", "span")
VMEM_LIMIT = 56 * 2**20


def nn(a, b):
    return lax.dot_general(a, b, (((1,), (0,)), ((), ())), preferred_element_type=F32)


def nt(a, b):
    return lax.dot_general(a, b, (((1,), (1,)), ((), ())), preferred_element_type=F32)


def tn(a, b):
    return lax.dot_general(a, b, (((0,), (0,)), ((), ())), preferred_element_type=F32)


def fine(a, b):
    a_hi = a.astype(BF16)
    a_lo = (a - a_hi.astype(F32)).astype(BF16)
    b_hi = b.astype(BF16)
    b_lo = (b - b_hi.astype(F32)).astype(BF16)
    return nn(jnp.concatenate([a_hi, a_hi, a_lo], 1), jnp.concatenate([b_hi, b_lo, b_hi], 0))


def grid_ids(size):
    return (
        lax.broadcasted_iota(jnp.int32, (size, size), 0),
        lax.broadcasted_iota(jnp.int32, (size, size), 1),
    )


def unit_inverse(lower_list):
    rows, cols = grid_ids(STRETCH)
    eye = (rows == cols).astype(F32)
    out = [eye - jnp.where((rows // 2) == (cols // 2), low, 0.0) for low in lower_list]
    half = 2
    while half < STRETCH:
        cross = ((rows // (2 * half)) == (cols // (2 * half))) & ((rows // half) != (cols // half))
        inner = [fine(jnp.where(cross, low, 0.0), inv) for low, inv in zip(lower_list, out)]
        out = [inv - fine(inv, mid) for inv, mid in zip(out, inner)]
        half *= 2
    return out


def column_of(table, index):
    lanes = lax.broadcasted_iota(jnp.int32, table.shape, 1)
    return jnp.sum(jnp.where(lanes == index, table, 0.0), -1, keepdims=True)


def mix_rows(ext_ref, conv_ref, allow):
    ext = ext_ref[...].astype(F32)
    conv = conv_ref[...].astype(F32)
    shifted = [
        (ext if tap == 0 else pltpu.roll(ext, tap, 0))[HALO:] * allow[tap]
        for tap in range(conv.shape[0])
    ]
    mixed = sum(conv[tap : tap + 1] * shifted[tap] for tap in range(conv.shape[0]))
    return shifted, mixed, conv


def local_kernel(
    keep_ref, eq_ref, ek_ref, ev_ref, cq_ref, ck_ref, cv_ref, rate_ref, allow_ref,
    q_ref, k_ref, v_ref, inv_ref, wk_ref, pre_ref, end_ref, read_ref, rmap_ref, nv_ref, np_ref,
):
    head = pl.program_id(0)
    allow_all = allow_ref[...]
    allow = [allow_all[:, tap : tap + 1] for tap in range(cq_ref.shape[0])]
    rate = column_of(rate_ref[...], head)

    def unit(ref, conv):
        _, mixed, _ = mix_rows(ref, conv, allow)
        act = mixed * jax.nn.sigmoid(mixed)
        return act

    act_q = unit(eq_ref, cq_ref)
    act_k = unit(ek_ref, ck_ref)
    act_v = unit(ev_ref, cv_ref)
    queries = (act_q * lax.rsqrt(jnp.sum(act_q * act_q, -1, keepdims=True) + EPSILON)).astype(BF16)
    keys = (act_k * lax.rsqrt(jnp.sum(act_k * act_k, -1, keepdims=True) + EPSILON)).astype(BF16)
    values = act_v.astype(BF16)
    q_ref[...] = queries
    k_ref[...] = keys
    v_ref[...] = values
    count = queries.shape[0] // STRETCH
    rows, cols = grid_ids(STRETCH)
    parts = [slice(n * STRETCH, (n + 1) * STRETCH) for n in range(count)]
    lows = []
    for part in parts:
        gram = nt(keys[part], keys[part])
        lows.append(jnp.where(rows > cols, gram * rate[part], 0.0))
    invs = unit_inverse(lows)
    size = keys.shape[1]
    drows, dcols = grid_ids(size)
    running = jnp.concatenate(
        [jnp.zeros((size, size), F32), (drows == dcols).astype(F32)], 0
    )
    for n, part in enumerate(parts):
        key, query = keys[part], queries[part]
        inv = invs[n].astype(BF16)
        inv_ref[0, part, :] = inv
        scaled = jnp.concatenate(
            [key.astype(F32) * rate[part], values[part].astype(F32) * rate[part]], 1
        ).astype(BF16)
        weighted = nn(inv, scaled)
        wkey = weighted[:, :size].astype(BF16)
        wk_ref[part, :] = wkey
        running = running * keep_ref[n]
        low_state = running.astype(BF16)
        pre_ref[0, n] = low_state
        back = nt(jnp.concatenate([wkey, query], 0), low_state)
        new = jnp.concatenate(
            [weighted[:, size:] - back[:STRETCH, :size], -back[:STRETCH, size:]], 1
        ).astype(BF16)
        nv_ref[part, :] = new[:, :size]
        np_ref[part, :] = new[:, size:]
        scores = jnp.where(rows >= cols, nt(query, key), 0.0).astype(BF16)
        out = back[STRETCH:] + nn(scores, new)
        read_ref[part, :] = out[:, :size]
        rmap_ref[part, :] = out[:, size:].astype(BF16)
        running = running + tn(new, key)
    end_ref[0] = running.astype(BF16)


def local_call(keep, ext, conv, rate, allow, heads):
    tok = rate.shape[0]
    width = ext.shape[1] // 3
    size = width // heads
    count = tok // STRETCH
    taps = conv.shape[0]
    rows = ext.shape[0]

    def third(i, r):
        return pl.BlockSpec((r, size), lambda h: (0, h + i * heads))

    def token_block():
        return pl.BlockSpec((tok, size), lambda h: (0, h))

    return pl.pallas_call(
        local_kernel,
        grid=(heads,),
        in_specs=[
            pl.BlockSpec(memory_space=pltpu.SMEM),
            third(0, rows), third(1, rows), third(2, rows),
            third(0, taps), third(1, taps), third(2, taps),
            pl.BlockSpec((tok, heads), lambda h: (0, 0)),
            pl.BlockSpec((tok, taps), lambda h: (0, 0)),
        ],
        out_specs=[
            token_block(), token_block(), token_block(),
            pl.BlockSpec((1, tok, STRETCH), lambda h: (h, 0, 0)),
            token_block(),
            pl.BlockSpec((1, count, 2 * size, size), lambda h: (h, 0, 0, 0)),
            pl.BlockSpec((1, 2 * size, size), lambda h: (h, 0, 0)),
            token_block(), token_block(), token_block(), token_block(),
        ],
        out_shape=[
            jax.ShapeDtypeStruct((tok, width), BF16),
            jax.ShapeDtypeStruct((tok, width), BF16),
            jax.ShapeDtypeStruct((tok, width), BF16),
            jax.ShapeDtypeStruct((heads, tok, STRETCH), BF16),
            jax.ShapeDtypeStruct((tok, width), BF16),
            jax.ShapeDtypeStruct((heads, count, 2 * size, size), BF16),
            jax.ShapeDtypeStruct((heads, 2 * size, size), BF16),
            jax.ShapeDtypeStruct((tok, width), F32),
            jax.ShapeDtypeStruct((tok, width), BF16),
            jax.ShapeDtypeStruct((tok, width), BF16),
            jax.ShapeDtypeStruct((tok, width), BF16),
        ],
        compiler_params=pltpu.CompilerParams(vmem_limit_bytes=VMEM_LIMIT),
        cost_estimate=pl.CostEstimate(flops=2 * 10**9, bytes_accessed=10**7, transcendentals=10**6),
        name="delta_local",
    )(keep, ext, ext, ext, conv, conv, conv, rate, allow)


def readout_kernel(state_ref, read_ref, rmap_ref, gain_ref, out_ref, normal_ref):
    readout = read_ref[...] + nt(rmap_ref[...], state_ref[0])
    inv = lax.rsqrt(jnp.mean(readout * readout, -1, keepdims=True) + EPSILON)
    out_ref[...] = readout
    normal_ref[...] = (readout * inv * gain_ref[...]).astype(BF16)


def readout_call(state, read, rmap, gain):
    heads, size, _ = state.shape
    tok, width = read.shape
    block = pl.BlockSpec((tok, size), lambda h: (0, h))
    return pl.pallas_call(
        readout_kernel,
        grid=(heads,),
        in_specs=[
            pl.BlockSpec((1, size, size), lambda h: (h, 0, 0)),
            block, block,
            pl.BlockSpec((1, size), lambda h: (0, 0)),
        ],
        out_specs=[block, block],
        out_shape=[
            jax.ShapeDtypeStruct((tok, width), F32),
            jax.ShapeDtypeStruct((tok, width), BF16),
        ],
        compiler_params=pltpu.CompilerParams(vmem_limit_bytes=VMEM_LIMIT),
        cost_estimate=pl.CostEstimate(flops=10**8, bytes_accessed=4 * 10**6, transcendentals=2000),
        name="delta_readout",
    )(state, read, rmap, gain)


def adjoint_kernel(
    keep_ref, gn_ref, read_ref, gain_ref, q_ref, k_ref, wk_ref, go_ref, adj_ref, gain_grad_ref
):
    grad, readout = gn_ref[...], read_ref[...]
    inv = lax.rsqrt(jnp.mean(readout * readout, -1, keepdims=True) + EPSILON)
    scaled = grad * gain_ref[...]
    grad_read = inv * scaled - readout * (inv * inv * inv) * jnp.mean(
        scaled * readout, -1, keepdims=True
    )
    gain_grad_ref[0] = jnp.sum(grad * readout * inv, 0, keepdims=True)
    grad_read = grad_read.astype(BF16)
    go_ref[...] = grad_read
    count = grad.shape[0] // STRETCH
    rows, cols = grid_ids(STRETCH)
    size = grad.shape[1]
    adj = jnp.zeros((size, size), F32)
    for n in range(count - 1, -1, -1):
        part = slice(n * STRETCH, (n + 1) * STRETCH)
        key, query, out = k_ref[part, :], q_ref[part, :], grad_read[part]
        scores = jnp.where(rows >= cols, nt(query, key), 0.0).astype(BF16)
        new_grad = tn(scores, out) + nt(key, adj.astype(BF16))
        adj = (
            adj
            + tn(
                jnp.concatenate([out, (-new_grad).astype(BF16)], 0),
                jnp.concatenate([query, wk_ref[part, :]], 0),
            )
        ) * keep_ref[n]
    adj_ref[0] = adj.astype(BF16)


def adjoint_call(keep, grad_normal, readout, gain, queries, keys, wkeys, heads):
    tok, width = readout.shape
    size = width // heads
    block = pl.BlockSpec((tok, size), lambda h: (0, h))
    return pl.pallas_call(
        adjoint_kernel,
        grid=(heads,),
        in_specs=[
            pl.BlockSpec(memory_space=pltpu.SMEM),
            block, block,
            pl.BlockSpec((1, size), lambda h: (0, 0)),
            block, block, block,
        ],
        out_specs=[
            block,
            pl.BlockSpec((1, size, size), lambda h: (h, 0, 0)),
            pl.BlockSpec((1, 1, size), lambda h: (h, 0, 0)),
        ],
        out_shape=[
            jax.ShapeDtypeStruct((tok, width), BF16),
            jax.ShapeDtypeStruct((heads, size, size), BF16),
            jax.ShapeDtypeStruct((heads, 1, size), F32),
        ],
        compiler_params=pltpu.CompilerParams(vmem_limit_bytes=VMEM_LIMIT),
        cost_estimate=pl.CostEstimate(flops=5 * 10**8, bytes_accessed=6 * 10**6, transcendentals=0),
        name="delta_adjoint",
    )(keep, grad_normal, readout, gain, queries, keys, wkeys)


def backward_kernel(
    keep_ref, din_ref, min_ref, pre_ref, go_ref, q_ref, k_ref, v_ref, inv_ref, wk_ref,
    nv_ref, np_ref, rate_ref, allow_ref,
    eq_ref, ek_ref, ev_ref, cq_ref, ck_ref, cv_ref,
    gext_ref, gconv_ref, grate_ref,
    gq_buf, gk_buf, gv_buf,
):
    head = pl.program_id(0)
    size = q_ref.shape[1]
    tok = q_ref.shape[0]
    count = tok // STRETCH
    rows, cols = grid_ids(STRETCH)
    rate = column_of(rate_ref[...], head)
    low_in = min_ref[0]
    adj = din_ref[0].astype(F32)
    grate_parts = [None] * count
    for n in range(count - 1, -1, -1):
        part = slice(n * STRETCH, (n + 1) * STRETCH)
        key, query, value, out = k_ref[part, :], q_ref[part, :], v_ref[part, :], go_ref[part, :]
        beta = rate[part]
        pre = pre_ref[0, n]
        state = (nn(low_in, pre[size:]) + pre[:size].astype(F32)).astype(BF16)
        new = (nt(np_ref[part, :], low_in) + nv_ref[part, :].astype(F32)).astype(BF16)
        low_adj = adj.astype(BF16)
        gram_both = nt(jnp.concatenate([key, query], 0), key)
        gram = gram_both[:STRETCH]
        scores = jnp.where(rows >= cols, gram_both[STRETCH:], 0.0).astype(BF16)
        new_grad = tn(scores, out) + nt(key, low_adj)
        low_new_grad = new_grad.astype(BF16)
        adj = (
            adj
            + tn(
                jnp.concatenate([out, -low_new_grad], 0),
                jnp.concatenate([query, wk_ref[part, :]], 0),
            )
        ) * keep_ref[n]
        grad_b = tn(inv_ref[0, part, :], low_new_grad)
        both = nt(jnp.concatenate([out, grad_b.astype(BF16)], 0), new)
        grad_scores = jnp.where(rows >= cols, both[:STRETCH], 0.0).astype(BF16)
        grad_low = jnp.where(rows > cols, -both[STRETCH:], 0.0)
        left = value.astype(F32) - nt(key, state)
        grate_parts[n] = jnp.sum(grad_low * gram, -1, keepdims=True) + jnp.sum(
            grad_b * left, -1, keepdims=True
        )
        grad_v = beta * grad_b
        grad_gram = beta * grad_low
        symmetric = (grad_gram + grad_gram.T).astype(BF16)
        by_state = nn(jnp.concatenate([out, -grad_v.astype(BF16)], 0), state)
        gq_buf[part, :] = by_state[:STRETCH] + nn(grad_scores, key)
        gk_buf[part, :] = (
            by_state[STRETCH:]
            + tn(grad_scores, query)
            + nn(jnp.concatenate([new, symmetric], 1), jnp.concatenate([low_adj, key], 0))
        )
        gv_buf[part, :] = grad_v
    grate = jnp.concatenate(grate_parts, 0)
    lanes = lax.broadcasted_iota(jnp.int32, grate_ref.shape, 1)
    before = jnp.where(head == 0, jnp.zeros(grate_ref.shape, F32), grate_ref[...])
    grate_ref[...] = jnp.where(lanes == head, grate, before)
    allow_all = allow_ref[...]
    allow = [allow_all[:, tap : tap + 1] for tap in range(cq_ref.shape[0])]
    zeros = jnp.zeros((HALO, size), F32)
    for i, (ext, conv_ref, buf) in enumerate(
        ((eq_ref, cq_ref, gq_buf), (ek_ref, ck_ref, gk_buf), (ev_ref, cv_ref, gv_buf))
    ):
        shifted, mixed, conv = mix_rows(ext, conv_ref, allow)
        sig = jax.nn.sigmoid(mixed)
        grad = buf[...]
        if i < 2:
            raw = mixed * sig
            inv = lax.rsqrt(jnp.sum(raw * raw, -1, keepdims=True) + EPSILON)
            grad = inv * grad - raw * (inv * inv * inv) * jnp.sum(grad * raw, -1, keepdims=True)
        grad = grad * (sig * (1.0 + mixed * (1.0 - sig)))
        total = None
        for tap in range(conv.shape[0]):
            gconv_ref[i, tap : tap + 1, :] = jnp.sum(grad * shifted[tap], 0, keepdims=True)
            term = jnp.concatenate([zeros, grad * (conv[tap : tap + 1] * allow[tap])], 0)
            if tap:
                term = pltpu.roll(term, tok + HALO - tap, 0)
            total = term if total is None else total + term
        gext_ref[i] = total.astype(BF16)


def backward_call(
    keep, state_grad, state, prefix, grad_read, queries, keys, values, invs, wkeys,
    new_v, new_p, rate, allow, ext, conv, heads,
):
    tok, width = queries.shape
    size = width // heads
    count = tok // STRETCH
    taps = conv.shape[0]
    rows = ext.shape[0]
    block = pl.BlockSpec((tok, size), lambda h: (0, h))
    square = pl.BlockSpec((1, size, size), lambda h: (h, 0, 0))

    def third(i, r):
        return pl.BlockSpec((r, size), lambda h: (0, h + i * heads))

    return pl.pallas_call(
        backward_kernel,
        grid=(heads,),
        in_specs=[
            pl.BlockSpec(memory_space=pltpu.SMEM),
            square, square,
            pl.BlockSpec((1, count, 2 * size, size), lambda h: (h, 0, 0, 0)),
            block, block, block, block,
            pl.BlockSpec((1, tok, STRETCH), lambda h: (h, 0, 0)),
            block, block, block,
            pl.BlockSpec((tok, heads), lambda h: (0, 0)),
            pl.BlockSpec((tok, taps), lambda h: (0, 0)),
            third(0, rows), third(1, rows), third(2, rows),
            third(0, taps), third(1, taps), third(2, taps),
        ],
        out_specs=[
            pl.BlockSpec((3, rows, size), lambda h: (0, 0, h)),
            pl.BlockSpec((3, taps, size), lambda h: (0, 0, h)),
            pl.BlockSpec((tok, heads), lambda h: (0, 0)),
        ],
        out_shape=[
            jax.ShapeDtypeStruct((3, rows, width), BF16),
            jax.ShapeDtypeStruct((3, taps, width), F32),
            jax.ShapeDtypeStruct((tok, heads), F32),
        ],
        scratch_shapes=[pltpu.VMEM((tok, size), F32)] * 3,
        compiler_params=pltpu.CompilerParams(vmem_limit_bytes=VMEM_LIMIT),
        cost_estimate=pl.CostEstimate(flops=2 * 10**9, bytes_accessed=12 * 10**6, transcendentals=10**6),
        name="delta_backward",
    )(
        keep, state_grad, state, prefix, grad_read, queries, keys, values, invs, wkeys,
        new_v, new_p, rate, allow, ext, ext, ext, conv, conv, conv,
    )


def silu_slope(pre_act, sig_value):
    return sig_value * (1.0 + pre_act * (1.0 - sig_value))


def norm_back(grad_in, values, inv_rms, gain_vec):
    scaled = grad_in * gain_vec
    return inv_rms * scaled - values * inv_rms**3 * jnp.mean(scaled * values, -1, keepdims=True)


def product(pattern, first, second, kind=F32):
    return jnp.einsum(pattern, first, second, preferred_element_type=F32).astype(kind)


def swap_core(block):
    streams, spans = lax.axis_size("stream"), lax.axis_size("span")
    pairs = [
        (s * spans + p, s * spans + (p ^ 1)) for s in range(streams) for p in range(spans)
    ]
    return lax.ppermute(block, AXES, pairs)


def pair_tokens(block):
    return jnp.concatenate([block, swap_core(block)], 0)


def pair_columns(block, spans):
    core = lax.axis_index("span") % 2
    rows, width = block.shape
    split = block.reshape(rows, spans // 2, 2, width // spans)
    mine = lax.dynamic_index_in_dim(split, core, 2, keepdims=False).reshape(rows, -1)
    theirs = lax.dynamic_index_in_dim(split, 1 - core, 2, keepdims=False).reshape(rows, -1)
    return jnp.concatenate([mine, swap_core(theirs)], 0)


def weight_grad(left, right, spans):
    grad = product("td,te->de", left, right, BF16)
    return grad.reshape(spans // 2, -1, grad.shape[1])


MESH = pl.DeviceIdType.MESH


class Place:
    def __init__(self, streams, spans):
        self.streams, self.spans, self.chips = streams, spans, spans // 2
        self.stream = lax.axis_index("stream")
        self.span = lax.axis_index("span")
        self.chip = lax.div(self.span, 2)
        self.core = lax.rem(self.span, 2)

    def beside(self, step):
        return (self.stream ^ step, self.span)

    def along(self, step):
        return (self.stream, 2 * self.shifted(step) + self.core)

    def shifted(self, step):
        return lax.rem(self.chip + step + self.chips, self.chips)

    def other(self):
        return (self.stream, 2 * self.chip + 1 - self.core)


def greet(places):
    barrier = pltpu.get_barrier_semaphore()
    for target in places:
        pl.semaphore_signal(barrier, inc=1, device_id=target, device_id_type=MESH)
    pl.semaphore_wait(barrier, len(places))


def quarter_of(rows, width, streams):
    if (width // 128) % streams == 0:
        return 1, streams
    return 2, streams // 2


def quarter_index(rows, width, streams, at, piece=0, pieces=1):
    down, across = quarter_of(rows, width, streams)
    r, c = rows // down, width // across
    row = pl.ds(0, rows) if down == 1 else pl.ds(pl.multiple_of(lax.div(at, across) * r, r), r)
    start = lax.rem(at, across) * c + piece * (c // pieces)
    return row, pl.ds(pl.multiple_of(start, 128), c // pieces)


def copy_to(source, target, send_sem, recv_sem, device):
    return pltpu.make_async_remote_copy(
        src_ref=source, dst_ref=target, send_sem=send_sem, recv_sem=recv_sem,
        device_id=device, device_id_type=MESH,
    )


class Gather:
    def __init__(self, place, shards, fulls, sems):
        self.place, self.shards, self.fulls = place, shards, fulls
        self.sems = sems
        self.units = []
        for w, shard in enumerate(shards):
            rows, width = shard.shape
            _, across = quarter_of(rows, width, place.streams)
            pieces = 2 if (width // across) % 256 == 0 else 1
            for piece in range(pieces):
                self.units.append((w, piece, pieces))

    @staticmethod
    def sem_shapes(shapes, streams, spans):
        units = 0
        for rows, width in shapes:
            _, across = quarter_of(rows, width, streams)
            units += 2 if (width // across) % 256 == 0 else 1
        slots = spans // 2
        dma = pltpu.SemaphoreType.DMA
        return [dma((units, slots, 4, 2)), dma((len(shapes), slots, 2)), dma((len(shapes),))]

    def part(self, unit, at, span=None):
        w, piece, pieces = self.units[unit]
        rows, width = self.shards[w].shape
        index = quarter_index(rows, width, self.place.streams, at, piece, pieces)
        if span is None:
            return self.shards[w].at[index]
        return self.fulls[w].at[(span,) + index]

    def source_span(self, k):
        return 2 * self.place.shifted(-k) + self.place.core

    def wire(self, unit, k, kind, span, at, device, source=None):
        region = self.part(unit, at, span)
        return copy_to(
            region if source is None else source, region,
            self.sems[0].at[unit, k, kind, 0], self.sems[0].at[unit, k, kind, 1], device,
        )

    def along(self, unit, k):
        p = self.place
        return self.wire(
            unit, k, 0, p.span, p.stream, p.along(k), self.part(unit, p.stream)
        )

    def along_wait(self, unit, k):
        p = self.place
        self.wire(unit, k, 0, self.source_span(k), p.stream, p.along(k)).wait_recv()

    def sideways(self, unit, k, step):
        p = self.place
        return self.wire(unit, k, step, self.source_span(k), p.stream, p.beside(step))

    def sideways_wait(self, unit, k, step):
        p = self.place
        self.wire(
            unit, k, step, self.source_span(k), p.stream ^ step, p.beside(step)
        ).wait_recv()

    def corner(self, unit, k):
        p = self.place
        first, second = (1, 2) if unit % 2 == 0 else (2, 1)
        return self.wire(
            unit, k, 3, self.source_span(k), p.stream ^ first, p.beside(second)
        )

    def corner_wait(self, unit, k):
        p = self.place
        self.wire(unit, k, 3, self.source_span(k), p.stream ^ 3, p.beside(1)).wait_recv()

    def across(self, w, k):
        p = self.place
        span = p.span if k == 0 else self.source_span(k)
        region = self.fulls[w].at[span]
        return copy_to(
            self.shards[w] if k == 0 else region, region,
            self.sems[1].at[w, k, 0], self.sems[1].at[w, k, 1], p.other(),
        )

    def across_wait(self, w, k):
        p = self.place
        span = 2 * p.shifted(-k) + 1 - p.core
        region = self.fulls[w].at[span]
        copy_to(
            region, region, self.sems[1].at[w, k, 0], self.sems[1].at[w, k, 1], p.other()
        ).wait_recv()

    def own(self, w):
        return pltpu.make_async_copy(
            self.shards[w], self.fulls[w].at[self.place.span], self.sems[2].at[w]
        )

    def neighbours(self):
        p = self.place
        return (
            [p.along(k) for k in range(1, p.chips)] + [p.beside(1), p.beside(2), p.other()]
        )

    def steps(self):
        p = self.place
        slots = range(1, p.chips)
        count = len(self.units)
        ends = {}
        for unit, (w, piece, pieces) in enumerate(self.units):
            if piece == pieces - 1:
                ends[unit] = w
        steps = []

        def begin(unit):
            w, piece, pieces = self.units[unit]
            for k in slots:
                self.along(unit, k).start()
            if piece == 0:
                self.across(w, 0).start()
                self.own(w).start()

        def beside(unit, k):
            self.along_wait(unit, k)
            self.sideways(unit, k, 1).start()
            self.sideways(unit, k, 2).start()

        def turn(unit, k):
            self.sideways_wait(unit, k, 1 if unit % 2 == 0 else 2)
            self.corner(unit, k).start()

        def close(w, k):
            for unit, (owner, _, _) in enumerate(self.units):
                if owner == w:
                    self.sideways_wait(unit, k, 2 if unit % 2 == 0 else 1)
                    self.corner_wait(unit, k)
            self.across(w, k).start()

        def finish(w):
            for k in range(p.chips):
                self.across_wait(w, k)
                self.across(w, k).wait_send()
            self.own(w).wait()
            for unit, (owner, _, _) in enumerate(self.units):
                if owner == w:
                    for k in slots:
                        self.along(unit, k).wait_send()
                        self.sideways(unit, k, 1).wait_send()
                        self.sideways(unit, k, 2).wait_send()
                        self.corner(unit, k).wait_send()

        for unit in range(min(2, count)):
            steps.append(functools.partial(begin, unit))
        for turn_at in range(count + 2):
            if turn_at + 2 < count:
                steps.append(functools.partial(begin, turn_at + 2))
            if turn_at < count:
                steps += [functools.partial(beside, turn_at, k) for k in slots]
            if 0 <= turn_at - 1 < count:
                steps += [functools.partial(turn, turn_at - 1, k) for k in slots]
            if turn_at - 2 in ends:
                steps += [functools.partial(close, ends[turn_at - 2], k) for k in slots]
        steps += [functools.partial(finish, w) for w in range(len(self.shards))]
        return steps


def gather_kernel(streams, spans, count, *refs):
    shards, fulls, sems = refs[:count], refs[count : 2 * count], refs[2 * count :]
    place = Place(streams, spans)
    work = Gather(place, shards, fulls, sems)
    greet(work.neighbours())
    for step in work.steps():
        step()


def gather_call(shards, collective_id):
    streams, spans = lax.axis_size("stream"), lax.axis_size("span")
    shapes = [shard.shape for shard in shards]
    outs = pl.pallas_call(
        functools.partial(gather_kernel, streams, spans, len(shards)),
        in_specs=[pl.BlockSpec(memory_space=pl.ANY)] * len(shards),
        out_specs=[pl.BlockSpec(memory_space=pl.ANY)] * len(shards),
        out_shape=[jax.ShapeDtypeStruct((spans,) + s.shape, s.dtype) for s in shards],
        scratch_shapes=Gather.sem_shapes(shapes, streams, spans),
        compiler_params=pltpu.CompilerParams(
            collective_id=collective_id, has_side_effects=True, vmem_limit_bytes=VMEM_LIMIT
        ),
        name="gather_weights",
    )(*shards)
    return outs


class Reduce:
    def __init__(self, place, grads, outs, bufs, sems):
        self.place, self.grads, self.outs, self.bufs, self.sems = place, grads, outs, bufs, sems

    @staticmethod
    def block(shape, streams):
        _, rows, width = shape
        down, across = quarter_of(rows, width, streams)
        return rows // down, width // across

    @staticmethod
    def scratch(shapes, streams):
        out = []
        dma = pltpu.SemaphoreType.DMA
        for shape in shapes:
            chips = shape[0]
            r, c = Reduce.block(shape, streams)
            out += [
                pltpu.VMEM((2, chips, r, c), BF16),
                pltpu.VMEM((2, chips, r, c), BF16),
                pltpu.VMEM((chips, r, c), BF16),
                pltpu.VMEM((chips, r, c), BF16),
                pltpu.VMEM((chips, r, c), BF16),
                pltpu.VMEM((streams, r, c), BF16),
            ]
        n = len(shapes)
        chips = shapes[0][0]
        out += [dma((n, 2, 3, 2)), dma((n, chips, 2)), dma((n, streams, 2))]
        return out

    def turn(self, w, half):
        return (1, 2) if (w + half) % 2 == 0 else (2, 1)

    def chips_of(self, half):
        n = self.place.chips // 2
        return half * n, n

    def region(self, w, half, at):
        _, rows, width = self.grads[w].shape
        start, n = self.chips_of(half)
        return (pl.ds(start, n),) + quarter_index(rows, width, self.place.streams, at)

    def first(self, w, half, slot):
        p = self.place
        a, b = self.turn(w, half)
        start, n = self.chips_of(half)
        at = p.stream ^ a if slot == 0 else p.stream ^ a ^ b
        return copy_to(
            self.grads[w].at[self.region(w, half, at)],
            self.bufs[w][0].at[slot, pl.ds(start, n)],
            self.sems[0].at[w, half, slot, 0], self.sems[0].at[w, half, slot, 1], p.beside(a),
        )

    def second(self, w, half):
        p = self.place
        _, b = self.turn(w, half)
        start, n = self.chips_of(half)
        return copy_to(
            self.bufs[w][1].at[1, pl.ds(start, n)], self.bufs[w][2].at[pl.ds(start, n)],
            self.sems[0].at[w, half, 2, 0], self.sems[0].at[w, half, 2, 1], p.beside(b),
        )

    def third(self, w, k):
        p = self.place
        return copy_to(
            self.bufs[w][3].at[p.shifted(k)], self.bufs[w][4].at[k],
            self.sems[1].at[w, k, 0], self.sems[1].at[w, k, 1], p.along(k),
        )

    def fourth(self, w, step):
        p = self.place
        return copy_to(
            self.bufs[w][5].at[0], self.bufs[w][5].at[step],
            self.sems[2].at[w, step, 0], self.sems[2].at[w, step, 1], p.beside(step),
        )

    def neighbours(self):
        p = self.place
        return [p.along(k) for k in range(1, p.chips)] + [
            p.beside(s) for s in range(1, p.streams)
        ]

    def begin(self, w):
        for half in range(2):
            for slot in (1, 0):
                self.first(w, half, slot).start()

    def add_first(self, w, half):
        p = self.place
        _, b = self.turn(w, half)
        start, n = self.chips_of(half)
        for slot in (1, 0):
            self.first(w, half, slot).wait_recv()
            at = p.stream ^ b if slot else p.stream
            _, row, col = self.region(w, half, at)
            for chip in range(start, start + n):
                self.bufs[w][1][slot, chip] = (
                    self.grads[w][chip, row, col].astype(F32)
                    + self.bufs[w][0][slot, chip].astype(F32)
                ).astype(BF16)
            if slot:
                self.second(w, half).start()

    def add_second(self, w, half):
        start, n = self.chips_of(half)
        self.second(w, half).wait_recv()
        for chip in range(start, start + n):
            self.bufs[w][3][chip] = (
                self.bufs[w][1][0, chip].astype(F32) + self.bufs[w][2][chip].astype(F32)
            ).astype(BF16)

    def spread(self, w):
        for k in range(1, self.place.chips):
            self.third(w, k).start()

    def add_third(self, w):
        p = self.place
        total = self.bufs[w][3][p.chip].astype(F32)
        for k in range(1, p.chips):
            self.third(w, k).wait_recv()
            total = total + self.bufs[w][4][k].astype(F32)
        self.bufs[w][5][0] = total.astype(BF16)
        for step in range(1, p.streams):
            self.fourth(w, step).start()

    def finish(self, w):
        p = self.place
        _, rows, width = self.grads[w].shape
        for step in range(p.streams):
            if step:
                self.fourth(w, step).wait_recv()
            row, col = quarter_index(rows, width, p.streams, p.stream ^ step)
            self.outs[w][row, col] = self.bufs[w][5][step]
        for half in range(2):
            for slot in range(2):
                self.first(w, half, slot).wait_send()
            self.second(w, half).wait_send()
        for k in range(1, p.chips):
            self.third(w, k).wait_send()
        for step in range(1, p.streams):
            self.fourth(w, step).wait_send()

    def steps(self):
        count = len(self.grads)
        steps = [functools.partial(self.begin, w) for w in range(count)]
        for t in range(count + 3):
            if t < count:
                steps += [functools.partial(self.add_first, t, half) for half in range(2)]
            if 0 <= t - 1 < count:
                steps += [functools.partial(self.add_second, t - 1, half) for half in range(2)]
                steps.append(functools.partial(self.spread, t - 1))
            if 0 <= t - 2 < count:
                steps.append(functools.partial(self.add_third, t - 2))
            if 0 <= t - 3 < count:
                steps.append(functools.partial(self.finish, t - 3))
        return steps


def reduce_kernel(streams, spans, count, *refs):
    grads, outs, rest = refs[:count], refs[count : 2 * count], refs[2 * count :]
    bufs = [rest[6 * w : 6 * w + 6] for w in range(count)]
    work = Reduce(Place(streams, spans), grads, outs, bufs, rest[6 * count :])
    greet(work.neighbours())
    for step in work.steps():
        step()


def reduce_call(grads, collective_id):
    streams, spans = lax.axis_size("stream"), lax.axis_size("span")
    shapes = [grad.shape for grad in grads]
    vmem = pl.BlockSpec(memory_space=pltpu.VMEM)
    return pl.pallas_call(
        functools.partial(reduce_kernel, streams, spans, len(grads)),
        in_specs=[vmem] * len(grads),
        out_specs=[vmem] * len(grads),
        out_shape=[jax.ShapeDtypeStruct(s[1:], BF16) for s in shapes],
        scratch_shapes=Reduce.scratch(shapes, streams),
        compiler_params=pltpu.CompilerParams(
            collective_id=collective_id, has_side_effects=True, vmem_limit_bytes=VMEM_LIMIT
        ),
        name="reduce_grads",
    )(*grads)


def chain_kernel(streams, spans, backward, *refs):
    p = Place(streams, spans)
    if backward:
        (adj_ref, p_low, p_high, p_chip, state_ref,
         swap, carry, outgo, sent, swap_sem, hop_sem, back_sem) = refs
    else:
        (map_ref, state_ref, p_low, p_high, p_chip,
         swap, carry, outgo, sent, s_chip, swap_sem, hop_sem, back_sem) = refs
    source = adj_ref if backward else map_ref
    heads, size = source.shape[0], source.shape[2]
    half = heads // 2
    mine = p.core * half
    theirs = (1 - p.core) * half
    ahead, behind = (-1, 1) if backward else (1, -1)
    edge_in = p.chips - 1 if backward else 0
    edge_out = 0 if backward else p.chips - 1
    greet([p.other(), p.along(1), p.along(-1)])
    swap_copy = copy_to(
        source.at[pl.ds(theirs, half)], swap, swap_sem.at[0], swap_sem.at[1], p.other()
    )
    swap_copy.start()
    swap_copy.wait_recv()
    low_core = p.core == 0
    for h in range(half):
        own, got = source[mine + h], swap[h]
        low = jnp.where(low_core, own, got)
        high = jnp.where(low_core, got, own)
        if backward:
            outgo[h] = low.astype(F32) + nt(high, p_low[h])
        else:
            joined = nn(low, high[size:])
            s_chip[h] = joined[:size] + high[:size].astype(F32)
            p_chip[h] = joined[size:].astype(BF16)
            p_low[h] = low[size:]
            p_high[h] = high[size:]
            outgo[h] = low[:size].astype(F32)

    def hop(h):
        return copy_to(
            sent.at[h], carry.at[h], hop_sem.at[h, 0], hop_sem.at[h, 1], p.along(ahead)
        )

    @pl.when(p.chip == edge_in)
    def _():
        carry[...] = jnp.zeros(carry.shape, BF16)

    for h in range(half):

        @pl.when(p.chip != edge_in)
        def _():
            hop(h).wait_recv()

        moved = nt(carry[h], p_chip[h]) + outgo[h] if backward else nn(carry[h], p_chip[h]) + s_chip[h]
        sent[h] = moved.astype(BF16)

        @pl.when(p.chip != edge_out)
        def _():
            hop(h).start()

    for h in range(half):
        state = carry[h]
        if backward:
            low_state = (nt(state, p_high[h]) + jnp.where(low_core, swap[h], source[mine + h]).astype(F32)).astype(BF16)
            keep = jnp.where(low_core, low_state, state)
            give = jnp.where(low_core, state, low_state)
        else:
            high_state = (nn(state, p_low[h]) + outgo[h]).astype(BF16)
            keep = jnp.where(low_core, state, high_state)
            give = jnp.where(low_core, high_state, state)
        state_ref[mine + h] = keep
        sent[half + h] = give
    back = copy_to(
        sent.at[pl.ds(half, half)], state_ref.at[pl.ds(mine, half)],
        back_sem.at[0], back_sem.at[1], p.other(),
    )
    back.start()
    copy_to(
        sent.at[pl.ds(half, half)], state_ref.at[pl.ds(theirs, half)],
        back_sem.at[0], back_sem.at[1], p.other(),
    ).wait_recv()
    back.wait_send()
    swap_copy.wait_send()

    @pl.when(p.chip != edge_out)
    def _():
        for h in range(half):
            hop(h).wait_send()


def chain_call(maps, carried, collective_id):
    streams, spans = lax.axis_size("stream"), lax.axis_size("span")
    backward = carried is not None
    heads, size = maps.shape[0], maps.shape[2]
    half = heads // 2
    vmem = pl.BlockSpec(memory_space=pltpu.VMEM)
    dma = pltpu.SemaphoreType.DMA
    square = jax.ShapeDtypeStruct((half, size, size), BF16)
    state = jax.ShapeDtypeStruct((heads, size, size), BF16)
    scratch = [
        pltpu.VMEM((half,) + maps.shape[1:], BF16),
        pltpu.VMEM((half, size, size), BF16),
        pltpu.VMEM((half, size, size), F32),
        pltpu.VMEM((heads, size, size), BF16),
    ]
    if not backward:
        scratch.append(pltpu.VMEM((half, size, size), F32))
    scratch += [dma((2,)), dma((half, 2)), dma((2,))]
    operands = [maps] + (list(carried) if backward else [])
    return pl.pallas_call(
        functools.partial(chain_kernel, streams, spans, backward),
        in_specs=[vmem] * len(operands),
        out_specs=[vmem] * (1 if backward else 4),
        out_shape=[state] if backward else [state, square, square, square],
        scratch_shapes=scratch,
        compiler_params=pltpu.CompilerParams(
            collective_id=collective_id, has_side_effects=True, vmem_limit_bytes=VMEM_LIMIT
        ),
        name="span_chain",
    )(*operands)


def local(
    tokens, cotangent, doc_stretches, w_qkv, conv_weight, w_beta, beta_bias, norm_attn, norm_head,
    w_out, norm_ffn, w_gate, w_up, w_down,
):
    tok_rows, model_width = tokens.shape[1:]
    heads = beta_bias.shape[0]
    size = model_width // heads
    count = tok_rows // STRETCH
    span_count = lax.axis_size("span")
    place = lax.axis_index("span")
    taps = conv_weight.shape[0]

    small = jnp.concatenate(
        [x.reshape(-1) for x in (conv_weight, w_beta, norm_attn, norm_ffn, norm_head)]
    )
    small_len = small.shape[0]
    small = jnp.pad(small, (0, 16 * 512 - small_len)).reshape(16, 512)
    full_qkv, smalls = gather_call([w_qkv, small], 1)
    full_out, full_gate, full_up, full_down = gather_call([w_out, w_gate, w_up, w_down], 2)
    full_qkv, full_out, full_gate, full_up, full_down = (
        w.reshape(-1, w.shape[2]) for w in (full_qkv, full_out, full_gate, full_up, full_down)
    )
    smalls = smalls.reshape(span_count, -1)

    def small_part(shape, start):
        length = 1
        for dim in shape:
            length *= dim
        return smalls[:, start : start + length].reshape((span_count,) + shape), start + length

    at = 0
    full_conv, at = small_part(conv_weight.shape, at)
    full_beta, at = small_part(w_beta.shape, at)
    gain_attn, at = small_part(norm_attn.shape, at)
    gain_ffn, at = small_part(norm_ffn.shape, at)
    gain_head, at = small_part(norm_head.shape, at)
    full_conv = jnp.swapaxes(full_conv, 0, 1).reshape(taps, -1)
    full_beta = full_beta.reshape(-1, heads)
    attn_gain = gain_attn.reshape(-1).astype(F32)
    ffn_gain = gain_ffn.reshape(-1).astype(F32)
    head_gain = gain_head.reshape(1, -1).astype(F32)

    stretch_ids = place * count + jnp.arange(count, dtype=jnp.int32)
    doc_lengths = doc_stretches[0]
    doc_begins = jnp.cumsum(doc_lengths) - doc_lengths
    stretch_start = jnp.any(stretch_ids[:, None] == doc_begins[None, :], axis=1).astype(F32)
    stretch_keep = 1.0 - stretch_start
    token_start = jnp.repeat(stretch_start, STRETCH)
    token_offset = jnp.arange(tok_rows, dtype=jnp.int32) % STRETCH
    allow = jnp.stack(
        [1.0 - token_start * (token_offset < tap).astype(F32) for tap in range(taps)], 1
    )

    ends = tokens[0, tok_rows - HALO :]
    before = lax.ppermute(
        ends, "span", [(i, i + 1) for i in range(span_count - 1)]
    )
    inputs_ext = jnp.concatenate([before, tokens[0]], 0).astype(F32)
    inv_ext = lax.rsqrt(jnp.mean(inputs_ext * inputs_ext, -1, keepdims=True) + EPSILON)
    normed_ext = (inputs_ext * inv_ext * attn_gain).astype(BF16)
    inputs_f, inv_first, normed = inputs_ext[HALO:], inv_ext[HALO:], normed_ext[HALO:]
    projected = jnp.dot(normed_ext, full_qkv, preferred_element_type=F32).astype(BF16)
    strength = jax.nn.sigmoid(
        jnp.dot(normed, full_beta, preferred_element_type=F32) + beta_bias
    )
    (
        queries, keys, values, invs, wkeys, prefix, device_map, read_local, read_map, new_v, new_p
    ) = local_call(stretch_keep, projected, full_conv, strength, allow, heads)
    state_in, p_low, p_high, p_chip = chain_call(device_map, None, 3)
    readout, normal_heads = readout_call(state_in, read_local, read_map, head_gain)

    middle = inputs_f + jnp.dot(normal_heads, full_out, preferred_element_type=F32)
    inv_second = lax.rsqrt(jnp.mean(middle * middle, -1, keepdims=True) + EPSILON)
    normed_ffn = (middle * inv_second * ffn_gain).astype(BF16)
    gate = jnp.dot(normed_ffn, full_gate, preferred_element_type=F32)
    up_part = jnp.dot(normed_ffn, full_up, preferred_element_type=F32)
    gate_sig = jax.nn.sigmoid(gate)
    gate_act = gate * gate_sig
    hidden = (gate_act * up_part).astype(BF16)
    grad_branch = cotangent[0]
    pair_cot = pair_tokens(grad_branch)
    half_down = weight_grad(pair_columns(hidden, span_count), pair_cot, span_count)
    grad_hidden = product("td,fd->tf", grad_branch, full_down)
    grad_gate_in = (grad_hidden * up_part * silu_slope(gate, gate_sig)).astype(BF16)
    grad_up_in = (grad_hidden * gate_act).astype(BF16)
    grad_nffn = product("tf,df->td", grad_gate_in, full_gate) + product(
        "tf,df->td", grad_up_in, full_up
    )
    pair_ffn = pair_columns(normed_ffn, span_count)
    half_gate = weight_grad(pair_ffn, pair_tokens(grad_gate_in), span_count)
    half_up = weight_grad(pair_ffn, pair_tokens(grad_up_in), span_count)
    result = middle + jnp.dot(hidden, full_down, preferred_element_type=F32)

    grad_norm_ffn = jnp.sum(grad_nffn * middle * inv_second, 0)
    grad_middle = grad_branch.astype(F32) + norm_back(grad_nffn, middle, inv_second, ffn_gain)
    grad_attn_in = grad_middle.astype(BF16)
    grad_normal = product("td,kd->tk", grad_attn_in, full_out)
    grad_read, device_adjoint, head_grads = adjoint_call(
        stretch_keep, grad_normal, readout, head_gain, queries, keys, wkeys, heads
    )
    pair_heads = pair_columns(normal_heads, span_count)
    half_out = weight_grad(pair_heads, pair_tokens(grad_attn_in), span_count)
    (state_grad,) = chain_call(device_adjoint, (p_low, p_high, p_chip), 4)
    grad_ext, grad_conv, grad_strength = backward_call(
        stretch_keep, state_grad, state_in, prefix, grad_read, queries, keys, values, invs, wkeys,
        new_v, new_p, strength, allow, projected, full_conv, heads,
    )
    pair_normed = pair_columns(normed_ext, span_count)
    half_q, half_k, half_v = (
        weight_grad(pair_normed, pair_tokens(grad_ext[i]), span_count) for i in range(3)
    )

    grad_logit = grad_strength * strength * (1.0 - strength)
    grad_logit_low = grad_logit.astype(BF16)
    grad_w_beta = product("td,th->dh", normed, grad_logit_low)
    grad_normed_ext = sum(
        product("te,de->td", grad_ext[i], full_qkv[:, i * model_width : (i + 1) * model_width])
        for i in range(3)
    )
    halo_back = lax.ppermute(
        grad_normed_ext[:HALO].astype(BF16), "span", [(i, i - 1) for i in range(1, span_count)]
    )
    grad_normed = (
        grad_normed_ext[HALO:]
        + product("th,dh->td", grad_logit_low, full_beta)
        + jnp.pad(halo_back.astype(F32), ((tok_rows - HALO, 0), (0, 0)))
    )
    grad_norm_attn = jnp.sum(grad_normed * inputs_f * inv_first, 0)
    grad_tokens = grad_middle + norm_back(grad_normed, inputs_f, inv_first, attn_gain)

    def by_span(array):
        return array.reshape(span_count, -1)

    grad_conv = jnp.swapaxes(grad_conv, 0, 1).reshape(taps, span_count, -1)
    packed = jnp.concatenate(
        [
            by_span(jnp.swapaxes(grad_conv, 0, 1)),
            by_span(grad_w_beta),
            by_span(grad_norm_attn),
            by_span(grad_norm_ffn),
            by_span(jnp.sum(head_grads, (0, 1))),
            jnp.broadcast_to(jnp.sum(grad_logit, 0)[None], (span_count, heads)),
        ],
        1,
    )
    packed = jnp.pad(packed, ((0, 0), (0, 16 * 512 - packed.shape[1])))
    packed = packed.astype(BF16).reshape(span_count // 2, 2, 16, 512)
    core = place % 2
    half_small = (
        lax.dynamic_index_in_dim(packed, core, 1, keepdims=False).astype(F32)
        + swap_core(lax.dynamic_index_in_dim(packed, 1 - core, 1, keepdims=False)).astype(F32)
    ).astype(BF16)
    parts = reduce_call(
        [half_down, half_gate, half_up, half_out, half_q, half_k, half_v, half_small], 5
    )
    part_down, part_gate, part_up, part_out = (x.astype(F32) for x in parts[:4])
    part_qkv = jnp.concatenate([x.astype(F32) for x in parts[4:7]], 1)
    part_small = parts[7].reshape(-1).astype(F32)
    sums = []
    at = 0
    for like in (conv_weight, w_beta, norm_attn, norm_ffn, norm_head, beta_bias):
        sums.append(part_small[at : at + like.size].reshape(like.shape))
        at += like.size

    return (
        result.astype(BF16)[None],
        grad_tokens[None],
        part_qkv,
        sums[0],
        sums[1],
        sums[5],
        sums[2],
        sums[4],
        part_out,
        sums[3],
        part_gate,
        part_up,
        part_down,
    )


def solution(mesh):
    in_specs = (
        P("stream", "span", None),
        P("stream", "span", None),
        P("stream", None),
        P("span", None),
        P(None, "span"),
        P("span", None),
        P(),
        P("span"),
        P("span"),
        P("span", None),
        P("span"),
        P("span", None),
        P("span", None),
        P("span", None),
    )
    out_specs = (
        P("stream", "span", None),
        P("stream", "span", None),
        P("span", None),
        P(None, "span"),
        P("span", None),
        P(),
        P("span"),
        P("span"),
        P("span", None),
        P("span"),
        P("span", None),
        P("span", None),
        P("span", None),
    )
    return jax.shard_map(local, mesh=mesh, in_specs=in_specs, out_specs=out_specs, check_vma=False)
```

```python
import functools

import jax
import jax.numpy as jnp
from jax import lax
from jax.experimental import pallas as pl
from jax.experimental.pallas import tpu as pltpu
from jax.sharding import PartitionSpec as P

STRETCH = 64
HALO = 16
EPSILON = 1e-06
F32 = jnp.float32
BF16 = jnp.bfloat16
AXES = ("stream", "span")
VMEM_LIMIT = 56 * 2**20


def nn(a, b):
    return lax.dot_general(a, b, (((1,), (0,)), ((), ())), preferred_element_type=F32)


def nt(a, b):
    return lax.dot_general(a, b, (((1,), (1,)), ((), ())), preferred_element_type=F32)


def tn(a, b):
    return lax.dot_general(a, b, (((0,), (0,)), ((), ())), preferred_element_type=F32)


def fine(a, b):
    a_hi = a.astype(BF16)
    a_lo = (a - a_hi.astype(F32)).astype(BF16)
    b_hi = b.astype(BF16)
    b_lo = (b - b_hi.astype(F32)).astype(BF16)
    return nn(jnp.concatenate([a_hi, a_hi, a_lo], 1), jnp.concatenate([b_hi, b_lo, b_hi], 0))


def grid_ids(size):
    return (
        lax.broadcasted_iota(jnp.int32, (size, size), 0),
        lax.broadcasted_iota(jnp.int32, (size, size), 1),
    )


def unit_inverse(lower_list):
    rows, cols = grid_ids(STRETCH)
    eye = (rows == cols).astype(F32)
    out = [eye - jnp.where((rows // 2) == (cols // 2), low, 0.0) for low in lower_list]
    half = 2
    while half < STRETCH:
        cross = ((rows // (2 * half)) == (cols // (2 * half))) & ((rows // half) != (cols // half))
        inner = [fine(jnp.where(cross, low, 0.0), inv) for low, inv in zip(lower_list, out)]
        out = [inv - fine(inv, mid) for inv, mid in zip(out, inner)]
        half *= 2
    return out


def column_of(table, index):
    lanes = lax.broadcasted_iota(jnp.int32, table.shape, 1)
    return jnp.sum(jnp.where(lanes == index, table, 0.0), -1, keepdims=True)


def mix_rows(ext_ref, conv_ref, allow):
    ext = ext_ref[...].astype(F32)
    conv = conv_ref[...].astype(F32)
    shifted = [
        (ext if tap == 0 else pltpu.roll(ext, tap, 0))[HALO:] * allow[tap]
        for tap in range(conv.shape[0])
    ]
    mixed = sum(conv[tap : tap + 1] * shifted[tap] for tap in range(conv.shape[0]))
    return shifted, mixed, conv


def local_kernel(
    keep_ref, eq_ref, ek_ref, ev_ref, cq_ref, ck_ref, cv_ref, rate_ref, allow_ref,
    q_ref, k_ref, v_ref, inv_ref, wk_ref, pre_ref, end_ref, read_ref, rmap_ref, nv_ref, np_ref,
):
    head = pl.program_id(0)
    allow_all = allow_ref[...]
    allow = [allow_all[:, tap : tap + 1] for tap in range(cq_ref.shape[0])]
    rate = column_of(rate_ref[...], head)

    def unit(ref, conv):
        _, mixed, _ = mix_rows(ref, conv, allow)
        act = mixed * jax.nn.sigmoid(mixed)
        return act

    act_q = unit(eq_ref, cq_ref)
    act_k = unit(ek_ref, ck_ref)
    act_v = unit(ev_ref, cv_ref)
    queries = (act_q * lax.rsqrt(jnp.sum(act_q * act_q, -1, keepdims=True) + EPSILON)).astype(BF16)
    keys = (act_k * lax.rsqrt(jnp.sum(act_k * act_k, -1, keepdims=True) + EPSILON)).astype(BF16)
    values = act_v.astype(BF16)
    q_ref[...] = queries
    k_ref[...] = keys
    v_ref[...] = values
    count = queries.shape[0] // STRETCH
    rows, cols = grid_ids(STRETCH)
    parts = [slice(n * STRETCH, (n + 1) * STRETCH) for n in range(count)]
    lows = []
    for part in parts:
        gram = nt(keys[part], keys[part])
        lows.append(jnp.where(rows > cols, gram * rate[part], 0.0))
    invs = unit_inverse(lows)
    size = keys.shape[1]
    drows, dcols = grid_ids(size)
    running = jnp.concatenate(
        [jnp.zeros((size, size), F32), (drows == dcols).astype(F32)], 0
    )
    for n, part in enumerate(parts):
        key, query = keys[part], queries[part]
        inv = invs[n].astype(BF16)
        inv_ref[0, part, :] = inv
        scaled = jnp.concatenate(
            [key.astype(F32) * rate[part], values[part].astype(F32) * rate[part]], 1
        ).astype(BF16)
        weighted = nn(inv, scaled)
        wkey = weighted[:, :size].astype(BF16)
        wk_ref[part, :] = wkey
        running = running * keep_ref[n]
        low_state = running.astype(BF16)
        pre_ref[0, n] = low_state
        back = nt(jnp.concatenate([wkey, query], 0), low_state)
        new = jnp.concatenate(
            [weighted[:, size:] - back[:STRETCH, :size], -back[:STRETCH, size:]], 1
        ).astype(BF16)
        nv_ref[part, :] = new[:, :size]
        np_ref[part, :] = new[:, size:]
        scores = jnp.where(rows >= cols, nt(query, key), 0.0).astype(BF16)
        out = back[STRETCH:] + nn(scores, new)
        read_ref[part, :] = out[:, :size]
        rmap_ref[part, :] = out[:, size:].astype(BF16)
        running = running + tn(new, key)
    end_ref[0] = running.astype(BF16)


def adjoint_kernel(
    keep_ref, gn_ref, read_ref, gain_ref, q_ref, k_ref, wk_ref, go_ref, adj_ref, gain_grad_ref
):
    grad, readout = gn_ref[...], read_ref[...]
    inv = lax.rsqrt(jnp.mean(readout * readout, -1, keepdims=True) + EPSILON)
    scaled = grad * gain_ref[...]
    grad_read = inv * scaled - readout * (inv * inv * inv) * jnp.mean(
        scaled * readout, -1, keepdims=True
    )
    gain_grad_ref[0] = jnp.sum(grad * readout * inv, 0, keepdims=True)
    grad_read = grad_read.astype(BF16)
    go_ref[...] = grad_read
    count = grad.shape[0] // STRETCH
    rows, cols = grid_ids(STRETCH)
    size = grad.shape[1]
    adj = jnp.zeros((size, size), F32)
    for n in range(count - 1, -1, -1):
        part = slice(n * STRETCH, (n + 1) * STRETCH)
        key, query, out = k_ref[part, :], q_ref[part, :], grad_read[part]
        scores = jnp.where(rows >= cols, nt(query, key), 0.0).astype(BF16)
        new_grad = tn(scores, out) + nt(key, adj.astype(BF16))
        adj = (
            adj
            + tn(
                jnp.concatenate([out, (-new_grad).astype(BF16)], 0),
                jnp.concatenate([query, wk_ref[part, :]], 0),
            )
        ) * keep_ref[n]
    adj_ref[0] = adj.astype(BF16)


def adjoint_call(keep, grad_normal, readout, gain, queries, keys, wkeys, heads):
    tok, width = readout.shape
    size = width // heads
    block = pl.BlockSpec((tok, size), lambda h: (0, h))
    return pl.pallas_call(
        adjoint_kernel,
        grid=(heads,),
        in_specs=[
            pl.BlockSpec(memory_space=pltpu.SMEM),
            block, block,
            pl.BlockSpec((1, size), lambda h: (0, 0)),
            block, block, block,
        ],
        out_specs=[
            block,
            pl.BlockSpec((1, size, size), lambda h: (h, 0, 0)),
            pl.BlockSpec((1, 1, size), lambda h: (h, 0, 0)),
        ],
        out_shape=[
            jax.ShapeDtypeStruct((tok, width), BF16),
            jax.ShapeDtypeStruct((heads, size, size), BF16),
            jax.ShapeDtypeStruct((heads, 1, size), F32),
        ],
        compiler_params=pltpu.CompilerParams(vmem_limit_bytes=VMEM_LIMIT),
        cost_estimate=pl.CostEstimate(flops=5 * 10**8, bytes_accessed=6 * 10**6, transcendentals=0),
        name="delta_adjoint",
    )(keep, grad_normal, readout, gain, queries, keys, wkeys)


def backward_kernel(
    keep_ref, din_ref, min_ref, pre_ref, go_ref, q_ref, k_ref, v_ref, inv_ref, wk_ref,
    nv_ref, np_ref, rate_ref, allow_ref,
    eq_ref, ek_ref, ev_ref, cq_ref, ck_ref, cv_ref,
    gext_ref, gconv_ref, grate_ref,
    gq_buf, gk_buf, gv_buf,
):
    head = pl.program_id(0)
    size = q_ref.shape[1]
    tok = q_ref.shape[0]
    count = tok // STRETCH
    rows, cols = grid_ids(STRETCH)
    rate = column_of(rate_ref[...], head)
    low_in = min_ref[0]
    adj = din_ref[0].astype(F32)
    grate_parts = [None] * count
    for n in range(count - 1, -1, -1):
        part = slice(n * STRETCH, (n + 1) * STRETCH)
        key, query, value, out = k_ref[part, :], q_ref[part, :], v_ref[part, :], go_ref[part, :]
        beta = rate[part]
        pre = pre_ref[0, n]
        state = (nn(low_in, pre[size:]) + pre[:size].astype(F32)).astype(BF16)
        new = (nt(np_ref[part, :], low_in) + nv_ref[part, :].astype(F32)).astype(BF16)
        low_adj = adj.astype(BF16)
        gram_both = nt(jnp.concatenate([key, query], 0), key)
        gram = gram_both[:STRETCH]
        scores = jnp.where(rows >= cols, gram_both[STRETCH:], 0.0).astype(BF16)
        new_grad = tn(scores, out) + nt(key, low_adj)
        low_new_grad = new_grad.astype(BF16)
        adj = (
            adj
            + tn(
                jnp.concatenate([out, -low_new_grad], 0),
                jnp.concatenate([query, wk_ref[part, :]], 0),
            )
        ) * keep_ref[n]
        grad_b = tn(inv_ref[0, part, :], low_new_grad)
        both = nt(jnp.concatenate([out, grad_b.astype(BF16)], 0), new)
        grad_scores = jnp.where(rows >= cols, both[:STRETCH], 0.0).astype(BF16)
        grad_low = jnp.where(rows > cols, -both[STRETCH:], 0.0)
        left = value.astype(F32) - nt(key, state)
        grate_parts[n] = jnp.sum(grad_low * gram, -1, keepdims=True) + jnp.sum(
            grad_b * left, -1, keepdims=True
        )
        grad_v = beta * grad_b
        grad_gram = beta * grad_low
        symmetric = (grad_gram + grad_gram.T).astype(BF16)
        by_state = nn(jnp.concatenate([out, -grad_v.astype(BF16)], 0), state)
        gq_buf[part, :] = by_state[:STRETCH] + nn(grad_scores, key)
        gk_buf[part, :] = (
            by_state[STRETCH:]
            + tn(grad_scores, query)
            + nn(jnp.concatenate([new, symmetric], 1), jnp.concatenate([low_adj, key], 0))
        )
        gv_buf[part, :] = grad_v
    grate = jnp.concatenate(grate_parts, 0)
    lanes = lax.broadcasted_iota(jnp.int32, grate_ref.shape, 1)
    before = jnp.where(head == 0, jnp.zeros(grate_ref.shape, F32), grate_ref[...])
    grate_ref[...] = jnp.where(lanes == head, grate, before)
    allow_all = allow_ref[...]
    allow = [allow_all[:, tap : tap + 1] for tap in range(cq_ref.shape[0])]
    zeros = jnp.zeros((HALO, size), F32)
    for i, (ext, conv_ref, buf) in enumerate(
        ((eq_ref, cq_ref, gq_buf), (ek_ref, ck_ref, gk_buf), (ev_ref, cv_ref, gv_buf))
    ):
        shifted, mixed, conv = mix_rows(ext, conv_ref, allow)
        sig = jax.nn.sigmoid(mixed)
        grad = buf[...]
        if i < 2:
            raw = mixed * sig
            inv = lax.rsqrt(jnp.sum(raw * raw, -1, keepdims=True) + EPSILON)
            grad = inv * grad - raw * (inv * inv * inv) * jnp.sum(grad * raw, -1, keepdims=True)
        grad = grad * (sig * (1.0 + mixed * (1.0 - sig)))
        total = None
        for tap in range(conv.shape[0]):
            gconv_ref[i, tap : tap + 1, :] = jnp.sum(grad * shifted[tap], 0, keepdims=True)
            term = jnp.concatenate([zeros, grad * (conv[tap : tap + 1] * allow[tap])], 0)
            if tap:
                term = pltpu.roll(term, tok + HALO - tap, 0)
            total = term if total is None else total + term
        gext_ref[i] = total.astype(BF16)


def backward_call(
    keep, state_grad, state, prefix, grad_read, queries, keys, values, invs, wkeys,
    new_v, new_p, rate, allow, ext, conv, heads,
):
    tok, width = queries.shape
    size = width // heads
    count = tok // STRETCH
    taps = conv.shape[0]
    rows = ext.shape[0]
    block = pl.BlockSpec((tok, size), lambda h: (0, h))
    square = pl.BlockSpec((1, size, size), lambda h: (h, 0, 0))

    def third(i, r):
        return pl.BlockSpec((r, size), lambda h: (0, h + i * heads))

    return pl.pallas_call(
        backward_kernel,
        grid=(heads,),
        in_specs=[
            pl.BlockSpec(memory_space=pltpu.SMEM),
            square, square,
            pl.BlockSpec((1, count, 2 * size, size), lambda h: (h, 0, 0, 0)),
            block, block, block, block,
            pl.BlockSpec((1, tok, STRETCH), lambda h: (h, 0, 0)),
            block, block, block,
            pl.BlockSpec((tok, heads), lambda h: (0, 0)),
            pl.BlockSpec((tok, taps), lambda h: (0, 0)),
            third(0, rows), third(1, rows), third(2, rows),
            third(0, taps), third(1, taps), third(2, taps),
        ],
        out_specs=[
            pl.BlockSpec((3, rows, size), lambda h: (0, 0, h)),
            pl.BlockSpec((3, taps, size), lambda h: (0, 0, h)),
            pl.BlockSpec((tok, heads), lambda h: (0, 0)),
        ],
        out_shape=[
            jax.ShapeDtypeStruct((3, rows, width), BF16),
            jax.ShapeDtypeStruct((3, taps, width), F32),
            jax.ShapeDtypeStruct((tok, heads), F32),
        ],
        scratch_shapes=[pltpu.VMEM((tok, size), F32)] * 3,
        compiler_params=pltpu.CompilerParams(vmem_limit_bytes=VMEM_LIMIT),
        cost_estimate=pl.CostEstimate(flops=2 * 10**9, bytes_accessed=12 * 10**6, transcendentals=10**6),
        name="delta_backward",
    )(
        keep, state_grad, state, prefix, grad_read, queries, keys, values, invs, wkeys,
        new_v, new_p, rate, allow, ext, ext, ext, conv, conv, conv,
    )


def silu_slope(pre_act, sig_value):
    return sig_value * (1.0 + pre_act * (1.0 - sig_value))


def norm_back(grad_in, values, inv_rms, gain_vec):
    scaled = grad_in * gain_vec
    return inv_rms * scaled - values * inv_rms**3 * jnp.mean(scaled * values, -1, keepdims=True)


def product(pattern, first, second, kind=F32):
    return jnp.einsum(pattern, first, second, preferred_element_type=F32).astype(kind)


def swap_core(block):
    streams, spans = lax.axis_size("stream"), lax.axis_size("span")
    pairs = [
        (s * spans + p, s * spans + (p ^ 1)) for s in range(streams) for p in range(spans)
    ]
    return lax.ppermute(block, AXES, pairs)


def pair_tokens(block):
    return jnp.concatenate([block, swap_core(block)], 0)


def pair_columns(block, spans):
    core = lax.axis_index("span") % 2
    rows, width = block.shape
    split = block.reshape(rows, spans // 2, 2, width // spans)
    mine = lax.dynamic_index_in_dim(split, core, 2, keepdims=False).reshape(rows, -1)
    theirs = lax.dynamic_index_in_dim(split, 1 - core, 2, keepdims=False).reshape(rows, -1)
    return jnp.concatenate([mine, swap_core(theirs)], 0)


def weight_grad(left, right, spans):
    grad = product("td,te->de", left, right, BF16)
    return grad.reshape(spans // 2, -1, grad.shape[1])


MESH = pl.DeviceIdType.MESH


class Place:
    def __init__(self, streams, spans):
        self.streams, self.spans, self.chips = streams, spans, spans // 2
        self.stream = lax.axis_index("stream")
        self.span = lax.axis_index("span")
        self.chip = lax.div(self.span, 2)
        self.core = lax.rem(self.span, 2)

    def beside(self, step):
        return (self.stream ^ step, self.span)

    def along(self, step):
        return (self.stream, 2 * self.shifted(step) + self.core)

    def shifted(self, step):
        return lax.rem(self.chip + step + self.chips, self.chips)

    def other(self):
        return (self.stream, 2 * self.chip + 1 - self.core)


def greet(places):
    barrier = pltpu.get_barrier_semaphore()
    for target in places:
        pl.semaphore_signal(barrier, inc=1, device_id=target, device_id_type=MESH)
    pl.semaphore_wait(barrier, len(places))


def quarter_of(rows, width, streams):
    if (width // 128) % streams == 0:
        return 1, streams
    return 2, streams // 2


def quarter_index(rows, width, streams, at, piece=0, pieces=1):
    down, across = quarter_of(rows, width, streams)
    r, c = rows // down, width // across
    row = pl.ds(0, rows) if down == 1 else pl.ds(pl.multiple_of(lax.div(at, across) * r, r), r)
    start = lax.rem(at, across) * c + piece * (c // pieces)
    return row, pl.ds(pl.multiple_of(start, 128), c // pieces)


def copy_to(source, target, send_sem, recv_sem, device):
    return pltpu.make_async_remote_copy(
        src_ref=source, dst_ref=target, send_sem=send_sem, recv_sem=recv_sem,
        device_id=device, device_id_type=MESH,
    )


class Gather:
    def __init__(self, place, shards, fulls, sems):
        self.place, self.shards, self.fulls = place, shards, fulls
        self.sems = sems
        self.units = []
        for w, shard in enumerate(shards):
            rows, width = shard.shape
            _, across = quarter_of(rows, width, place.streams)
            pieces = 2 if (width // across) % 256 == 0 else 1
            for piece in range(pieces):
                self.units.append((w, piece, pieces))

    @staticmethod
    def sem_shapes(shapes, streams, spans):
        units = 0
        for rows, width in shapes:
            _, across = quarter_of(rows, width, streams)
            units += 2 if (width // across) % 256 == 0 else 1
        slots = spans // 2
        dma = pltpu.SemaphoreType.DMA
        return [dma((units, slots, 4, 2)), dma((len(shapes), slots, 2)), dma((len(shapes),))]

    def part(self, unit, at, span=None):
        w, piece, pieces = self.units[unit]
        rows, width = self.shards[w].shape
        index = quarter_index(rows, width, self.place.streams, at, piece, pieces)
        if span is None:
            return self.shards[w].at[index]
        return self.fulls[w].at[(span,) + index]

    def source_span(self, k):
        return 2 * self.place.shifted(-k) + self.place.core

    def wire(self, unit, k, kind, span, at, device, source=None):
        region = self.part(unit, at, span)
        return copy_to(
            region if source is None else source, region,
            self.sems[0].at[unit, k, kind, 0], self.sems[0].at[unit, k, kind, 1], device,
        )

    def along(self, unit, k):
        p = self.place
        return self.wire(
            unit, k, 0, p.span, p.stream, p.along(k), self.part(unit, p.stream)
        )

    def along_wait(self, unit, k):
        p = self.place
        self.wire(unit, k, 0, self.source_span(k), p.stream, p.along(k)).wait_recv()

    def sideways(self, unit, k, step):
        p = self.place
        return self.wire(unit, k, step, self.source_span(k), p.stream, p.beside(step))

    def sideways_wait(self, unit, k, step):
        p = self.place
        self.wire(
            unit, k, step, self.source_span(k), p.stream ^ step, p.beside(step)
        ).wait_recv()

    @staticmethod
    def turns(unit, k):
        return (1, 2) if (unit + k) % 2 == 0 else (2, 1)

    def corner(self, unit, k):
        p = self.place
        first, second = self.turns(unit, k)
        return self.wire(
            unit, k, 3, self.source_span(k), p.stream ^ first, p.beside(second)
        )

    def corner_wait(self, unit, k):
        p = self.place
        self.wire(unit, k, 3, self.source_span(k), p.stream ^ 3, p.beside(1)).wait_recv()

    def across(self, w, k):
        p = self.place
        span = p.span if k == 0 else self.source_span(k)
        region = self.fulls[w].at[span]
        return copy_to(
            self.shards[w] if k == 0 else region, region,
            self.sems[1].at[w, k, 0], self.sems[1].at[w, k, 1], p.other(),
        )

    def across_wait(self, w, k):
        p = self.place
        span = 2 * p.shifted(-k) + 1 - p.core
        region = self.fulls[w].at[span]
        copy_to(
            region, region, self.sems[1].at[w, k, 0], self.sems[1].at[w, k, 1], p.other()
        ).wait_recv()

    def own(self, w):
        return pltpu.make_async_copy(
            self.shards[w], self.fulls[w].at[self.place.span], self.sems[2].at[w]
        )

    def neighbours(self):
        p = self.place
        return (
            [p.along(k) for k in range(1, p.chips)] + [p.beside(1), p.beside(2), p.other()]
        )

    def steps(self):
        p = self.place
        slots = range(1, p.chips)
        count = len(self.units)
        ends = {}
        for unit, (w, piece, pieces) in enumerate(self.units):
            if piece == pieces - 1:
                ends[unit] = w
        steps = []

        def begin(unit):
            w, piece, pieces = self.units[unit]
            for k in slots:
                self.along(unit, k).start()
            if piece == 0:
                self.across(w, 0).start()
                self.own(w).start()

        def beside(unit, k):
            self.along_wait(unit, k)
            self.sideways(unit, k, 1).start()
            self.sideways(unit, k, 2).start()

        def turn(unit, k):
            self.sideways_wait(unit, k, self.turns(unit, k)[0])
            self.corner(unit, k).start()

        def close(w, k):
            for unit, (owner, _, _) in enumerate(self.units):
                if owner == w:
                    self.sideways_wait(unit, k, self.turns(unit, k)[1])
                    self.corner_wait(unit, k)
            self.across(w, k).start()

        def finish(w):
            for k in range(p.chips):
                self.across_wait(w, k)
                self.across(w, k).wait_send()
            self.own(w).wait()
            for unit, (owner, _, _) in enumerate(self.units):
                if owner == w:
                    for k in slots:
                        self.along(unit, k).wait_send()
                        self.sideways(unit, k, 1).wait_send()
                        self.sideways(unit, k, 2).wait_send()
                        self.corner(unit, k).wait_send()

        for unit in range(min(2, count)):
            steps.append(functools.partial(begin, unit))
        for turn_at in range(count + 2):
            if turn_at + 2 < count:
                steps.append(functools.partial(begin, turn_at + 2))
            if turn_at < count:
                steps += [functools.partial(beside, turn_at, k) for k in slots]
            if 0 <= turn_at - 1 < count:
                steps += [functools.partial(turn, turn_at - 1, k) for k in slots]
            if turn_at - 2 in ends:
                steps += [functools.partial(close, ends[turn_at - 2], k) for k in slots]
        steps += [functools.partial(finish, w) for w in range(len(self.shards))]
        return steps


def gather_kernel(streams, spans, count, *refs):
    shards, fulls, sems = refs[:count], refs[count : 2 * count], refs[2 * count :]
    place = Place(streams, spans)
    work = Gather(place, shards, fulls, sems)
    greet(work.neighbours())
    for step in work.steps():
        step()


def gather_call(shards, collective_id):
    streams, spans = lax.axis_size("stream"), lax.axis_size("span")
    shapes = [shard.shape for shard in shards]
    outs = pl.pallas_call(
        functools.partial(gather_kernel, streams, spans, len(shards)),
        in_specs=[pl.BlockSpec(memory_space=pl.ANY)] * len(shards),
        out_specs=[pl.BlockSpec(memory_space=pl.ANY)] * len(shards),
        out_shape=[jax.ShapeDtypeStruct((spans,) + s.shape, s.dtype) for s in shards],
        scratch_shapes=Gather.sem_shapes(shapes, streams, spans),
        compiler_params=pltpu.CompilerParams(
            collective_id=collective_id, has_side_effects=True, vmem_limit_bytes=VMEM_LIMIT
        ),
        name="gather_weights",
    )(*shards)
    return outs


class Reduce:
    def __init__(self, place, grads, outs, bufs, sems):
        self.place, self.grads, self.outs, self.bufs, self.sems = place, grads, outs, bufs, sems

    @staticmethod
    def block(shape, streams):
        _, rows, width = shape
        down, across = quarter_of(rows, width, streams)
        return rows // down, width // across

    @staticmethod
    def scratch(shapes, kinds, streams):
        out = []
        dma = pltpu.SemaphoreType.DMA
        for shape, kind in zip(shapes, kinds):
            chips = shape[0]
            r, c = Reduce.block(shape, streams)
            out += [
                pltpu.VMEM((2, chips, r, c), kind),
                pltpu.VMEM((2, chips, r, c), kind),
                pltpu.VMEM((chips, r, c), kind),
                pltpu.VMEM((chips, r, c), kind),
                pltpu.VMEM((chips, r, c), kind),
                pltpu.VMEM((streams, r, c), kind),
            ]
        n = len(shapes)
        chips = shapes[0][0]
        out += [dma((n, 2, 3, 2)), dma((n, chips, 2)), dma((n, streams, 2))]
        return out

    def turn(self, w, half):
        return (1, 2) if (w + half) % 2 == 0 else (2, 1)

    def chips_of(self, half):
        n = self.place.chips // 2
        return half * n, n

    def region(self, w, half, at):
        _, rows, width = self.grads[w].shape
        start, n = self.chips_of(half)
        return (pl.ds(start, n),) + quarter_index(rows, width, self.place.streams, at)

    def first(self, w, half, slot):
        p = self.place
        a, b = self.turn(w, half)
        start, n = self.chips_of(half)
        at = p.stream ^ a if slot == 0 else p.stream ^ a ^ b
        return copy_to(
            self.grads[w].at[self.region(w, half, at)],
            self.bufs[w][0].at[slot, pl.ds(start, n)],
            self.sems[0].at[w, half, slot, 0], self.sems[0].at[w, half, slot, 1], p.beside(a),
        )

    def second(self, w, half):
        p = self.place
        _, b = self.turn(w, half)
        start, n = self.chips_of(half)
        return copy_to(
            self.bufs[w][1].at[1, pl.ds(start, n)], self.bufs[w][2].at[pl.ds(start, n)],
            self.sems[0].at[w, half, 2, 0], self.sems[0].at[w, half, 2, 1], p.beside(b),
        )

    def third(self, w, k):
        p = self.place
        return copy_to(
            self.bufs[w][3].at[p.shifted(k)], self.bufs[w][4].at[k],
            self.sems[1].at[w, k, 0], self.sems[1].at[w, k, 1], p.along(k),
        )

    def fourth(self, w, step):
        p = self.place
        return copy_to(
            self.bufs[w][5].at[0], self.bufs[w][5].at[step],
            self.sems[2].at[w, step, 0], self.sems[2].at[w, step, 1], p.beside(step),
        )

    def neighbours(self):
        p = self.place
        return [p.along(k) for k in range(1, p.chips)] + [
            p.beside(s) for s in range(1, p.streams)
        ]

    def begin(self, w):
        for half in range(2):
            for slot in (1, 0):
                self.first(w, half, slot).start()

    def add_first(self, w, half):
        p = self.place
        _, b = self.turn(w, half)
        start, n = self.chips_of(half)
        for slot in (1, 0):
            self.first(w, half, slot).wait_recv()
            at = p.stream ^ b if slot else p.stream
            _, row, col = self.region(w, half, at)
            for chip in range(start, start + n):
                self.bufs[w][1][slot, chip] = (
                    self.grads[w][chip, row, col].astype(F32)
                    + self.bufs[w][0][slot, chip].astype(F32)
                ).astype(self.grads[w].dtype)
            if slot:
                self.second(w, half).start()

    def add_second(self, w, half):
        start, n = self.chips_of(half)
        self.second(w, half).wait_recv()
        for chip in range(start, start + n):
            self.bufs[w][3][chip] = (
                self.bufs[w][1][0, chip].astype(F32) + self.bufs[w][2][chip].astype(F32)
            ).astype(self.grads[w].dtype)

    def spread(self, w):
        for k in range(1, self.place.chips):
            self.third(w, k).start()

    def add_third(self, w):
        p = self.place
        total = self.bufs[w][3][p.chip].astype(F32)
        for k in range(1, p.chips):
            self.third(w, k).wait_recv()
            total = total + self.bufs[w][4][k].astype(F32)
        self.bufs[w][5][0] = total.astype(self.grads[w].dtype)
        for step in range(1, p.streams):
            self.fourth(w, step).start()

    def finish(self, w):
        p = self.place
        _, rows, width = self.grads[w].shape
        for step in range(p.streams):
            if step:
                self.fourth(w, step).wait_recv()
            row, col = quarter_index(rows, width, p.streams, p.stream ^ step)
            self.outs[w][row, col] = self.bufs[w][5][step]
        for half in range(2):
            for slot in range(2):
                self.first(w, half, slot).wait_send()
            self.second(w, half).wait_send()
        for k in range(1, p.chips):
            self.third(w, k).wait_send()
        for step in range(1, p.streams):
            self.fourth(w, step).wait_send()

    def steps(self):
        count = len(self.grads)
        steps = [functools.partial(self.begin, w) for w in range(count)]
        for t in range(count + 3):
            if t < count:
                steps += [functools.partial(self.add_first, t, half) for half in range(2)]
            if 0 <= t - 1 < count:
                steps += [functools.partial(self.add_second, t - 1, half) for half in range(2)]
                steps.append(functools.partial(self.spread, t - 1))
            if 0 <= t - 2 < count:
                steps.append(functools.partial(self.add_third, t - 2))
            if 0 <= t - 3 < count:
                steps.append(functools.partial(self.finish, t - 3))
        return steps


def reduce_kernel(streams, spans, count, *refs):
    grads, outs, rest = refs[:count], refs[count : 2 * count], refs[2 * count :]
    bufs = [rest[6 * w : 6 * w + 6] for w in range(count)]
    work = Reduce(Place(streams, spans), grads, outs, bufs, rest[6 * count :])
    greet(work.neighbours())
    for step in work.steps():
        step()


def reduce_call(grads, collective_id):
    streams, spans = lax.axis_size("stream"), lax.axis_size("span")
    shapes = [grad.shape for grad in grads]
    vmem = pl.BlockSpec(memory_space=pltpu.VMEM)
    return pl.pallas_call(
        functools.partial(reduce_kernel, streams, spans, len(grads)),
        in_specs=[vmem] * len(grads),
        out_specs=[vmem] * len(grads),
        out_shape=[jax.ShapeDtypeStruct(g.shape[1:], g.dtype) for g in grads],
        scratch_shapes=Reduce.scratch(shapes, [g.dtype for g in grads], streams),
        compiler_params=pltpu.CompilerParams(
            collective_id=collective_id, has_side_effects=True, vmem_limit_bytes=VMEM_LIMIT
        ),
        name="reduce_grads",
    )(*grads)


def chain_body(p, backward, source, maps, state_ref, scratch):
    p_low, p_high, p_chip = maps
    swap, carry, outgo, sent = scratch[:4]
    swap_sem, hop_sem, back_sem = scratch[-3:]
    s_chip = None if backward else scratch[4]
    heads, size = source.shape[0], source.shape[2]
    half = heads // 2
    mine = p.core * half
    theirs = (1 - p.core) * half
    ahead, behind = (-1, 1) if backward else (1, -1)
    edge_in = p.chips - 1 if backward else 0
    edge_out = 0 if backward else p.chips - 1
    swap_copy = copy_to(
        source.at[pl.ds(theirs, half)], swap, swap_sem.at[0], swap_sem.at[1], p.other()
    )
    swap_copy.start()
    swap_copy.wait_recv()
    low_core = p.core == 0
    for h in range(half):
        own, got = source[mine + h], swap[h]
        low = jnp.where(low_core, own, got)
        high = jnp.where(low_core, got, own)
        if backward:
            outgo[h] = low.astype(F32) + nt(high, p_low[h])
        else:
            joined = nn(low, high[size:])
            s_chip[h] = joined[:size] + high[:size].astype(F32)
            p_chip[h] = joined[size:].astype(BF16)
            p_low[h] = low[size:]
            p_high[h] = high[size:]
            outgo[h] = low[:size].astype(F32)

    def hop(h):
        return copy_to(
            sent.at[h], carry.at[h], hop_sem.at[h, 0], hop_sem.at[h, 1], p.along(ahead)
        )

    @pl.when(p.chip == edge_in)
    def _():
        carry[...] = jnp.zeros(carry.shape, BF16)

    for h in range(half):

        @pl.when(p.chip != edge_in)
        def _():
            hop(h).wait_recv()

        moved = nt(carry[h], p_chip[h]) + outgo[h] if backward else nn(carry[h], p_chip[h]) + s_chip[h]
        sent[h] = moved.astype(BF16)

        @pl.when(p.chip != edge_out)
        def _():
            hop(h).start()

    for h in range(half):
        state = carry[h]
        if backward:
            low_state = (nt(state, p_high[h]) + jnp.where(low_core, swap[h], source[mine + h]).astype(F32)).astype(BF16)
            keep = jnp.where(low_core, low_state, state)
            give = jnp.where(low_core, state, low_state)
        else:
            high_state = (nn(state, p_low[h]) + outgo[h]).astype(BF16)
            keep = jnp.where(low_core, state, high_state)
            give = jnp.where(low_core, high_state, state)
        state_ref[mine + h] = keep
        sent[half + h] = give
    back = copy_to(
        sent.at[pl.ds(half, half)], state_ref.at[pl.ds(mine, half)],
        back_sem.at[0], back_sem.at[1], p.other(),
    )
    back.start()
    copy_to(
        sent.at[pl.ds(half, half)], state_ref.at[pl.ds(theirs, half)],
        back_sem.at[0], back_sem.at[1], p.other(),
    ).wait_recv()
    back.wait_send()
    swap_copy.wait_send()

    @pl.when(p.chip != edge_out)
    def _():
        for h in range(half):
            hop(h).wait_send()


def chain_scratch(heads, size, rows, backward):
    half = heads // 2
    dma = pltpu.SemaphoreType.DMA
    scratch = [
        pltpu.VMEM((half, rows, size), BF16),
        pltpu.VMEM((half, size, size), BF16),
        pltpu.VMEM((half, size, size), F32),
        pltpu.VMEM((heads, size, size), BF16),
    ]
    if not backward:
        scratch.append(pltpu.VMEM((half, size, size), F32))
    return scratch + [dma((2,)), dma((half, 2)), dma((2,))]


def chain_kernel(streams, spans, backward, *refs):
    p = Place(streams, spans)
    greet([p.other(), p.along(1), p.along(-1)])
    if backward:
        chain_body(p, True, refs[0], refs[1:4], refs[4], refs[5:])
    else:
        chain_body(p, False, refs[0], refs[2:5], refs[1], refs[5:])


def readout_body(readout, gain):
    inv = lax.rsqrt(jnp.mean(readout * readout, -1, keepdims=True) + EPSILON)
    return (readout * inv * gain).astype(BF16)


def spread_steps(steps, slots, index):
    count = len(steps)
    return steps[count * index // slots : count * (index + 1) // slots]


def forward_kernel(streams, spans, heads, weights, *refs):
    ins, refs = refs[:10], refs[10:]
    shards, refs = refs[:weights], refs[weights:]
    outs, refs = refs[:14], refs[14:]
    fulls, refs = refs[:weights], refs[weights:]
    gather_sems, refs = refs[:3], refs[3:]
    map_buf, read_buf, rmap_buf, state_buf = refs[:4]
    chain_bufs = refs[4:]
    gain_ref = ins[9]
    (q_ref, k_ref, v_ref, inv_ref, wk_ref, pre_ref, nv_ref, np_ref,
     state_ref, p_low, p_high, p_chip, out_ref, normal_ref) = outs
    step_id = pl.program_id(0)
    place = Place(streams, spans)
    work = Gather(place, shards, fulls, gather_sems)
    steps = work.steps()

    @pl.when(step_id == 0)
    def _():
        greet(work.neighbours())

    for index in range(heads + 1):

        @pl.when(step_id == index)
        def _():
            for step in spread_steps(steps, heads + 2, index):
                step()

    @pl.when(step_id < heads)
    def _():
        local_kernel(
            *ins[:9], q_ref, k_ref, v_ref, inv_ref, wk_ref, pre_ref, map_buf.at[pl.ds(step_id, 1)],
            read_buf.at[step_id], rmap_buf.at[step_id], nv_ref, np_ref,
        )

    @pl.when(step_id == heads)
    def _():
        chain_body(place, False, map_buf, (p_low, p_high, p_chip), state_buf, chain_bufs)
        state_ref[...] = state_buf[...]
        size = gain_ref.shape[1]
        for h in range(heads):
            cols = slice(h * size, (h + 1) * size)
            readout = read_buf[h] + nt(rmap_buf[h], state_buf[h])
            out_ref[:, cols] = readout
            normal_ref[:, cols] = readout_body(readout, gain_ref[...])
        for step in spread_steps(steps, heads + 2, heads + 1):
            step()


def forward_call(keep, ext, conv, rate, allow, gain, shards, heads, collective_id):
    streams, spans = lax.axis_size("stream"), lax.axis_size("span")
    tok = rate.shape[0]
    width = ext.shape[1] // 3
    size = width // heads
    count = tok // STRETCH
    taps = conv.shape[0]
    rows = ext.shape[0]
    half = heads // 2
    hbm = pl.BlockSpec(memory_space=pl.ANY)

    def at(i):
        return jnp.minimum(i, heads - 1)

    def third(i, r):
        return pl.BlockSpec((r, size), lambda h: (0, at(h) + i * heads))

    def token_block():
        return pl.BlockSpec((tok, size), lambda h: (0, at(h)))

    def whole(*shape):
        return pl.BlockSpec(shape, lambda h: (0,) * len(shape))

    token_shape = jax.ShapeDtypeStruct((tok, width), BF16)
    square = jax.ShapeDtypeStruct((half, size, size), BF16)
    shapes = [s.shape for s in shards]
    outs = pl.pallas_call(
        functools.partial(forward_kernel, streams, spans, heads, len(shards)),
        grid=(heads + 1,),
        in_specs=[
            pl.BlockSpec(memory_space=pltpu.SMEM),
            third(0, rows), third(1, rows), third(2, rows),
            third(0, taps), third(1, taps), third(2, taps),
            whole(tok, heads), whole(tok, taps), whole(1, size),
        ]
        + [hbm] * len(shards),
        out_specs=[
            token_block(), token_block(), token_block(),
            pl.BlockSpec((1, tok, STRETCH), lambda h: (at(h), 0, 0)),
            token_block(),
            pl.BlockSpec((1, count, 2 * size, size), lambda h: (at(h), 0, 0, 0)),
            token_block(), token_block(),
            whole(heads, size, size),
            whole(half, size, size), whole(half, size, size), whole(half, size, size),
            whole(tok, width), whole(tok, width),
        ]
        + [hbm] * len(shards),
        out_shape=[
            token_shape, token_shape, token_shape,
            jax.ShapeDtypeStruct((heads, tok, STRETCH), BF16),
            token_shape,
            jax.ShapeDtypeStruct((heads, count, 2 * size, size), BF16),
            token_shape, token_shape,
            jax.ShapeDtypeStruct((heads, size, size), BF16),
            square, square, square,
            jax.ShapeDtypeStruct((tok, width), F32),
            token_shape,
        ]
        + [jax.ShapeDtypeStruct((spans,) + s.shape, s.dtype) for s in shards],
        scratch_shapes=Gather.sem_shapes(shapes, streams, spans)
        + [
            pltpu.VMEM((heads, 2 * size, size), BF16),
            pltpu.VMEM((heads, tok, size), F32),
            pltpu.VMEM((heads, tok, size), BF16),
            pltpu.VMEM((heads, size, size), BF16),
        ]
        + chain_scratch(heads, size, 2 * size, False),
        compiler_params=pltpu.CompilerParams(
            collective_id=collective_id, has_side_effects=True, vmem_limit_bytes=VMEM_LIMIT
        ),
        name="delta_forward",
    )(keep, ext, ext, ext, conv, conv, conv, rate, allow, gain, *shards)
    return outs[:14], outs[14:]


def chain_call(maps, carried, collective_id):
    streams, spans = lax.axis_size("stream"), lax.axis_size("span")
    backward = carried is not None
    heads, size = maps.shape[0], maps.shape[2]
    half = heads // 2
    vmem = pl.BlockSpec(memory_space=pltpu.VMEM)
    square = jax.ShapeDtypeStruct((half, size, size), BF16)
    state = jax.ShapeDtypeStruct((heads, size, size), BF16)
    scratch = chain_scratch(heads, size, maps.shape[1], backward)
    operands = [maps] + (list(carried) if backward else [])
    return pl.pallas_call(
        functools.partial(chain_kernel, streams, spans, backward),
        in_specs=[vmem] * len(operands),
        out_specs=[vmem] * (1 if backward else 4),
        out_shape=[state] if backward else [state, square, square, square],
        scratch_shapes=scratch,
        compiler_params=pltpu.CompilerParams(
            collective_id=collective_id, has_side_effects=True, vmem_limit_bytes=VMEM_LIMIT
        ),
        name="span_chain",
    )(*operands)


def local(
    tokens, cotangent, doc_stretches, w_qkv, conv_weight, w_beta, beta_bias, norm_attn, norm_head,
    w_out, norm_ffn, w_gate, w_up, w_down,
):
    tok_rows, model_width = tokens.shape[1:]
    heads = beta_bias.shape[0]
    size = model_width // heads
    count = tok_rows // STRETCH
    span_count = lax.axis_size("span")
    place = lax.axis_index("span")
    taps = conv_weight.shape[0]

    small = jnp.concatenate(
        [x.reshape(-1) for x in (conv_weight, w_beta, norm_attn, norm_ffn, norm_head)]
    )
    small_len = small.shape[0]
    small = jnp.pad(small, (0, 16 * 512 - small_len)).reshape(16, 512)
    full_qkv, smalls = gather_call([w_qkv, small], 1)
    full_qkv = full_qkv.reshape(-1, full_qkv.shape[2])
    smalls = smalls.reshape(span_count, -1)

    def small_part(shape, start):
        length = 1
        for dim in shape:
            length *= dim
        return smalls[:, start : start + length].reshape((span_count,) + shape), start + length

    at = 0
    full_conv, at = small_part(conv_weight.shape, at)
    full_beta, at = small_part(w_beta.shape, at)
    gain_attn, at = small_part(norm_attn.shape, at)
    gain_ffn, at = small_part(norm_ffn.shape, at)
    gain_head, at = small_part(norm_head.shape, at)
    full_conv = jnp.swapaxes(full_conv, 0, 1).reshape(taps, -1)
    full_beta = full_beta.reshape(-1, heads)
    attn_gain = gain_attn.reshape(-1).astype(F32)
    ffn_gain = gain_ffn.reshape(-1).astype(F32)
    head_gain = gain_head.reshape(1, -1).astype(F32)

    stretch_ids = place * count + jnp.arange(count, dtype=jnp.int32)
    doc_lengths = doc_stretches[0]
    doc_begins = jnp.cumsum(doc_lengths) - doc_lengths
    stretch_start = jnp.any(stretch_ids[:, None] == doc_begins[None, :], axis=1).astype(F32)
    stretch_keep = 1.0 - stretch_start
    token_start = jnp.repeat(stretch_start, STRETCH)
    token_offset = jnp.arange(tok_rows, dtype=jnp.int32) % STRETCH
    allow = jnp.stack(
        [1.0 - token_start * (token_offset < tap).astype(F32) for tap in range(taps)], 1
    )

    ends = tokens[0, tok_rows - HALO :]
    before = lax.ppermute(
        ends, "span", [(i, i + 1) for i in range(span_count - 1)]
    )
    inputs_ext = jnp.concatenate([before, tokens[0]], 0).astype(F32)
    inv_ext = lax.rsqrt(jnp.mean(inputs_ext * inputs_ext, -1, keepdims=True) + EPSILON)
    normed_ext = (inputs_ext * inv_ext * attn_gain).astype(BF16)
    inputs_f, inv_first, normed = inputs_ext[HALO:], inv_ext[HALO:], normed_ext[HALO:]
    projected = jnp.dot(normed_ext, full_qkv, preferred_element_type=F32).astype(BF16)
    strength = jax.nn.sigmoid(
        jnp.dot(normed, full_beta, preferred_element_type=F32) + beta_bias
    )
    (
        queries, keys, values, invs, wkeys, prefix, new_v, new_p,
        state_in, p_low, p_high, p_chip, readout, normal_heads,
    ), rest = forward_call(
        stretch_keep, projected, full_conv, strength, allow, head_gain,
        [w_out, w_gate, w_up, w_down], heads, 2,
    )
    full_out, full_gate, full_up, full_down = (w.reshape(-1, w.shape[2]) for w in rest)

    middle = inputs_f + jnp.dot(normal_heads, full_out, preferred_element_type=F32)
    inv_second = lax.rsqrt(jnp.mean(middle * middle, -1, keepdims=True) + EPSILON)
    normed_ffn = (middle * inv_second * ffn_gain).astype(BF16)
    gate = jnp.dot(normed_ffn, full_gate, preferred_element_type=F32)
    up_part = jnp.dot(normed_ffn, full_up, preferred_element_type=F32)
    gate_sig = jax.nn.sigmoid(gate)
    gate_act = gate * gate_sig
    hidden = (gate_act * up_part).astype(BF16)
    grad_branch = cotangent[0]
    pair_cot = pair_tokens(grad_branch)
    half_down = weight_grad(pair_columns(hidden, span_count), pair_cot, span_count)
    grad_hidden = product("td,fd->tf", grad_branch, full_down)
    grad_gate_in = (grad_hidden * up_part * silu_slope(gate, gate_sig)).astype(BF16)
    grad_up_in = (grad_hidden * gate_act).astype(BF16)
    grad_nffn = product("tf,df->td", grad_gate_in, full_gate) + product(
        "tf,df->td", grad_up_in, full_up
    )
    pair_ffn = pair_columns(normed_ffn, span_count)
    half_gate = weight_grad(pair_ffn, pair_tokens(grad_gate_in), span_count)
    half_up = weight_grad(pair_ffn, pair_tokens(grad_up_in), span_count)
    result = middle + jnp.dot(hidden, full_down, preferred_element_type=F32)

    grad_norm_ffn = jnp.sum(grad_nffn * middle * inv_second, 0)
    grad_middle = grad_branch.astype(F32) + norm_back(grad_nffn, middle, inv_second, ffn_gain)
    grad_attn_in = grad_middle.astype(BF16)
    grad_normal = product("td,kd->tk", grad_attn_in, full_out)
    grad_read, device_adjoint, head_grads = adjoint_call(
        stretch_keep, grad_normal, readout, head_gain, queries, keys, wkeys, heads
    )
    pair_heads = pair_columns(normal_heads, span_count)
    half_out = weight_grad(pair_heads, pair_tokens(grad_attn_in), span_count)
    (state_grad,) = chain_call(device_adjoint, (p_low, p_high, p_chip), 4)
    grad_ext, grad_conv, grad_strength = backward_call(
        stretch_keep, state_grad, state_in, prefix, grad_read, queries, keys, values, invs, wkeys,
        new_v, new_p, strength, allow, projected, full_conv, heads,
    )
    pair_normed = pair_columns(normed_ext, span_count)
    half_q, half_k, half_v = (
        weight_grad(pair_normed, pair_tokens(grad_ext[i]), span_count) for i in range(3)
    )

    grad_logit = grad_strength * strength * (1.0 - strength)
    grad_logit_low = grad_logit.astype(BF16)
    grad_w_beta = product("td,th->dh", normed, grad_logit_low)
    grad_normed_ext = sum(
        product("te,de->td", grad_ext[i], full_qkv[:, i * model_width : (i + 1) * model_width])
        for i in range(3)
    )
    halo_back = lax.ppermute(
        grad_normed_ext[:HALO].astype(BF16), "span", [(i, i - 1) for i in range(1, span_count)]
    )
    grad_normed = (
        grad_normed_ext[HALO:]
        + product("th,dh->td", grad_logit_low, full_beta)
        + jnp.pad(halo_back.astype(F32), ((tok_rows - HALO, 0), (0, 0)))
    )
    grad_norm_attn = jnp.sum(grad_normed * inputs_f * inv_first, 0)
    grad_tokens = grad_middle + norm_back(grad_normed, inputs_f, inv_first, attn_gain)

    def by_span(array):
        return array.reshape(span_count, -1)

    grad_conv = jnp.swapaxes(grad_conv, 0, 1).reshape(taps, span_count, -1)
    packed = jnp.concatenate(
        [
            by_span(jnp.swapaxes(grad_conv, 0, 1)),
            by_span(grad_w_beta),
            by_span(grad_norm_attn),
            by_span(grad_norm_ffn),
            by_span(jnp.sum(head_grads, (0, 1))),
            jnp.broadcast_to(jnp.sum(grad_logit, 0)[None], (span_count, heads)),
        ],
        1,
    )
    packed = jnp.pad(packed, ((0, 0), (0, 16 * 512 - packed.shape[1])))
    packed = packed.reshape(span_count // 2, 2, 16, 512)
    core = place % 2
    half_small = lax.dynamic_index_in_dim(packed, core, 1, keepdims=False) + swap_core(
        lax.dynamic_index_in_dim(packed, 1 - core, 1, keepdims=False)
    )
    parts = reduce_call(
        [half_down, half_gate, half_up, half_out, half_q, half_k, half_v, half_small], 5
    )
    part_down, part_gate, part_up, part_out = (x.astype(F32) for x in parts[:4])
    part_qkv = jnp.concatenate([x.astype(F32) for x in parts[4:7]], 1)
    part_small = parts[7].reshape(-1)
    sums = []
    at = 0
    for like in (conv_weight, w_beta, norm_attn, norm_ffn, norm_head, beta_bias):
        sums.append(part_small[at : at + like.size].reshape(like.shape))
        at += like.size

    return (
        result.astype(BF16)[None],
        grad_tokens[None],
        part_qkv,
        sums[0],
        sums[1],
        sums[5],
        sums[2],
        sums[4],
        part_out,
        sums[3],
        part_gate,
        part_up,
        part_down,
    )


def solution(mesh):
    in_specs = (
        P("stream", "span", None),
        P("stream", "span", None),
        P("stream", None),
        P("span", None),
        P(None, "span"),
        P("span", None),
        P(),
        P("span"),
        P("span"),
        P("span", None),
        P("span"),
        P("span", None),
        P("span", None),
        P("span", None),
    )
    out_specs = (
        P("stream", "span", None),
        P("stream", "span", None),
        P("span", None),
        P(None, "span"),
        P("span", None),
        P(),
        P("span"),
        P("span"),
        P("span", None),
        P("span"),
        P("span", None),
        P("span", None),
        P("span", None),
    )
    return jax.shard_map(local, mesh=mesh, in_specs=in_specs, out_specs=out_specs, check_vma=False)
```

```python
import functools

import jax
import jax.numpy as jnp
from jax import lax
from jax.experimental import pallas as pl
from jax.experimental.pallas import tpu as pltpu
from jax.sharding import PartitionSpec as P

STRETCH = 64
HALO = 16
EPSILON = 1e-06
F32 = jnp.float32
BF16 = jnp.bfloat16
AXES = ("stream", "span")
VMEM_LIMIT = 56 * 2**20


def nn(a, b):
    return lax.dot_general(a, b, (((1,), (0,)), ((), ())), preferred_element_type=F32)


def nt(a, b):
    return lax.dot_general(a, b, (((1,), (1,)), ((), ())), preferred_element_type=F32)


def tn(a, b):
    return lax.dot_general(a, b, (((0,), (0,)), ((), ())), preferred_element_type=F32)


def fine(a, b):
    a_hi = a.astype(BF16)
    a_lo = (a - a_hi.astype(F32)).astype(BF16)
    b_hi = b.astype(BF16)
    b_lo = (b - b_hi.astype(F32)).astype(BF16)
    return nn(jnp.concatenate([a_hi, a_hi, a_lo], 1), jnp.concatenate([b_hi, b_lo, b_hi], 0))


def grid_ids(size):
    return (
        lax.broadcasted_iota(jnp.int32, (size, size), 0),
        lax.broadcasted_iota(jnp.int32, (size, size), 1),
    )


def unit_inverse(lower_list):
    rows, cols = grid_ids(STRETCH)
    eye = (rows == cols).astype(F32)
    out = [eye - jnp.where((rows // 2) == (cols // 2), low, 0.0) for low in lower_list]
    half = 2
    while half < STRETCH:
        cross = ((rows // (2 * half)) == (cols // (2 * half))) & ((rows // half) != (cols // half))
        inner = [fine(jnp.where(cross, low, 0.0), inv) for low, inv in zip(lower_list, out)]
        out = [inv - fine(inv, mid) for inv, mid in zip(out, inner)]
        half *= 2
    return out


def column_of(table, index):
    lanes = lax.broadcasted_iota(jnp.int32, table.shape, 1)
    return jnp.sum(jnp.where(lanes == index, table, 0.0), -1, keepdims=True)


def mix_rows(ext_ref, conv_ref, allow):
    ext = ext_ref[...].astype(F32)
    conv = conv_ref[...].astype(F32)
    shifted = [
        (ext if tap == 0 else pltpu.roll(ext, tap, 0))[HALO:] * allow[tap]
        for tap in range(conv.shape[0])
    ]
    mixed = sum(conv[tap : tap + 1] * shifted[tap] for tap in range(conv.shape[0]))
    return shifted, mixed, conv


def local_kernel(
    keep_ref, eq_ref, ek_ref, ev_ref, cq_ref, ck_ref, cv_ref, rate_ref, allow_ref,
    q_ref, k_ref, v_ref, inv_ref, wk_ref, pre_ref, end_ref, read_ref, rmap_ref, nv_ref, np_ref,
):
    head = pl.program_id(0)
    allow_all = allow_ref[...]
    allow = [allow_all[:, tap : tap + 1] for tap in range(cq_ref.shape[0])]
    rate = column_of(rate_ref[...], head)

    def unit(ref, conv):
        _, mixed, _ = mix_rows(ref, conv, allow)
        act = mixed * jax.nn.sigmoid(mixed)
        return act

    act_q = unit(eq_ref, cq_ref)
    act_k = unit(ek_ref, ck_ref)
    act_v = unit(ev_ref, cv_ref)
    queries = (act_q * lax.rsqrt(jnp.sum(act_q * act_q, -1, keepdims=True) + EPSILON)).astype(BF16)
    keys = (act_k * lax.rsqrt(jnp.sum(act_k * act_k, -1, keepdims=True) + EPSILON)).astype(BF16)
    values = act_v.astype(BF16)
    q_ref[...] = queries
    k_ref[...] = keys
    v_ref[...] = values
    count = queries.shape[0] // STRETCH
    rows, cols = grid_ids(STRETCH)
    parts = [slice(n * STRETCH, (n + 1) * STRETCH) for n in range(count)]
    lows = []
    for part in parts:
        gram = nt(keys[part], keys[part])
        lows.append(jnp.where(rows > cols, gram * rate[part], 0.0))
    invs = unit_inverse(lows)
    size = keys.shape[1]
    drows, dcols = grid_ids(size)
    running = jnp.concatenate(
        [jnp.zeros((size, size), F32), (drows == dcols).astype(F32)], 0
    )
    for n, part in enumerate(parts):
        key, query = keys[part], queries[part]
        inv = invs[n].astype(BF16)
        inv_ref[0, part, :] = inv
        scaled = jnp.concatenate(
            [key.astype(F32) * rate[part], values[part].astype(F32) * rate[part]], 1
        ).astype(BF16)
        weighted = nn(inv, scaled)
        wkey = weighted[:, :size].astype(BF16)
        wk_ref[part, :] = wkey
        running = running * keep_ref[n]
        low_state = running.astype(BF16)
        pre_ref[0, n] = low_state
        back = nt(jnp.concatenate([wkey, query], 0), low_state)
        new = jnp.concatenate(
            [weighted[:, size:] - back[:STRETCH, :size], -back[:STRETCH, size:]], 1
        ).astype(BF16)
        nv_ref[part, :] = new[:, :size]
        np_ref[part, :] = new[:, size:]
        scores = jnp.where(rows >= cols, nt(query, key), 0.0).astype(BF16)
        out = back[STRETCH:] + nn(scores, new)
        read_ref[part, :] = out[:, :size]
        rmap_ref[part, :] = out[:, size:].astype(BF16)
        running = running + tn(new, key)
    end_ref[0] = running.astype(BF16)


def adjoint_body(
    keep_ref, gn_ref, read_ref, gain_ref, q_ref, k_ref, wk_ref, go_ref, adj_ref, gain_grad_ref
):
    grad, readout = gn_ref[...], read_ref[...]
    inv = lax.rsqrt(jnp.mean(readout * readout, -1, keepdims=True) + EPSILON)
    scaled = grad * gain_ref[...]
    grad_read = inv * scaled - readout * (inv * inv * inv) * jnp.mean(
        scaled * readout, -1, keepdims=True
    )
    gain_grad_ref[0] = jnp.sum(grad * readout * inv, 0, keepdims=True)
    grad_read = grad_read.astype(BF16)
    go_ref[...] = grad_read
    count = grad.shape[0] // STRETCH
    rows, cols = grid_ids(STRETCH)
    size = grad.shape[1]
    adj = jnp.zeros((size, size), F32)
    for n in range(count - 1, -1, -1):
        part = slice(n * STRETCH, (n + 1) * STRETCH)
        key, query, out = k_ref[part, :], q_ref[part, :], grad_read[part]
        scores = jnp.where(rows >= cols, nt(query, key), 0.0).astype(BF16)
        new_grad = tn(scores, out) + nt(key, adj.astype(BF16))
        adj = (
            adj
            + tn(
                jnp.concatenate([out, (-new_grad).astype(BF16)], 0),
                jnp.concatenate([query, wk_ref[part, :]], 0),
            )
        ) * keep_ref[n]
    adj_ref[0] = adj.astype(BF16)


def backward_body(
    head, keep_ref, din_ref, min_ref, pre_ref, go_ref, q_ref, k_ref, v_ref, inv_ref, wk_ref,
    nv_ref, np_ref, rate_ref, allow_ref,
    eq_ref, ek_ref, ev_ref, cq_ref, ck_ref, cv_ref,
    gext_ref, gconv_ref, grate_ref,
    gq_buf, gk_buf, gv_buf,
):
    size = q_ref.shape[1]
    tok = q_ref.shape[0]
    count = tok // STRETCH
    rows, cols = grid_ids(STRETCH)
    rate = column_of(rate_ref[...], head)
    low_in = min_ref[0]
    adj = din_ref[0].astype(F32)
    grate_parts = [None] * count
    for n in range(count - 1, -1, -1):
        part = slice(n * STRETCH, (n + 1) * STRETCH)
        key, query, value, out = k_ref[part, :], q_ref[part, :], v_ref[part, :], go_ref[part, :]
        beta = rate[part]
        pre = pre_ref[0, n]
        state = (nn(low_in, pre[size:]) + pre[:size].astype(F32)).astype(BF16)
        new = (nt(np_ref[part, :], low_in) + nv_ref[part, :].astype(F32)).astype(BF16)
        low_adj = adj.astype(BF16)
        gram_both = nt(jnp.concatenate([key, query], 0), key)
        gram = gram_both[:STRETCH]
        scores = jnp.where(rows >= cols, gram_both[STRETCH:], 0.0).astype(BF16)
        new_grad = tn(scores, out) + nt(key, low_adj)
        low_new_grad = new_grad.astype(BF16)
        adj = (
            adj
            + tn(
                jnp.concatenate([out, -low_new_grad], 0),
                jnp.concatenate([query, wk_ref[part, :]], 0),
            )
        ) * keep_ref[n]
        grad_b = tn(inv_ref[0, part, :], low_new_grad)
        both = nt(jnp.concatenate([out, grad_b.astype(BF16)], 0), new)
        grad_scores = jnp.where(rows >= cols, both[:STRETCH], 0.0).astype(BF16)
        grad_low = jnp.where(rows > cols, -both[STRETCH:], 0.0)
        left = value.astype(F32) - nt(key, state)
        grate_parts[n] = jnp.sum(grad_low * gram, -1, keepdims=True) + jnp.sum(
            grad_b * left, -1, keepdims=True
        )
        grad_v = beta * grad_b
        grad_gram = beta * grad_low
        symmetric = (grad_gram + grad_gram.T).astype(BF16)
        by_state = nn(jnp.concatenate([out, -grad_v.astype(BF16)], 0), state)
        gq_buf[part, :] = by_state[:STRETCH] + nn(grad_scores, key)
        gk_buf[part, :] = (
            by_state[STRETCH:]
            + tn(grad_scores, query)
            + nn(jnp.concatenate([new, symmetric], 1), jnp.concatenate([low_adj, key], 0))
        )
        gv_buf[part, :] = grad_v
    grate = jnp.concatenate(grate_parts, 0)
    lanes = lax.broadcasted_iota(jnp.int32, grate_ref.shape, 1)
    before = jnp.where(head == 0, jnp.zeros(grate_ref.shape, F32), grate_ref[...])
    grate_ref[...] = jnp.where(lanes == head, grate, before)
    allow_all = allow_ref[...]
    allow = [allow_all[:, tap : tap + 1] for tap in range(cq_ref.shape[0])]
    zeros = jnp.zeros((HALO, size), F32)
    for i, (ext, conv_ref, buf) in enumerate(
        ((eq_ref, cq_ref, gq_buf), (ek_ref, ck_ref, gk_buf), (ev_ref, cv_ref, gv_buf))
    ):
        shifted, mixed, conv = mix_rows(ext, conv_ref, allow)
        sig = jax.nn.sigmoid(mixed)
        grad = buf[...]
        if i < 2:
            raw = mixed * sig
            inv = lax.rsqrt(jnp.sum(raw * raw, -1, keepdims=True) + EPSILON)
            grad = inv * grad - raw * (inv * inv * inv) * jnp.sum(grad * raw, -1, keepdims=True)
        grad = grad * (sig * (1.0 + mixed * (1.0 - sig)))
        total = None
        for tap in range(conv.shape[0]):
            gconv_ref[i, tap : tap + 1, :] = jnp.sum(grad * shifted[tap], 0, keepdims=True)
            term = jnp.concatenate([zeros, grad * (conv[tap : tap + 1] * allow[tap])], 0)
            if tap:
                term = pltpu.roll(term, tok + HALO - tap, 0)
            total = term if total is None else total + term
        gext_ref[i] = total.astype(BF16)


def silu_slope(pre_act, sig_value):
    return sig_value * (1.0 + pre_act * (1.0 - sig_value))


def norm_back(grad_in, values, inv_rms, gain_vec):
    scaled = grad_in * gain_vec
    return inv_rms * scaled - values * inv_rms**3 * jnp.mean(scaled * values, -1, keepdims=True)


def product(pattern, first, second, kind=F32):
    return jnp.einsum(pattern, first, second, preferred_element_type=F32).astype(kind)


def swap_core(block):
    streams, spans = lax.axis_size("stream"), lax.axis_size("span")
    pairs = [
        (s * spans + p, s * spans + (p ^ 1)) for s in range(streams) for p in range(spans)
    ]
    return lax.ppermute(block, AXES, pairs)


def pair_tokens(block):
    return jnp.concatenate([block, swap_core(block)], 0)


def pair_columns(block, spans):
    core = lax.axis_index("span") % 2
    rows, width = block.shape
    split = block.reshape(rows, spans // 2, 2, width // spans)
    mine = lax.dynamic_index_in_dim(split, core, 2, keepdims=False).reshape(rows, -1)
    theirs = lax.dynamic_index_in_dim(split, 1 - core, 2, keepdims=False).reshape(rows, -1)
    return jnp.concatenate([mine, swap_core(theirs)], 0)


def weight_grad(left, right, spans):
    grad = product("td,te->de", left, right, BF16)
    return grad.reshape(spans // 2, -1, grad.shape[1])


MESH = pl.DeviceIdType.MESH


class Place:
    def __init__(self, streams, spans):
        self.streams, self.spans, self.chips = streams, spans, spans // 2
        self.stream = lax.axis_index("stream")
        self.span = lax.axis_index("span")
        self.chip = lax.div(self.span, 2)
        self.core = lax.rem(self.span, 2)

    def beside(self, step):
        return (self.stream ^ step, self.span)

    def along(self, step):
        return (self.stream, 2 * self.shifted(step) + self.core)

    def shifted(self, step):
        return lax.rem(self.chip + step + self.chips, self.chips)

    def other(self):
        return (self.stream, 2 * self.chip + 1 - self.core)


def greet(places):
    barrier = pltpu.get_barrier_semaphore()
    for target in places:
        pl.semaphore_signal(barrier, inc=1, device_id=target, device_id_type=MESH)
    pl.semaphore_wait(barrier, len(places))


def quarter_of(rows, width, streams):
    if (width // 128) % streams == 0:
        return 1, streams
    return 2, streams // 2


def quarter_index(rows, width, streams, at, piece=0, pieces=1):
    down, across = quarter_of(rows, width, streams)
    r, c = rows // down, width // across
    row = pl.ds(0, rows) if down == 1 else pl.ds(pl.multiple_of(lax.div(at, across) * r, r), r)
    start = lax.rem(at, across) * c + piece * (c // pieces)
    return row, pl.ds(pl.multiple_of(start, 128), c // pieces)


def copy_to(source, target, send_sem, recv_sem, device):
    return pltpu.make_async_remote_copy(
        src_ref=source, dst_ref=target, send_sem=send_sem, recv_sem=recv_sem,
        device_id=device, device_id_type=MESH,
    )


class Gather:
    def __init__(self, place, shards, fulls, sems):
        self.place, self.shards, self.fulls = place, shards, fulls
        self.sems = sems
        self.units = []
        for w, shard in enumerate(shards):
            rows, width = shard.shape
            _, across = quarter_of(rows, width, place.streams)
            pieces = 2 if (width // across) % 256 == 0 else 1
            for piece in range(pieces):
                self.units.append((w, piece, pieces))

    @staticmethod
    def sem_shapes(shapes, streams, spans):
        units = 0
        for rows, width in shapes:
            _, across = quarter_of(rows, width, streams)
            units += 2 if (width // across) % 256 == 0 else 1
        slots = spans // 2
        dma = pltpu.SemaphoreType.DMA
        return [dma((units, slots, 4, 2)), dma((len(shapes), slots, 2)), dma((len(shapes),))]

    def part(self, unit, at, span=None):
        w, piece, pieces = self.units[unit]
        rows, width = self.shards[w].shape
        index = quarter_index(rows, width, self.place.streams, at, piece, pieces)
        if span is None:
            return self.shards[w].at[index]
        return self.fulls[w].at[(span,) + index]

    def source_span(self, k):
        return 2 * self.place.shifted(-k) + self.place.core

    def wire(self, unit, k, kind, span, at, device, source=None):
        region = self.part(unit, at, span)
        return copy_to(
            region if source is None else source, region,
            self.sems[0].at[unit, k, kind, 0], self.sems[0].at[unit, k, kind, 1], device,
        )

    def along(self, unit, k):
        p = self.place
        return self.wire(
            unit, k, 0, p.span, p.stream, p.along(k), self.part(unit, p.stream)
        )

    def along_wait(self, unit, k):
        p = self.place
        self.wire(unit, k, 0, self.source_span(k), p.stream, p.along(k)).wait_recv()

    def sideways(self, unit, k, step):
        p = self.place
        return self.wire(unit, k, step, self.source_span(k), p.stream, p.beside(step))

    def sideways_wait(self, unit, k, step):
        p = self.place
        self.wire(
            unit, k, step, self.source_span(k), p.stream ^ step, p.beside(step)
        ).wait_recv()

    @staticmethod
    def turns(unit, k):
        return (1, 2) if (unit + k) % 2 == 0 else (2, 1)

    def corner(self, unit, k):
        p = self.place
        first, second = self.turns(unit, k)
        return self.wire(
            unit, k, 3, self.source_span(k), p.stream ^ first, p.beside(second)
        )

    def corner_wait(self, unit, k):
        p = self.place
        self.wire(unit, k, 3, self.source_span(k), p.stream ^ 3, p.beside(1)).wait_recv()

    def across(self, w, k):
        p = self.place
        span = p.span if k == 0 else self.source_span(k)
        region = self.fulls[w].at[span]
        return copy_to(
            self.shards[w] if k == 0 else region, region,
            self.sems[1].at[w, k, 0], self.sems[1].at[w, k, 1], p.other(),
        )

    def across_wait(self, w, k):
        p = self.place
        span = 2 * p.shifted(-k) + 1 - p.core
        region = self.fulls[w].at[span]
        copy_to(
            region, region, self.sems[1].at[w, k, 0], self.sems[1].at[w, k, 1], p.other()
        ).wait_recv()

    def own(self, w):
        return pltpu.make_async_copy(
            self.shards[w], self.fulls[w].at[self.place.span], self.sems[2].at[w]
        )

    def neighbours(self):
        p = self.place
        return (
            [p.along(k) for k in range(1, p.chips)] + [p.beside(1), p.beside(2), p.other()]
        )

    def steps(self):
        p = self.place
        slots = range(1, p.chips)
        count = len(self.units)
        ends = {}
        for unit, (w, piece, pieces) in enumerate(self.units):
            if piece == pieces - 1:
                ends[unit] = w
        steps = []

        def begin(unit):
            w, piece, pieces = self.units[unit]
            for k in slots:
                self.along(unit, k).start()
            if piece == 0:
                self.across(w, 0).start()
                self.own(w).start()

        def beside(unit, k):
            self.along_wait(unit, k)
            self.sideways(unit, k, 1).start()
            self.sideways(unit, k, 2).start()

        def turn(unit, k):
            self.sideways_wait(unit, k, self.turns(unit, k)[0])
            self.corner(unit, k).start()

        def close(w, k):
            for unit, (owner, _, _) in enumerate(self.units):
                if owner == w:
                    self.sideways_wait(unit, k, self.turns(unit, k)[1])
                    self.corner_wait(unit, k)
            self.across(w, k).start()

        def finish(w):
            for k in range(p.chips):
                self.across_wait(w, k)
                self.across(w, k).wait_send()
            self.own(w).wait()
            for unit, (owner, _, _) in enumerate(self.units):
                if owner == w:
                    for k in slots:
                        self.along(unit, k).wait_send()
                        self.sideways(unit, k, 1).wait_send()
                        self.sideways(unit, k, 2).wait_send()
                        self.corner(unit, k).wait_send()

        for unit in range(min(2, count)):
            steps.append(functools.partial(begin, unit))
        for turn_at in range(count + 2):
            if turn_at + 2 < count:
                steps.append(functools.partial(begin, turn_at + 2))
            if turn_at < count:
                steps += [functools.partial(beside, turn_at, k) for k in slots]
            if 0 <= turn_at - 1 < count:
                steps += [functools.partial(turn, turn_at - 1, k) for k in slots]
            if turn_at - 2 in ends:
                steps += [functools.partial(close, ends[turn_at - 2], k) for k in slots]
        steps += [functools.partial(finish, w) for w in range(len(self.shards))]
        return steps


def gather_kernel(streams, spans, count, *refs):
    shards, fulls, sems = refs[:count], refs[count : 2 * count], refs[2 * count :]
    place = Place(streams, spans)
    work = Gather(place, shards, fulls, sems)
    greet(work.neighbours())
    for step in work.steps():
        step()


def gather_call(shards, collective_id):
    streams, spans = lax.axis_size("stream"), lax.axis_size("span")
    shapes = [shard.shape for shard in shards]
    outs = pl.pallas_call(
        functools.partial(gather_kernel, streams, spans, len(shards)),
        in_specs=[pl.BlockSpec(memory_space=pl.ANY)] * len(shards),
        out_specs=[pl.BlockSpec(memory_space=pl.ANY)] * len(shards),
        out_shape=[jax.ShapeDtypeStruct((spans,) + s.shape, s.dtype) for s in shards],
        scratch_shapes=Gather.sem_shapes(shapes, streams, spans),
        compiler_params=pltpu.CompilerParams(
            collective_id=collective_id, has_side_effects=True, vmem_limit_bytes=VMEM_LIMIT
        ),
        name="gather_weights",
    )(*shards)
    return outs


class Reduce:
    def __init__(self, place, grads, outs, bufs, sems):
        self.place, self.grads, self.outs, self.bufs, self.sems = place, grads, outs, bufs, sems

    @staticmethod
    def block(shape, streams):
        _, rows, width = shape
        down, across = quarter_of(rows, width, streams)
        return rows // down, width // across

    @staticmethod
    def scratch(shapes, kinds, streams):
        out = []
        dma = pltpu.SemaphoreType.DMA
        for shape, kind in zip(shapes, kinds):
            chips = shape[0]
            r, c = Reduce.block(shape, streams)
            out += [
                pltpu.VMEM((2, chips, r, c), kind),
                pltpu.VMEM((2, chips, r, c), kind),
                pltpu.VMEM((chips, r, c), kind),
                pltpu.VMEM((chips, r, c), kind),
                pltpu.VMEM((chips, r, c), kind),
                pltpu.VMEM((streams, r, c), kind),
            ]
        n = len(shapes)
        chips = shapes[0][0]
        out += [dma((n, 2, 3, 2)), dma((n, chips, 2)), dma((n, streams, 2))]
        return out

    def turn(self, w, half):
        return (1, 2) if (w + half) % 2 == 0 else (2, 1)

    def chips_of(self, half):
        n = self.place.chips // 2
        return half * n, n

    def region(self, w, half, at):
        _, rows, width = self.grads[w].shape
        start, n = self.chips_of(half)
        return (pl.ds(start, n),) + quarter_index(rows, width, self.place.streams, at)

    def first(self, w, half, slot):
        p = self.place
        a, b = self.turn(w, half)
        start, n = self.chips_of(half)
        at = p.stream ^ a if slot == 0 else p.stream ^ a ^ b
        return copy_to(
            self.grads[w].at[self.region(w, half, at)],
            self.bufs[w][0].at[slot, pl.ds(start, n)],
            self.sems[0].at[w, half, slot, 0], self.sems[0].at[w, half, slot, 1], p.beside(a),
        )

    def second(self, w, half):
        p = self.place
        _, b = self.turn(w, half)
        start, n = self.chips_of(half)
        return copy_to(
            self.bufs[w][1].at[1, pl.ds(start, n)], self.bufs[w][2].at[pl.ds(start, n)],
            self.sems[0].at[w, half, 2, 0], self.sems[0].at[w, half, 2, 1], p.beside(b),
        )

    def third(self, w, k):
        p = self.place
        return copy_to(
            self.bufs[w][3].at[p.shifted(k)], self.bufs[w][4].at[k],
            self.sems[1].at[w, k, 0], self.sems[1].at[w, k, 1], p.along(k),
        )

    def fourth(self, w, step):
        p = self.place
        return copy_to(
            self.bufs[w][5].at[0], self.bufs[w][5].at[step],
            self.sems[2].at[w, step, 0], self.sems[2].at[w, step, 1], p.beside(step),
        )

    def neighbours(self):
        p = self.place
        return [p.along(k) for k in range(1, p.chips)] + [
            p.beside(s) for s in range(1, p.streams)
        ]

    def begin(self, w):
        for half in range(2):
            for slot in (1, 0):
                self.first(w, half, slot).start()

    def add_first(self, w, half):
        p = self.place
        _, b = self.turn(w, half)
        start, n = self.chips_of(half)
        for slot in (1, 0):
            self.first(w, half, slot).wait_recv()
            at = p.stream ^ b if slot else p.stream
            _, row, col = self.region(w, half, at)
            for chip in range(start, start + n):
                self.bufs[w][1][slot, chip] = (
                    self.grads[w][chip, row, col].astype(F32)
                    + self.bufs[w][0][slot, chip].astype(F32)
                ).astype(self.grads[w].dtype)
            if slot:
                self.second(w, half).start()

    def add_second(self, w, half):
        start, n = self.chips_of(half)
        self.second(w, half).wait_recv()
        for chip in range(start, start + n):
            self.bufs[w][3][chip] = (
                self.bufs[w][1][0, chip].astype(F32) + self.bufs[w][2][chip].astype(F32)
            ).astype(self.grads[w].dtype)

    def spread(self, w):
        for k in range(1, self.place.chips):
            self.third(w, k).start()

    def add_third(self, w):
        p = self.place
        total = self.bufs[w][3][p.chip].astype(F32)
        for k in range(1, p.chips):
            self.third(w, k).wait_recv()
            total = total + self.bufs[w][4][k].astype(F32)
        self.bufs[w][5][0] = total.astype(self.grads[w].dtype)
        for step in range(1, p.streams):
            self.fourth(w, step).start()

    def finish(self, w):
        p = self.place
        _, rows, width = self.grads[w].shape
        for step in range(p.streams):
            if step:
                self.fourth(w, step).wait_recv()
            row, col = quarter_index(rows, width, p.streams, p.stream ^ step)
            self.outs[w][row, col] = self.bufs[w][5][step]
        for half in range(2):
            for slot in range(2):
                self.first(w, half, slot).wait_send()
            self.second(w, half).wait_send()
        for k in range(1, p.chips):
            self.third(w, k).wait_send()
        for step in range(1, p.streams):
            self.fourth(w, step).wait_send()

    def steps(self):
        count = len(self.grads)
        steps = [functools.partial(self.begin, w) for w in range(count)]
        for t in range(count + 3):
            if t < count:
                steps += [functools.partial(self.add_first, t, half) for half in range(2)]
            if 0 <= t - 1 < count:
                steps += [functools.partial(self.add_second, t - 1, half) for half in range(2)]
                steps.append(functools.partial(self.spread, t - 1))
            if 0 <= t - 2 < count:
                steps.append(functools.partial(self.add_third, t - 2))
            if 0 <= t - 3 < count:
                steps.append(functools.partial(self.finish, t - 3))
        return steps


def reduce_kernel(streams, spans, count, *refs):
    grads, outs, rest = refs[:count], refs[count : 2 * count], refs[2 * count :]
    bufs = [rest[6 * w : 6 * w + 6] for w in range(count)]
    work = Reduce(Place(streams, spans), grads, outs, bufs, rest[6 * count :])
    greet(work.neighbours())
    for step in work.steps():
        step()


def reduce_call(grads, collective_id):
    streams, spans = lax.axis_size("stream"), lax.axis_size("span")
    shapes = [grad.shape for grad in grads]
    vmem = pl.BlockSpec(memory_space=pltpu.VMEM)
    return pl.pallas_call(
        functools.partial(reduce_kernel, streams, spans, len(grads)),
        in_specs=[vmem] * len(grads),
        out_specs=[vmem] * len(grads),
        out_shape=[jax.ShapeDtypeStruct(g.shape[1:], g.dtype) for g in grads],
        scratch_shapes=Reduce.scratch(shapes, [g.dtype for g in grads], streams),
        compiler_params=pltpu.CompilerParams(
            collective_id=collective_id, has_side_effects=True, vmem_limit_bytes=VMEM_LIMIT
        ),
        name="reduce_grads",
    )(*grads)


def chain_body(p, backward, source, maps, state_ref, scratch):
    p_low, p_high, p_chip = maps
    swap, carry, outgo, sent = scratch[:4]
    swap_sem, hop_sem, back_sem = scratch[-3:]
    s_chip = None if backward else scratch[4]
    heads, size = source.shape[0], source.shape[2]
    half = heads // 2
    mine = p.core * half
    theirs = (1 - p.core) * half
    ahead, behind = (-1, 1) if backward else (1, -1)
    edge_in = p.chips - 1 if backward else 0
    edge_out = 0 if backward else p.chips - 1
    swap_copy = copy_to(
        source.at[pl.ds(theirs, half)], swap, swap_sem.at[0], swap_sem.at[1], p.other()
    )
    swap_copy.start()
    swap_copy.wait_recv()
    low_core = p.core == 0
    for h in range(half):
        own, got = source[mine + h], swap[h]
        low = jnp.where(low_core, own, got)
        high = jnp.where(low_core, got, own)
        if backward:
            outgo[h] = low.astype(F32) + nt(high, p_low[h])
        else:
            joined = nn(low, high[size:])
            s_chip[h] = joined[:size] + high[:size].astype(F32)
            p_chip[h] = joined[size:].astype(BF16)
            p_low[h] = low[size:]
            p_high[h] = high[size:]
            outgo[h] = low[:size].astype(F32)

    def hop(h):
        return copy_to(
            sent.at[h], carry.at[h], hop_sem.at[h, 0], hop_sem.at[h, 1], p.along(ahead)
        )

    @pl.when(p.chip == edge_in)
    def _():
        carry[...] = jnp.zeros(carry.shape, BF16)

    for h in range(half):

        @pl.when(p.chip != edge_in)
        def _():
            hop(h).wait_recv()

        moved = nt(carry[h], p_chip[h]) + outgo[h] if backward else nn(carry[h], p_chip[h]) + s_chip[h]
        sent[h] = moved.astype(BF16)

        @pl.when(p.chip != edge_out)
        def _():
            hop(h).start()

    for h in range(half):
        state = carry[h]
        if backward:
            low_state = (nt(state, p_high[h]) + jnp.where(low_core, swap[h], source[mine + h]).astype(F32)).astype(BF16)
            keep = jnp.where(low_core, low_state, state)
            give = jnp.where(low_core, state, low_state)
        else:
            high_state = (nn(state, p_low[h]) + outgo[h]).astype(BF16)
            keep = jnp.where(low_core, state, high_state)
            give = jnp.where(low_core, high_state, state)
        state_ref[mine + h] = keep
        sent[half + h] = give
    back = copy_to(
        sent.at[pl.ds(half, half)], state_ref.at[pl.ds(mine, half)],
        back_sem.at[0], back_sem.at[1], p.other(),
    )
    back.start()
    copy_to(
        sent.at[pl.ds(half, half)], state_ref.at[pl.ds(theirs, half)],
        back_sem.at[0], back_sem.at[1], p.other(),
    ).wait_recv()
    back.wait_send()
    swap_copy.wait_send()

    @pl.when(p.chip != edge_out)
    def _():
        for h in range(half):
            hop(h).wait_send()


def chain_scratch(heads, size, rows, backward):
    half = heads // 2
    dma = pltpu.SemaphoreType.DMA
    scratch = [
        pltpu.VMEM((half, rows, size), BF16),
        pltpu.VMEM((half, size, size), BF16),
        pltpu.VMEM((half, size, size), F32),
        pltpu.VMEM((heads, size, size), BF16),
    ]
    if not backward:
        scratch.append(pltpu.VMEM((half, size, size), F32))
    return scratch + [dma((2,)), dma((half, 2)), dma((2,))]


def readout_body(readout, gain):
    inv = lax.rsqrt(jnp.mean(readout * readout, -1, keepdims=True) + EPSILON)
    return (readout * inv * gain).astype(BF16)


def spread_steps(steps, slots, index):
    count = len(steps)
    return steps[count * index // slots : count * (index + 1) // slots]


def forward_kernel(streams, spans, heads, weights, *refs):
    ins, refs = refs[:10], refs[10:]
    shards, refs = refs[:weights], refs[weights:]
    outs, refs = refs[:14], refs[14:]
    fulls, refs = refs[:weights], refs[weights:]
    gather_sems, refs = refs[:3], refs[3:]
    map_buf, read_buf, rmap_buf, state_buf = refs[:4]
    chain_bufs = refs[4:]
    gain_ref = ins[9]
    (q_ref, k_ref, v_ref, inv_ref, wk_ref, pre_ref, nv_ref, np_ref,
     state_ref, p_low, p_high, p_chip, out_ref, normal_ref) = outs
    step_id = pl.program_id(0)
    place = Place(streams, spans)
    work = Gather(place, shards, fulls, gather_sems)
    steps = work.steps()

    @pl.when(step_id == 0)
    def _():
        greet(work.neighbours())

    for index in range(heads + 1):

        @pl.when(step_id == index)
        def _():
            for step in spread_steps(steps, heads + 2, index):
                step()

    @pl.when(step_id < heads)
    def _():
        local_kernel(
            *ins[:9], q_ref, k_ref, v_ref, inv_ref, wk_ref, pre_ref, map_buf.at[pl.ds(step_id, 1)],
            read_buf.at[step_id], rmap_buf.at[step_id], nv_ref, np_ref,
        )

    @pl.when(step_id == heads)
    def _():
        chain_body(place, False, map_buf, (p_low, p_high, p_chip), state_buf, chain_bufs)
        state_ref[...] = state_buf[...]
        size = gain_ref.shape[1]
        for h in range(heads):
            cols = slice(h * size, (h + 1) * size)
            readout = read_buf[h] + nt(rmap_buf[h], state_buf[h])
            out_ref[:, cols] = readout
            normal_ref[:, cols] = readout_body(readout, gain_ref[...])
        for step in spread_steps(steps, heads + 2, heads + 1):
            step()


def forward_call(keep, ext, conv, rate, allow, gain, shards, heads, collective_id):
    streams, spans = lax.axis_size("stream"), lax.axis_size("span")
    tok = rate.shape[0]
    width = ext.shape[1] // 3
    size = width // heads
    count = tok // STRETCH
    taps = conv.shape[0]
    rows = ext.shape[0]
    half = heads // 2
    hbm = pl.BlockSpec(memory_space=pl.ANY)

    def at(i):
        return jnp.minimum(i, heads - 1)

    def third(i, r):
        return pl.BlockSpec((r, size), lambda h: (0, at(h) + i * heads))

    def token_block():
        return pl.BlockSpec((tok, size), lambda h: (0, at(h)))

    def whole(*shape):
        return pl.BlockSpec(shape, lambda h: (0,) * len(shape))

    token_shape = jax.ShapeDtypeStruct((tok, width), BF16)
    square = jax.ShapeDtypeStruct((half, size, size), BF16)
    shapes = [s.shape for s in shards]
    outs = pl.pallas_call(
        functools.partial(forward_kernel, streams, spans, heads, len(shards)),
        grid=(heads + 1,),
        in_specs=[
            pl.BlockSpec(memory_space=pltpu.SMEM),
            third(0, rows), third(1, rows), third(2, rows),
            third(0, taps), third(1, taps), third(2, taps),
            whole(tok, heads), whole(tok, taps), whole(1, size),
        ]
        + [hbm] * len(shards),
        out_specs=[
            token_block(), token_block(), token_block(),
            pl.BlockSpec((1, tok, STRETCH), lambda h: (at(h), 0, 0)),
            token_block(),
            pl.BlockSpec((1, count, 2 * size, size), lambda h: (at(h), 0, 0, 0)),
            token_block(), token_block(),
            whole(heads, size, size),
            whole(half, size, size), whole(half, size, size), whole(half, size, size),
            whole(tok, width), whole(tok, width),
        ]
        + [hbm] * len(shards),
        out_shape=[
            token_shape, token_shape, token_shape,
            jax.ShapeDtypeStruct((heads, tok, STRETCH), BF16),
            token_shape,
            jax.ShapeDtypeStruct((heads, count, 2 * size, size), BF16),
            token_shape, token_shape,
            jax.ShapeDtypeStruct((heads, size, size), BF16),
            square, square, square,
            jax.ShapeDtypeStruct((tok, width), F32),
            token_shape,
        ]
        + [jax.ShapeDtypeStruct((spans,) + s.shape, s.dtype) for s in shards],
        scratch_shapes=Gather.sem_shapes(shapes, streams, spans)
        + [
            pltpu.VMEM((heads, 2 * size, size), BF16),
            pltpu.VMEM((heads, tok, size), F32),
            pltpu.VMEM((heads, tok, size), BF16),
            pltpu.VMEM((heads, size, size), BF16),
        ]
        + chain_scratch(heads, size, 2 * size, False),
        compiler_params=pltpu.CompilerParams(
            collective_id=collective_id, has_side_effects=True, vmem_limit_bytes=VMEM_LIMIT
        ),
        name="delta_forward",
    )(keep, ext, ext, ext, conv, conv, conv, rate, allow, gain, *shards)
    return outs[:14], outs[14:]


def backward_kernel(streams, spans, heads, weights, *refs):
    (keep_ref, gn_ref, read_ref, gain_ref, q_ref, k_ref, v_ref, wk_ref, inv_ref, min_ref, pre_ref,
     nv_ref, np_ref, rate_ref, allow_ref, eq_ref, ek_ref, ev_ref, cq_ref, ck_ref, cv_ref,
     p_low, p_high, p_chip) = refs[:24]
    refs = refs[24:]
    grads, refs = refs[:weights], refs[weights:]
    gext_ref, gconv_ref, grate_ref, gain_grad_ref = refs[:4]
    sums, refs = refs[4 : 4 + weights], refs[4 + weights :]
    bufs, refs = [refs[6 * w : 6 * w + 6] for w in range(weights)], refs[6 * weights :]
    reduce_sems, refs = refs[:3], refs[3:]
    go_buf, adj_buf, din_buf = refs[:3]
    row_bufs, chain_bufs = refs[3:6], refs[6:]
    step_id = pl.program_id(0)
    place = Place(streams, spans)
    work = Reduce(place, grads, sums, bufs, reduce_sems)
    steps = work.steps()
    slots = 2 * heads + 2

    @pl.when(step_id == 0)
    def _():
        greet(work.neighbours() + [place.other()])

    for index in range(2 * heads + 1):

        @pl.when(step_id == index)
        def _():
            for step in spread_steps(steps, slots, index):
                step()

    @pl.when(step_id < heads)
    def _():
        adjoint_body(
            keep_ref, gn_ref, read_ref, gain_ref, q_ref, k_ref, wk_ref,
            go_buf.at[step_id], adj_buf.at[pl.ds(step_id, 1)], gain_grad_ref,
        )

    @pl.when(step_id == heads)
    def _():
        chain_body(place, True, adj_buf, (p_low, p_high, p_chip), din_buf, chain_bufs)

    @pl.when(step_id > heads)
    def _():
        head = step_id - heads - 1
        backward_body(
            head, keep_ref, din_buf.at[pl.ds(head, 1)], min_ref, pre_ref, go_buf.at[head],
            q_ref, k_ref, v_ref, inv_ref, wk_ref, nv_ref, np_ref, rate_ref, allow_ref,
            eq_ref, ek_ref, ev_ref, cq_ref, ck_ref, cv_ref,
            gext_ref, gconv_ref, grate_ref, *row_bufs,
        )

    @pl.when(step_id == 2 * heads)
    def _():
        for step in spread_steps(steps, slots, slots - 1):
            step()


def backward_call(
    keep, grad_normal, readout, gain, queries, keys, values, wkeys, invs, state, prefix,
    new_v, new_p, rate, allow, ext, conv, maps, grads, heads, collective_id,
):
    streams, spans = lax.axis_size("stream"), lax.axis_size("span")
    tok, width = queries.shape
    size = width // heads
    count = tok // STRETCH
    taps = conv.shape[0]
    rows = ext.shape[0]
    half = heads // 2

    def first(i):
        return jnp.minimum(i, heads - 1)

    def second(i):
        return jnp.maximum(i - heads - 1, 0)

    def both(i):
        return jnp.where(i < heads, i, jnp.maximum(i - heads - 1, 0))

    def block(at):
        return pl.BlockSpec((tok, size), lambda h: (0, at(h)))

    def third(i, r):
        return pl.BlockSpec((r, size), lambda h: (0, second(h) + i * heads))

    def whole(*shape):
        return pl.BlockSpec(shape, lambda h: (0,) * len(shape))

    vmem = pl.BlockSpec(memory_space=pltpu.VMEM)
    shapes = [g.shape for g in grads]
    outs = pl.pallas_call(
        functools.partial(backward_kernel, streams, spans, heads, len(grads)),
        grid=(2 * heads + 1,),
        in_specs=[
            pl.BlockSpec(memory_space=pltpu.SMEM),
            block(first), block(first), whole(1, size),
            block(both), block(both), block(second), block(both),
            pl.BlockSpec((1, tok, STRETCH), lambda h: (second(h), 0, 0)),
            pl.BlockSpec((1, size, size), lambda h: (second(h), 0, 0)),
            pl.BlockSpec((1, count, 2 * size, size), lambda h: (second(h), 0, 0, 0)),
            block(second), block(second),
            whole(tok, heads), whole(tok, taps),
            third(0, rows), third(1, rows), third(2, rows),
            third(0, taps), third(1, taps), third(2, taps),
            whole(half, size, size), whole(half, size, size), whole(half, size, size),
        ]
        + [vmem] * len(grads),
        out_specs=[
            pl.BlockSpec((3, rows, size), lambda h: (0, 0, second(h))),
            pl.BlockSpec((3, taps, size), lambda h: (0, 0, second(h))),
            whole(tok, heads),
            pl.BlockSpec((1, 1, size), lambda h: (first(h), 0, 0)),
        ]
        + [vmem] * len(grads),
        out_shape=[
            jax.ShapeDtypeStruct((3, rows, width), BF16),
            jax.ShapeDtypeStruct((3, taps, width), F32),
            jax.ShapeDtypeStruct((tok, heads), F32),
            jax.ShapeDtypeStruct((heads, 1, size), F32),
        ]
        + [jax.ShapeDtypeStruct(g.shape[1:], g.dtype) for g in grads],
        scratch_shapes=Reduce.scratch(shapes, [g.dtype for g in grads], streams)
        + [
            pltpu.VMEM((heads, tok, size), BF16),
            pltpu.VMEM((heads, size, size), BF16),
            pltpu.VMEM((heads, size, size), BF16),
        ]
        + [pltpu.VMEM((tok, size), F32)] * 3
        + chain_scratch(heads, size, size, True),
        compiler_params=pltpu.CompilerParams(
            collective_id=collective_id, has_side_effects=True, vmem_limit_bytes=VMEM_LIMIT
        ),
        name="delta_backward",
    )(
        keep, grad_normal, readout, gain, queries, keys, values, wkeys, invs, state, prefix,
        new_v, new_p, rate, allow, ext, ext, ext, conv, conv, conv, *maps, *grads,
    )
    return outs[:4], outs[4:]


def local(
    tokens, cotangent, doc_stretches, w_qkv, conv_weight, w_beta, beta_bias, norm_attn, norm_head,
    w_out, norm_ffn, w_gate, w_up, w_down,
):
    tok_rows, model_width = tokens.shape[1:]
    heads = beta_bias.shape[0]
    size = model_width // heads
    count = tok_rows // STRETCH
    span_count = lax.axis_size("span")
    place = lax.axis_index("span")
    taps = conv_weight.shape[0]

    small = jnp.concatenate(
        [x.reshape(-1) for x in (conv_weight, w_beta, norm_attn, norm_ffn, norm_head)]
    )
    small_len = small.shape[0]
    small = jnp.pad(small, (0, 16 * 512 - small_len)).reshape(16, 512)
    full_qkv, smalls = gather_call([w_qkv, small], 1)
    full_qkv = full_qkv.reshape(-1, full_qkv.shape[2])
    smalls = smalls.reshape(span_count, -1)

    def small_part(shape, start):
        length = 1
        for dim in shape:
            length *= dim
        return smalls[:, start : start + length].reshape((span_count,) + shape), start + length

    at = 0
    full_conv, at = small_part(conv_weight.shape, at)
    full_beta, at = small_part(w_beta.shape, at)
    gain_attn, at = small_part(norm_attn.shape, at)
    gain_ffn, at = small_part(norm_ffn.shape, at)
    gain_head, at = small_part(norm_head.shape, at)
    full_conv = jnp.swapaxes(full_conv, 0, 1).reshape(taps, -1)
    full_beta = full_beta.reshape(-1, heads)
    attn_gain = gain_attn.reshape(-1).astype(F32)
    ffn_gain = gain_ffn.reshape(-1).astype(F32)
    head_gain = gain_head.reshape(1, -1).astype(F32)

    stretch_ids = place * count + jnp.arange(count, dtype=jnp.int32)
    doc_lengths = doc_stretches[0]
    doc_begins = jnp.cumsum(doc_lengths) - doc_lengths
    stretch_start = jnp.any(stretch_ids[:, None] == doc_begins[None, :], axis=1).astype(F32)
    stretch_keep = 1.0 - stretch_start
    token_start = jnp.repeat(stretch_start, STRETCH)
    token_offset = jnp.arange(tok_rows, dtype=jnp.int32) % STRETCH
    allow = jnp.stack(
        [1.0 - token_start * (token_offset < tap).astype(F32) for tap in range(taps)], 1
    )

    ends = tokens[0, tok_rows - HALO :]
    before = lax.ppermute(
        ends, "span", [(i, i + 1) for i in range(span_count - 1)]
    )
    inputs_ext = jnp.concatenate([before, tokens[0]], 0).astype(F32)
    inv_ext = lax.rsqrt(jnp.mean(inputs_ext * inputs_ext, -1, keepdims=True) + EPSILON)
    normed_ext = (inputs_ext * inv_ext * attn_gain).astype(BF16)
    inputs_f, inv_first, normed = inputs_ext[HALO:], inv_ext[HALO:], normed_ext[HALO:]
    projected = jnp.dot(normed_ext, full_qkv, preferred_element_type=F32).astype(BF16)
    strength = jax.nn.sigmoid(
        jnp.dot(normed, full_beta, preferred_element_type=F32) + beta_bias
    )
    (
        queries, keys, values, invs, wkeys, prefix, new_v, new_p,
        state_in, p_low, p_high, p_chip, readout, normal_heads,
    ), rest = forward_call(
        stretch_keep, projected, full_conv, strength, allow, head_gain,
        [w_out, w_gate, w_up, w_down], heads, 2,
    )
    full_out, full_gate, full_up, full_down = (w.reshape(-1, w.shape[2]) for w in rest)

    middle = inputs_f + jnp.dot(normal_heads, full_out, preferred_element_type=F32)
    inv_second = lax.rsqrt(jnp.mean(middle * middle, -1, keepdims=True) + EPSILON)
    normed_ffn = (middle * inv_second * ffn_gain).astype(BF16)
    gate = jnp.dot(normed_ffn, full_gate, preferred_element_type=F32)
    up_part = jnp.dot(normed_ffn, full_up, preferred_element_type=F32)
    gate_sig = jax.nn.sigmoid(gate)
    gate_act = gate * gate_sig
    hidden = (gate_act * up_part).astype(BF16)
    grad_branch = cotangent[0]
    pair_cot = pair_tokens(grad_branch)
    half_down = weight_grad(pair_columns(hidden, span_count), pair_cot, span_count)
    grad_hidden = product("td,fd->tf", grad_branch, full_down)
    grad_gate_in = (grad_hidden * up_part * silu_slope(gate, gate_sig)).astype(BF16)
    grad_up_in = (grad_hidden * gate_act).astype(BF16)
    grad_nffn = product("tf,df->td", grad_gate_in, full_gate) + product(
        "tf,df->td", grad_up_in, full_up
    )
    pair_ffn = pair_columns(normed_ffn, span_count)
    half_gate = weight_grad(pair_ffn, pair_tokens(grad_gate_in), span_count)
    half_up = weight_grad(pair_ffn, pair_tokens(grad_up_in), span_count)
    result = middle + jnp.dot(hidden, full_down, preferred_element_type=F32)

    grad_norm_ffn = jnp.sum(grad_nffn * middle * inv_second, 0)
    grad_middle = grad_branch.astype(F32) + norm_back(grad_nffn, middle, inv_second, ffn_gain)
    grad_attn_in = grad_middle.astype(BF16)
    grad_normal = product("td,kd->tk", grad_attn_in, full_out)
    pair_heads = pair_columns(normal_heads, span_count)
    half_out = weight_grad(pair_heads, pair_tokens(grad_attn_in), span_count)
    (grad_ext, grad_conv, grad_strength, head_grads), ffn_parts = backward_call(
        stretch_keep, grad_normal, readout, head_gain, queries, keys, values, wkeys, invs,
        state_in, prefix, new_v, new_p, strength, allow, projected, full_conv,
        (p_low, p_high, p_chip), [half_down, half_gate, half_up], heads, 4,
    )
    pair_normed = pair_columns(normed_ext, span_count)
    half_q, half_k, half_v = (
        weight_grad(pair_normed, pair_tokens(grad_ext[i]), span_count) for i in range(3)
    )

    grad_logit = grad_strength * strength * (1.0 - strength)
    grad_logit_low = grad_logit.astype(BF16)
    grad_w_beta = product("td,th->dh", normed, grad_logit_low)
    grad_normed_ext = sum(
        product("te,de->td", grad_ext[i], full_qkv[:, i * model_width : (i + 1) * model_width])
        for i in range(3)
    )
    halo_back = lax.ppermute(
        grad_normed_ext[:HALO].astype(BF16), "span", [(i, i - 1) for i in range(1, span_count)]
    )
    grad_normed = (
        grad_normed_ext[HALO:]
        + product("th,dh->td", grad_logit_low, full_beta)
        + jnp.pad(halo_back.astype(F32), ((tok_rows - HALO, 0), (0, 0)))
    )
    grad_norm_attn = jnp.sum(grad_normed * inputs_f * inv_first, 0)
    grad_tokens = grad_middle + norm_back(grad_normed, inputs_f, inv_first, attn_gain)

    def by_span(array):
        return array.reshape(span_count, -1)

    grad_conv = jnp.swapaxes(grad_conv, 0, 1).reshape(taps, span_count, -1)
    packed = jnp.concatenate(
        [
            by_span(jnp.swapaxes(grad_conv, 0, 1)),
            by_span(grad_w_beta),
            by_span(grad_norm_attn),
            by_span(grad_norm_ffn),
            by_span(jnp.sum(head_grads, (0, 1))),
            jnp.broadcast_to(jnp.sum(grad_logit, 0)[None], (span_count, heads)),
        ],
        1,
    )
    packed = jnp.pad(packed, ((0, 0), (0, 16 * 512 - packed.shape[1])))
    packed = packed.reshape(span_count // 2, 2, 16, 512)
    core = place % 2
    half_small = lax.dynamic_index_in_dim(packed, core, 1, keepdims=False) + swap_core(
        lax.dynamic_index_in_dim(packed, 1 - core, 1, keepdims=False)
    )
    parts = reduce_call([half_out, half_q, half_k, half_v, half_small], 5)
    part_down, part_gate, part_up = (x.astype(F32) for x in ffn_parts)
    part_out = parts[0].astype(F32)
    part_qkv = jnp.concatenate([x.astype(F32) for x in parts[1:4]], 1)
    part_small = parts[4].reshape(-1)
    sums = []
    at = 0
    for like in (conv_weight, w_beta, norm_attn, norm_ffn, norm_head, beta_bias):
        sums.append(part_small[at : at + like.size].reshape(like.shape))
        at += like.size

    return (
        result.astype(BF16)[None],
        grad_tokens[None],
        part_qkv,
        sums[0],
        sums[1],
        sums[5],
        sums[2],
        sums[4],
        part_out,
        sums[3],
        part_gate,
        part_up,
        part_down,
    )


def solution(mesh):
    in_specs = (
        P("stream", "span", None),
        P("stream", "span", None),
        P("stream", None),
        P("span", None),
        P(None, "span"),
        P("span", None),
        P(),
        P("span"),
        P("span"),
        P("span", None),
        P("span"),
        P("span", None),
        P("span", None),
        P("span", None),
    )
    out_specs = (
        P("stream", "span", None),
        P("stream", "span", None),
        P("span", None),
        P(None, "span"),
        P("span", None),
        P(),
        P("span"),
        P("span"),
        P("span", None),
        P("span"),
        P("span", None),
        P("span", None),
        P("span", None),
    )
    return jax.shard_map(local, mesh=mesh, in_specs=in_specs, out_specs=out_specs, check_vma=False)
```

```python
import functools

import jax
import jax.numpy as jnp
from jax import lax
from jax.experimental import pallas as pl
from jax.experimental.pallas import tpu as pltpu
from jax.sharding import PartitionSpec as P

STRETCH = 64
HALO = 16
EPSILON = 1e-06
F32 = jnp.float32
BF16 = jnp.bfloat16
AXES = ("stream", "span")
VMEM_LIMIT = 56 * 2**20
GATHER_PIECE = 24 * 1024
GATHER_AHEAD = 4
GATHER_LAG = 2
REDUCE_PIECE = 100 * 1024
REDUCE_AHEAD = 6
FORWARD_SLOTS = 12


def nn(a, b):
    return lax.dot_general(a, b, (((1,), (0,)), ((), ())), preferred_element_type=F32)


def nt(a, b):
    return lax.dot_general(a, b, (((1,), (1,)), ((), ())), preferred_element_type=F32)


def tn(a, b):
    return lax.dot_general(a, b, (((0,), (0,)), ((), ())), preferred_element_type=F32)


def fine(a, b):
    a_hi = a.astype(BF16)
    a_lo = (a - a_hi.astype(F32)).astype(BF16)
    b_hi = b.astype(BF16)
    b_lo = (b - b_hi.astype(F32)).astype(BF16)
    return nn(jnp.concatenate([a_hi, a_hi, a_lo], 1), jnp.concatenate([b_hi, b_lo, b_hi], 0))


def grid_ids(size):
    return (
        lax.broadcasted_iota(jnp.int32, (size, size), 0),
        lax.broadcasted_iota(jnp.int32, (size, size), 1),
    )


def unit_inverse(lower_list):
    rows, cols = grid_ids(STRETCH)
    eye = (rows == cols).astype(F32)
    out = [eye - jnp.where((rows // 2) == (cols // 2), low, 0.0) for low in lower_list]
    half = 2
    while half < STRETCH:
        cross = ((rows // (2 * half)) == (cols // (2 * half))) & ((rows // half) != (cols // half))
        inner = [fine(jnp.where(cross, low, 0.0), inv) for low, inv in zip(lower_list, out)]
        out = [inv - fine(inv, mid) for inv, mid in zip(out, inner)]
        half *= 2
    return out


def column_of(table, index):
    lanes = lax.broadcasted_iota(jnp.int32, table.shape, 1)
    return jnp.sum(jnp.where(lanes == index, table, 0.0), -1, keepdims=True)


def mix_rows(ext, conv_ref, allow):
    ext = ext.astype(F32)
    conv = conv_ref[...].astype(F32)
    shifted = [
        (ext if tap == 0 else pltpu.roll(ext, tap, 0))[HALO:] * allow[tap]
        for tap in range(conv.shape[0])
    ]
    mixed = sum(conv[tap : tap + 1] * shifted[tap] for tap in range(conv.shape[0]))
    return shifted, mixed, conv


def local_kernel(
    keep_ref, normed_ref, wq_ref, wkey_ref, wv_ref, cq_ref, ck_ref, cv_ref, rate_ref, allow_ref,
    ext_ref, q_ref, k_ref, v_ref, inv_ref, wk_ref, pre_ref, end_ref, read_ref, rmap_ref, nv_ref, np_ref,
):
    head = pl.program_id(0)
    allow_all = allow_ref[...]
    allow = [allow_all[:, tap : tap + 1] for tap in range(cq_ref.shape[0])]
    rate = column_of(rate_ref[...], head)

    normed = normed_ref[...]

    def activation(index, weight_ref, conv_ref):
        ext = nn(normed, weight_ref[...]).astype(BF16)
        ext_ref[index] = ext
        _, mixed, _ = mix_rows(ext, conv_ref, allow)
        return mixed * jax.nn.sigmoid(mixed)

    act_q = activation(0, wq_ref, cq_ref)
    act_k = activation(1, wkey_ref, ck_ref)
    act_v = activation(2, wv_ref, cv_ref)
    queries = (act_q * lax.rsqrt(jnp.sum(act_q * act_q, -1, keepdims=True) + EPSILON)).astype(BF16)
    keys = (act_k * lax.rsqrt(jnp.sum(act_k * act_k, -1, keepdims=True) + EPSILON)).astype(BF16)
    values = act_v.astype(BF16)
    q_ref[...] = queries
    k_ref[...] = keys
    v_ref[...] = values
    count = queries.shape[0] // STRETCH
    rows, cols = grid_ids(STRETCH)
    parts = [slice(n * STRETCH, (n + 1) * STRETCH) for n in range(count)]
    lows = []
    for part in parts:
        gram = nt(keys[part], keys[part])
        lows.append(jnp.where(rows > cols, gram * rate[part], 0.0))
    invs = unit_inverse(lows)
    size = keys.shape[1]
    drows, dcols = grid_ids(size)
    running = jnp.concatenate(
        [jnp.zeros((size, size), F32), (drows == dcols).astype(F32)], 0
    )
    for n, part in enumerate(parts):
        key, query = keys[part], queries[part]
        inv = invs[n].astype(BF16)
        inv_ref[0, part, :] = inv
        scaled = jnp.concatenate(
            [key.astype(F32) * rate[part], values[part].astype(F32) * rate[part]], 1
        ).astype(BF16)
        weighted = nn(inv, scaled)
        wkey = weighted[:, :size].astype(BF16)
        wk_ref[part, :] = wkey
        running = running * keep_ref[n]
        low_state = running.astype(BF16)
        pre_ref[0, n] = low_state
        back = nt(jnp.concatenate([wkey, query], 0), low_state)
        new = jnp.concatenate(
            [weighted[:, size:] - back[:STRETCH, :size], -back[:STRETCH, size:]], 1
        ).astype(BF16)
        nv_ref[part, :] = new[:, :size]
        np_ref[part, :] = new[:, size:]
        scores = jnp.where(rows >= cols, nt(query, key), 0.0).astype(BF16)
        out = back[STRETCH:] + nn(scores, new)
        read_ref[part, :] = out[:, :size]
        rmap_ref[part, :] = out[:, size:].astype(BF16)
        running = running + tn(new, key)
    end_ref[0] = running.astype(BF16)


def adjoint_body(
    keep_ref, gn_ref, read_ref, gain_ref, q_ref, k_ref, wk_ref, go_ref, adj_ref, gain_grad_ref
):
    grad, readout = gn_ref[...], read_ref[...]
    inv = lax.rsqrt(jnp.mean(readout * readout, -1, keepdims=True) + EPSILON)
    scaled = grad * gain_ref[...]
    grad_read = inv * scaled - readout * (inv * inv * inv) * jnp.mean(
        scaled * readout, -1, keepdims=True
    )
    gain_grad_ref[0] = jnp.sum(grad * readout * inv, 0, keepdims=True)
    grad_read = grad_read.astype(BF16)
    go_ref[...] = grad_read
    count = grad.shape[0] // STRETCH
    rows, cols = grid_ids(STRETCH)
    size = grad.shape[1]
    adj = jnp.zeros((size, size), F32)
    for n in range(count - 1, -1, -1):
        part = slice(n * STRETCH, (n + 1) * STRETCH)
        key, query, out = k_ref[part, :], q_ref[part, :], grad_read[part]
        scores = jnp.where(rows >= cols, nt(query, key), 0.0).astype(BF16)
        new_grad = tn(scores, out) + nt(key, adj.astype(BF16))
        adj = (
            adj
            + tn(
                jnp.concatenate([out, (-new_grad).astype(BF16)], 0),
                jnp.concatenate([query, wk_ref[part, :]], 0),
            )
        ) * keep_ref[n]
    adj_ref[0] = adj.astype(BF16)


def backward_body(
    head, begins, keep_ref, din_ref, min_ref, pre_ref, go_ref, q_ref, k_ref, v_ref, inv_ref, wk_ref,
    nv_ref, np_ref, rate_ref, allow_ref,
    eq_ref, ek_ref, ev_ref, cq_ref, ck_ref, cv_ref,
    gext_ref, gconv_ref, grate_ref,
    gq_buf, gk_buf, gv_buf,
):
    size = q_ref.shape[1]
    tok = q_ref.shape[0]
    count = tok // STRETCH
    rows, cols = grid_ids(STRETCH)
    rate = column_of(rate_ref[...], head)
    low_in = min_ref[0]
    adj = din_ref[0].astype(F32)
    grate_parts = [None] * count
    for n in range(count - 1, -1, -1):
        part = slice(n * STRETCH, (n + 1) * STRETCH)
        key, query, value, out = k_ref[part, :], q_ref[part, :], v_ref[part, :], go_ref[part, :]
        beta = rate[part]
        pre = pre_ref[0, n]
        state = (nn(low_in, pre[size:]) + pre[:size].astype(F32)).astype(BF16)
        new = (nt(np_ref[part, :], low_in) + nv_ref[part, :].astype(F32)).astype(BF16)
        low_adj = adj.astype(BF16)
        gram_both = nt(jnp.concatenate([key, query], 0), key)
        gram = gram_both[:STRETCH]
        scores = jnp.where(rows >= cols, gram_both[STRETCH:], 0.0).astype(BF16)
        new_grad = tn(scores, out) + nt(key, low_adj)
        low_new_grad = new_grad.astype(BF16)
        adj = (
            adj
            + tn(
                jnp.concatenate([out, -low_new_grad], 0),
                jnp.concatenate([query, wk_ref[part, :]], 0),
            )
        ) * keep_ref[n]
        grad_b = tn(inv_ref[0, part, :], low_new_grad)
        both = nt(jnp.concatenate([out, grad_b.astype(BF16)], 0), new)
        grad_scores = jnp.where(rows >= cols, both[:STRETCH], 0.0).astype(BF16)
        grad_low = jnp.where(rows > cols, -both[STRETCH:], 0.0)
        left = value.astype(F32) - nt(key, state)
        grate_parts[n] = jnp.sum(grad_low * gram, -1, keepdims=True) + jnp.sum(
            grad_b * left, -1, keepdims=True
        )
        grad_v = beta * grad_b
        grad_gram = beta * grad_low
        symmetric = (grad_gram + grad_gram.T).astype(BF16)
        by_state = nn(jnp.concatenate([out, -grad_v.astype(BF16)], 0), state)
        gq_buf[part, :] = by_state[:STRETCH] + nn(grad_scores, key)
        gk_buf[part, :] = (
            by_state[STRETCH:]
            + tn(grad_scores, query)
            + nn(jnp.concatenate([new, symmetric], 1), jnp.concatenate([low_adj, key], 0))
        )
        gv_buf[part, :] = grad_v
    grate = jnp.concatenate(grate_parts, 0)
    lanes = lax.broadcasted_iota(jnp.int32, grate_ref.shape, 1)
    before = jnp.where(begins, jnp.zeros(grate_ref.shape, F32), grate_ref[...])
    grate_ref[...] = jnp.where(lanes == head, grate, before)
    allow_all = allow_ref[...]
    allow = [allow_all[:, tap : tap + 1] for tap in range(cq_ref.shape[0])]
    zeros = jnp.zeros((HALO, size), F32)
    for i, (ext, conv_ref, buf) in enumerate(
        ((eq_ref, cq_ref, gq_buf), (ek_ref, ck_ref, gk_buf), (ev_ref, cv_ref, gv_buf))
    ):
        shifted, mixed, conv = mix_rows(ext[0], conv_ref, allow)
        sig = jax.nn.sigmoid(mixed)
        grad = buf[...]
        if i < 2:
            raw = mixed * sig
            inv = lax.rsqrt(jnp.sum(raw * raw, -1, keepdims=True) + EPSILON)
            grad = inv * grad - raw * (inv * inv * inv) * jnp.sum(grad * raw, -1, keepdims=True)
        grad = grad * (sig * (1.0 + mixed * (1.0 - sig)))
        total = None
        for tap in range(conv.shape[0]):
            gconv_ref[i, tap : tap + 1, :] = jnp.sum(grad * shifted[tap], 0, keepdims=True)
            term = jnp.concatenate([zeros, grad * (conv[tap : tap + 1] * allow[tap])], 0)
            if tap:
                term = pltpu.roll(term, tok + HALO - tap, 0)
            total = term if total is None else total + term
        gext_ref[:, i * size : (i + 1) * size] = total.astype(BF16)


def feed_kernel(
    core_ref, heads_ref, tok_ref, cot_ref, out_w_ref, gain_ref, gate_ref, up_ref, down_ref,
    nffn_ref, hidden_ref, mine_ref, theirs_ref, result_ref, gmid_ref, gattn_ref, gnormal_ref,
    ggain_ref, mid_buf, grad_buf, res_buf,
):
    step_id = pl.program_id(0)
    cot = cot_ref[...]

    @pl.when(step_id == 0)
    def _():
        middle = tok_ref[...].astype(F32) + nn(heads_ref[...], out_w_ref[...])
        inv = lax.rsqrt(jnp.mean(middle * middle, -1, keepdims=True) + EPSILON)
        mid_buf[...] = middle
        nffn_ref[...] = (middle * inv * gain_ref[...]).astype(BF16)
        grad_buf[...] = jnp.zeros(grad_buf.shape, F32)
        res_buf[...] = middle

    normed = nffn_ref[...]
    gate_w, up_w, down_w = gate_ref[...], up_ref[...], down_ref[...]
    gate = nn(normed, gate_w)
    up = nn(normed, up_w)
    grad_hidden = nt(cot, down_w)
    sig = jax.nn.sigmoid(gate)
    act = gate * sig
    hidden = (act * up).astype(BF16)
    grad_gate = (grad_hidden * up * (sig * (1.0 + gate * (1.0 - sig)))).astype(BF16)
    grad_up = (grad_hidden * act).astype(BF16)
    low = core_ref[0] == 0
    hidden_ref[...] = hidden
    mine_ref[...] = jnp.where(low, grad_gate, grad_up)
    theirs_ref[...] = jnp.where(low, grad_up, grad_gate)
    grad_buf[...] += nt(grad_gate, gate_w) + nt(grad_up, up_w)
    res_buf[...] += nn(hidden, down_w)

    @pl.when(step_id == pl.num_programs(0) - 1)
    def _():
        result_ref[...] = res_buf[...].astype(BF16)
        middle, grad = mid_buf[...], grad_buf[...]
        inv = lax.rsqrt(jnp.mean(middle * middle, -1, keepdims=True) + EPSILON)
        ggain_ref[...] = jnp.sum(grad * middle * inv, 0, keepdims=True)
        scaled = grad * gain_ref[...]
        total = cot.astype(F32) + inv * scaled - middle * (inv * inv * inv) * jnp.mean(
            scaled * middle, -1, keepdims=True
        )
        gmid_ref[...] = total
        low_total = total.astype(BF16)
        gattn_ref[...] = low_total
        gnormal_ref[...] = nt(low_total, out_w_ref[...])


def feed_call(core, normal_heads, tokens, cotangent, w_out, gain, w_gate, w_up, w_down):
    tok, width = tokens.shape
    units = w_gate.shape[1]
    step = 256

    def whole(*shape):
        return pl.BlockSpec(shape, lambda f: (0,) * len(shape))

    wide = pl.BlockSpec((tok, step), lambda f: (0, f))
    rows = whole(tok, width)
    return pl.pallas_call(
        feed_kernel,
        grid=(units // step,),
        in_specs=[
            pl.BlockSpec(memory_space=pltpu.SMEM),
            rows, rows, rows, whole(width, width), whole(1, width),
            pl.BlockSpec((width, step), lambda f: (0, f)),
            pl.BlockSpec((width, step), lambda f: (0, f)),
            pl.BlockSpec((step, width), lambda f: (f, 0)),
        ],
        out_specs=[rows, wide, wide, wide, rows, rows, rows, rows, whole(1, width)],
        out_shape=[
            jax.ShapeDtypeStruct((tok, width), BF16),
            jax.ShapeDtypeStruct((tok, units), BF16),
            jax.ShapeDtypeStruct((tok, units), BF16),
            jax.ShapeDtypeStruct((tok, units), BF16),
            jax.ShapeDtypeStruct((tok, width), BF16),
            jax.ShapeDtypeStruct((tok, width), F32),
            jax.ShapeDtypeStruct((tok, width), BF16),
            jax.ShapeDtypeStruct((tok, width), F32),
            jax.ShapeDtypeStruct((1, width), F32),
        ],
        scratch_shapes=[pltpu.VMEM((tok, width), F32)] * 3,
        compiler_params=pltpu.CompilerParams(vmem_limit_bytes=VMEM_LIMIT),
        cost_estimate=pl.CostEstimate(
            flops=10**10, bytes_accessed=3 * 10**7, transcendentals=10**6
        ),
        name="feed_forward",
    )(core, normal_heads, tokens, cotangent, w_out, gain, w_gate, w_up, w_down)


def norm_back(grad_in, values, inv_rms, gain_vec):
    scaled = grad_in * gain_vec
    return inv_rms * scaled - values * inv_rms**3 * jnp.mean(scaled * values, -1, keepdims=True)


def product(pattern, first, second, kind=F32):
    return jnp.einsum(pattern, first, second, preferred_element_type=F32).astype(kind)


def swap_core(block):
    streams, spans = lax.axis_size("stream"), lax.axis_size("span")
    pairs = [
        (s * spans + p, s * spans + (p ^ 1)) for s in range(streams) for p in range(spans)
    ]
    return lax.ppermute(block, AXES, pairs)


def pair_tokens(block):
    return jnp.concatenate([block, swap_core(block)], 0)


def pair_half(block):
    width = block.shape[1] // 2
    core = lax.axis_index("span") % 2
    mine = lax.dynamic_slice_in_dim(block, core * width, width, 1)
    theirs = lax.dynamic_slice_in_dim(block, (1 - core) * width, width, 1)
    return jnp.concatenate([mine, swap_core(theirs)], 0)


def weight_grad(left, right, spans):
    grad = product("td,te->de", left, right, BF16)
    return grad.reshape(spans, -1, grad.shape[1])


MESH = pl.DeviceIdType.MESH


class Place:
    def __init__(self, streams, spans):
        self.streams, self.spans, self.chips = streams, spans, spans // 2
        self.stream = lax.axis_index("stream")
        self.span = lax.axis_index("span")
        self.chip = lax.div(self.span, 2)
        self.core = lax.rem(self.span, 2)

    def beside(self, step):
        return (self.stream ^ step, self.span)

    def along(self, step):
        return (self.stream, 2 * self.shifted(step) + self.core)

    def shifted(self, step):
        return lax.rem(self.chip + step + self.chips, self.chips)

    def other(self):
        return (self.stream, 2 * self.chip + 1 - self.core)


def greet(places):
    barrier = pltpu.get_barrier_semaphore()
    for target in places:
        pl.semaphore_signal(barrier, inc=1, device_id=target, device_id_type=MESH)
    pl.semaphore_wait(barrier, len(places))


def quarter_of(rows, width, streams):
    if (width // 128) % streams == 0:
        return 1, streams
    return 2, streams // 2


def pieces_of(rows, width, streams, most):
    down, across = quarter_of(rows, width, streams)
    r, c = rows // down, width // across
    best = (1, 1)
    for cut_r in range(1, max(r // 16, 1) + 1):
        for cut_c in range(1, c // 128 + 1):
            if (cut_r > 1 and r % (16 * cut_r)) or c % (128 * cut_c):
                continue
            small = r * c <= most * cut_r * cut_c
            best_small = r * c <= most * best[0] * best[1]
            fewer = (cut_r * cut_c, cut_c) < (best[0] * best[1], best[1])
            if (small and (not best_small or fewer)) or (not best_small and not fewer):
                best = (cut_r, cut_c)
    return best


def units_of(shapes, streams, most):
    units = []
    for w, (rows, width) in enumerate(shapes):
        cut_r, cut_c = pieces_of(rows, width, streams, most)
        units += [(w, i, j, cut_r, cut_c) for i in range(cut_r) for j in range(cut_c)]
    return units


def quarter_index(rows, width, streams, at, unit):
    _, i, j, cut_r, cut_c = unit
    down, across = quarter_of(rows, width, streams)
    r, c = rows // down, width // across
    pr, pc = r // cut_r, c // cut_c
    if down == 1:
        row = pl.ds(i * pr, pr)
    else:
        row = pl.ds(pl.multiple_of(lax.div(at, across) * r + i * pr, pr), pr)
    start = lax.rem(at, across) * c + j * pc
    return row, pl.ds(pl.multiple_of(start, 128), pc)


def copy_to(source, target, send_sem, recv_sem, device):
    return pltpu.make_async_remote_copy(
        src_ref=source, dst_ref=target, send_sem=send_sem, recv_sem=recv_sem,
        device_id=device, device_id_type=MESH,
    )


class Gather:
    def __init__(self, place, shards, fulls, sems):
        self.place, self.shards, self.fulls = place, shards, fulls
        self.sems = sems
        self.units = units_of([x.shape for x in shards], place.streams, GATHER_PIECE)

    @staticmethod
    def sem_shapes(shapes, streams, spans):
        units = len(units_of(shapes, streams, GATHER_PIECE))
        slots = spans // 2
        dma = pltpu.SemaphoreType.DMA
        return [dma((units, slots, 4, 2)), dma((len(shapes), slots, 2)), dma((len(shapes),))]

    def part(self, unit, at, span=None):
        w = self.units[unit][0]
        rows, width = self.shards[w].shape
        index = quarter_index(rows, width, self.place.streams, at, self.units[unit])
        if span is None:
            return self.shards[w].at[index]
        return self.fulls[w].at[(span,) + index]

    def source_span(self, k):
        return 2 * self.place.shifted(-k) + self.place.core

    def wire(self, unit, k, kind, span, at, device, source=None):
        region = self.part(unit, at, span)
        return copy_to(
            region if source is None else source, region,
            self.sems[0].at[unit, k, kind, 0], self.sems[0].at[unit, k, kind, 1], device,
        )

    def along(self, unit, k):
        p = self.place
        return self.wire(
            unit, k, 0, p.span, p.stream, p.along(k), self.part(unit, p.stream)
        )

    def along_wait(self, unit, k):
        p = self.place
        self.wire(unit, k, 0, self.source_span(k), p.stream, p.along(k)).wait_recv()

    def sideways(self, unit, k, step):
        p = self.place
        return self.wire(unit, k, step, self.source_span(k), p.stream, p.beside(step))

    def sideways_wait(self, unit, k, step):
        p = self.place
        self.wire(
            unit, k, step, self.source_span(k), p.stream ^ step, p.beside(step)
        ).wait_recv()

    @staticmethod
    def turns(unit, k):
        return (1, 2) if (unit + k) % 2 == 0 else (2, 1)

    def corner(self, unit, k):
        p = self.place
        first, second = self.turns(unit, k)
        return self.wire(
            unit, k, 3, self.source_span(k), p.stream ^ first, p.beside(second)
        )

    def corner_wait(self, unit, k):
        p = self.place
        self.wire(unit, k, 3, self.source_span(k), p.stream ^ 3, p.beside(1)).wait_recv()

    def across(self, w, k):
        p = self.place
        span = p.span if k == 0 else self.source_span(k)
        region = self.fulls[w].at[span]
        return copy_to(
            self.shards[w] if k == 0 else region, region,
            self.sems[1].at[w, k, 0], self.sems[1].at[w, k, 1], p.other(),
        )

    def across_wait(self, w, k):
        p = self.place
        span = 2 * p.shifted(-k) + 1 - p.core
        region = self.fulls[w].at[span]
        copy_to(
            region, region, self.sems[1].at[w, k, 0], self.sems[1].at[w, k, 1], p.other()
        ).wait_recv()

    def own(self, w):
        return pltpu.make_async_copy(
            self.shards[w], self.fulls[w].at[self.place.span], self.sems[2].at[w]
        )

    def neighbours(self):
        p = self.place
        return (
            [p.along(k) for k in range(1, p.chips)] + [p.beside(1), p.beside(2), p.other()]
        )

    def steps(self):
        p = self.place
        slots = range(1, p.chips)
        count = len(self.units)
        owner = [unit[0] for unit in self.units]
        ends = {u: w for u, w in enumerate(owner) if u + 1 == count or owner[u + 1] != w}
        starts = {u for u, w in enumerate(owner) if u == 0 or owner[u - 1] != w}
        steps = []

        def begin(unit):
            for k in slots:
                self.along(unit, k).start()

        def hand_over(w):
            self.across(w, 0).start()
            self.own(w).start()

        def beside(unit, k):
            self.along_wait(unit, k)
            self.sideways(unit, k, 1).start()
            self.sideways(unit, k, 2).start()

        def turn(unit, k):
            self.sideways_wait(unit, k, self.turns(unit, k)[0])
            self.corner(unit, k).start()

        def close(w, k):
            for unit in range(count):
                if owner[unit] == w:
                    self.sideways_wait(unit, k, self.turns(unit, k)[1])
                    self.corner_wait(unit, k)
            self.across(w, k).start()

        def finish(w):
            for k in range(p.chips):
                self.across_wait(w, k)
                self.across(w, k).wait_send()
            self.own(w).wait()
            for unit in range(count):
                if owner[unit] == w:
                    for k in slots:
                        self.along(unit, k).wait_send()
                        self.sideways(unit, k, 1).wait_send()
                        self.sideways(unit, k, 2).wait_send()
                        self.corner(unit, k).wait_send()

        ahead, lag = GATHER_AHEAD, GATHER_LAG
        for unit in range(min(ahead, count)):
            steps.append(functools.partial(begin, unit))
        for t in range(count + 2 * lag):
            if t < count:
                steps += [functools.partial(beside, t, k) for k in slots]
                if t in starts:
                    steps.append(functools.partial(hand_over, owner[t]))
            if t + ahead < count:
                steps.append(functools.partial(begin, t + ahead))
            if 0 <= t - lag < count:
                steps += [functools.partial(turn, t - lag, k) for k in slots]
            if t - 2 * lag in ends:
                steps += [functools.partial(close, ends[t - 2 * lag], k) for k in slots]
        steps += [functools.partial(finish, w) for w in range(len(self.shards))]
        return steps


def gather_kernel(streams, spans, count, *refs):
    shards, fulls, sems = refs[:count], refs[count : 2 * count], refs[2 * count :]
    place = Place(streams, spans)
    work = Gather(place, shards, fulls, sems)
    greet(work.neighbours())
    for step in work.steps():
        step()


def gather_call(shards, collective_id):
    streams, spans = lax.axis_size("stream"), lax.axis_size("span")
    shapes = [shard.shape for shard in shards]
    outs = pl.pallas_call(
        functools.partial(gather_kernel, streams, spans, len(shards)),
        in_specs=[pl.BlockSpec(memory_space=pltpu.VMEM)] * len(shards),
        out_specs=[pl.BlockSpec(memory_space=pl.ANY)] * len(shards),
        out_shape=[jax.ShapeDtypeStruct((spans,) + s.shape, s.dtype) for s in shards],
        scratch_shapes=Gather.sem_shapes(shapes, streams, spans),
        compiler_params=pltpu.CompilerParams(
            collective_id=collective_id, has_side_effects=True, vmem_limit_bytes=VMEM_LIMIT
        ),
        name="gather_weights",
    )(*shards)
    return outs


class Reduce:
    def __init__(self, place, grads, targets, bufs, sems):
        self.place, self.grads, self.bufs, self.sems = place, grads, bufs, sems
        self.targets = targets
        self.units = self.cut([g.shape for g in grads], place.streams)

    @staticmethod
    def cut(shapes, streams):
        return units_of([s[1:] for s in shapes], streams, REDUCE_PIECE // shapes[0][0])

    @staticmethod
    def block(shape, streams):
        _, rows, width = shape
        down, across = quarter_of(rows, width, streams)
        return rows // down, width // across

    @staticmethod
    def scratch(shapes, kinds, streams):
        out = []
        dma = pltpu.SemaphoreType.DMA
        spans = shapes[0][0]
        for shape, kind in zip(shapes, kinds):
            r, c = Reduce.block(shape, streams)
            out += [
                pltpu.VMEM((2, spans, r, c), kind),
                pltpu.VMEM((2, spans, r, c), kind),
                pltpu.VMEM((spans, r, c), kind),
                pltpu.VMEM((spans, r, c), kind),
                pltpu.VMEM((spans, r, c), kind),
                pltpu.VMEM((r, c), kind),
                pltpu.VMEM((streams, 2, r, c), kind),
            ]
        n = len(Reduce.cut(shapes, streams))
        out += [dma((n, 3, 2)), dma((n, spans // 2, 2)), dma((n, streams, 2))]
        return out

    @staticmethod
    def turn(unit):
        return (1, 2) if unit % 2 == 0 else (2, 1)

    def inner(self, unit):
        w, i, j, cut_r, cut_c = self.units[unit]
        r, c = self.block(self.grads[w].shape, self.place.streams)
        r, c = r // cut_r, c // cut_c
        return pl.ds(i * r, r), pl.ds(j * c, c)

    def outer(self, unit, at):
        _, rows, width = self.grads[self.units[unit][0]].shape
        return quarter_index(rows, width, self.place.streams, at, self.units[unit])

    def buf(self, unit, which):
        return self.bufs[self.units[unit][0]][which]

    def first(self, unit, slot):
        p = self.place
        a, b = self.turn(unit)
        spans = pl.ds(0, p.spans)
        at = p.stream ^ a if slot == 0 else p.stream ^ a ^ b
        return copy_to(
            self.grads[self.units[unit][0]].at[(spans,) + self.outer(unit, at)],
            self.buf(unit, 0).at[(slot, spans) + self.inner(unit)],
            self.sems[0].at[unit, slot, 0], self.sems[0].at[unit, slot, 1], p.beside(a),
        )

    def second(self, unit):
        p = self.place
        _, b = self.turn(unit)
        spans = pl.ds(0, p.spans)
        return copy_to(
            self.buf(unit, 1).at[(1, spans) + self.inner(unit)],
            self.buf(unit, 2).at[(spans,) + self.inner(unit)],
            self.sems[0].at[unit, 2, 0], self.sems[0].at[unit, 2, 1], p.beside(b),
        )

    def third(self, unit, k):
        p = self.place
        return copy_to(
            self.buf(unit, 3).at[(pl.ds(2 * p.shifted(k), 2),) + self.inner(unit)],
            self.buf(unit, 4).at[(pl.ds(2 * k, 2),) + self.inner(unit)],
            self.sems[1].at[unit, k, 0], self.sems[1].at[unit, k, 1], p.along(k),
        )

    def swap(self, unit):
        p = self.place
        return copy_to(
            self.buf(unit, 5).at[self.inner(unit)],
            self.buf(unit, 6).at[(0, p.core) + self.inner(unit)],
            self.sems[2].at[unit, 0, 0], self.sems[2].at[unit, 0, 1], p.other(),
        )

    def fourth(self, unit, step):
        p = self.place
        return copy_to(
            self.buf(unit, 6).at[(0, pl.ds(0, 2)) + self.inner(unit)],
            self.buf(unit, 6).at[(step, pl.ds(0, 2)) + self.inner(unit)],
            self.sems[2].at[unit, step, 0], self.sems[2].at[unit, step, 1], p.beside(step),
        )

    def neighbours(self):
        p = self.place
        return [p.along(k) for k in range(1, p.chips)] + [
            p.beside(s) for s in range(1, p.streams)
        ] + [p.other()]

    def begin(self, unit):
        for slot in (1, 0):
            self.first(unit, slot).start()

    def add_first(self, unit):
        p = self.place
        _, b = self.turn(unit)
        grad = self.grads[self.units[unit][0]]
        inner = self.inner(unit)
        for slot in (1, 0):
            self.first(unit, slot).wait_recv()
            outer = self.outer(unit, p.stream ^ b if slot else p.stream)
            for span in range(p.spans):
                self.buf(unit, 1)[(slot, span) + inner] = (
                    grad[(span,) + outer].astype(F32)
                    + self.buf(unit, 0)[(slot, span) + inner].astype(F32)
                ).astype(grad.dtype)
            if slot:
                self.second(unit).start()

    def add_second(self, unit):
        p = self.place
        inner = self.inner(unit)
        self.second(unit).wait_recv()
        for span in range(p.spans):
            self.buf(unit, 3)[(span,) + inner] = (
                self.buf(unit, 1)[(0, span) + inner].astype(F32)
                + self.buf(unit, 2)[(span,) + inner].astype(F32)
            ).astype(self.buf(unit, 3).dtype)
        for k in range(1, p.chips):
            self.third(unit, k).start()

    def add_third(self, unit):
        p = self.place
        inner = self.inner(unit)
        kind = self.buf(unit, 5).dtype
        for k in range(1, p.chips):
            self.third(unit, k).wait_recv()
        for mine in (False, True):
            core = p.core if mine else 1 - p.core
            total = self.buf(unit, 3)[(2 * p.chip + core,) + inner].astype(F32)
            for k in range(1, p.chips):
                total = total + self.buf(unit, 4)[(2 * k + core,) + inner].astype(F32)
            if mine:
                self.buf(unit, 6)[(0, p.core) + inner] = total.astype(kind)
            else:
                self.buf(unit, 5)[inner] = total.astype(kind)
                self.swap(unit).start()

    def spread(self, unit):
        self.swap(unit).wait_recv()
        for step in range(1, self.place.streams):
            self.fourth(unit, step).start()

    def finish(self, unit):
        p = self.place
        for step in range(p.streams):
            if step:
                self.fourth(unit, step).wait_recv()
            row, col = self.outer(unit, p.stream ^ step)
            for part in range(2):
                out, start = self.targets[self.units[unit][0]][part]
                col_at = pl.ds(pl.multiple_of(start + col.start, 128), col.size)
                out[row, col_at] = self.buf(unit, 6)[(step, part) + self.inner(unit)]
        self.swap(unit).wait_send()
        for slot in range(2):
            self.first(unit, slot).wait_send()
        self.second(unit).wait_send()
        for k in range(1, p.chips):
            self.third(unit, k).wait_send()
        for step in range(1, p.streams):
            self.fourth(unit, step).wait_send()

    def steps(self):
        count = len(self.units)
        ahead = REDUCE_AHEAD
        steps = [functools.partial(self.begin, u) for u in range(min(ahead, count))]
        lags = (
            (0, self.add_first), (3, self.add_second), (6, self.add_third), (7, self.spread),
            (10, self.finish),
        )
        for t in range(count + 10):
            for lag, act in lags:
                if 0 <= t - lag < count:
                    steps.append(functools.partial(act, t - lag))
                if lag == 0 and t + ahead < count:
                    steps.append(functools.partial(self.begin, t + ahead))
        return steps


def split_columns(out, width):
    return [(out, 0), (out, width)]


def reduce_kernel(streams, spans, *refs):
    grads, outs, rest = refs[:5], refs[5:8], refs[8:]
    half = grads[0].shape[2]
    targets = [split_columns(outs[0], half)]
    targets += [[(outs[1], 2 * i * half), (outs[1], (2 * i + 1) * half)] for i in range(3)]
    targets += [split_columns(outs[2], grads[4].shape[2])]
    bufs = [rest[7 * w : 7 * w + 7] for w in range(5)]
    work = Reduce(Place(streams, spans), grads, targets, bufs, rest[35:])
    greet(work.neighbours())
    for step in work.steps():
        step()


def reduce_call(grads, collective_id):
    streams, spans = lax.axis_size("stream"), lax.axis_size("span")
    shapes = [grad.shape for grad in grads]
    vmem = pl.BlockSpec(memory_space=pltpu.VMEM)
    rows, width = shapes[0][1:]
    small_rows, small_width = shapes[4][1:]
    return pl.pallas_call(
        functools.partial(reduce_kernel, streams, spans),
        in_specs=[vmem] * len(grads),
        out_specs=[vmem] * 3,
        out_shape=[
            jax.ShapeDtypeStruct((rows, 2 * width), BF16),
            jax.ShapeDtypeStruct((rows, 6 * width), BF16),
            jax.ShapeDtypeStruct((small_rows, 2 * small_width), F32),
        ],
        scratch_shapes=Reduce.scratch(shapes, [g.dtype for g in grads], streams),
        compiler_params=pltpu.CompilerParams(
            collective_id=collective_id, has_side_effects=True, vmem_limit_bytes=VMEM_LIMIT
        ),
        name="reduce_grads",
    )(*grads)


def chain_body(p, backward, source, maps, state_ref, scratch):
    p_low, p_high, p_chip = maps
    swap, carry, outgo, sent = scratch[:4]
    swap_sem, hop_sem, back_sem = scratch[-3:]
    s_chip = None if backward else scratch[4]
    heads, size = source.shape[0], source.shape[2]
    half = heads // 2
    mine = p.core * half
    theirs = (1 - p.core) * half
    ahead, behind = (-1, 1) if backward else (1, -1)
    edge_in = p.chips - 1 if backward else 0
    edge_out = 0 if backward else p.chips - 1
    swap_copy = copy_to(
        source.at[pl.ds(theirs, half)], swap, swap_sem.at[0], swap_sem.at[1], p.other()
    )
    swap_copy.start()
    swap_copy.wait_recv()
    low_core = p.core == 0
    for h in range(half):
        own, got = source[mine + h], swap[h]
        low = jnp.where(low_core, own, got)
        high = jnp.where(low_core, got, own)
        if backward:
            outgo[h] = low.astype(F32) + nt(high, p_low[h])
        else:
            joined = nn(low, high[size:])
            s_chip[h] = joined[:size] + high[:size].astype(F32)
            p_chip[h] = joined[size:].astype(BF16)
            p_low[h] = low[size:]
            p_high[h] = high[size:]
            outgo[h] = low[:size].astype(F32)

    def hop(h):
        return copy_to(
            sent.at[h], carry.at[h], hop_sem.at[h, 0], hop_sem.at[h, 1], p.along(ahead)
        )

    @pl.when(p.chip == edge_in)
    def _():
        carry[...] = jnp.zeros(carry.shape, BF16)

    for h in range(half):

        @pl.when(p.chip != edge_in)
        def _():
            hop(h).wait_recv()

        moved = nt(carry[h], p_chip[h]) + outgo[h] if backward else nn(carry[h], p_chip[h]) + s_chip[h]
        sent[h] = moved.astype(BF16)

        @pl.when(p.chip != edge_out)
        def _():
            hop(h).start()

    for h in range(half):
        state = carry[h]
        if backward:
            low_state = (nt(state, p_high[h]) + jnp.where(low_core, swap[h], source[mine + h]).astype(F32)).astype(BF16)
            keep = jnp.where(low_core, low_state, state)
            give = jnp.where(low_core, state, low_state)
        else:
            high_state = (nn(state, p_low[h]) + outgo[h]).astype(BF16)
            keep = jnp.where(low_core, state, high_state)
            give = jnp.where(low_core, high_state, state)
        state_ref[mine + h] = keep
        sent[half + h] = give
    back = copy_to(
        sent.at[pl.ds(half, half)], state_ref.at[pl.ds(mine, half)],
        back_sem.at[0], back_sem.at[1], p.other(),
    )
    back.start()
    copy_to(
        sent.at[pl.ds(half, half)], state_ref.at[pl.ds(theirs, half)],
        back_sem.at[0], back_sem.at[1], p.other(),
    ).wait_recv()
    back.wait_send()
    swap_copy.wait_send()

    @pl.when(p.chip != edge_out)
    def _():
        for h in range(half):
            hop(h).wait_send()


def chain_scratch(heads, size, rows, backward):
    half = heads // 2
    dma = pltpu.SemaphoreType.DMA
    scratch = [
        pltpu.VMEM((half, rows, size), BF16),
        pltpu.VMEM((half, size, size), BF16),
        pltpu.VMEM((half, size, size), F32),
        pltpu.VMEM((heads, size, size), BF16),
    ]
    if not backward:
        scratch.append(pltpu.VMEM((half, size, size), F32))
    return scratch + [dma((2,)), dma((half, 2)), dma((2,))]


def readout_body(readout, gain):
    inv = lax.rsqrt(jnp.mean(readout * readout, -1, keepdims=True) + EPSILON)
    return (readout * inv * gain).astype(BF16)


def spread_steps(steps, slots, index):
    count = len(steps)
    return steps[count * index // slots : count * (index + 1) // slots]


def forward_kernel(streams, spans, heads, weights, *refs):
    ins, refs = refs[:11], refs[11:]
    shards, refs = refs[:weights], refs[weights:]
    outs, refs = refs[:15], refs[15:]
    fulls, refs = refs[:weights], refs[weights:]
    gather_sems, refs = refs[:3], refs[3:]
    map_buf, read_buf, rmap_buf, state_buf = refs[:4]
    chain_bufs = refs[4:]
    gain_ref = ins[10]
    (ext_ref, q_ref, k_ref, v_ref, inv_ref, wk_ref, pre_ref, nv_ref, np_ref,
     state_ref, p_low, p_high, p_chip, out_ref, normal_ref) = outs
    step_id = pl.program_id(0)
    place = Place(streams, spans)
    work = Gather(place, shards, fulls, gather_sems)
    steps = work.steps()

    @pl.when(step_id == 0)
    def _():
        greet(work.neighbours())

    for index in range(heads + 1):

        @pl.when(step_id == index)
        def _():
            for step in spread_steps(steps, FORWARD_SLOTS, index):
                step()

    @pl.when(step_id < heads)
    def _():
        local_kernel(
            *ins[:10], ext_ref, q_ref, k_ref, v_ref, inv_ref, wk_ref, pre_ref, map_buf.at[pl.ds(step_id, 1)],
            read_buf.at[step_id], rmap_buf.at[step_id], nv_ref, np_ref,
        )

    @pl.when(step_id == heads)
    def _():
        chain_body(
            place, False, map_buf, (p_low, p_high, p_chip), state_buf, chain_bufs,
        )
        state_ref[...] = state_buf[...]
        size = gain_ref.shape[1]
        for h in range(heads):
            cols = slice(h * size, (h + 1) * size)
            readout = read_buf[h] + nt(rmap_buf[h], state_buf[h])
            out_ref[:, cols] = readout
            normal_ref[:, cols] = readout_body(readout, gain_ref[...])
        for index in range(heads + 1, 20):
            for step in spread_steps(steps, FORWARD_SLOTS, index):
                step()


def forward_call(
    keep, normed, w_qkv, conv, rate, allow, gain, shards, heads, collective_id
):
    streams, spans = lax.axis_size("stream"), lax.axis_size("span")
    tok = rate.shape[0]
    rows, width = normed.shape
    size = width // heads
    count = tok // STRETCH
    taps = conv.shape[0]
    half = heads // 2
    hbm = pl.BlockSpec(memory_space=pl.ANY)

    def at(i):
        return jnp.minimum(i, heads - 1)

    def third(i, r):
        return pl.BlockSpec((r, size), lambda h: (0, at(h) + i * heads))

    def token_block():
        return pl.BlockSpec((tok, size), lambda h: (0, at(h)))

    def whole(*shape):
        return pl.BlockSpec(shape, lambda h: (0,) * len(shape))

    token_shape = jax.ShapeDtypeStruct((tok, width), BF16)
    square = jax.ShapeDtypeStruct((half, size, size), BF16)
    shapes = [s.shape for s in shards]
    outs = pl.pallas_call(
        functools.partial(forward_kernel, streams, spans, heads, len(shards)),
        grid=(heads + 1,),
        in_specs=[
            pl.BlockSpec(memory_space=pltpu.SMEM),
            whole(rows, width),
            third(0, width), third(1, width), third(2, width),
            third(0, taps), third(1, taps), third(2, taps),
            whole(tok, heads), whole(tok, taps), whole(1, size),
        ]
        + [pl.BlockSpec(memory_space=pltpu.VMEM)] * len(shards),
        out_specs=[
            pl.BlockSpec((3, rows, size), lambda h: (0, 0, at(h))),
            token_block(), token_block(), token_block(),
            pl.BlockSpec((1, tok, STRETCH), lambda h: (at(h), 0, 0)),
            token_block(),
            pl.BlockSpec((1, count, 2 * size, size), lambda h: (at(h), 0, 0, 0)),
            token_block(), token_block(),
            whole(heads, size, size),
            whole(half, size, size), whole(half, size, size), whole(half, size, size),
            whole(tok, width), whole(tok, width),
        ]
        + [hbm] * len(shards),
        out_shape=[
            jax.ShapeDtypeStruct((3, rows, width), BF16),
            token_shape, token_shape, token_shape,
            jax.ShapeDtypeStruct((heads, tok, STRETCH), BF16),
            token_shape,
            jax.ShapeDtypeStruct((heads, count, 2 * size, size), BF16),
            token_shape, token_shape,
            jax.ShapeDtypeStruct((heads, size, size), BF16),
            square, square, square,
            jax.ShapeDtypeStruct((tok, width), F32),
            token_shape,
        ]
        + [jax.ShapeDtypeStruct((spans,) + s.shape, s.dtype) for s in shards],
        scratch_shapes=Gather.sem_shapes(shapes, streams, spans)
        + [
            pltpu.VMEM((heads, 2 * size, size), BF16),
            pltpu.VMEM((heads, tok, size), F32),
            pltpu.VMEM((heads, tok, size), BF16),
            pltpu.VMEM((heads, size, size), BF16),
        ]
        + chain_scratch(heads, size, 2 * size, False),
        compiler_params=pltpu.CompilerParams(
            collective_id=collective_id, has_side_effects=True, vmem_limit_bytes=VMEM_LIMIT
        ),
        name="delta_forward",
    )(keep, normed, w_qkv, w_qkv, w_qkv, conv, conv, conv, rate, allow, gain, *shards)
    return outs[:15], outs[15:]


def head_of(turn, heads):
    return lax.rem(turn, 2) * (heads // 2) + lax.div(turn, 2)


def backward_kernel(streams, spans, heads, weights, *refs):
    (keep_ref, gn_ref, read_ref, gain_ref, q_ref, k_ref, v_ref, wk_ref, inv_ref, min_ref, pre_ref,
     nv_ref, np_ref, rate_ref, allow_ref, eq_ref, ek_ref, ev_ref, cq_ref, ck_ref, cv_ref,
     p_low, p_high, p_chip, pair_ref, wq_ref, wkey_ref, wv_ref) = refs[:28]
    refs = refs[28:]
    grads, refs = refs[:weights], refs[weights:]
    gconv_ref, grate_ref, gain_grad_ref, gnormed_ref = refs[:4]
    halves, sums, refs = refs[4:7], refs[7:10], refs[10:]
    bufs, refs = [refs[7 * w : 7 * w + 7] for w in range(weights)], refs[7 * weights :]
    reduce_sems, refs = refs[:3], refs[3:]
    go_buf, adj_buf, din_buf = refs[:3]
    pair_buf, own_buf, got_buf, pair_sem = refs[3:7]
    row_bufs, chain_bufs = refs[7:10], refs[10:]
    step_id = pl.program_id(0)
    place = Place(streams, spans)
    targets = [
        split_columns(sums[0], grads[0].shape[2]),
        [(sums[1], 0), (sums[2], 0)],
    ]
    work = Reduce(place, grads, targets, bufs, reduce_sems)
    steps = work.steps()
    slots = 3 * heads
    size = gain_ref.shape[1]

    def hand_over(turn):
        head, slot = head_of(turn, heads), lax.div(turn, 2)
        return copy_to(
            own_buf.at[head], got_buf.at[slot], pair_sem.at[slot, 0], pair_sem.at[slot, 1],
            place.other(),
        )

    def weigh(turn):
        @pl.when(place.core == lax.rem(turn, 2))
        def _():
            hand_over(turn).wait_recv()
            slot = lax.div(turn, 2)
            both = jnp.concatenate([own_buf[head_of(turn, heads)], got_buf[slot]], 0)
            grad = nn(pair_buf[...], both).astype(BF16)
            lanes = pl.ds(pl.multiple_of(slot * size, size), size)
            for i in range(3):
                rows = halves[i].shape[1]
                halves[i][:, :, lanes] = grad[:, i * size : (i + 1) * size].reshape(-1, rows, size)

        @pl.when(place.core != lax.rem(turn, 2))
        def _():
            hand_over(turn).wait_send()

    @pl.when(step_id == 0)
    def _():
        greet(work.neighbours())
        pair_buf[...] = pair_ref[...].T

    for index in range(2 * heads + 1):

        @pl.when(step_id == index)
        def _():
            for step in spread_steps(steps, slots, index):
                step()

    @pl.when(step_id < heads)
    def _():
        adjoint_body(
            keep_ref, gn_ref, read_ref, gain_ref, q_ref, k_ref, wk_ref,
            go_buf.at[step_id], adj_buf.at[pl.ds(step_id, 1)], gain_grad_ref,
        )

    @pl.when(step_id == heads)
    def _():
        chain_body(place, True, adj_buf, (p_low, p_high, p_chip), din_buf, chain_bufs)

    @pl.when(step_id > heads + 1)
    def _():
        weigh(step_id - heads - 2)

    @pl.when(step_id > heads)
    def _():
        turn = step_id - heads - 1
        head = head_of(turn, heads)
        own = own_buf.at[head]
        backward_body(
            head, turn == 0, keep_ref, din_buf.at[pl.ds(head, 1)], min_ref, pre_ref,
            go_buf.at[head], q_ref, k_ref, v_ref, inv_ref, wk_ref, nv_ref, np_ref, rate_ref,
            allow_ref, eq_ref, ek_ref, ev_ref, cq_ref, ck_ref, cv_ref,
            own, gconv_ref, grate_ref, *row_bufs,
        )

        @pl.when(place.core != lax.rem(turn, 2))
        def _():
            hand_over(turn).start()

        part = nt(own[...], jnp.concatenate([wq_ref[...], wkey_ref[...], wv_ref[...]], 1))
        before = jnp.where(turn == 0, jnp.zeros_like(part), gnormed_ref[...])
        gnormed_ref[...] = before + part

    @pl.when(step_id == 2 * heads)
    def _():
        weigh(heads - 1)
        for index in range(2 * heads + 1, slots):
            for step in spread_steps(steps, slots, index):
                step()


def backward_call(
    keep, grad_normal, readout, gain, queries, keys, values, wkeys, invs, state, prefix,
    new_v, new_p, rate, allow, ext, conv, maps, pair_normed, w_qkv, grads, heads, collective_id,
):
    streams, spans = lax.axis_size("stream"), lax.axis_size("span")
    tok, width = queries.shape
    size = width // heads
    count = tok // STRETCH
    taps = conv.shape[0]
    rows = ext.shape[1]
    half = heads // 2

    def first(i):
        return jnp.minimum(i, heads - 1)

    def second(i):
        return head_of(jnp.maximum(i - heads - 1, 0), heads)

    def both(i):
        return jnp.where(i < heads, i, second(i))

    def block(at):
        return pl.BlockSpec((tok, size), lambda h: (0, at(h)))

    def third(i, r):
        return pl.BlockSpec((r, size), lambda h: (0, second(h) + i * heads))

    def part(i):
        return pl.BlockSpec((1, rows, size), lambda h: (i, 0, second(h)))

    def whole(*shape):
        return pl.BlockSpec(shape, lambda h: (0,) * len(shape))

    vmem = pl.BlockSpec(memory_space=pltpu.VMEM)
    shapes = [g.shape for g in grads]
    outs = pl.pallas_call(
        functools.partial(backward_kernel, streams, spans, heads, len(grads)),
        grid=(2 * heads + 1,),
        in_specs=[
            pl.BlockSpec(memory_space=pltpu.SMEM),
            block(first), block(first), whole(1, size),
            block(both), block(both), block(second), block(both),
            pl.BlockSpec((1, tok, STRETCH), lambda h: (second(h), 0, 0)),
            pl.BlockSpec((1, size, size), lambda h: (second(h), 0, 0)),
            pl.BlockSpec((1, count, 2 * size, size), lambda h: (second(h), 0, 0, 0)),
            block(second), block(second),
            whole(tok, heads), whole(tok, taps),
            part(0), part(1), part(2),
            third(0, taps), third(1, taps), third(2, taps),
            whole(half, size, size), whole(half, size, size), whole(half, size, size),
            vmem, third(0, width), third(1, width), third(2, width),
        ]
        + [vmem] * len(grads),
        out_specs=[
            pl.BlockSpec((3, taps, size), lambda h: (0, 0, second(h))),
            whole(tok, heads),
            pl.BlockSpec((1, 1, size), lambda h: (first(h), 0, 0)),
            whole(rows, width),
        ]
        + [vmem] * 6,
        out_shape=[
            jax.ShapeDtypeStruct((3, taps, width), F32),
            jax.ShapeDtypeStruct((tok, heads), F32),
            jax.ShapeDtypeStruct((heads, 1, size), F32),
            jax.ShapeDtypeStruct((rows, width), F32),
        ]
        + [jax.ShapeDtypeStruct((spans, width // spans, width // 2), BF16)] * 3
        + [
            jax.ShapeDtypeStruct((shapes[0][1], 2 * shapes[0][2]), BF16),
            jax.ShapeDtypeStruct(shapes[1][1:], BF16),
            jax.ShapeDtypeStruct(shapes[1][1:], BF16),
        ],
        scratch_shapes=Reduce.scratch(shapes, [g.dtype for g in grads], streams)
        + [
            pltpu.VMEM((heads, tok, size), BF16),
            pltpu.VMEM((heads, size, size), BF16),
            pltpu.VMEM((heads, size, size), BF16),
            pltpu.VMEM((width, 2 * rows), BF16),
            pltpu.VMEM((heads, rows, 3 * size), BF16),
            pltpu.VMEM((half, rows, 3 * size), BF16),
            pltpu.SemaphoreType.DMA((half, 2)),
        ]
        + [pltpu.VMEM((tok, size), F32)] * 3
        + chain_scratch(heads, size, size, True),
        compiler_params=pltpu.CompilerParams(
            collective_id=collective_id, has_side_effects=True, vmem_limit_bytes=VMEM_LIMIT
        ),
        name="delta_backward",
    )(
        keep, grad_normal, readout, gain, queries, keys, values, wkeys, invs, state, prefix,
        new_v, new_p, rate, allow, ext, ext, ext, conv, conv, conv, *maps, pair_normed,
        w_qkv, w_qkv, w_qkv, *grads,
    )
    return outs[:4], outs[4:7], outs[7:]


def local(
    tokens, cotangent, doc_stretches, w_qkv, conv_weight, w_beta, beta_bias, norm_attn, norm_head,
    w_out, norm_ffn, w_gate, w_up, w_down,
):
    tok_rows, model_width = tokens.shape[1:]
    heads = beta_bias.shape[0]
    size = model_width // heads
    count = tok_rows // STRETCH
    span_count = lax.axis_size("span")
    place = lax.axis_index("span")
    taps = conv_weight.shape[0]

    small = jnp.concatenate(
        [x.reshape(-1) for x in (conv_weight, w_beta, norm_attn, norm_ffn, norm_head)]
    )
    small_len = small.shape[0]
    small = jnp.pad(small, (0, 16 * 512 - small_len)).reshape(16, 512)
    full_qkv, smalls = gather_call([w_qkv, small], 1)
    full_qkv = full_qkv.reshape(-1, full_qkv.shape[2])
    smalls = smalls.reshape(span_count, -1)

    def small_part(shape, start):
        length = 1
        for dim in shape:
            length *= dim
        return smalls[:, start : start + length].reshape((span_count,) + shape), start + length

    at = 0
    full_conv, at = small_part(conv_weight.shape, at)
    full_beta, at = small_part(w_beta.shape, at)
    gain_attn, at = small_part(norm_attn.shape, at)
    gain_ffn, at = small_part(norm_ffn.shape, at)
    gain_head, at = small_part(norm_head.shape, at)
    full_conv = jnp.swapaxes(full_conv, 0, 1).reshape(taps, -1)
    full_beta = full_beta.reshape(-1, heads)
    attn_gain = gain_attn.reshape(-1).astype(F32)
    ffn_gain = gain_ffn.reshape(-1).astype(F32)
    head_gain = gain_head.reshape(1, -1).astype(F32)

    stretch_ids = place * count + jnp.arange(count, dtype=jnp.int32)
    doc_lengths = doc_stretches[0]
    doc_begins = jnp.cumsum(doc_lengths) - doc_lengths
    stretch_start = jnp.any(stretch_ids[:, None] == doc_begins[None, :], axis=1).astype(F32)
    stretch_keep = 1.0 - stretch_start
    token_start = jnp.repeat(stretch_start, STRETCH)
    token_offset = jnp.arange(tok_rows, dtype=jnp.int32) % STRETCH
    allow = jnp.stack(
        [1.0 - token_start * (token_offset < tap).astype(F32) for tap in range(taps)], 1
    )

    ends = tokens[0, tok_rows - HALO :]
    before = lax.ppermute(
        ends, "span", [(i, i + 1) for i in range(span_count - 1)]
    )
    inputs_ext = jnp.concatenate([before, tokens[0]], 0).astype(F32)
    inv_ext = lax.rsqrt(jnp.mean(inputs_ext * inputs_ext, -1, keepdims=True) + EPSILON)
    normed_ext = (inputs_ext * inv_ext * attn_gain).astype(BF16)
    inputs_f, inv_first, normed = inputs_ext[HALO:], inv_ext[HALO:], normed_ext[HALO:]
    strength = jax.nn.sigmoid(
        jnp.dot(normed, full_beta, preferred_element_type=F32) + beta_bias
    )
    (
        projected, queries, keys, values, invs, wkeys, prefix, new_v, new_p,
        state_in, p_low, p_high, p_chip, readout, normal_heads,
    ), rest = forward_call(
        stretch_keep, normed_ext, full_qkv, full_conv, strength, allow, head_gain,
        [w_out, w_gate, w_up, w_down], heads, 2,
    )
    full_out, full_gate, full_up, full_down = (w.reshape(-1, w.shape[2]) for w in rest)

    (
        normed_ffn, hidden, gate_mine, gate_theirs, result, grad_middle, grad_attn_in, grad_normal,
        grad_norm_ffn,
    ) = feed_call(
        jnp.reshape(place % 2, (1,)).astype(jnp.int32), normal_heads, tokens[0], cotangent[0],
        full_out, ffn_gain[None], full_gate, full_up, full_down,
    )
    half_down = weight_grad(pair_tokens(hidden), pair_half(cotangent[0]), span_count)
    half_ffn = weight_grad(
        pair_tokens(normed_ffn), jnp.concatenate([gate_mine, swap_core(gate_theirs)], 0), span_count
    )
    half_out = weight_grad(pair_tokens(normal_heads), pair_half(grad_attn_in), span_count)
    (
        (grad_conv, grad_strength, head_grads, grad_normed_ext), (half_q, half_k, half_v), ffn_parts
    ) = backward_call(
        stretch_keep, grad_normal, readout, head_gain, queries, keys, values, wkeys, invs,
        state_in, prefix, new_v, new_p, strength, allow, projected, full_conv,
        (p_low, p_high, p_chip), pair_tokens(normed_ext), full_qkv, [half_down, half_ffn], heads, 4,
    )
    grad_logit = grad_strength * strength * (1.0 - strength)
    grad_logit_low = grad_logit.astype(BF16)
    grad_w_beta = product("td,th->dh", normed, grad_logit_low)
    halo_back = lax.ppermute(
        grad_normed_ext[:HALO].astype(BF16), "span", [(i, i - 1) for i in range(1, span_count)]
    )
    grad_normed = (
        grad_normed_ext[HALO:]
        + product("th,dh->td", grad_logit_low, full_beta)
        + jnp.pad(halo_back.astype(F32), ((tok_rows - HALO, 0), (0, 0)))
    )
    grad_norm_attn = jnp.sum(grad_normed * inputs_f * inv_first, 0)
    grad_tokens = grad_middle + norm_back(grad_normed, inputs_f, inv_first, attn_gain)

    def by_span(array):
        return array.reshape(span_count, -1)

    grad_conv = jnp.swapaxes(grad_conv, 0, 1).reshape(taps, span_count, -1)
    packed = jnp.concatenate(
        [
            by_span(jnp.swapaxes(grad_conv, 0, 1)),
            by_span(grad_w_beta),
            by_span(grad_norm_attn),
            by_span(grad_norm_ffn),
            by_span(jnp.sum(head_grads, (0, 1))),
            jnp.broadcast_to(jnp.sum(grad_logit, 0)[None], (span_count, heads)),
        ],
        1,
    )
    packed = jnp.pad(packed, ((0, 0), (0, 16 * 1024 - packed.shape[1])))
    packed = packed.reshape(span_count, 16, 2, 512)
    core = place % 2
    half_small = lax.dynamic_index_in_dim(packed, core, 2, keepdims=False) + swap_core(
        lax.dynamic_index_in_dim(packed, 1 - core, 2, keepdims=False)
    )
    parts = reduce_call([half_out, half_q, half_k, half_v, half_small], 5)
    part_down, part_gate, part_up = (x.astype(F32) for x in ffn_parts)
    part_out, part_qkv = parts[0].astype(F32), parts[1].astype(F32)
    part_small = parts[2].reshape(-1)
    sums = []
    at = 0
    for like in (conv_weight, w_beta, norm_attn, norm_ffn, norm_head, beta_bias):
        sums.append(part_small[at : at + like.size].reshape(like.shape))
        at += like.size

    return (
        result[None],
        grad_tokens[None],
        part_qkv,
        sums[0],
        sums[1],
        sums[5],
        sums[2],
        sums[4],
        part_out,
        sums[3],
        part_gate,
        part_up,
        part_down,
    )


def solution(mesh):
    in_specs = (
        P("stream", "span", None),
        P("stream", "span", None),
        P("stream", None),
        P("span", None),
        P(None, "span"),
        P("span", None),
        P(),
        P("span"),
        P("span"),
        P("span", None),
        P("span"),
        P("span", None),
        P("span", None),
        P("span", None),
    )
    out_specs = (
        P("stream", "span", None),
        P("stream", "span", None),
        P("span", None),
        P(None, "span"),
        P("span", None),
        P(),
        P("span"),
        P("span"),
        P("span", None),
        P("span"),
        P("span", None),
        P("span", None),
        P("span", None),
    )
    return jax.shard_map(local, mesh=mesh, in_specs=in_specs, out_specs=out_specs, check_vma=False)
```

```python
import functools

import jax
import jax.numpy as jnp
from jax import lax
from jax.experimental import pallas as pl
from jax.experimental.pallas import tpu as pltpu
from jax.sharding import PartitionSpec as P

STRETCH = 64
HALO = 16
GROUP = 2
EPSILON = 1e-06
F32 = jnp.float32
BF16 = jnp.bfloat16
AXES = ("stream", "span")
VMEM_LIMIT = 56 * 2**20
GATHER_PIECE = 24 * 1024
GATHER_AHEAD = 4
GATHER_LAG = 2
REDUCE_PIECE = 100 * 1024
REDUCE_AHEAD = 6
FORWARD_SLOTS = 12
BACKWARD_SLOTS = 11


def nn(a, b):
    return lax.dot_general(a, b, (((1,), (0,)), ((), ())), preferred_element_type=F32)


def nt(a, b):
    return lax.dot_general(a, b, (((1,), (1,)), ((), ())), preferred_element_type=F32)


def tn(a, b):
    return lax.dot_general(a, b, (((0,), (0,)), ((), ())), preferred_element_type=F32)


def fine(a, b):
    a_hi = a.astype(BF16)
    a_lo = (a - a_hi.astype(F32)).astype(BF16)
    b_hi = b.astype(BF16)
    b_lo = (b - b_hi.astype(F32)).astype(BF16)
    return nn(jnp.concatenate([a_hi, a_hi, a_lo], 1), jnp.concatenate([b_hi, b_lo, b_hi], 0))


def grid_ids(size):
    return (
        lax.broadcasted_iota(jnp.int32, (size, size), 0),
        lax.broadcasted_iota(jnp.int32, (size, size), 1),
    )


def unit_inverse(lower_list):
    rows, cols = grid_ids(STRETCH)
    eye = (rows == cols).astype(F32)
    out = [eye - jnp.where((rows // 2) == (cols // 2), low, 0.0) for low in lower_list]
    half = 2
    while half < STRETCH:
        cross = ((rows // (2 * half)) == (cols // (2 * half))) & ((rows // half) != (cols // half))
        inner = [fine(jnp.where(cross, low, 0.0), inv) for low, inv in zip(lower_list, out)]
        out = [inv - fine(inv, mid) for inv, mid in zip(out, inner)]
        half *= 2
    return out


def column_of(table, index):
    lanes = lax.broadcasted_iota(jnp.int32, table.shape, 1)
    return jnp.sum(jnp.where(lanes == index, table, 0.0), -1, keepdims=True)


def mix_rows(ext, conv_ref, allow):
    ext = ext.astype(F32)
    conv = conv_ref.astype(F32)
    shifted = [
        (ext if tap == 0 else pltpu.roll(ext, tap, 0))[HALO:] * allow[tap]
        for tap in range(conv.shape[0])
    ]
    mixed = sum(conv[tap : tap + 1] * shifted[tap] for tap in range(conv.shape[0]))
    return shifted, mixed, conv


def local_kernel(
    keep_ref, normed_ref, wq_ref, wkey_ref, wv_ref, cq_ref, ck_ref, cv_ref, rate_ref, allow_ref,
    ext_ref, q_ref, k_ref, v_ref, inv_ref, wk_ref, pre_ref, end_ref, read_ref, rmap_ref, nv_ref, np_ref,
):
    head = pl.program_id(0)
    allow_all = allow_ref[...]
    allow = [allow_all[:, tap : tap + 1] for tap in range(cq_ref.shape[0])]
    rate = column_of(rate_ref[...], head)

    normed = normed_ref[...]

    def activation(index, weight_ref, conv_ref):
        ext = nn(normed, weight_ref[...]).astype(BF16)
        ext_ref[index] = ext
        _, mixed, _ = mix_rows(ext, conv_ref[...], allow)
        return mixed * jax.nn.sigmoid(mixed)

    act_q = activation(0, wq_ref, cq_ref)
    act_k = activation(1, wkey_ref, ck_ref)
    act_v = activation(2, wv_ref, cv_ref)
    queries = (act_q * lax.rsqrt(jnp.sum(act_q * act_q, -1, keepdims=True) + EPSILON)).astype(BF16)
    keys = (act_k * lax.rsqrt(jnp.sum(act_k * act_k, -1, keepdims=True) + EPSILON)).astype(BF16)
    values = act_v.astype(BF16)
    q_ref[...] = queries
    k_ref[...] = keys
    v_ref[...] = values
    count = queries.shape[0] // STRETCH
    rows, cols = grid_ids(STRETCH)
    parts = [slice(n * STRETCH, (n + 1) * STRETCH) for n in range(count)]
    lows = []
    for part in parts:
        gram = nt(keys[part], keys[part])
        lows.append(jnp.where(rows > cols, gram * rate[part], 0.0))
    invs = unit_inverse(lows)
    size = keys.shape[1]
    drows, dcols = grid_ids(size)
    running = jnp.concatenate(
        [jnp.zeros((size, size), F32), (drows == dcols).astype(F32)], 0
    )
    for n, part in enumerate(parts):
        key, query = keys[part], queries[part]
        inv = invs[n].astype(BF16)
        inv_ref[0, part, :] = inv
        scaled = jnp.concatenate(
            [key.astype(F32) * rate[part], values[part].astype(F32) * rate[part]], 1
        ).astype(BF16)
        weighted = nn(inv, scaled)
        wkey = weighted[:, :size].astype(BF16)
        wk_ref[part, :] = wkey
        running = running * keep_ref[n]
        low_state = running.astype(BF16)
        pre_ref[0, n] = low_state
        back = nt(jnp.concatenate([wkey, query], 0), low_state)
        new = jnp.concatenate(
            [weighted[:, size:] - back[:STRETCH, :size], -back[:STRETCH, size:]], 1
        ).astype(BF16)
        nv_ref[part, :] = new[:, :size]
        np_ref[part, :] = new[:, size:]
        scores = jnp.where(rows >= cols, nt(query, key), 0.0).astype(BF16)
        out = back[STRETCH:] + nn(scores, new)
        read_ref[part, :] = out[:, :size]
        rmap_ref[part, :] = out[:, size:].astype(BF16)
        running = running + tn(new, key)
    end_ref[0] = running.astype(BF16)


def lanes_of(index, size):
    return slice(index * size, (index + 1) * size)


def adjoint_body(
    keep_ref, gn_ref, read_ref, gain_ref, q_ref, k_ref, wk_ref, go_ref, adj_ref, gain_grad_ref
):
    size = gain_ref.shape[1]
    tok = gn_ref.shape[0]
    grads = []
    for g in range(GROUP):
        grad, readout = gn_ref[:, lanes_of(g, size)], read_ref[:, lanes_of(g, size)]
        inv = lax.rsqrt(jnp.mean(readout * readout, -1, keepdims=True) + EPSILON)
        scaled = grad * gain_ref[...]
        grad_read = inv * scaled - readout * (inv * inv * inv) * jnp.mean(
            scaled * readout, -1, keepdims=True
        )
        gain_grad_ref[g] = jnp.sum(grad * readout * inv, 0, keepdims=True)
        grads.append(grad_read.astype(BF16))
        go_ref[:, lanes_of(g, size)] = grads[g]
    rows, cols = grid_ids(STRETCH)
    adj = [jnp.zeros((size, size), F32)] * GROUP
    for n in range(tok // STRETCH - 1, -1, -1):
        part = slice(n * STRETCH, (n + 1) * STRETCH)
        for g in range(GROUP):
            lanes = lanes_of(g, size)
            key, query, out = k_ref[part, lanes], q_ref[part, lanes], grads[g][part]
            scores = jnp.where(rows >= cols, nt(query, key), 0.0).astype(BF16)
            new_grad = tn(scores, out) + nt(key, adj[g].astype(BF16))
            adj[g] = (
                adj[g]
                + tn(
                    jnp.concatenate([out, (-new_grad).astype(BF16)], 0),
                    jnp.concatenate([query, wk_ref[part, lanes]], 0),
                )
            ) * keep_ref[n]
    for g in range(GROUP):
        adj_ref[g] = adj[g].astype(BF16)


def backward_body(
    turn, keep_ref, din_ref, min_ref, pre_ref, go_ref, q_ref, k_ref, v_ref, inv_ref, wk_ref,
    nv_ref, np_ref, rate_ref, allow_ref,
    eq_ref, ek_ref, ev_ref, cq_ref, ck_ref, cv_ref,
    gext_ref, gconv_ref, grate_ref,
    gq_buf, gk_buf, gv_buf,
):
    size = min_ref.shape[1]
    tok = q_ref.shape[0]
    count = tok // STRETCH
    rows, cols = grid_ids(STRETCH)
    rates = [column_of(rate_ref[...], GROUP * turn + g) for g in range(GROUP)]
    low_in = [min_ref[g] for g in range(GROUP)]
    adj = [din_ref[g].astype(F32) for g in range(GROUP)]
    grate_parts = [[None] * count for _ in range(GROUP)]
    for n in range(count - 1, -1, -1):
        part = slice(n * STRETCH, (n + 1) * STRETCH)
        for g in range(GROUP):
            lanes = lanes_of(g, size)
            key, query, value = k_ref[part, lanes], q_ref[part, lanes], v_ref[part, lanes]
            out = go_ref[part, lanes]
            beta = rates[g][part]
            pre = pre_ref[g, n]
            state = (nn(low_in[g], pre[size:]) + pre[:size].astype(F32)).astype(BF16)
            new = (nt(np_ref[part, lanes], low_in[g]) + nv_ref[part, lanes].astype(F32)).astype(BF16)
            low_adj = adj[g].astype(BF16)
            gram_both = nt(jnp.concatenate([key, query], 0), key)
            gram = gram_both[:STRETCH]
            scores = jnp.where(rows >= cols, gram_both[STRETCH:], 0.0).astype(BF16)
            new_grad = tn(scores, out) + nt(key, low_adj)
            low_new_grad = new_grad.astype(BF16)
            adj[g] = (
                adj[g]
                + tn(
                    jnp.concatenate([out, -low_new_grad], 0),
                    jnp.concatenate([query, wk_ref[part, lanes]], 0),
                )
            ) * keep_ref[n]
            grad_b = tn(inv_ref[g, part, :], low_new_grad)
            both = nt(jnp.concatenate([out, grad_b.astype(BF16)], 0), new)
            grad_scores = jnp.where(rows >= cols, both[:STRETCH], 0.0).astype(BF16)
            grad_low = jnp.where(rows > cols, -both[STRETCH:], 0.0)
            left = value.astype(F32) - nt(key, state)
            grate_parts[g][n] = jnp.sum(grad_low * gram, -1, keepdims=True) + jnp.sum(
                grad_b * left, -1, keepdims=True
            )
            grad_v = beta * grad_b
            grad_gram = beta * grad_low
            symmetric = (grad_gram + grad_gram.T).astype(BF16)
            by_state = nn(jnp.concatenate([out, -grad_v.astype(BF16)], 0), state)
            gq_buf[part, lanes] = by_state[:STRETCH] + nn(grad_scores, key)
            gk_buf[part, lanes] = (
                by_state[STRETCH:]
                + tn(grad_scores, query)
                + nn(jnp.concatenate([new, symmetric], 1), jnp.concatenate([low_adj, key], 0))
            )
            gv_buf[part, lanes] = grad_v
    heads_at = lax.broadcasted_iota(jnp.int32, grate_ref.shape, 1)
    grate = jnp.where(turn == 0, jnp.zeros(grate_ref.shape, F32), grate_ref[...])
    for g in range(GROUP):
        grate = jnp.where(
            heads_at == GROUP * turn + g, jnp.concatenate(grate_parts[g], 0), grate
        )
    grate_ref[...] = grate
    allow_all = allow_ref[...]
    allow = [allow_all[:, tap : tap + 1] for tap in range(cq_ref.shape[0])]
    zeros = jnp.zeros((HALO, size), F32)
    for i, (ext, conv_ref, buf) in enumerate(
        ((eq_ref, cq_ref, gq_buf), (ek_ref, ck_ref, gk_buf), (ev_ref, cv_ref, gv_buf))
    ):
        for g in range(GROUP):
            lanes = lanes_of(g, size)
            shifted, mixed, conv = mix_rows(ext[0, :, lanes], conv_ref[:, lanes], allow)
            sig = jax.nn.sigmoid(mixed)
            grad = buf[:, lanes]
            if i < 2:
                raw = mixed * sig
                inv = lax.rsqrt(jnp.sum(raw * raw, -1, keepdims=True) + EPSILON)
                grad = inv * grad - raw * (inv * inv * inv) * jnp.sum(grad * raw, -1, keepdims=True)
            grad = grad * (sig * (1.0 + mixed * (1.0 - sig)))
            total = None
            for tap in range(conv.shape[0]):
                gconv_ref[i, tap : tap + 1, lanes] = jnp.sum(grad * shifted[tap], 0, keepdims=True)
                term = jnp.concatenate([zeros, grad * (conv[tap : tap + 1] * allow[tap])], 0)
                if tap:
                    term = pltpu.roll(term, tok + HALO - tap, 0)
                total = term if total is None else total + term
            gext_ref[g, :, lanes_of(i, size)] = total.astype(BF16)


def norm_back(grad_in, values, inv_rms, gain_vec):
    scaled = grad_in * gain_vec
    return inv_rms * scaled - values * inv_rms**3 * jnp.mean(scaled * values, -1, keepdims=True)


def product(pattern, first, second, kind=F32):
    return jnp.einsum(pattern, first, second, preferred_element_type=F32).astype(kind)


def swap_core(block):
    streams, spans = lax.axis_size("stream"), lax.axis_size("span")
    pairs = [
        (s * spans + p, s * spans + (p ^ 1)) for s in range(streams) for p in range(spans)
    ]
    return lax.ppermute(block, AXES, pairs)


def pair_tokens(block):
    return jnp.concatenate([block, swap_core(block)], 0)


def pair_half(block):
    width = block.shape[1] // 2
    core = lax.axis_index("span") % 2
    mine = lax.dynamic_slice_in_dim(block, core * width, width, 1)
    theirs = lax.dynamic_slice_in_dim(block, (1 - core) * width, width, 1)
    return jnp.concatenate([mine, swap_core(theirs)], 0)


def weight_grad(left, right, spans):
    grad = product("td,te->de", left, right, BF16)
    return grad.reshape(spans, -1, grad.shape[1])


MESH = pl.DeviceIdType.MESH


class Place:
    def __init__(self, streams, spans):
        self.streams, self.spans, self.chips = streams, spans, spans // 2
        self.stream = lax.axis_index("stream")
        self.span = lax.axis_index("span")
        self.chip = lax.div(self.span, 2)
        self.core = lax.rem(self.span, 2)

    def beside(self, step):
        return (self.stream ^ step, self.span)

    def along(self, step):
        return (self.stream, 2 * self.shifted(step) + self.core)

    def shifted(self, step):
        return lax.rem(self.chip + step + self.chips, self.chips)

    def other(self):
        return (self.stream, 2 * self.chip + 1 - self.core)


def greet(places):
    barrier = pltpu.get_barrier_semaphore()
    for target in places:
        pl.semaphore_signal(barrier, inc=1, device_id=target, device_id_type=MESH)
    pl.semaphore_wait(barrier, len(places))


def quarter_of(rows, width, streams):
    if (width // 128) % streams == 0:
        return 1, streams
    return 2, streams // 2


def pieces_of(rows, width, streams, most):
    down, across = quarter_of(rows, width, streams)
    r, c = rows // down, width // across
    best = (1, 1)
    for cut_r in range(1, max(r // 16, 1) + 1):
        for cut_c in range(1, c // 128 + 1):
            if (cut_r > 1 and r % (16 * cut_r)) or c % (128 * cut_c):
                continue
            small = r * c <= most * cut_r * cut_c
            best_small = r * c <= most * best[0] * best[1]
            fewer = (cut_r * cut_c, cut_c) < (best[0] * best[1], best[1])
            if (small and (not best_small or fewer)) or (not best_small and not fewer):
                best = (cut_r, cut_c)
    return best


def units_of(shapes, streams, most):
    units = []
    for w, (rows, width) in enumerate(shapes):
        cut_r, cut_c = pieces_of(rows, width, streams, most)
        units += [(w, i, j, cut_r, cut_c) for i in range(cut_r) for j in range(cut_c)]
    return units


def quarter_index(rows, width, streams, at, unit):
    _, i, j, cut_r, cut_c = unit
    down, across = quarter_of(rows, width, streams)
    r, c = rows // down, width // across
    pr, pc = r // cut_r, c // cut_c
    if down == 1:
        row = pl.ds(i * pr, pr)
    else:
        row = pl.ds(pl.multiple_of(lax.div(at, across) * r + i * pr, pr), pr)
    start = lax.rem(at, across) * c + j * pc
    return row, pl.ds(pl.multiple_of(start, 128), pc)


def copy_to(source, target, send_sem, recv_sem, device):
    return pltpu.make_async_remote_copy(
        src_ref=source, dst_ref=target, send_sem=send_sem, recv_sem=recv_sem,
        device_id=device, device_id_type=MESH,
    )


class Gather:
    def __init__(self, place, shards, fulls, sems):
        self.place, self.shards, self.fulls = place, shards, fulls
        self.sems = sems
        self.units = units_of([x.shape for x in shards], place.streams, GATHER_PIECE)

    @staticmethod
    def sem_shapes(shapes, streams, spans):
        units = len(units_of(shapes, streams, GATHER_PIECE))
        slots = spans // 2
        dma = pltpu.SemaphoreType.DMA
        return [dma((units, slots, 4, 2)), dma((len(shapes), slots, 2)), dma((len(shapes),))]

    def part(self, unit, at, span=None):
        w = self.units[unit][0]
        rows, width = self.shards[w].shape
        index = quarter_index(rows, width, self.place.streams, at, self.units[unit])
        if span is None:
            return self.shards[w].at[index]
        return self.fulls[w].at[(span,) + index]

    def source_span(self, k):
        return 2 * self.place.shifted(-k) + self.place.core

    def wire(self, unit, k, kind, span, at, device, source=None):
        region = self.part(unit, at, span)
        return copy_to(
            region if source is None else source, region,
            self.sems[0].at[unit, k, kind, 0], self.sems[0].at[unit, k, kind, 1], device,
        )

    def along(self, unit, k):
        p = self.place
        return self.wire(
            unit, k, 0, p.span, p.stream, p.along(k), self.part(unit, p.stream)
        )

    def along_wait(self, unit, k):
        p = self.place
        self.wire(unit, k, 0, self.source_span(k), p.stream, p.along(k)).wait_recv()

    def sideways(self, unit, k, step):
        p = self.place
        return self.wire(unit, k, step, self.source_span(k), p.stream, p.beside(step))

    def sideways_wait(self, unit, k, step):
        p = self.place
        self.wire(
            unit, k, step, self.source_span(k), p.stream ^ step, p.beside(step)
        ).wait_recv()

    @staticmethod
    def turns(unit, k):
        return (1, 2) if (unit + k) % 2 == 0 else (2, 1)

    def corner(self, unit, k):
        p = self.place
        first, second = self.turns(unit, k)
        return self.wire(
            unit, k, 3, self.source_span(k), p.stream ^ first, p.beside(second)
        )

    def corner_wait(self, unit, k):
        p = self.place
        self.wire(unit, k, 3, self.source_span(k), p.stream ^ 3, p.beside(1)).wait_recv()

    def across(self, w, k):
        p = self.place
        span = p.span if k == 0 else self.source_span(k)
        region = self.fulls[w].at[span]
        return copy_to(
            self.shards[w] if k == 0 else region, region,
            self.sems[1].at[w, k, 0], self.sems[1].at[w, k, 1], p.other(),
        )

    def across_wait(self, w, k):
        p = self.place
        span = 2 * p.shifted(-k) + 1 - p.core
        region = self.fulls[w].at[span]
        copy_to(
            region, region, self.sems[1].at[w, k, 0], self.sems[1].at[w, k, 1], p.other()
        ).wait_recv()

    def own(self, w):
        return pltpu.make_async_copy(
            self.shards[w], self.fulls[w].at[self.place.span], self.sems[2].at[w]
        )

    def neighbours(self):
        p = self.place
        return (
            [p.along(k) for k in range(1, p.chips)] + [p.beside(1), p.beside(2), p.other()]
        )

    def steps(self):
        p = self.place
        slots = range(1, p.chips)
        count = len(self.units)
        owner = [unit[0] for unit in self.units]
        ends = {u: w for u, w in enumerate(owner) if u + 1 == count or owner[u + 1] != w}
        starts = {u for u, w in enumerate(owner) if u == 0 or owner[u - 1] != w}
        steps = []

        def begin(unit):
            for k in slots:
                self.along(unit, k).start()

        def hand_over(w):
            self.across(w, 0).start()
            self.own(w).start()

        def beside(unit, k):
            self.along_wait(unit, k)
            self.sideways(unit, k, 1).start()
            self.sideways(unit, k, 2).start()

        def turn(unit, k):
            self.sideways_wait(unit, k, self.turns(unit, k)[0])
            self.corner(unit, k).start()

        def close(w, k):
            for unit in range(count):
                if owner[unit] == w:
                    self.sideways_wait(unit, k, self.turns(unit, k)[1])
                    self.corner_wait(unit, k)
            self.across(w, k).start()

        def finish(w):
            for k in range(p.chips):
                self.across_wait(w, k)
                self.across(w, k).wait_send()
            self.own(w).wait()
            for unit in range(count):
                if owner[unit] == w:
                    for k in slots:
                        self.along(unit, k).wait_send()
                        self.sideways(unit, k, 1).wait_send()
                        self.sideways(unit, k, 2).wait_send()
                        self.corner(unit, k).wait_send()

        ahead, lag = GATHER_AHEAD, GATHER_LAG
        for unit in range(min(ahead, count)):
            steps.append(functools.partial(begin, unit))
        for t in range(count + 2 * lag):
            if t < count:
                steps += [functools.partial(beside, t, k) for k in slots]
                if t in starts:
                    steps.append(functools.partial(hand_over, owner[t]))
            if t + ahead < count:
                steps.append(functools.partial(begin, t + ahead))
            if 0 <= t - lag < count:
                steps += [functools.partial(turn, t - lag, k) for k in slots]
            if t - 2 * lag in ends:
                steps += [functools.partial(close, ends[t - 2 * lag], k) for k in slots]
        steps += [functools.partial(finish, w) for w in range(len(self.shards))]
        return steps


def gather_kernel(streams, spans, count, *refs):
    shards, fulls, sems = refs[:count], refs[count : 2 * count], refs[2 * count :]
    place = Place(streams, spans)
    work = Gather(place, shards, fulls, sems)
    greet(work.neighbours())
    for step in work.steps():
        step()


def gather_call(shards, collective_id):
    streams, spans = lax.axis_size("stream"), lax.axis_size("span")
    shapes = [shard.shape for shard in shards]
    outs = pl.pallas_call(
        functools.partial(gather_kernel, streams, spans, len(shards)),
        in_specs=[pl.BlockSpec(memory_space=pltpu.VMEM)] * len(shards),
        out_specs=[pl.BlockSpec(memory_space=pl.ANY)] * len(shards),
        out_shape=[jax.ShapeDtypeStruct((spans,) + s.shape, s.dtype) for s in shards],
        scratch_shapes=Gather.sem_shapes(shapes, streams, spans),
        compiler_params=pltpu.CompilerParams(
            collective_id=collective_id, has_side_effects=True, vmem_limit_bytes=VMEM_LIMIT
        ),
        name="gather_weights",
    )(*shards)
    return outs


class Reduce:
    def __init__(self, place, grads, targets, bufs, sems, share):
        self.place, self.grads, self.bufs, self.sems = place, grads, bufs, sems
        self.targets = targets
        self.units = self.cut([g.shape for g in grads], place.streams)
        self.modes = self.plan(self.units, [g.shape for g in grads], place.streams, share)

    @staticmethod
    def cut(shapes, streams):
        units = units_of([s[1:] for s in shapes], streams, REDUCE_PIECE // shapes[0][0])
        sizes = [sum(u[0] == w for u in units) for w in range(len(shapes))]
        order = []
        for w, size in enumerate(sizes):
            own = [u for u in units if u[0] == w]
            order += [((n + 0.5) / size, w, u) for n, u in enumerate(own)]
        return [u for _, _, u in sorted(order)]

    @staticmethod
    def plan(units, shapes, streams, share):
        whole = part = 0
        modes = []
        loads = [[0, 0], [0, 0]]
        for w, _, _, cut_r, cut_c in units:
            _, rows, width = shapes[w]
            size = rows * width // (cut_r * cut_c)
            plain = quarter_of(rows, width, streams)[0] == 1 and cut_c == 1 and rows > 16
            whole += size
            first = plain and part + size <= share * whole
            part += size if first else 0
            load = loads[first]
            way = load.index(min(load))
            load[way] += size
            modes.append((first, (1, 2) if way == 0 else (2, 1)))
        return modes

    @staticmethod
    def block(shape, streams):
        _, rows, width = shape
        down, across = quarter_of(rows, width, streams)
        return rows // down, width // across

    @staticmethod
    def scratch(shapes, kinds, streams):
        out = []
        dma = pltpu.SemaphoreType.DMA
        spans = shapes[0][0]
        for shape, kind in zip(shapes, kinds):
            r, c = Reduce.block(shape, streams)
            out += [
                pltpu.VMEM((2, spans, r, c), kind),
                pltpu.VMEM((2, spans, r, c), kind),
                pltpu.VMEM((spans, r, c), kind),
                pltpu.VMEM((spans, r, c), kind),
                pltpu.VMEM((spans, r, c), kind),
                pltpu.VMEM((r, c), kind),
                pltpu.VMEM((streams, 2, r, c), kind),
            ]
            across = quarter_of(*shape[1:], streams)[1]
            out += [
                pltpu.VMEM((spans, r, c * across) if across == streams else (2, 16, 128), kind),
                pltpu.VMEM((2, r, c * across) if across == streams else (2, 16, 128), kind),
            ]
        n = len(Reduce.cut(shapes, streams))
        out += [dma((n, 3, 2)), dma((n, spans // 2, 2)), dma((n, streams, 2))]
        return out

    def turn(self, unit):
        return self.modes[unit][1]

    def chips_first(self, unit):
        return self.modes[unit][0]

    def inner(self, unit):
        w, i, j, cut_r, cut_c = self.units[unit]
        r, c = self.block(self.grads[w].shape, self.place.streams)
        r, c = r // cut_r, c // cut_c
        return pl.ds(i * r, r), pl.ds(j * c, c)

    def outer(self, unit, at):
        _, rows, width = self.grads[self.units[unit][0]].shape
        return quarter_index(rows, width, self.place.streams, at, self.units[unit])

    def buf(self, unit, which):
        return self.bufs[self.units[unit][0]][which]

    def count(self, unit):
        return 2 if self.chips_first(unit) else self.place.spans

    def first(self, unit, slot):
        p = self.place
        a, b = self.turn(unit)
        spans = pl.ds(0, self.count(unit))
        at = p.stream ^ a if slot == 0 else p.stream ^ a ^ b
        source = self.buf(unit, 8) if self.chips_first(unit) else self.grads[self.units[unit][0]]
        return copy_to(
            source.at[(spans,) + self.outer(unit, at)],
            self.buf(unit, 0).at[(slot, spans) + self.inner(unit)],
            self.sems[0].at[unit, slot, 0], self.sems[0].at[unit, slot, 1], p.beside(a),
        )

    def second(self, unit):
        p = self.place
        _, b = self.turn(unit)
        spans = pl.ds(0, self.count(unit))
        return copy_to(
            self.buf(unit, 1).at[(1, spans) + self.inner(unit)],
            self.buf(unit, 2).at[(spans,) + self.inner(unit)],
            self.sems[0].at[unit, 2, 0], self.sems[0].at[unit, 2, 1], p.beside(b),
        )

    def third(self, unit, k):
        p = self.place
        if self.chips_first(unit):
            rows, _ = self.inner(unit)
            return copy_to(
                self.grads[self.units[unit][0]].at[pl.ds(2 * p.shifted(k), 2), rows],
                self.buf(unit, 7).at[pl.ds(2 * k, 2), rows],
                self.sems[1].at[unit, k, 0], self.sems[1].at[unit, k, 1], p.along(k),
            )
        return copy_to(
            self.buf(unit, 3).at[(pl.ds(2 * p.shifted(k), 2),) + self.inner(unit)],
            self.buf(unit, 4).at[(pl.ds(2 * k, 2),) + self.inner(unit)],
            self.sems[1].at[unit, k, 0], self.sems[1].at[unit, k, 1], p.along(k),
        )

    def swap(self, unit):
        p = self.place
        return copy_to(
            self.buf(unit, 5).at[self.inner(unit)],
            self.buf(unit, 6).at[(0, p.core) + self.inner(unit)],
            self.sems[2].at[unit, 0, 0], self.sems[2].at[unit, 0, 1], p.other(),
        )

    def fourth(self, unit, step):
        p = self.place
        return copy_to(
            self.buf(unit, 6).at[(0, pl.ds(0, 2)) + self.inner(unit)],
            self.buf(unit, 6).at[(step, pl.ds(0, 2)) + self.inner(unit)],
            self.sems[2].at[unit, step, 0], self.sems[2].at[unit, step, 1], p.beside(step),
        )

    def neighbours(self):
        p = self.place
        return [p.along(k) for k in range(1, p.chips)] + [
            p.beside(s) for s in range(1, p.streams)
        ] + [p.other()]

    def begin(self, unit):
        if self.chips_first(unit):
            for k in range(1, self.place.chips):
                self.third(unit, k).start()
            return
        for slot in (1, 0):
            self.first(unit, slot).start()

    def add_first(self, unit):
        if self.chips_first(unit):
            self.sum_chips(unit)
            for slot in (1, 0):
                self.first(unit, slot).start()
            return
        self.sum_first(unit, self.grads[self.units[unit][0]])

    def sum_chips(self, unit):
        p = self.place
        grad = self.grads[self.units[unit][0]]
        rows, _ = self.inner(unit)
        for k in range(1, p.chips):
            self.third(unit, k).wait_recv()
        for part in range(2):
            total = grad[2 * p.chip + part, rows, :].astype(F32)
            for k in range(1, p.chips):
                total = total + self.buf(unit, 7)[2 * k + part, rows, :].astype(F32)
            self.buf(unit, 8)[part, rows, :] = total.astype(grad.dtype)

    def sum_first(self, unit, grad):
        p = self.place
        _, b = self.turn(unit)
        inner = self.inner(unit)
        for slot in (1, 0):
            self.first(unit, slot).wait_recv()
            outer = self.outer(unit, p.stream ^ b if slot else p.stream)
            for span in range(self.count(unit)):
                self.buf(unit, 1)[(slot, span) + inner] = (
                    grad[(span,) + outer].astype(F32)
                    + self.buf(unit, 0)[(slot, span) + inner].astype(F32)
                ).astype(grad.dtype)
            if slot:
                self.second(unit).start()

    def add_second(self, unit):
        p = self.place
        if self.chips_first(unit):
            self.sum_first(unit, self.buf(unit, 8))
            return
        inner = self.inner(unit)
        self.second(unit).wait_recv()
        for span in range(p.spans):
            self.buf(unit, 3)[(span,) + inner] = (
                self.buf(unit, 1)[(0, span) + inner].astype(F32)
                + self.buf(unit, 2)[(span,) + inner].astype(F32)
            ).astype(self.buf(unit, 3).dtype)
        for k in range(1, p.chips):
            self.third(unit, k).start()

    def add_third(self, unit):
        p = self.place
        inner = self.inner(unit)
        kind = self.buf(unit, 5).dtype
        if self.chips_first(unit):
            self.second(unit).wait_recv()
        else:
            for k in range(1, p.chips):
                self.third(unit, k).wait_recv()
        for mine in (False, True):
            core = p.core if mine else 1 - p.core
            if self.chips_first(unit):
                total = self.buf(unit, 1)[(0, core) + inner].astype(F32)
                total = total + self.buf(unit, 2)[(core,) + inner].astype(F32)
            else:
                total = self.buf(unit, 3)[(2 * p.chip + core,) + inner].astype(F32)
                for k in range(1, p.chips):
                    total = total + self.buf(unit, 4)[(2 * k + core,) + inner].astype(F32)
            if mine:
                self.buf(unit, 6)[(0, p.core) + inner] = total.astype(kind)
            else:
                self.buf(unit, 5)[inner] = total.astype(kind)
                self.swap(unit).start()

    def spread(self, unit):
        self.swap(unit).wait_recv()
        for step in range(1, self.place.streams):
            self.fourth(unit, step).start()

    def finish(self, unit):
        p = self.place
        for step in range(p.streams):
            if step:
                self.fourth(unit, step).wait_recv()
            row, col = self.outer(unit, p.stream ^ step)
            for part in range(2):
                out, start, stride = self.targets[self.units[unit][0]][part]
                col_at = pl.ds(pl.multiple_of(start + stride * col.start, 128), col.size)
                out[row, col_at] = self.buf(unit, 6)[(step, part) + self.inner(unit)]
        self.swap(unit).wait_send()
        for slot in range(2):
            self.first(unit, slot).wait_send()
        self.second(unit).wait_send()
        for k in range(1, p.chips):
            self.third(unit, k).wait_send()
        for step in range(1, p.streams):
            self.fourth(unit, step).wait_send()

    def steps(self):
        count = len(self.units)
        ahead = REDUCE_AHEAD
        steps = [functools.partial(self.begin, u) for u in range(min(ahead, count))]
        lags = (
            (0, self.add_first), (3, self.add_second), (6, self.add_third), (7, self.spread),
            (10, self.finish),
        )
        for t in range(count + 10):
            for lag, act in lags:
                if 0 <= t - lag < count:
                    steps.append(functools.partial(act, t - lag))
                if lag == 0 and t + ahead < count:
                    steps.append(functools.partial(self.begin, t + ahead))
        return steps


def split_columns(out, width):
    return [(out, 0, 1), (out, width, 1)]


def reduce_kernel(streams, spans, *refs):
    grads, outs, rest = refs[:5], refs[5:8], refs[8:]
    half = grads[0].shape[2]
    targets = [split_columns(outs[0], half)]
    targets += [
        [(outs[1], 2 * i * half, 2), (outs[1], 2 * i * half + 128, 2)] for i in range(3)
    ]
    targets += [split_columns(outs[2], grads[4].shape[2])]
    bufs = [rest[9 * w : 9 * w + 9] for w in range(5)]
    work = Reduce(Place(streams, spans), grads, targets, bufs, rest[45:], 0.3)
    greet(work.neighbours())
    for step in work.steps():
        step()


def reduce_call(grads, collective_id):
    streams, spans = lax.axis_size("stream"), lax.axis_size("span")
    shapes = [grad.shape for grad in grads]
    vmem = pl.BlockSpec(memory_space=pltpu.VMEM)
    rows, width = shapes[0][1:]
    small_rows, small_width = shapes[4][1:]
    return pl.pallas_call(
        functools.partial(reduce_kernel, streams, spans),
        in_specs=[vmem] * len(grads),
        out_specs=[vmem] * 3,
        out_shape=[
            jax.ShapeDtypeStruct((rows, 2 * width), BF16),
            jax.ShapeDtypeStruct((rows, 6 * width), BF16),
            jax.ShapeDtypeStruct((small_rows, 2 * small_width), F32),
        ],
        scratch_shapes=Reduce.scratch(shapes, [g.dtype for g in grads], streams),
        compiler_params=pltpu.CompilerParams(
            collective_id=collective_id, has_side_effects=True, vmem_limit_bytes=VMEM_LIMIT
        ),
        name="reduce_grads",
    )(*grads)


def chain_body(p, backward, source, maps, state_ref, scratch):
    p_low, p_high, p_chip = maps
    swap, carry, outgo, sent = scratch[:4]
    swap_sem, hop_sem, back_sem = scratch[-3:]
    s_chip = None if backward else scratch[4]
    heads, size = source.shape[0], source.shape[2]
    half = heads // 2
    mine = p.core * half
    theirs = (1 - p.core) * half
    ahead, behind = (-1, 1) if backward else (1, -1)
    edge_in = p.chips - 1 if backward else 0
    edge_out = 0 if backward else p.chips - 1
    swap_copy = copy_to(
        source.at[pl.ds(theirs, half)], swap, swap_sem.at[0], swap_sem.at[1], p.other()
    )
    swap_copy.start()
    swap_copy.wait_recv()
    low_core = p.core == 0
    for h in range(half):
        own, got = source[mine + h], swap[h]
        low = jnp.where(low_core, own, got)
        high = jnp.where(low_core, got, own)
        if backward:
            outgo[h] = low.astype(F32) + nt(high, p_low[h])
        else:
            joined = nn(low, high[size:])
            s_chip[h] = joined[:size] + high[:size].astype(F32)
            p_chip[h] = joined[size:].astype(BF16)
            p_low[h] = low[size:]
            p_high[h] = high[size:]
            outgo[h] = low[:size].astype(F32)

    def hop(h):
        return copy_to(
            sent.at[h], carry.at[h], hop_sem.at[h, 0], hop_sem.at[h, 1], p.along(ahead)
        )

    @pl.when(p.chip == edge_in)
    def _():
        carry[...] = jnp.zeros(carry.shape, BF16)

    for h in range(half):

        @pl.when(p.chip != edge_in)
        def _():
            hop(h).wait_recv()

        moved = nt(carry[h], p_chip[h]) + outgo[h] if backward else nn(carry[h], p_chip[h]) + s_chip[h]
        sent[h] = moved.astype(BF16)

        @pl.when(p.chip != edge_out)
        def _():
            hop(h).start()

    for h in range(half):
        state = carry[h]
        if backward:
            low_state = (nt(state, p_high[h]) + jnp.where(low_core, swap[h], source[mine + h]).astype(F32)).astype(BF16)
            keep = jnp.where(low_core, low_state, state)
            give = jnp.where(low_core, state, low_state)
        else:
            high_state = (nn(state, p_low[h]) + outgo[h]).astype(BF16)
            keep = jnp.where(low_core, state, high_state)
            give = jnp.where(low_core, high_state, state)
        state_ref[mine + h] = keep
        sent[half + h] = give
    back = copy_to(
        sent.at[pl.ds(half, half)], state_ref.at[pl.ds(mine, half)],
        back_sem.at[0], back_sem.at[1], p.other(),
    )
    back.start()
    copy_to(
        sent.at[pl.ds(half, half)], state_ref.at[pl.ds(theirs, half)],
        back_sem.at[0], back_sem.at[1], p.other(),
    ).wait_recv()
    back.wait_send()
    swap_copy.wait_send()

    @pl.when(p.chip != edge_out)
    def _():
        for h in range(half):
            hop(h).wait_send()


def chain_scratch(heads, size, rows, backward):
    half = heads // 2
    dma = pltpu.SemaphoreType.DMA
    scratch = [
        pltpu.VMEM((half, rows, size), BF16),
        pltpu.VMEM((half, size, size), BF16),
        pltpu.VMEM((half, size, size), F32),
        pltpu.VMEM((heads, size, size), BF16),
    ]
    if not backward:
        scratch.append(pltpu.VMEM((half, size, size), F32))
    return scratch + [dma((2,)), dma((half, 2)), dma((2,))]


def readout_body(readout, gain):
    inv = lax.rsqrt(jnp.mean(readout * readout, -1, keepdims=True) + EPSILON)
    return (readout * inv * gain).astype(BF16)


def spread_steps(steps, first, slots, index):
    if index == 0:
        return steps[:first]
    rest = steps[first:]
    count = len(rest)
    return rest[count * (index - 1) // slots : count * index // slots]


def forward_kernel(streams, spans, heads, weights, *refs):
    ins, refs = refs[:11], refs[11:]
    shards, refs = refs[:weights], refs[weights:]
    outs, refs = refs[:15], refs[15:]
    fulls, refs = refs[:weights], refs[weights:]
    gather_sems, refs = refs[:3], refs[3:]
    map_buf, read_buf, rmap_buf, state_buf = refs[:4]
    chain_bufs = refs[4:]
    gain_ref = ins[10]
    (ext_ref, q_ref, k_ref, v_ref, inv_ref, wk_ref, pre_ref, nv_ref, np_ref,
     state_ref, p_low, p_high, p_chip, out_ref, normal_ref) = outs
    step_id = pl.program_id(0)
    place = Place(streams, spans)
    work = Gather(place, shards, fulls, gather_sems)
    steps = work.steps()

    @pl.when(step_id == 0)
    def _():
        greet(work.neighbours())

    for index in range(heads + 1):

        @pl.when(step_id == index)
        def _():
            for step in spread_steps(steps, GATHER_AHEAD, FORWARD_SLOTS, index):
                step()

    @pl.when(step_id < heads)
    def _():
        local_kernel(
            *ins[:10], ext_ref, q_ref, k_ref, v_ref, inv_ref, wk_ref, pre_ref, map_buf.at[pl.ds(step_id, 1)],
            read_buf.at[step_id], rmap_buf.at[step_id], nv_ref, np_ref,
        )

    @pl.when(step_id == heads)
    def _():
        chain_body(
            place, False, map_buf, (p_low, p_high, p_chip), state_buf, chain_bufs,
        )
        state_ref[...] = state_buf[...]
        size = gain_ref.shape[1]
        for h in range(heads):
            cols = slice(h * size, (h + 1) * size)
            readout = read_buf[h] + nt(rmap_buf[h], state_buf[h])
            out_ref[:, cols] = readout
            normal_ref[:, cols] = readout_body(readout, gain_ref[...])
        for index in range(heads + 1, 20):
            for step in spread_steps(steps, GATHER_AHEAD, FORWARD_SLOTS, index):
                step()


def forward_call(
    keep, normed, w_qkv, conv, rate, allow, gain, shards, heads, collective_id
):
    streams, spans = lax.axis_size("stream"), lax.axis_size("span")
    tok = rate.shape[0]
    rows, width = normed.shape
    size = width // heads
    count = tok // STRETCH
    taps = conv.shape[0]
    half = heads // 2
    hbm = pl.BlockSpec(memory_space=pl.ANY)

    def at(i):
        return jnp.minimum(i, heads - 1)

    def third(i, r):
        return pl.BlockSpec((r, size), lambda h: (0, at(h) + i * heads))

    def token_block():
        return pl.BlockSpec((tok, size), lambda h: (0, at(h)))

    def whole(*shape):
        return pl.BlockSpec(shape, lambda h: (0,) * len(shape))

    token_shape = jax.ShapeDtypeStruct((tok, width), BF16)
    square = jax.ShapeDtypeStruct((half, size, size), BF16)
    shapes = [s.shape for s in shards]
    outs = pl.pallas_call(
        functools.partial(forward_kernel, streams, spans, heads, len(shards)),
        grid=(heads + 1,),
        in_specs=[
            pl.BlockSpec(memory_space=pltpu.SMEM),
            whole(rows, width),
            third(0, width), third(1, width), third(2, width),
            third(0, taps), third(1, taps), third(2, taps),
            whole(tok, heads), whole(tok, taps), whole(1, size),
        ]
        + [pl.BlockSpec(memory_space=pltpu.VMEM)] * len(shards),
        out_specs=[
            pl.BlockSpec((3, rows, size), lambda h: (0, 0, at(h))),
            token_block(), token_block(), token_block(),
            pl.BlockSpec((1, tok, STRETCH), lambda h: (at(h), 0, 0)),
            token_block(),
            pl.BlockSpec((1, count, 2 * size, size), lambda h: (at(h), 0, 0, 0)),
            token_block(), token_block(),
            whole(heads, size, size),
            whole(half, size, size), whole(half, size, size), whole(half, size, size),
            whole(tok, width), whole(tok, width),
        ]
        + [hbm] * len(shards),
        out_shape=[
            jax.ShapeDtypeStruct((3, rows, width), BF16),
            token_shape, token_shape, token_shape,
            jax.ShapeDtypeStruct((heads, tok, STRETCH), BF16),
            token_shape,
            jax.ShapeDtypeStruct((heads, count, 2 * size, size), BF16),
            token_shape, token_shape,
            jax.ShapeDtypeStruct((heads, size, size), BF16),
            square, square, square,
            jax.ShapeDtypeStruct((tok, width), F32),
            token_shape,
        ]
        + [jax.ShapeDtypeStruct((spans,) + s.shape, s.dtype) for s in shards],
        scratch_shapes=Gather.sem_shapes(shapes, streams, spans)
        + [
            pltpu.VMEM((heads, 2 * size, size), BF16),
            pltpu.VMEM((heads, tok, size), F32),
            pltpu.VMEM((heads, tok, size), BF16),
            pltpu.VMEM((heads, size, size), BF16),
        ]
        + chain_scratch(heads, size, 2 * size, False),
        compiler_params=pltpu.CompilerParams(
            collective_id=collective_id, has_side_effects=True, vmem_limit_bytes=VMEM_LIMIT
        ),
        name="delta_forward",
    )(keep, normed, w_qkv, w_qkv, w_qkv, conv, conv, conv, rate, allow, gain, *shards)
    return outs[:15], outs[15:]


def backward_kernel(streams, spans, heads, weights, *refs):
    (keep_ref, gn_ref, read_ref, gain_ref, q_ref, k_ref, v_ref, wk_ref, inv_ref, min_ref, pre_ref,
     nv_ref, np_ref, rate_ref, allow_ref, eq_ref, ek_ref, ev_ref, cq_ref, ck_ref, cv_ref,
     p_low, p_high, p_chip, pair_ref, wq_ref, wkey_ref, wv_ref) = refs[:28]
    refs = refs[28:]
    grads, refs = refs[:weights], refs[weights:]
    gconv_ref, grate_ref, gain_grad_ref, gnormed_ref = refs[:4]
    halves, sums, refs = refs[4:7], refs[7:10], refs[10:]
    bufs, refs = [refs[9 * w : 9 * w + 9] for w in range(weights)], refs[9 * weights :]
    reduce_sems, refs = refs[:3], refs[3:]
    go_buf, adj_buf, din_buf = refs[:3]
    pair_buf, own_buf, got_buf, pair_sem = refs[3:7]
    row_bufs, chain_bufs = refs[7:10], refs[10:]
    step_id = pl.program_id(0)
    turns = heads // GROUP
    place = Place(streams, spans)
    targets = [
        split_columns(sums[0], grads[0].shape[2]),
        [(sums[1], 0, 1), (sums[2], 0, 1)],
    ]
    work = Reduce(place, grads, targets, bufs, reduce_sems, 0.2)
    steps = work.steps()
    slots = BACKWARD_SLOTS
    size = gain_ref.shape[1]

    def hand_over(turn):
        return copy_to(
            own_buf.at[GROUP * turn + 1 - place.core], got_buf.at[turn],
            pair_sem.at[turn, 0], pair_sem.at[turn, 1], place.other(),
        )

    def weigh(turn):
        hand_over(turn).wait_recv()
        both = jnp.concatenate([own_buf[GROUP * turn + place.core], got_buf[turn]], 0)
        grad = nn(pair_buf[...], both).astype(BF16)
        lanes = pl.ds(pl.multiple_of(turn * size, size), size)
        for i in range(3):
            rows = halves[i].shape[1]
            halves[i][:, :, lanes] = grad[:, lanes_of(i, size)].reshape(-1, rows, size)
        hand_over(turn).wait_send()

    @pl.when(step_id == 0)
    def _():
        greet(work.neighbours())
        pair_buf[...] = pair_ref[...].T

    for index in range(2 * turns + 1):

        @pl.when(step_id == index)
        def _():
            for step in spread_steps(steps, REDUCE_AHEAD, slots, index):
                step()

    @pl.when(step_id < turns)
    def _():
        adjoint_body(
            keep_ref, gn_ref, read_ref, gain_ref, q_ref, k_ref, wk_ref,
            go_buf.at[step_id], adj_buf.at[pl.ds(GROUP * step_id, GROUP)], gain_grad_ref,
        )

    @pl.when(step_id == turns)
    def _():
        chain_body(place, True, adj_buf, (p_low, p_high, p_chip), din_buf, chain_bufs)

    @pl.when(step_id > turns + 1)
    def _():
        weigh(step_id - turns - 2)

    @pl.when(step_id > turns)
    def _():
        turn = step_id - turns - 1
        pair = pl.ds(GROUP * turn, GROUP)
        own = own_buf.at[pair]
        backward_body(
            turn, keep_ref, din_buf.at[pair], min_ref, pre_ref, go_buf.at[turn],
            q_ref, k_ref, v_ref, inv_ref, wk_ref, nv_ref, np_ref, rate_ref, allow_ref,
            eq_ref, ek_ref, ev_ref, cq_ref, ck_ref, cv_ref,
            own, gconv_ref, grate_ref, *row_bufs,
        )
        hand_over(turn).start()
        part = None
        for i, weight in enumerate((wq_ref, wkey_ref, wv_ref)):
            grad = jnp.concatenate([own[g, :, lanes_of(i, size)] for g in range(GROUP)], 1)
            term = nt(grad, weight[...])
            part = term if part is None else part + term
        before = jnp.where(turn == 0, jnp.zeros_like(part), gnormed_ref[...])
        gnormed_ref[...] = before + part

    @pl.when(step_id == 2 * turns)
    def _():
        weigh(turns - 1)
        for index in range(2 * turns + 1, slots + 1):
            for step in spread_steps(steps, REDUCE_AHEAD, slots, index):
                step()


def backward_call(
    keep, grad_normal, readout, gain, queries, keys, values, wkeys, invs, state, prefix,
    new_v, new_p, rate, allow, ext, conv, maps, pair_normed, w_qkv, grads, heads, collective_id,
):
    streams, spans = lax.axis_size("stream"), lax.axis_size("span")
    tok, width = queries.shape
    size = width // heads
    count = tok // STRETCH
    taps = conv.shape[0]
    rows = ext.shape[1]
    half = heads // 2

    turns = heads // GROUP
    wide = GROUP * size

    def first(i):
        return jnp.minimum(i, turns - 1)

    def second(i):
        return jnp.maximum(i - turns - 1, 0)

    def both(i):
        return jnp.where(i < turns, i, second(i))

    def block(at):
        return pl.BlockSpec((tok, wide), lambda h: (0, at(h)))

    def third(i, r):
        return pl.BlockSpec((r, wide), lambda h: (0, second(h) + i * turns))

    def part(i):
        return pl.BlockSpec((1, rows, wide), lambda h: (i, 0, second(h)))

    def whole(*shape):
        return pl.BlockSpec(shape, lambda h: (0,) * len(shape))

    vmem = pl.BlockSpec(memory_space=pltpu.VMEM)
    shapes = [g.shape for g in grads]
    outs = pl.pallas_call(
        functools.partial(backward_kernel, streams, spans, heads, len(grads)),
        grid=(2 * turns + 1,),
        in_specs=[
            pl.BlockSpec(memory_space=pltpu.SMEM),
            block(first), block(first), whole(1, size),
            block(both), block(both), block(second), block(both),
            pl.BlockSpec((GROUP, tok, STRETCH), lambda h: (second(h), 0, 0)),
            pl.BlockSpec((GROUP, size, size), lambda h: (second(h), 0, 0)),
            pl.BlockSpec((GROUP, count, 2 * size, size), lambda h: (second(h), 0, 0, 0)),
            block(second), block(second),
            whole(tok, heads), whole(tok, taps),
            part(0), part(1), part(2),
            third(0, taps), third(1, taps), third(2, taps),
            whole(half, size, size), whole(half, size, size), whole(half, size, size),
            vmem, third(0, width), third(1, width), third(2, width),
        ]
        + [vmem] * len(grads),
        out_specs=[
            pl.BlockSpec((3, taps, wide), lambda h: (0, 0, second(h))),
            whole(tok, heads),
            pl.BlockSpec((GROUP, 1, size), lambda h: (first(h), 0, 0)),
            whole(rows, width),
        ]
        + [vmem] * 6,
        out_shape=[
            jax.ShapeDtypeStruct((3, taps, width), F32),
            jax.ShapeDtypeStruct((tok, heads), F32),
            jax.ShapeDtypeStruct((heads, 1, size), F32),
            jax.ShapeDtypeStruct((rows, width), F32),
        ]
        + [jax.ShapeDtypeStruct((spans, width // spans, width // 2), BF16)] * 3
        + [
            jax.ShapeDtypeStruct((shapes[0][1], 2 * shapes[0][2]), BF16),
            jax.ShapeDtypeStruct(shapes[1][1:], BF16),
            jax.ShapeDtypeStruct(shapes[1][1:], BF16),
        ],
        scratch_shapes=Reduce.scratch(shapes, [g.dtype for g in grads], streams)
        + [
            pltpu.VMEM((turns, tok, wide), BF16),
            pltpu.VMEM((heads, size, size), BF16),
            pltpu.VMEM((heads, size, size), BF16),
            pltpu.VMEM((width, 2 * rows), BF16),
            pltpu.VMEM((heads, rows, 3 * size), BF16),
            pltpu.VMEM((turns, rows, 3 * size), BF16),
            pltpu.SemaphoreType.DMA((turns, 2)),
        ]
        + [pltpu.VMEM((tok, wide), F32)] * 3
        + chain_scratch(heads, size, size, True),
        compiler_params=pltpu.CompilerParams(
            collective_id=collective_id, has_side_effects=True, vmem_limit_bytes=VMEM_LIMIT
        ),
        name="delta_backward",
    )(
        keep, grad_normal, readout, gain, queries, keys, values, wkeys, invs, state, prefix,
        new_v, new_p, rate, allow, ext, ext, ext, conv, conv, conv, *maps, pair_normed,
        w_qkv, w_qkv, w_qkv, *grads,
    )
    return outs[:4], outs[4:7], outs[7:]


def feed_kernel(
    streams, spans,
    heads_ref, tok_ref, cot_ref, out_w_ref, gain_ref, gate_ref, up_ref, down_ref,
    result_ref, gmid_ref, gattn_ref, gnormal_ref, ggain_ref, ffn_grad_ref, down_grad_ref,
    mid_buf, grad_buf, res_buf, normed_buf, turned_buf, cot_buf, hid_buf, mine_buf, give_buf,
    hid_got, mine_got, row_sem, unit_sem,
):
    step_id = pl.program_id(0)
    last = pl.num_programs(0) - 1
    place = Place(streams, spans)
    width = cot_ref.shape[1]
    half = width // 2
    tok = cot_ref.shape[0]

    def exchange(source, target, sems):
        return copy_to(source, target, sems.at[0], sems.at[1], place.other())

    def rows(which):
        buf = normed_buf if which == 0 else cot_buf
        return exchange(buf.at[0 if which == 0 else 2], buf.at[1], row_sem.at[which])

    def units(step, which):
        source, target = (hid_buf, hid_got) if which == 0 else (give_buf, mine_got)
        return exchange(source.at[step], target.at[step], unit_sem.at[step, which])

    @pl.when(step_id == 0)
    def _():
        greet([place.other()])
        for own in range(2):
            which = place.core if own else 1 - place.core
            lanes = pl.ds(pl.multiple_of(which * half, half), half)
            cot_buf[0 if own else 2] = cot_ref[:, lanes]
        rows(1).start()
        middle = tok_ref[...].astype(F32) + nn(heads_ref[...], out_w_ref[...])
        inv = lax.rsqrt(jnp.mean(middle * middle, -1, keepdims=True) + EPSILON)
        mid_buf[...] = middle
        normed_buf[0] = (middle * inv * gain_ref[...]).astype(BF16)
        rows(0).start()
        grad_buf[...] = jnp.zeros(grad_buf.shape, F32)
        res_buf[...] = middle

    @pl.when(step_id == 1)
    def _():
        rows(0).wait_recv()
        rows(1).wait_recv()
        turned_buf[:, :tok] = normed_buf[0].T
        turned_buf[:, tok:] = normed_buf[1].T

    @pl.when(step_id < last)
    def _():
        normed = normed_buf[0]
        gate_w, up_w, down_w = gate_ref[...], up_ref[...], down_ref[...]
        gate = nn(normed, gate_w)
        up = nn(normed, up_w)
        grad_hidden = nt(cot_ref[...], down_w)
        sig = jax.nn.sigmoid(gate)
        act = gate * sig
        hidden = (act * up).astype(BF16)
        grad_gate = (grad_hidden * up * (sig * (1.0 + gate * (1.0 - sig)))).astype(BF16)
        grad_up = (grad_hidden * act).astype(BF16)
        low = place.core == 0
        hid_buf[step_id] = hidden
        mine_buf[step_id] = jnp.where(low, grad_gate, grad_up)
        give_buf[step_id] = jnp.where(low, grad_up, grad_gate)
        units(step_id, 0).start()
        units(step_id, 1).start()
        grad_buf[...] += nt(grad_gate, gate_w) + nt(grad_up, up_w)
        res_buf[...] += nn(hidden, down_w)

    @pl.when(step_id == last)
    def _():
        result_ref[...] = res_buf[...].astype(BF16)
        middle, grad = mid_buf[...], grad_buf[...]
        inv = lax.rsqrt(jnp.mean(middle * middle, -1, keepdims=True) + EPSILON)
        ggain_ref[...] = jnp.sum(grad * middle * inv, 0, keepdims=True)
        scaled = grad * gain_ref[...]
        total = cot_ref[...].astype(F32) + inv * scaled - middle * (inv * inv * inv) * jnp.mean(
            scaled * middle, -1, keepdims=True
        )
        gmid_ref[...] = total
        low_total = total.astype(BF16)
        gattn_ref[...] = low_total
        gnormal_ref[...] = nt(low_total, out_w_ref[...])

    @pl.when(step_id > 0)
    def _():
        before = step_id - 1
        units(before, 0).wait_recv()
        units(before, 1).wait_recv()
        mine = jnp.concatenate([mine_buf[before], mine_got[before]], 0)
        grad = nn(turned_buf[...], mine).astype(BF16)
        ffn_grad_ref[...] = grad.reshape(ffn_grad_ref.shape)
        both = jnp.concatenate([hid_buf[before], hid_got[before]], 0)
        cot = jnp.concatenate([cot_buf[0], cot_buf[1]], 0)
        down_grad_ref[...] = tn(both, cot).astype(BF16)

    @pl.when(step_id == last)
    def _():
        for which in range(2):
            rows(which).wait_send()
            for step in range(hid_buf.shape[0]):
                units(step, which).wait_send()


def feed_call(normal_heads, tokens, cotangent, w_out, gain, w_gate, w_up, w_down, collective_id):
    streams, spans = lax.axis_size("stream"), lax.axis_size("span")
    tok, width = tokens.shape
    units = w_gate.shape[1]
    step = 256
    count = units // step
    dma = pltpu.SemaphoreType.DMA

    def now(f):
        return jnp.minimum(f, count - 1)

    def before(f):
        return jnp.maximum(f - 1, 0)

    def whole(*shape):
        return pl.BlockSpec(shape, lambda f: (0,) * len(shape))

    rows = whole(tok, width)
    square = pltpu.VMEM((count, tok, step), BF16)
    return pl.pallas_call(
        functools.partial(feed_kernel, streams, spans),
        grid=(count + 1,),
        in_specs=[
            rows, rows, rows, whole(width, width), whole(1, width),
            pl.BlockSpec((width, step), lambda f: (0, now(f))),
            pl.BlockSpec((width, step), lambda f: (0, now(f))),
            pl.BlockSpec((step, width), lambda f: (now(f), 0)),
        ],
        out_specs=[
            rows, rows, rows, rows, whole(1, width),
            pl.BlockSpec((spans, width // spans, step), lambda f: (0, 0, before(f))),
            pl.BlockSpec((step, width // 2), lambda f: (before(f), 0)),
        ],
        out_shape=[
            jax.ShapeDtypeStruct((tok, width), BF16),
            jax.ShapeDtypeStruct((tok, width), F32),
            jax.ShapeDtypeStruct((tok, width), BF16),
            jax.ShapeDtypeStruct((tok, width), F32),
            jax.ShapeDtypeStruct((1, width), F32),
            jax.ShapeDtypeStruct((spans, width // spans, units), BF16),
            jax.ShapeDtypeStruct((units, width // 2), BF16),
        ],
        scratch_shapes=[pltpu.VMEM((tok, width), F32)] * 3
        + [
            pltpu.VMEM((2, tok, width), BF16),
            pltpu.VMEM((width, 2 * tok), BF16),
            pltpu.VMEM((3, tok, width // 2), BF16),
            square, square, square, square, square,
            dma((2, 2)), dma((count, 2, 2)),
        ],
        compiler_params=pltpu.CompilerParams(
            collective_id=collective_id, has_side_effects=True, vmem_limit_bytes=VMEM_LIMIT
        ),
        name="feed_forward",
    )(normal_heads, tokens, cotangent, w_out, gain, w_gate, w_up, w_down)


def local(
    tokens, cotangent, doc_stretches, w_qkv, conv_weight, w_beta, beta_bias, norm_attn, norm_head,
    w_out, norm_ffn, w_gate, w_up, w_down,
):
    tok_rows, model_width = tokens.shape[1:]
    heads = beta_bias.shape[0]
    size = model_width // heads
    count = tok_rows // STRETCH
    span_count = lax.axis_size("span")
    place = lax.axis_index("span")
    taps = conv_weight.shape[0]

    small = jnp.concatenate(
        [x.reshape(-1) for x in (conv_weight, w_beta, norm_attn, norm_ffn, norm_head)]
    )
    small_len = small.shape[0]
    small = jnp.pad(small, (0, 16 * 512 - small_len)).reshape(16, 512)
    full_qkv, smalls = gather_call([w_qkv, small], 1)
    full_qkv = full_qkv.reshape(-1, full_qkv.shape[2])
    smalls = smalls.reshape(span_count, -1)

    def small_part(shape, start):
        length = 1
        for dim in shape:
            length *= dim
        return smalls[:, start : start + length].reshape((span_count,) + shape), start + length

    at = 0
    full_conv, at = small_part(conv_weight.shape, at)
    full_beta, at = small_part(w_beta.shape, at)
    gain_attn, at = small_part(norm_attn.shape, at)
    gain_ffn, at = small_part(norm_ffn.shape, at)
    gain_head, at = small_part(norm_head.shape, at)
    full_conv = jnp.swapaxes(full_conv, 0, 1).reshape(taps, -1)
    full_beta = full_beta.reshape(-1, heads)
    attn_gain = gain_attn.reshape(-1).astype(F32)
    ffn_gain = gain_ffn.reshape(-1).astype(F32)
    head_gain = gain_head.reshape(1, -1).astype(F32)

    stretch_ids = place * count + jnp.arange(count, dtype=jnp.int32)
    doc_lengths = doc_stretches[0]
    doc_begins = jnp.cumsum(doc_lengths) - doc_lengths
    stretch_start = jnp.any(stretch_ids[:, None] == doc_begins[None, :], axis=1).astype(F32)
    stretch_keep = 1.0 - stretch_start
    token_start = jnp.repeat(stretch_start, STRETCH)
    token_offset = jnp.arange(tok_rows, dtype=jnp.int32) % STRETCH
    allow = jnp.stack(
        [1.0 - token_start * (token_offset < tap).astype(F32) for tap in range(taps)], 1
    )

    ends = tokens[0, tok_rows - HALO :]
    before = lax.ppermute(
        ends, "span", [(i, i + 1) for i in range(span_count - 1)]
    )
    inputs_ext = jnp.concatenate([before, tokens[0]], 0).astype(F32)
    inv_ext = lax.rsqrt(jnp.mean(inputs_ext * inputs_ext, -1, keepdims=True) + EPSILON)
    normed_ext = (inputs_ext * inv_ext * attn_gain).astype(BF16)
    inputs_f, inv_first, normed = inputs_ext[HALO:], inv_ext[HALO:], normed_ext[HALO:]
    strength = jax.nn.sigmoid(
        jnp.dot(normed, full_beta, preferred_element_type=F32) + beta_bias
    )
    (
        projected, queries, keys, values, invs, wkeys, prefix, new_v, new_p,
        state_in, p_low, p_high, p_chip, readout, normal_heads,
    ), rest = forward_call(
        stretch_keep, normed_ext, full_qkv, full_conv, strength, allow, head_gain,
        [w_out, w_gate, w_up, w_down], heads, 2,
    )
    full_out, full_gate, full_up, full_down = (w.reshape(-1, w.shape[2]) for w in rest)

    (
        result, grad_middle, grad_attn_in, grad_normal, grad_norm_ffn, half_ffn, half_down
    ) = feed_call(
        normal_heads, tokens[0], cotangent[0], full_out, ffn_gain[None], full_gate, full_up,
        full_down, 3,
    )
    half_down = half_down.reshape(span_count, -1, half_down.shape[1])
    half_out = weight_grad(pair_tokens(normal_heads), pair_half(grad_attn_in), span_count)
    (
        (grad_conv, grad_strength, head_grads, grad_normed_ext), (half_q, half_k, half_v), ffn_parts
    ) = backward_call(
        stretch_keep, grad_normal, readout, head_gain, queries, keys, values, wkeys, invs,
        state_in, prefix, new_v, new_p, strength, allow, projected, full_conv,
        (p_low, p_high, p_chip), pair_tokens(normed_ext), full_qkv, [half_down, half_ffn], heads, 4,
    )
    grad_logit = grad_strength * strength * (1.0 - strength)
    grad_logit_low = grad_logit.astype(BF16)
    grad_w_beta = product("td,th->dh", normed, grad_logit_low)
    halo_back = lax.ppermute(
        grad_normed_ext[:HALO].astype(BF16), "span", [(i, i - 1) for i in range(1, span_count)]
    )
    grad_normed = (
        grad_normed_ext[HALO:]
        + product("th,dh->td", grad_logit_low, full_beta)
        + jnp.pad(halo_back.astype(F32), ((tok_rows - HALO, 0), (0, 0)))
    )
    grad_norm_attn = jnp.sum(grad_normed * inputs_f * inv_first, 0)
    grad_tokens = grad_middle + norm_back(grad_normed, inputs_f, inv_first, attn_gain)

    def by_span(array):
        return array.reshape(span_count, -1)

    grad_conv = jnp.swapaxes(grad_conv, 0, 1).reshape(taps, span_count, -1)
    packed = jnp.concatenate(
        [
            by_span(jnp.swapaxes(grad_conv, 0, 1)),
            by_span(grad_w_beta),
            by_span(grad_norm_attn),
            by_span(grad_norm_ffn),
            by_span(jnp.sum(head_grads, (0, 1))),
            jnp.broadcast_to(jnp.sum(grad_logit, 0)[None], (span_count, heads)),
        ],
        1,
    )
    packed = jnp.pad(packed, ((0, 0), (0, 16 * 1024 - packed.shape[1])))
    packed = packed.reshape(span_count, 16, 2, 512)
    core = place % 2
    half_small = lax.dynamic_index_in_dim(packed, core, 2, keepdims=False) + swap_core(
        lax.dynamic_index_in_dim(packed, 1 - core, 2, keepdims=False)
    )
    parts = reduce_call([half_out, half_q, half_k, half_v, half_small], 5)
    part_down, part_gate, part_up = (x.astype(F32) for x in ffn_parts)
    part_out, part_qkv = parts[0].astype(F32), parts[1].astype(F32)
    part_small = parts[2].reshape(-1)
    sums = []
    at = 0
    for like in (conv_weight, w_beta, norm_attn, norm_ffn, norm_head, beta_bias):
        sums.append(part_small[at : at + like.size].reshape(like.shape))
        at += like.size

    return (
        result[None],
        grad_tokens[None],
        part_qkv,
        sums[0],
        sums[1],
        sums[5],
        sums[2],
        sums[4],
        part_out,
        sums[3],
        part_gate,
        part_up,
        part_down,
    )


def solution(mesh):
    in_specs = (
        P("stream", "span", None),
        P("stream", "span", None),
        P("stream", None),
        P("span", None),
        P(None, "span"),
        P("span", None),
        P(),
        P("span"),
        P("span"),
        P("span", None),
        P("span"),
        P("span", None),
        P("span", None),
        P("span", None),
    )
    out_specs = (
        P("stream", "span", None),
        P("stream", "span", None),
        P("span", None),
        P(None, "span"),
        P("span", None),
        P(),
        P("span"),
        P("span"),
        P("span", None),
        P("span"),
        P("span", None),
        P("span", None),
        P("span", None),
    )
    return jax.shard_map(local, mesh=mesh, in_specs=in_specs, out_specs=out_specs, check_vma=False)
```

```python
import functools

import jax
import jax.numpy as jnp
from jax import lax
from jax.experimental import pallas as pl
from jax.experimental.pallas import tpu as pltpu
from jax.sharding import PartitionSpec as P

STRETCH = 64
HALO = 16
GROUP = 2
EPSILON = 1e-06
F32 = jnp.float32
BF16 = jnp.bfloat16
AXES = ("stream", "span")
VMEM_LIMIT = 60 * 2**20
GATHER_PIECE = 24 * 1024
GATHER_AHEAD = 3
GATHER_LAG = 2
REDUCE_PIECE = 100 * 1024
REDUCE_AHEAD = 6
FORWARD_SLOTS = 11
BACKWARD_SLOTS = 11


def nn(a, b):
    return lax.dot_general(a, b, (((1,), (0,)), ((), ())), preferred_element_type=F32)


def nt(a, b):
    return lax.dot_general(a, b, (((1,), (1,)), ((), ())), preferred_element_type=F32)


def tn(a, b):
    return lax.dot_general(a, b, (((0,), (0,)), ((), ())), preferred_element_type=F32)


def fine(a, b):
    a_hi = a.astype(BF16)
    a_lo = (a - a_hi.astype(F32)).astype(BF16)
    b_hi = b.astype(BF16)
    b_lo = (b - b_hi.astype(F32)).astype(BF16)
    return nn(jnp.concatenate([a_hi, a_hi, a_lo], 1), jnp.concatenate([b_hi, b_lo, b_hi], 0))


def grid_ids(size):
    return (
        lax.broadcasted_iota(jnp.int32, (size, size), 0),
        lax.broadcasted_iota(jnp.int32, (size, size), 1),
    )


def unit_inverse(lower_list):
    rows, cols = grid_ids(STRETCH)
    eye = (rows == cols).astype(F32)
    out = [eye - jnp.where((rows // 2) == (cols // 2), low, 0.0) for low in lower_list]
    half = 2
    while half < STRETCH:
        cross = ((rows // (2 * half)) == (cols // (2 * half))) & ((rows // half) != (cols // half))
        inner = [fine(jnp.where(cross, low, 0.0), inv) for low, inv in zip(lower_list, out)]
        out = [inv - fine(inv, mid) for inv, mid in zip(out, inner)]
        half *= 2
    return out


def column_of(table, index):
    lanes = lax.broadcasted_iota(jnp.int32, table.shape, 1)
    return jnp.sum(jnp.where(lanes == index, table, 0.0), -1, keepdims=True)


def mix_rows(ext, conv_ref, allow):
    ext = ext.astype(F32)
    conv = conv_ref.astype(F32)
    shifted = [
        (ext if tap == 0 else pltpu.roll(ext, tap, 0))[HALO:] * allow[tap]
        for tap in range(conv.shape[0])
    ]
    mixed = sum(conv[tap : tap + 1] * shifted[tap] for tap in range(conv.shape[0]))
    return shifted, mixed, conv


def local_kernel(
    keep_ref, normed_ref, wq_ref, wkey_ref, wv_ref, cq_ref, ck_ref, cv_ref, rate_ref, allow_ref,
    ext_ref, q_ref, k_ref, v_ref, inv_ref, wk_ref, pre_ref, end_ref, read_ref, rmap_ref, nv_ref, np_ref,
):
    head = pl.program_id(0)
    allow_all = allow_ref[...]
    allow = [allow_all[:, tap : tap + 1] for tap in range(cq_ref.shape[0])]
    rate = column_of(rate_ref[...], head)

    normed = normed_ref[...]

    def activation(index, weight_ref, conv_ref):
        ext = nn(normed, weight_ref[...]).astype(BF16)
        ext_ref[index] = ext
        _, mixed, _ = mix_rows(ext, conv_ref[...], allow)
        return mixed * jax.nn.sigmoid(mixed)

    act_q = activation(0, wq_ref, cq_ref)
    act_k = activation(1, wkey_ref, ck_ref)
    act_v = activation(2, wv_ref, cv_ref)
    queries = (act_q * lax.rsqrt(jnp.sum(act_q * act_q, -1, keepdims=True) + EPSILON)).astype(BF16)
    keys = (act_k * lax.rsqrt(jnp.sum(act_k * act_k, -1, keepdims=True) + EPSILON)).astype(BF16)
    values = act_v.astype(BF16)
    q_ref[...] = queries
    k_ref[...] = keys
    v_ref[...] = values
    count = queries.shape[0] // STRETCH
    rows, cols = grid_ids(STRETCH)
    parts = [slice(n * STRETCH, (n + 1) * STRETCH) for n in range(count)]
    lows = []
    for part in parts:
        gram = nt(keys[part], keys[part])
        lows.append(jnp.where(rows > cols, gram * rate[part], 0.0))
    invs = unit_inverse(lows)
    size = keys.shape[1]
    drows, dcols = grid_ids(size)
    running = jnp.concatenate(
        [jnp.zeros((size, size), F32), (drows == dcols).astype(F32)], 0
    )
    for n, part in enumerate(parts):
        key, query = keys[part], queries[part]
        inv = invs[n].astype(BF16)
        inv_ref[0, part, :] = inv
        scaled = jnp.concatenate(
            [key.astype(F32) * rate[part], values[part].astype(F32) * rate[part]], 1
        ).astype(BF16)
        weighted = nn(inv, scaled)
        wkey = weighted[:, :size].astype(BF16)
        wk_ref[part, :] = wkey
        running = running * keep_ref[n]
        low_state = running.astype(BF16)
        pre_ref[0, n] = low_state
        back = nt(jnp.concatenate([wkey, query], 0), low_state)
        new = jnp.concatenate(
            [weighted[:, size:] - back[:STRETCH, :size], -back[:STRETCH, size:]], 1
        ).astype(BF16)
        nv_ref[part, :] = new[:, :size]
        np_ref[part, :] = new[:, size:]
        scores = jnp.where(rows >= cols, nt(query, key), 0.0).astype(BF16)
        out = back[STRETCH:] + nn(scores, new)
        read_ref[part, :] = out[:, :size]
        rmap_ref[part, :] = out[:, size:].astype(BF16)
        running = running + tn(new, key)
    end_ref[0] = running.astype(BF16)


def lanes_of(index, size):
    return slice(index * size, (index + 1) * size)


def adjoint_body(
    keep_ref, gn_ref, read_ref, gain_ref, q_ref, k_ref, wk_ref, go_ref, adj_ref, gain_grad_ref
):
    size = gain_ref.shape[1]
    tok = gn_ref.shape[0]
    grads = []
    for g in range(GROUP):
        grad, readout = gn_ref[:, lanes_of(g, size)], read_ref[:, lanes_of(g, size)]
        inv = lax.rsqrt(jnp.mean(readout * readout, -1, keepdims=True) + EPSILON)
        scaled = grad * gain_ref[...]
        grad_read = inv * scaled - readout * (inv * inv * inv) * jnp.mean(
            scaled * readout, -1, keepdims=True
        )
        gain_grad_ref[g] = jnp.sum(grad * readout * inv, 0, keepdims=True)
        grads.append(grad_read.astype(BF16))
        go_ref[:, lanes_of(g, size)] = grads[g]
    rows, cols = grid_ids(STRETCH)
    adj = [jnp.zeros((size, size), F32)] * GROUP
    for n in range(tok // STRETCH - 1, -1, -1):
        part = slice(n * STRETCH, (n + 1) * STRETCH)
        for g in range(GROUP):
            lanes = lanes_of(g, size)
            key, query, out = k_ref[part, lanes], q_ref[part, lanes], grads[g][part]
            scores = jnp.where(rows >= cols, nt(query, key), 0.0).astype(BF16)
            new_grad = tn(scores, out) + nt(key, adj[g].astype(BF16))
            adj[g] = (
                adj[g]
                + tn(
                    jnp.concatenate([out, (-new_grad).astype(BF16)], 0),
                    jnp.concatenate([query, wk_ref[part, lanes]], 0),
                )
            ) * keep_ref[n]
    for g in range(GROUP):
        adj_ref[g] = adj[g].astype(BF16)


def backward_body(
    turn, keep_ref, din_ref, min_ref, pre_ref, go_ref, q_ref, k_ref, v_ref, inv_ref, wk_ref,
    nv_ref, np_ref, rate_ref, allow_ref,
    eq_ref, ek_ref, ev_ref, cq_ref, ck_ref, cv_ref,
    gext_ref, gconv_ref, grate_ref,
    gq_buf, gk_buf, gv_buf,
):
    size = min_ref.shape[1]
    tok = q_ref.shape[0]
    count = tok // STRETCH
    rows, cols = grid_ids(STRETCH)
    rates = [column_of(rate_ref[...], GROUP * turn + g) for g in range(GROUP)]
    low_in = [min_ref[g] for g in range(GROUP)]
    adj = [din_ref[g].astype(F32) for g in range(GROUP)]
    grate_parts = [[None] * count for _ in range(GROUP)]
    for n in range(count - 1, -1, -1):
        part = slice(n * STRETCH, (n + 1) * STRETCH)
        for g in range(GROUP):
            lanes = lanes_of(g, size)
            key, query, value = k_ref[part, lanes], q_ref[part, lanes], v_ref[part, lanes]
            out = go_ref[part, lanes]
            beta = rates[g][part]
            pre = pre_ref[g, n]
            state = (nn(low_in[g], pre[size:]) + pre[:size].astype(F32)).astype(BF16)
            new = (nt(np_ref[part, lanes], low_in[g]) + nv_ref[part, lanes].astype(F32)).astype(BF16)
            low_adj = adj[g].astype(BF16)
            gram_both = nt(jnp.concatenate([key, query], 0), key)
            gram = gram_both[:STRETCH]
            scores = jnp.where(rows >= cols, gram_both[STRETCH:], 0.0).astype(BF16)
            new_grad = tn(scores, out) + nt(key, low_adj)
            low_new_grad = new_grad.astype(BF16)
            adj[g] = (
                adj[g]
                + tn(
                    jnp.concatenate([out, -low_new_grad], 0),
                    jnp.concatenate([query, wk_ref[part, lanes]], 0),
                )
            ) * keep_ref[n]
            grad_b = tn(inv_ref[g, part, :], low_new_grad)
            both = nt(jnp.concatenate([out, grad_b.astype(BF16)], 0), new)
            grad_scores = jnp.where(rows >= cols, both[:STRETCH], 0.0).astype(BF16)
            grad_low = jnp.where(rows > cols, -both[STRETCH:], 0.0)
            left = value.astype(F32) - nt(key, state)
            grate_parts[g][n] = jnp.sum(grad_low * gram, -1, keepdims=True) + jnp.sum(
                grad_b * left, -1, keepdims=True
            )
            grad_v = beta * grad_b
            grad_gram = beta * grad_low
            symmetric = (grad_gram + grad_gram.T).astype(BF16)
            by_state = nn(jnp.concatenate([out, -grad_v.astype(BF16)], 0), state)
            gq_buf[part, lanes] = by_state[:STRETCH] + nn(grad_scores, key)
            gk_buf[part, lanes] = (
                by_state[STRETCH:]
                + tn(grad_scores, query)
                + nn(jnp.concatenate([new, symmetric], 1), jnp.concatenate([low_adj, key], 0))
            )
            gv_buf[part, lanes] = grad_v
    heads_at = lax.broadcasted_iota(jnp.int32, grate_ref.shape, 1)
    grate = jnp.where(turn == 0, jnp.zeros(grate_ref.shape, F32), grate_ref[...])
    for g in range(GROUP):
        grate = jnp.where(
            heads_at == GROUP * turn + g, jnp.concatenate(grate_parts[g], 0), grate
        )
    grate_ref[...] = grate
    allow_all = allow_ref[...]
    allow = [allow_all[:, tap : tap + 1] for tap in range(cq_ref.shape[0])]
    zeros = jnp.zeros((HALO, size), F32)
    for i, (ext, conv_ref, buf) in enumerate(
        ((eq_ref, cq_ref, gq_buf), (ek_ref, ck_ref, gk_buf), (ev_ref, cv_ref, gv_buf))
    ):
        for g in range(GROUP):
            lanes = lanes_of(g, size)
            shifted, mixed, conv = mix_rows(ext[0, :, lanes], conv_ref[:, lanes], allow)
            sig = jax.nn.sigmoid(mixed)
            grad = buf[:, lanes]
            if i < 2:
                raw = mixed * sig
                inv = lax.rsqrt(jnp.sum(raw * raw, -1, keepdims=True) + EPSILON)
                grad = inv * grad - raw * (inv * inv * inv) * jnp.sum(grad * raw, -1, keepdims=True)
            grad = grad * (sig * (1.0 + mixed * (1.0 - sig)))
            total = None
            for tap in range(conv.shape[0]):
                gconv_ref[i, tap : tap + 1, lanes] = jnp.sum(grad * shifted[tap], 0, keepdims=True)
                term = jnp.concatenate([zeros, grad * (conv[tap : tap + 1] * allow[tap])], 0)
                if tap:
                    term = pltpu.roll(term, tok + HALO - tap, 0)
                total = term if total is None else total + term
            gext_ref[g, :, lanes_of(i, size)] = total.astype(BF16)


def norm_back(grad_in, values, inv_rms, gain_vec):
    scaled = grad_in * gain_vec
    return inv_rms * scaled - values * inv_rms**3 * jnp.mean(scaled * values, -1, keepdims=True)


def product(pattern, first, second, kind=F32):
    return jnp.einsum(pattern, first, second, preferred_element_type=F32).astype(kind)


def swap_core(block):
    streams, spans = lax.axis_size("stream"), lax.axis_size("span")
    pairs = [
        (s * spans + p, s * spans + (p ^ 1)) for s in range(streams) for p in range(spans)
    ]
    return lax.ppermute(block, AXES, pairs)


def pair_tokens(block):
    return jnp.concatenate([block, swap_core(block)], 0)


def pair_half(block):
    width = block.shape[1] // 2
    core = lax.axis_index("span") % 2
    mine = lax.dynamic_slice_in_dim(block, core * width, width, 1)
    theirs = lax.dynamic_slice_in_dim(block, (1 - core) * width, width, 1)
    return jnp.concatenate([mine, swap_core(theirs)], 0)


def weight_grad(left, right, spans):
    grad = product("td,te->de", left, right, BF16)
    return grad.reshape(spans, -1, grad.shape[1])


MESH = pl.DeviceIdType.MESH


class Place:
    def __init__(self, streams, spans):
        self.streams, self.spans, self.chips = streams, spans, spans // 2
        self.stream = lax.axis_index("stream")
        self.span = lax.axis_index("span")
        self.chip = lax.div(self.span, 2)
        self.core = lax.rem(self.span, 2)

    def beside(self, step):
        return (self.stream ^ step, self.span)

    def along(self, step):
        return (self.stream, 2 * self.shifted(step) + self.core)

    def shifted(self, step):
        return lax.rem(self.chip + step + self.chips, self.chips)

    def other(self):
        return (self.stream, 2 * self.chip + 1 - self.core)

    def span_at(self, step):
        return (self.stream, lax.rem(self.span + step + self.spans, self.spans))

    def either_side(self):
        return [self.span_at(1), self.span_at(-1)]


def greet(places):
    barrier = pltpu.get_barrier_semaphore()
    for target in places:
        pl.semaphore_signal(barrier, inc=1, device_id=target, device_id_type=MESH)
    pl.semaphore_wait(barrier, len(places))


def quarter_of(rows, width, streams):
    if (width // 128) % streams == 0:
        return 1, streams
    return 2, streams // 2


def pieces_of(rows, width, streams, most):
    down, across = quarter_of(rows, width, streams)
    r, c = rows // down, width // across
    best = (1, 1)
    for cut_r in range(1, max(r // 16, 1) + 1):
        for cut_c in range(1, c // 128 + 1):
            if (cut_r > 1 and r % (16 * cut_r)) or c % (128 * cut_c):
                continue
            small = r * c <= most * cut_r * cut_c
            best_small = r * c <= most * best[0] * best[1]
            fewer = (cut_r * cut_c, cut_c) < (best[0] * best[1], best[1])
            if (small and (not best_small or fewer)) or (not best_small and not fewer):
                best = (cut_r, cut_c)
    return best


def units_of(shapes, streams, most):
    units = []
    for w, (rows, width) in enumerate(shapes):
        cut_r, cut_c = pieces_of(rows, width, streams, most)
        units += [(w, i, j, cut_r, cut_c) for i in range(cut_r) for j in range(cut_c)]
    return units


def quarter_index(rows, width, streams, at, unit):
    _, i, j, cut_r, cut_c = unit
    down, across = quarter_of(rows, width, streams)
    r, c = rows // down, width // across
    pr, pc = r // cut_r, c // cut_c
    if down == 1:
        row = pl.ds(i * pr, pr)
    else:
        row = pl.ds(pl.multiple_of(lax.div(at, across) * r + i * pr, pr), pr)
    start = lax.rem(at, across) * c + j * pc
    return row, pl.ds(pl.multiple_of(start, 128), pc)


def copy_to(source, target, send_sem, recv_sem, device):
    return pltpu.make_async_remote_copy(
        src_ref=source, dst_ref=target, send_sem=send_sem, recv_sem=recv_sem,
        device_id=device, device_id_type=MESH,
    )


class Gather:
    def __init__(self, place, shards, fulls, sems):
        self.place, self.shards, self.fulls = place, shards, fulls
        self.sems = sems
        self.units = units_of([x.shape for x in shards], place.streams, GATHER_PIECE)

    @staticmethod
    def sem_shapes(shapes, streams, spans):
        units = len(units_of(shapes, streams, GATHER_PIECE))
        slots = spans // 2
        dma = pltpu.SemaphoreType.DMA
        return [dma((units, slots, 4, 2)), dma((len(shapes), slots, 2)), dma((len(shapes),))]

    def part(self, unit, at, span=None):
        w = self.units[unit][0]
        rows, width = self.shards[w].shape
        index = quarter_index(rows, width, self.place.streams, at, self.units[unit])
        if span is None:
            return self.shards[w].at[index]
        return self.fulls[w].at[(span,) + index]

    def source_span(self, k):
        return 2 * self.place.shifted(-k) + self.place.core

    def wire(self, unit, k, kind, span, at, device, source=None):
        region = self.part(unit, at, span)
        return copy_to(
            region if source is None else source, region,
            self.sems[0].at[unit, k, kind, 0], self.sems[0].at[unit, k, kind, 1], device,
        )

    def along(self, unit, k):
        p = self.place
        return self.wire(
            unit, k, 0, p.span, p.stream, p.along(k), self.part(unit, p.stream)
        )

    def along_wait(self, unit, k):
        p = self.place
        self.wire(unit, k, 0, self.source_span(k), p.stream, p.along(k)).wait_recv()

    def sideways(self, unit, k, step):
        p = self.place
        return self.wire(unit, k, step, self.source_span(k), p.stream, p.beside(step))

    def sideways_wait(self, unit, k, step):
        p = self.place
        self.wire(
            unit, k, step, self.source_span(k), p.stream ^ step, p.beside(step)
        ).wait_recv()

    @staticmethod
    def turns(unit, k):
        return (1, 2) if (unit + k) % 2 == 0 else (2, 1)

    def corner(self, unit, k):
        p = self.place
        first, second = self.turns(unit, k)
        return self.wire(
            unit, k, 3, self.source_span(k), p.stream ^ first, p.beside(second)
        )

    def corner_wait(self, unit, k):
        p = self.place
        self.wire(unit, k, 3, self.source_span(k), p.stream ^ 3, p.beside(1)).wait_recv()

    def across(self, w, k):
        p = self.place
        span = p.span if k == 0 else self.source_span(k)
        region = self.fulls[w].at[span]
        return copy_to(
            self.shards[w] if k == 0 else region, region,
            self.sems[1].at[w, k, 0], self.sems[1].at[w, k, 1], p.other(),
        )

    def across_wait(self, w, k):
        p = self.place
        span = 2 * p.shifted(-k) + 1 - p.core
        region = self.fulls[w].at[span]
        copy_to(
            region, region, self.sems[1].at[w, k, 0], self.sems[1].at[w, k, 1], p.other()
        ).wait_recv()

    def own(self, w):
        return pltpu.make_async_copy(
            self.shards[w], self.fulls[w].at[self.place.span], self.sems[2].at[w]
        )

    def neighbours(self):
        p = self.place
        return (
            [p.along(k) for k in range(1, p.chips)] + [p.beside(1), p.beside(2), p.other()]
        )

    def steps(self):
        p = self.place
        slots = range(1, p.chips)
        count = len(self.units)
        owner = [unit[0] for unit in self.units]
        ends = {u: w for u, w in enumerate(owner) if u + 1 == count or owner[u + 1] != w}
        starts = {u for u, w in enumerate(owner) if u == 0 or owner[u - 1] != w}
        steps = []

        def begin(unit):
            for k in slots:
                self.along(unit, k).start()

        def hand_over(w):
            self.across(w, 0).start()
            self.own(w).start()

        def beside(unit, k):
            self.along_wait(unit, k)
            self.sideways(unit, k, 1).start()
            self.sideways(unit, k, 2).start()

        def turn(unit, k):
            self.sideways_wait(unit, k, self.turns(unit, k)[0])
            self.corner(unit, k).start()

        def close(w, k):
            for unit in range(count):
                if owner[unit] == w:
                    self.sideways_wait(unit, k, self.turns(unit, k)[1])
                    self.corner_wait(unit, k)
            self.across(w, k).start()

        def finish(w):
            for k in range(p.chips):
                self.across_wait(w, k)
                self.across(w, k).wait_send()
            self.own(w).wait()
            for unit in range(count):
                if owner[unit] == w:
                    for k in slots:
                        self.along(unit, k).wait_send()
                        self.sideways(unit, k, 1).wait_send()
                        self.sideways(unit, k, 2).wait_send()
                        self.corner(unit, k).wait_send()

        ahead, lag = GATHER_AHEAD, GATHER_LAG
        for unit in range(min(ahead, count)):
            steps.append(functools.partial(begin, unit))
        for t in range(count + 2 * lag):
            if t < count:
                steps += [functools.partial(beside, t, k) for k in slots]
                if t in starts:
                    steps.append(functools.partial(hand_over, owner[t]))
            if t + ahead < count:
                steps.append(functools.partial(begin, t + ahead))
            if 0 <= t - lag < count:
                steps += [functools.partial(turn, t - lag, k) for k in slots]
            if t - 2 * lag in ends:
                steps += [functools.partial(close, ends[t - 2 * lag], k) for k in slots]
        steps += [functools.partial(finish, w) for w in range(len(self.shards))]
        return steps


def gather_kernel(streams, spans, count, *refs):
    shards, tok_ref, fulls = refs[:count], refs[count], refs[count + 1 : 2 * count + 1]
    halo_ref, sems, halo_sem = refs[2 * count + 1], refs[2 * count + 2 : -1], refs[-1]
    place = Place(streams, spans)
    work = Gather(place, shards, fulls, sems)
    greet(work.neighbours() + place.either_side())
    halo = copy_to(
        tok_ref.at[pl.ds(tok_ref.shape[0] - HALO, HALO)], halo_ref, halo_sem.at[0], halo_sem.at[1],
        place.span_at(1),
    )
    halo.start()
    for step in work.steps():
        step()
    halo.wait()


def gather_call(shards, tokens, collective_id):
    streams, spans = lax.axis_size("stream"), lax.axis_size("span")
    shapes = [shard.shape for shard in shards]
    hbm = pl.BlockSpec(memory_space=pl.ANY)
    return pl.pallas_call(
        functools.partial(gather_kernel, streams, spans, len(shards)),
        in_specs=[pl.BlockSpec(memory_space=pltpu.VMEM)] * len(shards) + [hbm],
        out_specs=[hbm] * (len(shards) + 1),
        out_shape=[jax.ShapeDtypeStruct((spans,) + s.shape, s.dtype) for s in shards]
        + [jax.ShapeDtypeStruct((HALO, tokens.shape[1]), tokens.dtype)],
        scratch_shapes=Gather.sem_shapes(shapes, streams, spans) + [pltpu.SemaphoreType.DMA((2,))],
        compiler_params=pltpu.CompilerParams(
            collective_id=collective_id, has_side_effects=True, vmem_limit_bytes=VMEM_LIMIT
        ),
        name="gather_weights",
    )(*shards, tokens)


class Reduce:
    def __init__(self, place, grads, targets, bufs, sems, share):
        self.place, self.grads, self.bufs, self.sems = place, grads, bufs, sems
        self.targets = targets
        self.units = self.cut([g.shape for g in grads], place.streams)
        self.modes = self.plan(self.units, [g.shape for g in grads], place.streams, share)

    @staticmethod
    def cut(shapes, streams):
        units = units_of([s[1:] for s in shapes], streams, REDUCE_PIECE // shapes[0][0])
        sizes = [sum(u[0] == w for u in units) for w in range(len(shapes))]
        order = []
        for w, size in enumerate(sizes):
            own = [u for u in units if u[0] == w]
            order += [((n + 0.5) / size, w, u) for n, u in enumerate(own)]
        return [u for _, _, u in sorted(order)]

    @staticmethod
    def plan(units, shapes, streams, share):
        whole = part = 0
        modes = []
        loads = [[0, 0], [0, 0]]
        for w, _, _, cut_r, cut_c in units:
            _, rows, width = shapes[w]
            size = rows * width // (cut_r * cut_c)
            plain = quarter_of(rows, width, streams)[0] == 1 and cut_c == 1 and rows > 16
            whole += size
            first = plain and part + size <= share * whole
            part += size if first else 0
            load = loads[first]
            way = load.index(min(load))
            load[way] += size
            modes.append((first, (1, 2) if way == 0 else (2, 1)))
        return modes

    @staticmethod
    def block(shape, streams):
        _, rows, width = shape
        down, across = quarter_of(rows, width, streams)
        return rows // down, width // across

    @staticmethod
    def scratch(shapes, kinds, streams):
        out = []
        dma = pltpu.SemaphoreType.DMA
        spans = shapes[0][0]
        for shape, kind in zip(shapes, kinds):
            r, c = Reduce.block(shape, streams)
            out += [
                pltpu.VMEM((2, spans, r, c), kind),
                pltpu.VMEM((2, spans, r, c), kind),
                pltpu.VMEM((spans, r, c), kind),
                pltpu.VMEM((spans, r, c), kind),
                pltpu.VMEM((spans, r, c), kind),
                pltpu.VMEM((r, c), kind),
                pltpu.VMEM((streams, 2, r, c), kind),
            ]
            across = quarter_of(*shape[1:], streams)[1]
            out += [
                pltpu.VMEM((spans, r, c * across) if across == streams else (2, 16, 128), kind),
                pltpu.VMEM((2, r, c * across) if across == streams else (2, 16, 128), kind),
            ]
        n = len(Reduce.cut(shapes, streams))
        out += [dma((n, 3, 2)), dma((n, spans // 2, 2)), dma((n, streams, 2))]
        return out

    def turn(self, unit):
        return self.modes[unit][1]

    def chips_first(self, unit):
        return self.modes[unit][0]

    def inner(self, unit):
        w, i, j, cut_r, cut_c = self.units[unit]
        r, c = self.block(self.grads[w].shape, self.place.streams)
        r, c = r // cut_r, c // cut_c
        return pl.ds(i * r, r), pl.ds(j * c, c)

    def outer(self, unit, at):
        _, rows, width = self.grads[self.units[unit][0]].shape
        return quarter_index(rows, width, self.place.streams, at, self.units[unit])

    def buf(self, unit, which):
        return self.bufs[self.units[unit][0]][which]

    def count(self, unit):
        return 2 if self.chips_first(unit) else self.place.spans

    def first(self, unit, slot):
        p = self.place
        a, b = self.turn(unit)
        spans = pl.ds(0, self.count(unit))
        at = p.stream ^ a if slot == 0 else p.stream ^ a ^ b
        source = self.buf(unit, 8) if self.chips_first(unit) else self.grads[self.units[unit][0]]
        return copy_to(
            source.at[(spans,) + self.outer(unit, at)],
            self.buf(unit, 0).at[(slot, spans) + self.inner(unit)],
            self.sems[0].at[unit, slot, 0], self.sems[0].at[unit, slot, 1], p.beside(a),
        )

    def second(self, unit):
        p = self.place
        _, b = self.turn(unit)
        spans = pl.ds(0, self.count(unit))
        return copy_to(
            self.buf(unit, 1).at[(1, spans) + self.inner(unit)],
            self.buf(unit, 2).at[(spans,) + self.inner(unit)],
            self.sems[0].at[unit, 2, 0], self.sems[0].at[unit, 2, 1], p.beside(b),
        )

    def third(self, unit, k):
        p = self.place
        if self.chips_first(unit):
            rows, _ = self.inner(unit)
            return copy_to(
                self.grads[self.units[unit][0]].at[pl.ds(2 * p.shifted(k), 2), rows],
                self.buf(unit, 7).at[pl.ds(2 * k, 2), rows],
                self.sems[1].at[unit, k, 0], self.sems[1].at[unit, k, 1], p.along(k),
            )
        return copy_to(
            self.buf(unit, 3).at[(pl.ds(2 * p.shifted(k), 2),) + self.inner(unit)],
            self.buf(unit, 4).at[(pl.ds(2 * k, 2),) + self.inner(unit)],
            self.sems[1].at[unit, k, 0], self.sems[1].at[unit, k, 1], p.along(k),
        )

    def swap(self, unit):
        p = self.place
        return copy_to(
            self.buf(unit, 5).at[self.inner(unit)],
            self.buf(unit, 6).at[(0, p.core) + self.inner(unit)],
            self.sems[2].at[unit, 0, 0], self.sems[2].at[unit, 0, 1], p.other(),
        )

    def fourth(self, unit, step):
        p = self.place
        return copy_to(
            self.buf(unit, 6).at[(0, pl.ds(0, 2)) + self.inner(unit)],
            self.buf(unit, 6).at[(step, pl.ds(0, 2)) + self.inner(unit)],
            self.sems[2].at[unit, step, 0], self.sems[2].at[unit, step, 1], p.beside(step),
        )

    def neighbours(self):
        p = self.place
        return [p.along(k) for k in range(1, p.chips)] + [
            p.beside(s) for s in range(1, p.streams)
        ] + [p.other()]

    def begin(self, unit):
        if self.chips_first(unit):
            for k in range(1, self.place.chips):
                self.third(unit, k).start()
            return
        for slot in (1, 0):
            self.first(unit, slot).start()

    def add_first(self, unit):
        if self.chips_first(unit):
            self.sum_chips(unit)
            for slot in (1, 0):
                self.first(unit, slot).start()
            return
        self.sum_first(unit, self.grads[self.units[unit][0]])

    def sum_chips(self, unit):
        p = self.place
        grad = self.grads[self.units[unit][0]]
        rows, _ = self.inner(unit)
        for k in range(1, p.chips):
            self.third(unit, k).wait_recv()
        for part in range(2):
            total = grad[2 * p.chip + part, rows, :].astype(F32)
            for k in range(1, p.chips):
                total = total + self.buf(unit, 7)[2 * k + part, rows, :].astype(F32)
            self.buf(unit, 8)[part, rows, :] = total.astype(grad.dtype)

    def sum_first(self, unit, grad):
        p = self.place
        _, b = self.turn(unit)
        inner = self.inner(unit)
        for slot in (1, 0):
            self.first(unit, slot).wait_recv()
            outer = self.outer(unit, p.stream ^ b if slot else p.stream)
            for span in range(self.count(unit)):
                self.buf(unit, 1)[(slot, span) + inner] = (
                    grad[(span,) + outer].astype(F32)
                    + self.buf(unit, 0)[(slot, span) + inner].astype(F32)
                ).astype(grad.dtype)
            if slot:
                self.second(unit).start()

    def add_second(self, unit):
        p = self.place
        if self.chips_first(unit):
            self.sum_first(unit, self.buf(unit, 8))
            return
        inner = self.inner(unit)
        self.second(unit).wait_recv()
        for span in range(p.spans):
            self.buf(unit, 3)[(span,) + inner] = (
                self.buf(unit, 1)[(0, span) + inner].astype(F32)
                + self.buf(unit, 2)[(span,) + inner].astype(F32)
            ).astype(self.buf(unit, 3).dtype)
        for k in range(1, p.chips):
            self.third(unit, k).start()

    def add_third(self, unit):
        p = self.place
        inner = self.inner(unit)
        kind = self.buf(unit, 5).dtype
        if self.chips_first(unit):
            self.second(unit).wait_recv()
        else:
            for k in range(1, p.chips):
                self.third(unit, k).wait_recv()
        for mine in (False, True):
            core = p.core if mine else 1 - p.core
            if self.chips_first(unit):
                total = self.buf(unit, 1)[(0, core) + inner].astype(F32)
                total = total + self.buf(unit, 2)[(core,) + inner].astype(F32)
            else:
                total = self.buf(unit, 3)[(2 * p.chip + core,) + inner].astype(F32)
                for k in range(1, p.chips):
                    total = total + self.buf(unit, 4)[(2 * k + core,) + inner].astype(F32)
            if mine:
                self.buf(unit, 6)[(0, p.core) + inner] = total.astype(kind)
            else:
                self.buf(unit, 5)[inner] = total.astype(kind)
                self.swap(unit).start()

    def spread(self, unit):
        self.swap(unit).wait_recv()
        for step in range(1, self.place.streams):
            self.fourth(unit, step).start()

    def finish(self, unit):
        p = self.place
        for step in range(p.streams):
            if step:
                self.fourth(unit, step).wait_recv()
            row, col = self.outer(unit, p.stream ^ step)
            for part in range(2):
                out, start, stride = self.targets[self.units[unit][0]][part]
                col_at = pl.ds(pl.multiple_of(start + stride * col.start, 128), col.size)
                out[row, col_at] = self.buf(unit, 6)[(step, part) + self.inner(unit)]
        self.swap(unit).wait_send()
        for slot in range(2):
            self.first(unit, slot).wait_send()
        self.second(unit).wait_send()
        for k in range(1, p.chips):
            self.third(unit, k).wait_send()
        for step in range(1, p.streams):
            self.fourth(unit, step).wait_send()

    def steps(self):
        count = len(self.units)
        ahead = REDUCE_AHEAD
        steps = [functools.partial(self.begin, u) for u in range(min(ahead, count))]
        lags = (
            (0, self.add_first), (3, self.add_second), (6, self.add_third), (7, self.spread),
            (10, self.finish),
        )
        for t in range(count + 10):
            for lag, act in lags:
                if 0 <= t - lag < count:
                    steps.append(functools.partial(act, t - lag))
                if lag == 0 and t + ahead < count:
                    steps.append(functools.partial(self.begin, t + ahead))
        return steps


def split_columns(out, width):
    return [(out, 0, 1), (out, width, 1)]


def reduce_kernel(streams, spans, *refs):
    grads, outs, rest = refs[:5], refs[5:8], refs[8:]
    half = grads[0].shape[2]
    targets = [split_columns(outs[0], half)]
    targets += [
        [(outs[1], 2 * i * half, 2), (outs[1], 2 * i * half + 128, 2)] for i in range(3)
    ]
    targets += [split_columns(outs[2], grads[4].shape[2])]
    bufs = [rest[9 * w : 9 * w + 9] for w in range(5)]
    work = Reduce(Place(streams, spans), grads, targets, bufs, rest[45:], 0.3)
    greet(work.neighbours())
    for step in work.steps():
        step()


def reduce_call(grads, collective_id):
    streams, spans = lax.axis_size("stream"), lax.axis_size("span")
    shapes = [grad.shape for grad in grads]
    vmem = pl.BlockSpec(memory_space=pltpu.VMEM)
    rows, width = shapes[0][1:]
    small_rows, small_width = shapes[4][1:]
    return pl.pallas_call(
        functools.partial(reduce_kernel, streams, spans),
        in_specs=[vmem] * len(grads),
        out_specs=[vmem] * 3,
        out_shape=[
            jax.ShapeDtypeStruct((rows, 2 * width), BF16),
            jax.ShapeDtypeStruct((rows, 6 * width), BF16),
            jax.ShapeDtypeStruct((small_rows, 2 * small_width), F32),
        ],
        scratch_shapes=Reduce.scratch(shapes, [g.dtype for g in grads], streams),
        compiler_params=pltpu.CompilerParams(
            collective_id=collective_id, has_side_effects=True, vmem_limit_bytes=VMEM_LIMIT
        ),
        name="reduce_grads",
    )(*grads)


def chain_body(p, backward, source, maps, state_ref, scratch):
    p_low, p_high, p_chip = maps
    swap, carry, outgo, sent = scratch[:4]
    swap_sem, hop_sem, back_sem = scratch[-3:]
    s_chip = None if backward else scratch[4]
    heads, size = source.shape[0], source.shape[2]
    half = heads // 2
    mine = p.core * half
    theirs = (1 - p.core) * half
    ahead, behind = (-1, 1) if backward else (1, -1)
    edge_in = p.chips - 1 if backward else 0
    edge_out = 0 if backward else p.chips - 1
    swap_copy = copy_to(
        source.at[pl.ds(theirs, half)], swap, swap_sem.at[0], swap_sem.at[1], p.other()
    )
    swap_copy.start()
    swap_copy.wait_recv()
    low_core = p.core == 0
    for h in range(half):
        own, got = source[mine + h], swap[h]
        low = jnp.where(low_core, own, got)
        high = jnp.where(low_core, got, own)
        if backward:
            outgo[h] = low.astype(F32) + nt(high, p_low[h])
        else:
            joined = nn(low, high[size:])
            s_chip[h] = joined[:size] + high[:size].astype(F32)
            p_chip[h] = joined[size:].astype(BF16)
            p_low[h] = low[size:]
            p_high[h] = high[size:]
            outgo[h] = low[:size].astype(F32)

    def hop(h):
        return copy_to(
            sent.at[h], carry.at[h], hop_sem.at[h, 0], hop_sem.at[h, 1], p.along(ahead)
        )

    @pl.when(p.chip == edge_in)
    def _():
        carry[...] = jnp.zeros(carry.shape, BF16)

    for h in range(half):

        @pl.when(p.chip != edge_in)
        def _():
            hop(h).wait_recv()

        moved = nt(carry[h], p_chip[h]) + outgo[h] if backward else nn(carry[h], p_chip[h]) + s_chip[h]
        sent[h] = moved.astype(BF16)

        @pl.when(p.chip != edge_out)
        def _():
            hop(h).start()

    for h in range(half):
        state = carry[h]
        if backward:
            low_state = (nt(state, p_high[h]) + jnp.where(low_core, swap[h], source[mine + h]).astype(F32)).astype(BF16)
            keep = jnp.where(low_core, low_state, state)
            give = jnp.where(low_core, state, low_state)
        else:
            high_state = (nn(state, p_low[h]) + outgo[h]).astype(BF16)
            keep = jnp.where(low_core, state, high_state)
            give = jnp.where(low_core, high_state, state)
        state_ref[mine + h] = keep
        sent[half + h] = give
    back = copy_to(
        sent.at[pl.ds(half, half)], state_ref.at[pl.ds(mine, half)],
        back_sem.at[0], back_sem.at[1], p.other(),
    )
    back.start()
    copy_to(
        sent.at[pl.ds(half, half)], state_ref.at[pl.ds(theirs, half)],
        back_sem.at[0], back_sem.at[1], p.other(),
    ).wait_recv()
    back.wait_send()
    swap_copy.wait_send()

    @pl.when(p.chip != edge_out)
    def _():
        for h in range(half):
            hop(h).wait_send()


def chain_scratch(heads, size, rows, backward):
    half = heads // 2
    dma = pltpu.SemaphoreType.DMA
    scratch = [
        pltpu.VMEM((half, rows, size), BF16),
        pltpu.VMEM((half, size, size), BF16),
        pltpu.VMEM((half, size, size), F32),
        pltpu.VMEM((heads, size, size), BF16),
    ]
    if not backward:
        scratch.append(pltpu.VMEM((half, size, size), F32))
    return scratch + [dma((2,)), dma((half, 2)), dma((2,))]


def readout_body(readout, gain):
    inv = lax.rsqrt(jnp.mean(readout * readout, -1, keepdims=True) + EPSILON)
    return (readout * inv * gain).astype(BF16)


def spread_steps(steps, first, slots, index):
    if index == 0:
        return steps[:first]
    rest = steps[first:]
    count = len(rest)
    return rest[count * (index - 1) // slots : count * index // slots]


def forward_kernel(streams, spans, heads, weights, *refs):
    ins, refs = refs[:11], refs[11:]
    shards, refs = refs[:weights], refs[weights:]
    outs, refs = refs[:15], refs[15:]
    fulls, refs = refs[:weights], refs[weights:]
    gather_sems, refs = refs[:3], refs[3:]
    map_buf, read_buf, rmap_buf, state_buf = refs[:4]
    chain_bufs = refs[4:]
    gain_ref = ins[10]
    (ext_ref, q_ref, k_ref, v_ref, inv_ref, wk_ref, pre_ref, nv_ref, np_ref,
     state_ref, p_low, p_high, p_chip, out_ref, normal_ref) = outs
    step_id = pl.program_id(0)
    place = Place(streams, spans)
    work = Gather(place, shards, fulls, gather_sems)
    steps = work.steps()

    @pl.when(step_id == 0)
    def _():
        greet(work.neighbours())

    for index in range(heads + 1):

        @pl.when(step_id == index)
        def _():
            for step in spread_steps(steps, GATHER_AHEAD, FORWARD_SLOTS, index):
                step()

    @pl.when(step_id < heads)
    def _():
        local_kernel(
            *ins[:10], ext_ref, q_ref, k_ref, v_ref, inv_ref, wk_ref, pre_ref, map_buf.at[pl.ds(step_id, 1)],
            read_buf.at[step_id], rmap_buf.at[step_id], nv_ref, np_ref,
        )

    @pl.when(step_id == heads)
    def _():
        chain_body(
            place, False, map_buf, (p_low, p_high, p_chip), state_buf, chain_bufs,
        )
        state_ref[...] = state_buf[...]
        size = gain_ref.shape[1]
        for h in range(heads):
            cols = slice(h * size, (h + 1) * size)
            readout = read_buf[h] + nt(rmap_buf[h], state_buf[h])
            out_ref[:, cols] = readout
            normal_ref[:, cols] = readout_body(readout, gain_ref[...])
        for index in range(heads + 1, 20):
            for step in spread_steps(steps, GATHER_AHEAD, FORWARD_SLOTS, index):
                step()


def forward_call(
    keep, normed, w_qkv, conv, rate, allow, gain, shards, heads, collective_id
):
    streams, spans = lax.axis_size("stream"), lax.axis_size("span")
    tok = rate.shape[0]
    rows, width = normed.shape
    size = width // heads
    count = tok // STRETCH
    taps = conv.shape[0]
    half = heads // 2
    hbm = pl.BlockSpec(memory_space=pl.ANY)

    def at(i):
        return jnp.minimum(i, heads - 1)

    def third(i, r):
        return pl.BlockSpec((r, size), lambda h: (0, at(h) + i * heads))

    def token_block():
        return pl.BlockSpec((tok, size), lambda h: (0, at(h)))

    def whole(*shape):
        return pl.BlockSpec(shape, lambda h: (0,) * len(shape))

    token_shape = jax.ShapeDtypeStruct((tok, width), BF16)
    square = jax.ShapeDtypeStruct((half, size, size), BF16)
    shapes = [s.shape for s in shards]
    outs = pl.pallas_call(
        functools.partial(forward_kernel, streams, spans, heads, len(shards)),
        grid=(heads + 1,),
        in_specs=[
            pl.BlockSpec(memory_space=pltpu.SMEM),
            whole(rows, width),
            third(0, width), third(1, width), third(2, width),
            third(0, taps), third(1, taps), third(2, taps),
            whole(tok, heads), whole(tok, taps), whole(1, size),
        ]
        + [pl.BlockSpec(memory_space=pltpu.VMEM)] * len(shards),
        out_specs=[
            pl.BlockSpec((3, rows, size), lambda h: (0, 0, at(h))),
            token_block(), token_block(), token_block(),
            pl.BlockSpec((1, tok, STRETCH), lambda h: (at(h), 0, 0)),
            token_block(),
            pl.BlockSpec((1, count, 2 * size, size), lambda h: (at(h), 0, 0, 0)),
            token_block(), token_block(),
            whole(heads, size, size),
            whole(half, size, size), whole(half, size, size), whole(half, size, size),
            whole(tok, width), whole(tok, width),
        ]
        + [hbm] * len(shards),
        out_shape=[
            jax.ShapeDtypeStruct((3, rows, width), BF16),
            token_shape, token_shape, token_shape,
            jax.ShapeDtypeStruct((heads, tok, STRETCH), BF16),
            token_shape,
            jax.ShapeDtypeStruct((heads, count, 2 * size, size), BF16),
            token_shape, token_shape,
            jax.ShapeDtypeStruct((heads, size, size), BF16),
            square, square, square,
            jax.ShapeDtypeStruct((tok, width), F32),
            token_shape,
        ]
        + [jax.ShapeDtypeStruct((spans,) + s.shape, s.dtype) for s in shards],
        scratch_shapes=Gather.sem_shapes(shapes, streams, spans)
        + [
            pltpu.VMEM((heads, 2 * size, size), BF16),
            pltpu.VMEM((heads, tok, size), F32),
            pltpu.VMEM((heads, tok, size), BF16),
            pltpu.VMEM((heads, size, size), BF16),
        ]
        + chain_scratch(heads, size, 2 * size, False),
        compiler_params=pltpu.CompilerParams(
            collective_id=collective_id, has_side_effects=True, vmem_limit_bytes=VMEM_LIMIT
        ),
        name="delta_forward",
    )(keep, normed, w_qkv, w_qkv, w_qkv, conv, conv, conv, rate, allow, gain, *shards)
    return outs[:15], outs[15:]


def backward_kernel(streams, spans, heads, weights, *refs):
    (keep_ref, gn_ref, read_ref, gain_ref, q_ref, k_ref, v_ref, wk_ref, inv_ref, min_ref, pre_ref,
     nv_ref, np_ref, rate_ref, allow_ref, eq_ref, ek_ref, ev_ref, cq_ref, ck_ref, cv_ref,
     p_low, p_high, p_chip, pair_ref, wq_ref, wkey_ref, wv_ref, heads_ref, attn_ref) = refs[:30]
    refs = refs[30:]
    grads, refs = refs[:weights], refs[weights:]
    gconv_ref, grate_ref, gain_grad_ref, gnormed_ref = refs[:4]
    halves, edge_ref, out_grad_ref, sums, refs = refs[4:7], refs[7], refs[8], refs[9:12], refs[12:]
    bufs, refs = [refs[9 * w : 9 * w + 9] for w in range(weights)], refs[9 * weights :]
    reduce_sems, refs = refs[:3], refs[3:]
    go_buf, adj_buf, din_buf = refs[:3]
    pair_buf, own_buf, got_buf, pair_sem = refs[3:7]
    edge_buf, edge_got, attn_give, attn_got, edge_sem = refs[7:12]
    row_bufs, chain_bufs = refs[12:15], refs[15:]
    step_id = pl.program_id(0)
    turns = heads // GROUP
    place = Place(streams, spans)
    targets = [
        split_columns(sums[0], grads[0].shape[2]),
        [(sums[1], 0, 1), (sums[2], 0, 1)],
    ]
    work = Reduce(place, grads, targets, bufs, reduce_sems, 0.2)
    steps = work.steps()
    slots = BACKWARD_SLOTS
    size = gain_ref.shape[1]

    def hand_over(turn):
        return copy_to(
            own_buf.at[GROUP * turn + 1 - place.core], got_buf.at[turn],
            pair_sem.at[turn, 0], pair_sem.at[turn, 1], place.other(),
        )

    def weigh(turn):
        hand_over(turn).wait_recv()
        both = jnp.concatenate([own_buf[GROUP * turn + place.core], got_buf[turn]], 0)
        grad = nn(pair_buf[...], both).astype(BF16)
        lanes = pl.ds(pl.multiple_of(turn * size, size), size)
        for i in range(3):
            rows = halves[i].shape[1]
            halves[i][:, :, lanes] = grad[:, lanes_of(i, size)].reshape(-1, rows, size)
        hand_over(turn).wait_send()

    half = attn_got.shape[1]

    def columns(core):
        return attn_ref[:, pl.ds(pl.multiple_of(core * half, half), half)]

    attn_copy = copy_to(attn_give, attn_got, edge_sem.at[0], edge_sem.at[1], place.other())
    edge_copy = copy_to(edge_buf, edge_got, edge_sem.at[2], edge_sem.at[3], place.span_at(-1))

    @pl.when(step_id == 0)
    def _():
        greet(work.neighbours() + place.either_side())
        attn_give[...] = columns(1 - place.core)
        attn_copy.start()
        pair_buf[...] = pair_ref[...].T

    @pl.when(step_id == 1)
    def _():
        attn_copy.wait()
        both = jnp.concatenate([columns(place.core), attn_got[...]], 0)
        out_grad_ref[...] = tn(heads_ref[...], both).astype(BF16).reshape(out_grad_ref.shape)

    for index in range(2 * turns + 1):

        @pl.when(step_id == index)
        def _():
            for step in spread_steps(steps, REDUCE_AHEAD, slots, index):
                step()

    @pl.when(step_id < turns)
    def _():
        adjoint_body(
            keep_ref, gn_ref, read_ref, gain_ref, q_ref, k_ref, wk_ref,
            go_buf.at[step_id], adj_buf.at[pl.ds(GROUP * step_id, GROUP)], gain_grad_ref,
        )

    @pl.when(step_id == turns)
    def _():
        chain_body(place, True, adj_buf, (p_low, p_high, p_chip), din_buf, chain_bufs)

    @pl.when(step_id > turns + 1)
    def _():
        weigh(step_id - turns - 2)

    @pl.when(step_id > turns)
    def _():
        turn = step_id - turns - 1
        pair = pl.ds(GROUP * turn, GROUP)
        own = own_buf.at[pair]
        backward_body(
            turn, keep_ref, din_buf.at[pair], min_ref, pre_ref, go_buf.at[turn],
            q_ref, k_ref, v_ref, inv_ref, wk_ref, nv_ref, np_ref, rate_ref, allow_ref,
            eq_ref, ek_ref, ev_ref, cq_ref, ck_ref, cv_ref,
            own, gconv_ref, grate_ref, *row_bufs,
        )
        hand_over(turn).start()
        part = None
        for i, weight in enumerate((wq_ref, wkey_ref, wv_ref)):
            grad = jnp.concatenate([own[g, :, lanes_of(i, size)] for g in range(GROUP)], 1)
            term = nt(grad, weight[...])
            part = term if part is None else part + term
        before = jnp.where(turn == 0, jnp.zeros_like(part), gnormed_ref[...])
        gnormed_ref[...] = before + part

    @pl.when(step_id == 2 * turns)
    def _():
        edge_buf[...] = gnormed_ref[:HALO, :].astype(BF16)
        edge_copy.start()
        weigh(turns - 1)
        for index in range(2 * turns + 1, slots + 1):
            for step in spread_steps(steps, REDUCE_AHEAD, slots, index):
                step()
        edge_copy.wait()
        edge_ref[...] = edge_got[...]


def backward_call(
    keep, grad_normal, readout, gain, queries, keys, values, wkeys, invs, state, prefix,
    new_v, new_p, rate, allow, ext, conv, maps, pair_normed, w_qkv,
    pair_heads, grad_attn, grads, heads, collective_id,
):
    streams, spans = lax.axis_size("stream"), lax.axis_size("span")
    tok, width = queries.shape
    size = width // heads
    count = tok // STRETCH
    taps = conv.shape[0]
    rows = ext.shape[1]
    half = heads // 2

    turns = heads // GROUP
    wide = GROUP * size

    def first(i):
        return jnp.minimum(i, turns - 1)

    def second(i):
        return jnp.maximum(i - turns - 1, 0)

    def both(i):
        return jnp.where(i < turns, i, second(i))

    def block(at):
        return pl.BlockSpec((tok, wide), lambda h: (0, at(h)))

    def third(i, r):
        return pl.BlockSpec((r, wide), lambda h: (0, second(h) + i * turns))

    def part(i):
        return pl.BlockSpec((1, rows, wide), lambda h: (i, 0, second(h)))

    def whole(*shape):
        return pl.BlockSpec(shape, lambda h: (0,) * len(shape))

    vmem = pl.BlockSpec(memory_space=pltpu.VMEM)
    shapes = [g.shape for g in grads]
    outs = pl.pallas_call(
        functools.partial(backward_kernel, streams, spans, heads, len(grads)),
        grid=(2 * turns + 1,),
        in_specs=[
            pl.BlockSpec(memory_space=pltpu.SMEM),
            block(first), block(first), whole(1, size),
            block(both), block(both), block(second), block(both),
            pl.BlockSpec((GROUP, tok, STRETCH), lambda h: (second(h), 0, 0)),
            pl.BlockSpec((GROUP, size, size), lambda h: (second(h), 0, 0)),
            pl.BlockSpec((GROUP, count, 2 * size, size), lambda h: (second(h), 0, 0, 0)),
            block(second), block(second),
            whole(tok, heads), whole(tok, taps),
            part(0), part(1), part(2),
            third(0, taps), third(1, taps), third(2, taps),
            whole(half, size, size), whole(half, size, size), whole(half, size, size),
            vmem, third(0, width), third(1, width), third(2, width), vmem, vmem,
        ]
        + [vmem] * len(grads),
        out_specs=[
            pl.BlockSpec((3, taps, wide), lambda h: (0, 0, second(h))),
            whole(tok, heads),
            pl.BlockSpec((GROUP, 1, size), lambda h: (first(h), 0, 0)),
            whole(rows, width),
        ]
        + [vmem] * 8,
        out_shape=[
            jax.ShapeDtypeStruct((3, taps, width), F32),
            jax.ShapeDtypeStruct((tok, heads), F32),
            jax.ShapeDtypeStruct((heads, 1, size), F32),
            jax.ShapeDtypeStruct((rows, width), F32),
        ]
        + [jax.ShapeDtypeStruct((spans, width // spans, width // 2), BF16)] * 3
        + [
            jax.ShapeDtypeStruct((HALO, width), BF16),
            jax.ShapeDtypeStruct((spans, width // spans, width // 2), BF16),
        ]
        + [
            jax.ShapeDtypeStruct((shapes[0][1], 2 * shapes[0][2]), BF16),
            jax.ShapeDtypeStruct(shapes[1][1:], BF16),
            jax.ShapeDtypeStruct(shapes[1][1:], BF16),
        ],
        scratch_shapes=Reduce.scratch(shapes, [g.dtype for g in grads], streams)
        + [
            pltpu.VMEM((turns, tok, wide), BF16),
            pltpu.VMEM((heads, size, size), BF16),
            pltpu.VMEM((heads, size, size), BF16),
            pltpu.VMEM((width, 2 * rows), BF16),
            pltpu.VMEM((heads, rows, 3 * size), BF16),
            pltpu.VMEM((turns, rows, 3 * size), BF16),
            pltpu.SemaphoreType.DMA((turns, 2)),
            pltpu.VMEM((HALO, width), BF16),
            pltpu.VMEM((HALO, width), BF16),
            pltpu.VMEM((tok, width // 2), BF16),
            pltpu.VMEM((tok, width // 2), BF16),
            pltpu.SemaphoreType.DMA((4,)),
        ]
        + [pltpu.VMEM((tok, wide), F32)] * 3
        + chain_scratch(heads, size, size, True),
        compiler_params=pltpu.CompilerParams(
            collective_id=collective_id, has_side_effects=True, vmem_limit_bytes=VMEM_LIMIT
        ),
        name="delta_backward",
    )(
        keep, grad_normal, readout, gain, queries, keys, values, wkeys, invs, state, prefix,
        new_v, new_p, rate, allow, ext, ext, ext, conv, conv, conv, *maps, pair_normed,
        w_qkv, w_qkv, w_qkv, pair_heads, grad_attn, *grads,
    )
    return outs[:4], outs[4:9], outs[9:]


def feed_kernel(
    streams, spans,
    heads_ref, tok_ref, cot_ref, out_w_ref, gain_ref, gate_ref, up_ref, down_ref,
    result_ref, gmid_ref, gattn_ref, gnormal_ref, ggain_ref, ffn_grad_ref, down_grad_ref,
    mid_buf, grad_buf, res_buf, normed_buf, turned_buf, cot_buf, hid_buf, mine_buf, give_buf,
    hid_got, mine_got, row_sem, unit_sem,
):
    step_id = pl.program_id(0)
    last = pl.num_programs(0) - 1
    place = Place(streams, spans)
    width = cot_ref.shape[1]
    half = width // 2
    tok = cot_ref.shape[0]

    def exchange(source, target, sems):
        return copy_to(source, target, sems.at[0], sems.at[1], place.other())

    def rows(which):
        buf = normed_buf if which == 0 else cot_buf
        return exchange(buf.at[0 if which == 0 else 2], buf.at[1], row_sem.at[which])

    def units(step, which):
        source, target = (hid_buf, hid_got) if which == 0 else (give_buf, mine_got)
        return exchange(source.at[step], target.at[step], unit_sem.at[step, which])

    @pl.when(step_id == 0)
    def _():
        greet([place.other()])
        for own in range(2):
            which = place.core if own else 1 - place.core
            lanes = pl.ds(pl.multiple_of(which * half, half), half)
            cot_buf[0 if own else 2] = cot_ref[:, lanes]
        rows(1).start()
        middle = tok_ref[...].astype(F32) + nn(heads_ref[...], out_w_ref[...])
        inv = lax.rsqrt(jnp.mean(middle * middle, -1, keepdims=True) + EPSILON)
        mid_buf[...] = middle
        normed_buf[0] = (middle * inv * gain_ref[...]).astype(BF16)
        rows(0).start()
        grad_buf[...] = jnp.zeros(grad_buf.shape, F32)
        res_buf[...] = middle

    @pl.when(step_id == 1)
    def _():
        rows(0).wait_recv()
        rows(1).wait_recv()
        turned_buf[:, :tok] = normed_buf[0].T
        turned_buf[:, tok:] = normed_buf[1].T

    @pl.when(step_id < last)
    def _():
        normed = normed_buf[0]
        gate_w, up_w, down_w = gate_ref[...], up_ref[...], down_ref[...]
        gate = nn(normed, gate_w)
        up = nn(normed, up_w)
        grad_hidden = nt(cot_ref[...], down_w)
        sig = jax.nn.sigmoid(gate)
        act = gate * sig
        hidden = (act * up).astype(BF16)
        grad_gate = (grad_hidden * up * (sig * (1.0 + gate * (1.0 - sig)))).astype(BF16)
        grad_up = (grad_hidden * act).astype(BF16)
        low = place.core == 0
        hid_buf[step_id] = hidden
        mine_buf[step_id] = jnp.where(low, grad_gate, grad_up)
        give_buf[step_id] = jnp.where(low, grad_up, grad_gate)
        units(step_id, 0).start()
        units(step_id, 1).start()
        grad_buf[...] += nt(grad_gate, gate_w) + nt(grad_up, up_w)
        res_buf[...] += nn(hidden, down_w)

    @pl.when(step_id == last)
    def _():
        result_ref[...] = res_buf[...].astype(BF16)
        middle, grad = mid_buf[...], grad_buf[...]
        inv = lax.rsqrt(jnp.mean(middle * middle, -1, keepdims=True) + EPSILON)
        ggain_ref[...] = jnp.sum(grad * middle * inv, 0, keepdims=True)
        scaled = grad * gain_ref[...]
        total = cot_ref[...].astype(F32) + inv * scaled - middle * (inv * inv * inv) * jnp.mean(
            scaled * middle, -1, keepdims=True
        )
        gmid_ref[...] = total
        low_total = total.astype(BF16)
        gattn_ref[...] = low_total
        gnormal_ref[...] = nt(low_total, out_w_ref[...])

    @pl.when(step_id > 0)
    def _():
        before = step_id - 1
        units(before, 0).wait_recv()
        units(before, 1).wait_recv()
        mine = jnp.concatenate([mine_buf[before], mine_got[before]], 0)
        grad = nn(turned_buf[...], mine).astype(BF16)
        ffn_grad_ref[...] = grad.reshape(ffn_grad_ref.shape)
        both = jnp.concatenate([hid_buf[before], hid_got[before]], 0)
        cot = jnp.concatenate([cot_buf[0], cot_buf[1]], 0)
        down_grad_ref[...] = tn(both, cot).astype(BF16)

    @pl.when(step_id == last)
    def _():
        for which in range(2):
            rows(which).wait_send()
            for step in range(hid_buf.shape[0]):
                units(step, which).wait_send()


def feed_call(normal_heads, tokens, cotangent, w_out, gain, w_gate, w_up, w_down, collective_id):
    streams, spans = lax.axis_size("stream"), lax.axis_size("span")
    tok, width = tokens.shape
    units = w_gate.shape[1]
    step = 256
    count = units // step
    dma = pltpu.SemaphoreType.DMA

    def now(f):
        return jnp.minimum(f, count - 1)

    def before(f):
        return jnp.maximum(f - 1, 0)

    def whole(*shape):
        return pl.BlockSpec(shape, lambda f: (0,) * len(shape))

    rows = whole(tok, width)
    square = pltpu.VMEM((count, tok, step), BF16)
    return pl.pallas_call(
        functools.partial(feed_kernel, streams, spans),
        grid=(count + 1,),
        in_specs=[
            rows, rows, rows, whole(width, width), whole(1, width),
            pl.BlockSpec((width, step), lambda f: (0, now(f))),
            pl.BlockSpec((width, step), lambda f: (0, now(f))),
            pl.BlockSpec((step, width), lambda f: (now(f), 0)),
        ],
        out_specs=[
            rows, rows, rows, rows, whole(1, width),
            pl.BlockSpec((spans, width // spans, step), lambda f: (0, 0, before(f))),
            pl.BlockSpec((step, width // 2), lambda f: (before(f), 0)),
        ],
        out_shape=[
            jax.ShapeDtypeStruct((tok, width), BF16),
            jax.ShapeDtypeStruct((tok, width), F32),
            jax.ShapeDtypeStruct((tok, width), BF16),
            jax.ShapeDtypeStruct((tok, width), F32),
            jax.ShapeDtypeStruct((1, width), F32),
            jax.ShapeDtypeStruct((spans, width // spans, units), BF16),
            jax.ShapeDtypeStruct((units, width // 2), BF16),
        ],
        scratch_shapes=[pltpu.VMEM((tok, width), F32)] * 3
        + [
            pltpu.VMEM((2, tok, width), BF16),
            pltpu.VMEM((width, 2 * tok), BF16),
            pltpu.VMEM((3, tok, width // 2), BF16),
            square, square, square, square, square,
            dma((2, 2)), dma((count, 2, 2)),
        ],
        compiler_params=pltpu.CompilerParams(
            collective_id=collective_id, has_side_effects=True, vmem_limit_bytes=VMEM_LIMIT
        ),
        name="feed_forward",
    )(normal_heads, tokens, cotangent, w_out, gain, w_gate, w_up, w_down)


def local(
    tokens, cotangent, doc_stretches, w_qkv, conv_weight, w_beta, beta_bias, norm_attn, norm_head,
    w_out, norm_ffn, w_gate, w_up, w_down,
):
    tok_rows, model_width = tokens.shape[1:]
    heads = beta_bias.shape[0]
    size = model_width // heads
    count = tok_rows // STRETCH
    span_count = lax.axis_size("span")
    place = lax.axis_index("span")
    taps = conv_weight.shape[0]

    small = jnp.concatenate(
        [x.reshape(-1) for x in (conv_weight, w_beta, norm_attn, norm_ffn, norm_head)]
    )
    small_len = small.shape[0]
    small = jnp.pad(small, (0, 16 * 512 - small_len)).reshape(16, 512)
    full_qkv, smalls, before = gather_call([w_qkv, small], tokens[0], 1)
    full_qkv = full_qkv.reshape(-1, full_qkv.shape[2])
    smalls = smalls.reshape(span_count, -1)

    def small_part(shape, start):
        length = 1
        for dim in shape:
            length *= dim
        return smalls[:, start : start + length].reshape((span_count,) + shape), start + length

    at = 0
    full_conv, at = small_part(conv_weight.shape, at)
    full_beta, at = small_part(w_beta.shape, at)
    gain_attn, at = small_part(norm_attn.shape, at)
    gain_ffn, at = small_part(norm_ffn.shape, at)
    gain_head, at = small_part(norm_head.shape, at)
    full_conv = jnp.swapaxes(full_conv, 0, 1).reshape(taps, -1)
    full_beta = full_beta.reshape(-1, heads)
    attn_gain = gain_attn.reshape(-1).astype(F32)
    ffn_gain = gain_ffn.reshape(-1).astype(F32)
    head_gain = gain_head.reshape(1, -1).astype(F32)

    stretch_ids = place * count + jnp.arange(count, dtype=jnp.int32)
    doc_lengths = doc_stretches[0]
    doc_begins = jnp.cumsum(doc_lengths) - doc_lengths
    stretch_start = jnp.any(stretch_ids[:, None] == doc_begins[None, :], axis=1).astype(F32)
    stretch_keep = 1.0 - stretch_start
    token_start = jnp.repeat(stretch_start, STRETCH)
    token_offset = jnp.arange(tok_rows, dtype=jnp.int32) % STRETCH
    allow = jnp.stack(
        [1.0 - token_start * (token_offset < tap).astype(F32) for tap in range(taps)], 1
    )

    inputs_ext = jnp.concatenate([before, tokens[0]], 0).astype(F32)
    inv_ext = lax.rsqrt(jnp.mean(inputs_ext * inputs_ext, -1, keepdims=True) + EPSILON)
    normed_ext = (inputs_ext * inv_ext * attn_gain).astype(BF16)
    inputs_f, inv_first, normed = inputs_ext[HALO:], inv_ext[HALO:], normed_ext[HALO:]
    strength = jax.nn.sigmoid(
        jnp.dot(normed, full_beta, preferred_element_type=F32) + beta_bias
    )
    (
        projected, queries, keys, values, invs, wkeys, prefix, new_v, new_p,
        state_in, p_low, p_high, p_chip, readout, normal_heads,
    ), rest = forward_call(
        stretch_keep, normed_ext, full_qkv, full_conv, strength, allow, head_gain,
        [w_out, w_gate, w_up, w_down], heads, 2,
    )
    full_out, full_gate, full_up, full_down = (w.reshape(-1, w.shape[2]) for w in rest)

    (
        result, grad_middle, grad_attn_in, grad_normal, grad_norm_ffn, half_ffn, half_down
    ) = feed_call(
        normal_heads, tokens[0], cotangent[0], full_out, ffn_gain[None], full_gate, full_up,
        full_down, 3,
    )
    half_down = half_down.reshape(span_count, -1, half_down.shape[1])
    (
        (grad_conv, grad_strength, head_grads, grad_normed_ext),
        (half_q, half_k, half_v, halo_back, half_out),
        ffn_parts,
    ) = backward_call(
        stretch_keep, grad_normal, readout, head_gain, queries, keys, values, wkeys, invs,
        state_in, prefix, new_v, new_p, strength, allow, projected, full_conv,
        (p_low, p_high, p_chip), pair_tokens(normed_ext), full_qkv, pair_tokens(normal_heads),
        grad_attn_in, [half_down, half_ffn], heads, 4,
    )
    grad_logit = grad_strength * strength * (1.0 - strength)
    grad_logit_low = grad_logit.astype(BF16)
    grad_w_beta = product("td,th->dh", normed, grad_logit_low)
    grad_normed = (
        grad_normed_ext[HALO:]
        + product("th,dh->td", grad_logit_low, full_beta)
        + jnp.pad(halo_back.astype(F32), ((tok_rows - HALO, 0), (0, 0)))
    )
    grad_norm_attn = jnp.sum(grad_normed * inputs_f * inv_first, 0)
    grad_tokens = grad_middle + norm_back(grad_normed, inputs_f, inv_first, attn_gain)

    def by_span(array):
        return array.reshape(span_count, -1)

    grad_conv = jnp.swapaxes(grad_conv, 0, 1).reshape(taps, span_count, -1)
    packed = jnp.concatenate(
        [
            by_span(jnp.swapaxes(grad_conv, 0, 1)),
            by_span(grad_w_beta),
            by_span(grad_norm_attn),
            by_span(grad_norm_ffn),
            by_span(jnp.sum(head_grads, (0, 1))),
            jnp.broadcast_to(jnp.sum(grad_logit, 0)[None], (span_count, heads)),
        ],
        1,
    )
    packed = jnp.pad(packed, ((0, 0), (0, 16 * 1024 - packed.shape[1])))
    packed = packed.reshape(span_count, 16, 2, 512)
    core = place % 2
    half_small = lax.dynamic_index_in_dim(packed, core, 2, keepdims=False) + swap_core(
        lax.dynamic_index_in_dim(packed, 1 - core, 2, keepdims=False)
    )
    parts = reduce_call([half_out, half_q, half_k, half_v, half_small], 5)
    part_down, part_gate, part_up = (x.astype(F32) for x in ffn_parts)
    part_out, part_qkv = parts[0].astype(F32), parts[1].astype(F32)
    part_small = parts[2].reshape(-1)
    sums = []
    at = 0
    for like in (conv_weight, w_beta, norm_attn, norm_ffn, norm_head, beta_bias):
        sums.append(part_small[at : at + like.size].reshape(like.shape))
        at += like.size

    return (
        result[None],
        grad_tokens[None],
        part_qkv,
        sums[0],
        sums[1],
        sums[5],
        sums[2],
        sums[4],
        part_out,
        sums[3],
        part_gate,
        part_up,
        part_down,
    )


def solution(mesh):
    in_specs = (
        P("stream", "span", None),
        P("stream", "span", None),
        P("stream", None),
        P("span", None),
        P(None, "span"),
        P("span", None),
        P(),
        P("span"),
        P("span"),
        P("span", None),
        P("span"),
        P("span", None),
        P("span", None),
        P("span", None),
    )
    out_specs = (
        P("stream", "span", None),
        P("stream", "span", None),
        P("span", None),
        P(None, "span"),
        P("span", None),
        P(),
        P("span"),
        P("span"),
        P("span", None),
        P("span"),
        P("span", None),
        P("span", None),
        P("span", None),
    )
    return jax.shard_map(local, mesh=mesh, in_specs=in_specs, out_specs=out_specs, check_vma=False)
```

```python
import functools

import jax
import jax.numpy as jnp
from jax import lax
from jax.experimental import pallas as pl
from jax.experimental.pallas import tpu as pltpu
from jax.sharding import PartitionSpec as P

STRETCH = 64
HALO = 16
GROUP = 2
EPSILON = 1e-06
F32 = jnp.float32
BF16 = jnp.bfloat16
AXES = ("stream", "span")
VMEM_LIMIT = 60 * 2**20
GATHER_PIECE = 24 * 1024
GATHER_AHEAD = 3
GATHER_LAG = 2
REDUCE_PIECE = 100 * 1024
REDUCE_AHEAD = 6
FORWARD_SLOTS = 10
BACKWARD_SLOTS = 11


def nn(a, b):
    return lax.dot_general(a, b, (((1,), (0,)), ((), ())), preferred_element_type=F32)


def nt(a, b):
    return lax.dot_general(a, b, (((1,), (1,)), ((), ())), preferred_element_type=F32)


def tn(a, b):
    return lax.dot_general(a, b, (((0,), (0,)), ((), ())), preferred_element_type=F32)


def fine(a, b):
    a_hi = a.astype(BF16)
    a_lo = (a - a_hi.astype(F32)).astype(BF16)
    b_hi = b.astype(BF16)
    b_lo = (b - b_hi.astype(F32)).astype(BF16)
    return nn(jnp.concatenate([a_hi, a_hi, a_lo], 1), jnp.concatenate([b_hi, b_lo, b_hi], 0))


def grid_ids(size):
    return (
        lax.broadcasted_iota(jnp.int32, (size, size), 0),
        lax.broadcasted_iota(jnp.int32, (size, size), 1),
    )


def unit_inverse(lower_list):
    rows, cols = grid_ids(STRETCH)
    eye = (rows == cols).astype(F32)
    out = [eye - jnp.where((rows // 2) == (cols // 2), low, 0.0) for low in lower_list]
    half = 2
    while half < STRETCH:
        cross = ((rows // (2 * half)) == (cols // (2 * half))) & ((rows // half) != (cols // half))
        inner = [fine(jnp.where(cross, low, 0.0), inv) for low, inv in zip(lower_list, out)]
        out = [inv - fine(inv, mid) for inv, mid in zip(out, inner)]
        half *= 2
    return out


def column_of(table, index):
    lanes = lax.broadcasted_iota(jnp.int32, table.shape, 1)
    return jnp.sum(jnp.where(lanes == index, table, 0.0), -1, keepdims=True)


def mix_rows(ext, conv_ref, allow):
    ext = ext.astype(F32)
    conv = conv_ref.astype(F32)
    shifted = [
        (ext if tap == 0 else pltpu.roll(ext, tap, 0))[HALO:] * allow[tap]
        for tap in range(conv.shape[0])
    ]
    mixed = sum(conv[tap : tap + 1] * shifted[tap] for tap in range(conv.shape[0]))
    return shifted, mixed, conv


def local_kernel(
    keep_ref, normed_ref, wq_ref, wkey_ref, wv_ref, cq_ref, ck_ref, cv_ref, rate_ref, allow_ref,
    ext_ref, q_ref, k_ref, v_ref, inv_ref, wk_ref, pre_ref, end_ref, read_ref, rmap_ref, nv_ref, np_ref,
):
    head = pl.program_id(0)
    allow_all = allow_ref[...]
    allow = [allow_all[:, tap : tap + 1] for tap in range(cq_ref.shape[0])]
    rate = column_of(rate_ref[...], head)

    normed = normed_ref[...]

    def activation(index, weight_ref, conv_ref):
        ext = nn(normed, weight_ref[...]).astype(BF16)
        ext_ref[index] = ext
        _, mixed, _ = mix_rows(ext, conv_ref[...], allow)
        return mixed * jax.nn.sigmoid(mixed)

    act_q = activation(0, wq_ref, cq_ref)
    act_k = activation(1, wkey_ref, ck_ref)
    act_v = activation(2, wv_ref, cv_ref)
    queries = (act_q * lax.rsqrt(jnp.sum(act_q * act_q, -1, keepdims=True) + EPSILON)).astype(BF16)
    keys = (act_k * lax.rsqrt(jnp.sum(act_k * act_k, -1, keepdims=True) + EPSILON)).astype(BF16)
    values = act_v.astype(BF16)
    q_ref[...] = queries
    k_ref[...] = keys
    v_ref[...] = values
    count = queries.shape[0] // STRETCH
    rows, cols = grid_ids(STRETCH)
    parts = [slice(n * STRETCH, (n + 1) * STRETCH) for n in range(count)]
    lows = []
    for part in parts:
        gram = nt(keys[part], keys[part])
        lows.append(jnp.where(rows > cols, gram * rate[part], 0.0))
    invs = unit_inverse(lows)
    size = keys.shape[1]
    drows, dcols = grid_ids(size)
    running = jnp.concatenate(
        [jnp.zeros((size, size), F32), (drows == dcols).astype(F32)], 0
    )
    for n, part in enumerate(parts):
        key, query = keys[part], queries[part]
        inv = invs[n].astype(BF16)
        inv_ref[0, part, :] = inv
        scaled = jnp.concatenate(
            [key.astype(F32) * rate[part], values[part].astype(F32) * rate[part]], 1
        ).astype(BF16)
        weighted = nn(inv, scaled)
        wkey = weighted[:, :size].astype(BF16)
        wk_ref[part, :] = wkey
        running = running * keep_ref[n]
        low_state = running.astype(BF16)
        pre_ref[0, n] = low_state
        back = nt(jnp.concatenate([wkey, query], 0), low_state)
        new = jnp.concatenate(
            [weighted[:, size:] - back[:STRETCH, :size], -back[:STRETCH, size:]], 1
        ).astype(BF16)
        nv_ref[part, :] = new[:, :size]
        np_ref[part, :] = new[:, size:]
        scores = jnp.where(rows >= cols, nt(query, key), 0.0).astype(BF16)
        out = back[STRETCH:] + nn(scores, new)
        read_ref[part, :] = out[:, :size]
        rmap_ref[part, :] = out[:, size:].astype(BF16)
        running = running + tn(new, key)
    end_ref[0] = running.astype(BF16)


def lanes_of(index, size):
    return slice(index * size, (index + 1) * size)


def adjoint_body(
    keep_ref, gn_ref, read_ref, gain_ref, q_ref, k_ref, wk_ref, go_ref, adj_ref, gain_grad_ref
):
    size = gain_ref.shape[1]
    tok = gn_ref.shape[0]
    grads = []
    for g in range(GROUP):
        grad, readout = gn_ref[:, lanes_of(g, size)], read_ref[:, lanes_of(g, size)]
        inv = lax.rsqrt(jnp.mean(readout * readout, -1, keepdims=True) + EPSILON)
        scaled = grad * gain_ref[...]
        grad_read = inv * scaled - readout * (inv * inv * inv) * jnp.mean(
            scaled * readout, -1, keepdims=True
        )
        gain_grad_ref[g] = jnp.sum(grad * readout * inv, 0, keepdims=True)
        grads.append(grad_read.astype(BF16))
        go_ref[:, lanes_of(g, size)] = grads[g]
    rows, cols = grid_ids(STRETCH)
    adj = [jnp.zeros((size, size), F32)] * GROUP
    for n in range(tok // STRETCH - 1, -1, -1):
        part = slice(n * STRETCH, (n + 1) * STRETCH)
        for g in range(GROUP):
            lanes = lanes_of(g, size)
            key, query, out = k_ref[part, lanes], q_ref[part, lanes], grads[g][part]
            scores = jnp.where(rows >= cols, nt(query, key), 0.0).astype(BF16)
            new_grad = tn(scores, out) + nt(key, adj[g].astype(BF16))
            adj[g] = (
                adj[g]
                + tn(
                    jnp.concatenate([out, (-new_grad).astype(BF16)], 0),
                    jnp.concatenate([query, wk_ref[part, lanes]], 0),
                )
            ) * keep_ref[n]
    for g in range(GROUP):
        adj_ref[g] = adj[g].astype(BF16)


def backward_body(
    turn, keep_ref, din_ref, min_ref, pre_ref, go_ref, q_ref, k_ref, v_ref, inv_ref, wk_ref,
    nv_ref, np_ref, rate_ref, allow_ref,
    eq_ref, ek_ref, ev_ref, cq_ref, ck_ref, cv_ref,
    gext_ref, gconv_ref, grate_ref,
    gq_buf, gk_buf, gv_buf,
):
    size = min_ref.shape[1]
    tok = q_ref.shape[0]
    count = tok // STRETCH
    rows, cols = grid_ids(STRETCH)
    rates = [column_of(rate_ref[...], GROUP * turn + g) for g in range(GROUP)]
    low_in = [min_ref[g] for g in range(GROUP)]
    adj = [din_ref[g].astype(F32) for g in range(GROUP)]
    grate_parts = [[None] * count for _ in range(GROUP)]
    for n in range(count - 1, -1, -1):
        part = slice(n * STRETCH, (n + 1) * STRETCH)
        for g in range(GROUP):
            lanes = lanes_of(g, size)
            key, query, value = k_ref[part, lanes], q_ref[part, lanes], v_ref[part, lanes]
            out = go_ref[part, lanes]
            beta = rates[g][part]
            pre = pre_ref[g, n]
            state = (nn(low_in[g], pre[size:]) + pre[:size].astype(F32)).astype(BF16)
            new = (nt(np_ref[part, lanes], low_in[g]) + nv_ref[part, lanes].astype(F32)).astype(BF16)
            low_adj = adj[g].astype(BF16)
            gram_both = nt(jnp.concatenate([key, query], 0), key)
            gram = gram_both[:STRETCH]
            scores = jnp.where(rows >= cols, gram_both[STRETCH:], 0.0).astype(BF16)
            new_grad = tn(scores, out) + nt(key, low_adj)
            low_new_grad = new_grad.astype(BF16)
            adj[g] = (
                adj[g]
                + tn(
                    jnp.concatenate([out, -low_new_grad], 0),
                    jnp.concatenate([query, wk_ref[part, lanes]], 0),
                )
            ) * keep_ref[n]
            grad_b = tn(inv_ref[g, part, :], low_new_grad)
            both = nt(jnp.concatenate([out, grad_b.astype(BF16)], 0), new)
            grad_scores = jnp.where(rows >= cols, both[:STRETCH], 0.0).astype(BF16)
            grad_low = jnp.where(rows > cols, -both[STRETCH:], 0.0)
            left = value.astype(F32) - nt(key, state)
            grate_parts[g][n] = jnp.sum(grad_low * gram, -1, keepdims=True) + jnp.sum(
                grad_b * left, -1, keepdims=True
            )
            grad_v = beta * grad_b
            grad_gram = beta * grad_low
            symmetric = (grad_gram + grad_gram.T).astype(BF16)
            by_state = nn(jnp.concatenate([out, -grad_v.astype(BF16)], 0), state)
            gq_buf[part, lanes] = by_state[:STRETCH] + nn(grad_scores, key)
            gk_buf[part, lanes] = (
                by_state[STRETCH:]
                + tn(grad_scores, query)
                + nn(jnp.concatenate([new, symmetric], 1), jnp.concatenate([low_adj, key], 0))
            )
            gv_buf[part, lanes] = grad_v
    heads_at = lax.broadcasted_iota(jnp.int32, grate_ref.shape, 1)
    grate = jnp.where(turn == 0, jnp.zeros(grate_ref.shape, F32), grate_ref[...])
    for g in range(GROUP):
        grate = jnp.where(
            heads_at == GROUP * turn + g, jnp.concatenate(grate_parts[g], 0), grate
        )
    grate_ref[...] = grate
    allow_all = allow_ref[...]
    allow = [allow_all[:, tap : tap + 1] for tap in range(cq_ref.shape[0])]
    zeros = jnp.zeros((HALO, size), F32)
    for i, (ext, conv_ref, buf) in enumerate(
        ((eq_ref, cq_ref, gq_buf), (ek_ref, ck_ref, gk_buf), (ev_ref, cv_ref, gv_buf))
    ):
        for g in range(GROUP):
            lanes = lanes_of(g, size)
            shifted, mixed, conv = mix_rows(ext[0, :, lanes], conv_ref[:, lanes], allow)
            sig = jax.nn.sigmoid(mixed)
            grad = buf[:, lanes]
            if i < 2:
                raw = mixed * sig
                inv = lax.rsqrt(jnp.sum(raw * raw, -1, keepdims=True) + EPSILON)
                grad = inv * grad - raw * (inv * inv * inv) * jnp.sum(grad * raw, -1, keepdims=True)
            grad = grad * (sig * (1.0 + mixed * (1.0 - sig)))
            total = None
            for tap in range(conv.shape[0]):
                gconv_ref[i, tap : tap + 1, lanes] = jnp.sum(grad * shifted[tap], 0, keepdims=True)
                term = jnp.concatenate([zeros, grad * (conv[tap : tap + 1] * allow[tap])], 0)
                if tap:
                    term = pltpu.roll(term, tok + HALO - tap, 0)
                total = term if total is None else total + term
            gext_ref[g, :, lanes_of(i, size)] = total.astype(BF16)


def norm_back(grad_in, values, inv_rms, gain_vec):
    scaled = grad_in * gain_vec
    return inv_rms * scaled - values * inv_rms**3 * jnp.mean(scaled * values, -1, keepdims=True)


def product(pattern, first, second, kind=F32):
    return jnp.einsum(pattern, first, second, preferred_element_type=F32).astype(kind)


def swap_core(block):
    streams, spans = lax.axis_size("stream"), lax.axis_size("span")
    pairs = [
        (s * spans + p, s * spans + (p ^ 1)) for s in range(streams) for p in range(spans)
    ]
    return lax.ppermute(block, AXES, pairs)


def pair_tokens(block):
    return jnp.concatenate([block, swap_core(block)], 0)


def pair_half(block):
    width = block.shape[1] // 2
    core = lax.axis_index("span") % 2
    mine = lax.dynamic_slice_in_dim(block, core * width, width, 1)
    theirs = lax.dynamic_slice_in_dim(block, (1 - core) * width, width, 1)
    return jnp.concatenate([mine, swap_core(theirs)], 0)


def weight_grad(left, right, spans):
    grad = product("td,te->de", left, right, BF16)
    return grad.reshape(spans, -1, grad.shape[1])


MESH = pl.DeviceIdType.MESH


class Place:
    def __init__(self, streams, spans):
        self.streams, self.spans, self.chips = streams, spans, spans // 2
        self.stream = lax.axis_index("stream")
        self.span = lax.axis_index("span")
        self.chip = lax.div(self.span, 2)
        self.core = lax.rem(self.span, 2)

    def beside(self, step):
        return (self.stream ^ step, self.span)

    def along(self, step):
        return (self.stream, 2 * self.shifted(step) + self.core)

    def shifted(self, step):
        return lax.rem(self.chip + step + self.chips, self.chips)

    def other(self):
        return (self.stream, 2 * self.chip + 1 - self.core)

    def span_at(self, step):
        return (self.stream, lax.rem(self.span + step + self.spans, self.spans))

    def either_side(self):
        return [self.span_at(1), self.span_at(-1)]


def greet(places):
    barrier = pltpu.get_barrier_semaphore()
    for target in places:
        pl.semaphore_signal(barrier, inc=1, device_id=target, device_id_type=MESH)
    pl.semaphore_wait(barrier, len(places))


def quarter_of(rows, width, streams):
    if (width // 128) % streams == 0:
        return 1, streams
    return 2, streams // 2


def pieces_of(rows, width, streams, most):
    down, across = quarter_of(rows, width, streams)
    r, c = rows // down, width // across
    best = (1, 1)
    for cut_r in range(1, max(r // 16, 1) + 1):
        for cut_c in range(1, c // 128 + 1):
            if (cut_r > 1 and r % (16 * cut_r)) or c % (128 * cut_c):
                continue
            small = r * c <= most * cut_r * cut_c
            best_small = r * c <= most * best[0] * best[1]
            fewer = (cut_r * cut_c, cut_c) < (best[0] * best[1], best[1])
            if (small and (not best_small or fewer)) or (not best_small and not fewer):
                best = (cut_r, cut_c)
    return best


def units_of(shapes, streams, most):
    units = []
    for w, (rows, width) in enumerate(shapes):
        cut_r, cut_c = pieces_of(rows, width, streams, most)
        units += [(w, i, j, cut_r, cut_c) for i in range(cut_r) for j in range(cut_c)]
    return units


def quarter_index(rows, width, streams, at, unit):
    _, i, j, cut_r, cut_c = unit
    down, across = quarter_of(rows, width, streams)
    r, c = rows // down, width // across
    pr, pc = r // cut_r, c // cut_c
    if down == 1:
        row = pl.ds(i * pr, pr)
    else:
        row = pl.ds(pl.multiple_of(lax.div(at, across) * r + i * pr, pr), pr)
    start = lax.rem(at, across) * c + j * pc
    return row, pl.ds(pl.multiple_of(start, 128), pc)


def copy_to(source, target, send_sem, recv_sem, device):
    return pltpu.make_async_remote_copy(
        src_ref=source, dst_ref=target, send_sem=send_sem, recv_sem=recv_sem,
        device_id=device, device_id_type=MESH,
    )


class Gather:
    def __init__(self, place, shards, fulls, sems):
        self.place, self.shards, self.fulls = place, shards, fulls
        self.sems = sems
        self.units = units_of([x.shape for x in shards], place.streams, GATHER_PIECE)

    @staticmethod
    def sem_shapes(shapes, streams, spans):
        units = len(units_of(shapes, streams, GATHER_PIECE))
        slots = spans // 2
        dma = pltpu.SemaphoreType.DMA
        return [dma((units, slots, 4, 2)), dma((len(shapes), slots, 2)), dma((len(shapes),))]

    def part(self, unit, at, span=None):
        w = self.units[unit][0]
        rows, width = self.shards[w].shape
        index = quarter_index(rows, width, self.place.streams, at, self.units[unit])
        if span is None:
            return self.shards[w].at[index]
        return self.fulls[w].at[(span,) + index]

    def source_span(self, k):
        return 2 * self.place.shifted(-k) + self.place.core

    def wire(self, unit, k, kind, span, at, device, source=None):
        region = self.part(unit, at, span)
        return copy_to(
            region if source is None else source, region,
            self.sems[0].at[unit, k, kind, 0], self.sems[0].at[unit, k, kind, 1], device,
        )

    def along(self, unit, k):
        p = self.place
        return self.wire(
            unit, k, 0, p.span, p.stream, p.along(k), self.part(unit, p.stream)
        )

    def along_wait(self, unit, k):
        p = self.place
        self.wire(unit, k, 0, self.source_span(k), p.stream, p.along(k)).wait_recv()

    def sideways(self, unit, k, step):
        p = self.place
        return self.wire(unit, k, step, self.source_span(k), p.stream, p.beside(step))

    def sideways_wait(self, unit, k, step):
        p = self.place
        self.wire(
            unit, k, step, self.source_span(k), p.stream ^ step, p.beside(step)
        ).wait_recv()

    @staticmethod
    def turns(unit, k):
        return (1, 2) if (unit + k) % 2 == 0 else (2, 1)

    def corner(self, unit, k):
        p = self.place
        first, second = self.turns(unit, k)
        return self.wire(
            unit, k, 3, self.source_span(k), p.stream ^ first, p.beside(second)
        )

    def corner_wait(self, unit, k):
        p = self.place
        self.wire(unit, k, 3, self.source_span(k), p.stream ^ 3, p.beside(1)).wait_recv()

    def across(self, w, k):
        p = self.place
        span = p.span if k == 0 else self.source_span(k)
        region = self.fulls[w].at[span]
        return copy_to(
            self.shards[w] if k == 0 else region, region,
            self.sems[1].at[w, k, 0], self.sems[1].at[w, k, 1], p.other(),
        )

    def across_wait(self, w, k):
        p = self.place
        span = 2 * p.shifted(-k) + 1 - p.core
        region = self.fulls[w].at[span]
        copy_to(
            region, region, self.sems[1].at[w, k, 0], self.sems[1].at[w, k, 1], p.other()
        ).wait_recv()

    def own(self, w):
        return pltpu.make_async_copy(
            self.shards[w], self.fulls[w].at[self.place.span], self.sems[2].at[w]
        )

    def neighbours(self):
        p = self.place
        return (
            [p.along(k) for k in range(1, p.chips)] + [p.beside(1), p.beside(2), p.other()]
        )

    def steps(self):
        p = self.place
        slots = range(1, p.chips)
        count = len(self.units)
        owner = [unit[0] for unit in self.units]
        ends = {u: w for u, w in enumerate(owner) if u + 1 == count or owner[u + 1] != w}
        starts = {u for u, w in enumerate(owner) if u == 0 or owner[u - 1] != w}
        steps = []

        def begin(unit):
            for k in slots:
                self.along(unit, k).start()

        def hand_over(w):
            self.across(w, 0).start()
            self.own(w).start()

        def beside(unit, k):
            self.along_wait(unit, k)
            self.sideways(unit, k, 1).start()
            self.sideways(unit, k, 2).start()

        def turn(unit, k):
            self.sideways_wait(unit, k, self.turns(unit, k)[0])
            self.corner(unit, k).start()

        def close(w, k):
            for unit in range(count):
                if owner[unit] == w:
                    self.sideways_wait(unit, k, self.turns(unit, k)[1])
                    self.corner_wait(unit, k)
            self.across(w, k).start()

        def finish(w):
            for k in range(p.chips):
                self.across_wait(w, k)
                self.across(w, k).wait_send()
            self.own(w).wait()
            for unit in range(count):
                if owner[unit] == w:
                    for k in slots:
                        self.along(unit, k).wait_send()
                        self.sideways(unit, k, 1).wait_send()
                        self.sideways(unit, k, 2).wait_send()
                        self.corner(unit, k).wait_send()

        ahead, lag = GATHER_AHEAD, GATHER_LAG
        for unit in range(min(ahead, count)):
            steps.append(functools.partial(begin, unit))
        for t in range(count + 2 * lag):
            if t < count:
                steps += [functools.partial(beside, t, k) for k in slots]
                if t in starts:
                    steps.append(functools.partial(hand_over, owner[t]))
            if t + ahead < count:
                steps.append(functools.partial(begin, t + ahead))
            if 0 <= t - lag < count:
                steps += [functools.partial(turn, t - lag, k) for k in slots]
            if t - 2 * lag in ends:
                steps += [functools.partial(close, ends[t - 2 * lag], k) for k in slots]
        steps += [functools.partial(finish, w) for w in range(len(self.shards))]
        return steps


def gather_kernel(streams, spans, count, *refs):
    shards, tok_ref, fulls = refs[:count], refs[count], refs[count + 1 : 2 * count + 1]
    halo_ref, sems, halo_sem = refs[2 * count + 1], refs[2 * count + 2 : -1], refs[-1]
    place = Place(streams, spans)
    work = Gather(place, shards, fulls, sems)
    greet(work.neighbours() + place.either_side())
    halo = copy_to(
        tok_ref.at[pl.ds(tok_ref.shape[0] - HALO, HALO)], halo_ref, halo_sem.at[0], halo_sem.at[1],
        place.span_at(1),
    )
    halo.start()
    for step in work.steps():
        step()
    halo.wait()


def gather_call(shards, tokens, collective_id):
    streams, spans = lax.axis_size("stream"), lax.axis_size("span")
    shapes = [shard.shape for shard in shards]
    hbm = pl.BlockSpec(memory_space=pl.ANY)
    return pl.pallas_call(
        functools.partial(gather_kernel, streams, spans, len(shards)),
        in_specs=[pl.BlockSpec(memory_space=pltpu.VMEM)] * len(shards) + [hbm],
        out_specs=[hbm] * (len(shards) + 1),
        out_shape=[jax.ShapeDtypeStruct((spans,) + s.shape, s.dtype) for s in shards]
        + [jax.ShapeDtypeStruct((HALO, tokens.shape[1]), tokens.dtype)],
        scratch_shapes=Gather.sem_shapes(shapes, streams, spans) + [pltpu.SemaphoreType.DMA((2,))],
        compiler_params=pltpu.CompilerParams(
            collective_id=collective_id, has_side_effects=True, vmem_limit_bytes=VMEM_LIMIT
        ),
        name="gather_weights",
    )(*shards, tokens)


class Reduce:
    def __init__(self, place, grads, targets, bufs, sems, share):
        self.place, self.grads, self.bufs, self.sems = place, grads, bufs, sems
        self.targets = targets
        self.units = self.cut([g.shape for g in grads], place.streams)
        self.modes = self.plan(self.units, [g.shape for g in grads], place.streams, share)

    @staticmethod
    def cut(shapes, streams):
        return units_of([s[1:] for s in shapes], streams, REDUCE_PIECE // shapes[0][0])

    @staticmethod
    def plan(units, shapes, streams, share):
        whole = part = 0
        modes = []
        loads = [[0, 0], [0, 0]]
        for w, _, _, cut_r, cut_c in units:
            _, rows, width = shapes[w]
            size = rows * width // (cut_r * cut_c)
            plain = quarter_of(rows, width, streams)[0] == 1 and cut_c == 1 and rows > 16
            whole += size
            first = plain and part + size <= share * whole
            part += size if first else 0
            load = loads[first]
            way = load.index(min(load))
            load[way] += size
            modes.append((first, (1, 2) if way == 0 else (2, 1)))
        return modes

    @staticmethod
    def block(shape, streams):
        _, rows, width = shape
        down, across = quarter_of(rows, width, streams)
        return rows // down, width // across

    @staticmethod
    def scratch(shapes, kinds, streams):
        out = []
        dma = pltpu.SemaphoreType.DMA
        spans = shapes[0][0]
        for shape, kind in zip(shapes, kinds):
            r, c = Reduce.block(shape, streams)
            out += [
                pltpu.VMEM((2, spans, r, c), kind),
                pltpu.VMEM((2, spans, r, c), kind),
                pltpu.VMEM((spans, r, c), kind),
                pltpu.VMEM((spans, r, c), kind),
                pltpu.VMEM((spans, r, c), kind),
                pltpu.VMEM((r, c), kind),
                pltpu.VMEM((streams, 2, r, c), kind),
            ]
            across = quarter_of(*shape[1:], streams)[1]
            out += [
                pltpu.VMEM((spans, r, c * across) if across == streams else (2, 16, 128), kind),
                pltpu.VMEM((2, r, c * across) if across == streams else (2, 16, 128), kind),
            ]
        n = len(Reduce.cut(shapes, streams))
        out += [dma((n, 3, 2)), dma((n, spans // 2, 2)), dma((n, streams, 2))]
        return out

    def turn(self, unit):
        return self.modes[unit][1]

    def chips_first(self, unit):
        return self.modes[unit][0]

    def inner(self, unit):
        w, i, j, cut_r, cut_c = self.units[unit]
        r, c = self.block(self.grads[w].shape, self.place.streams)
        r, c = r // cut_r, c // cut_c
        return pl.ds(i * r, r), pl.ds(j * c, c)

    def outer(self, unit, at):
        _, rows, width = self.grads[self.units[unit][0]].shape
        return quarter_index(rows, width, self.place.streams, at, self.units[unit])

    def buf(self, unit, which):
        return self.bufs[self.units[unit][0]][which]

    def count(self, unit):
        return 2 if self.chips_first(unit) else self.place.spans

    def first(self, unit, slot):
        p = self.place
        a, b = self.turn(unit)
        spans = pl.ds(0, self.count(unit))
        at = p.stream ^ a if slot == 0 else p.stream ^ a ^ b
        source = self.buf(unit, 8) if self.chips_first(unit) else self.grads[self.units[unit][0]]
        return copy_to(
            source.at[(spans,) + self.outer(unit, at)],
            self.buf(unit, 0).at[(slot, spans) + self.inner(unit)],
            self.sems[0].at[unit, slot, 0], self.sems[0].at[unit, slot, 1], p.beside(a),
        )

    def second(self, unit):
        p = self.place
        _, b = self.turn(unit)
        spans = pl.ds(0, self.count(unit))
        return copy_to(
            self.buf(unit, 1).at[(1, spans) + self.inner(unit)],
            self.buf(unit, 2).at[(spans,) + self.inner(unit)],
            self.sems[0].at[unit, 2, 0], self.sems[0].at[unit, 2, 1], p.beside(b),
        )

    def third(self, unit, k):
        p = self.place
        if self.chips_first(unit):
            rows, _ = self.inner(unit)
            return copy_to(
                self.grads[self.units[unit][0]].at[pl.ds(2 * p.shifted(k), 2), rows],
                self.buf(unit, 7).at[pl.ds(2 * k, 2), rows],
                self.sems[1].at[unit, k, 0], self.sems[1].at[unit, k, 1], p.along(k),
            )
        return copy_to(
            self.buf(unit, 3).at[(pl.ds(2 * p.shifted(k), 2),) + self.inner(unit)],
            self.buf(unit, 4).at[(pl.ds(2 * k, 2),) + self.inner(unit)],
            self.sems[1].at[unit, k, 0], self.sems[1].at[unit, k, 1], p.along(k),
        )

    def swap(self, unit):
        p = self.place
        return copy_to(
            self.buf(unit, 5).at[self.inner(unit)],
            self.buf(unit, 6).at[(0, p.core) + self.inner(unit)],
            self.sems[2].at[unit, 0, 0], self.sems[2].at[unit, 0, 1], p.other(),
        )

    def fourth(self, unit, step):
        p = self.place
        return copy_to(
            self.buf(unit, 6).at[(0, pl.ds(0, 2)) + self.inner(unit)],
            self.buf(unit, 6).at[(step, pl.ds(0, 2)) + self.inner(unit)],
            self.sems[2].at[unit, step, 0], self.sems[2].at[unit, step, 1], p.beside(step),
        )

    def neighbours(self):
        p = self.place
        return [p.along(k) for k in range(1, p.chips)] + [
            p.beside(s) for s in range(1, p.streams)
        ] + [p.other()]

    def begin(self, unit):
        if self.chips_first(unit):
            for k in range(1, self.place.chips):
                self.third(unit, k).start()
            return
        for slot in (1, 0):
            self.first(unit, slot).start()

    def add_first(self, unit):
        if self.chips_first(unit):
            self.sum_chips(unit)
            for slot in (1, 0):
                self.first(unit, slot).start()
            return
        self.sum_first(unit, self.grads[self.units[unit][0]])

    def sum_chips(self, unit):
        p = self.place
        grad = self.grads[self.units[unit][0]]
        rows, _ = self.inner(unit)
        for k in range(1, p.chips):
            self.third(unit, k).wait_recv()
        for part in range(2):
            total = grad[2 * p.chip + part, rows, :].astype(F32)
            for k in range(1, p.chips):
                total = total + self.buf(unit, 7)[2 * k + part, rows, :].astype(F32)
            self.buf(unit, 8)[part, rows, :] = total.astype(grad.dtype)

    def sum_first(self, unit, grad):
        p = self.place
        _, b = self.turn(unit)
        inner = self.inner(unit)
        for slot in (1, 0):
            self.first(unit, slot).wait_recv()
            outer = self.outer(unit, p.stream ^ b if slot else p.stream)
            for span in range(self.count(unit)):
                self.buf(unit, 1)[(slot, span) + inner] = (
                    grad[(span,) + outer].astype(F32)
                    + self.buf(unit, 0)[(slot, span) + inner].astype(F32)
                ).astype(grad.dtype)
            if slot:
                self.second(unit).start()

    def add_second(self, unit):
        p = self.place
        if self.chips_first(unit):
            self.sum_first(unit, self.buf(unit, 8))
            return
        inner = self.inner(unit)
        self.second(unit).wait_recv()
        for span in range(p.spans):
            self.buf(unit, 3)[(span,) + inner] = (
                self.buf(unit, 1)[(0, span) + inner].astype(F32)
                + self.buf(unit, 2)[(span,) + inner].astype(F32)
            ).astype(self.buf(unit, 3).dtype)
        for k in range(1, p.chips):
            self.third(unit, k).start()

    def add_third(self, unit):
        p = self.place
        inner = self.inner(unit)
        kind = self.buf(unit, 5).dtype
        if self.chips_first(unit):
            self.second(unit).wait_recv()
        else:
            for k in range(1, p.chips):
                self.third(unit, k).wait_recv()
        for mine in (False, True):
            core = p.core if mine else 1 - p.core
            if self.chips_first(unit):
                total = self.buf(unit, 1)[(0, core) + inner].astype(F32)
                total = total + self.buf(unit, 2)[(core,) + inner].astype(F32)
            else:
                total = self.buf(unit, 3)[(2 * p.chip + core,) + inner].astype(F32)
                for k in range(1, p.chips):
                    total = total + self.buf(unit, 4)[(2 * k + core,) + inner].astype(F32)
            if mine:
                self.buf(unit, 6)[(0, p.core) + inner] = total.astype(kind)
            else:
                self.buf(unit, 5)[inner] = total.astype(kind)
                self.swap(unit).start()

    def spread(self, unit):
        self.swap(unit).wait_recv()
        for step in range(1, self.place.streams):
            self.fourth(unit, step).start()

    def finish(self, unit):
        p = self.place
        for step in range(p.streams):
            if step:
                self.fourth(unit, step).wait_recv()
            row, col = self.outer(unit, p.stream ^ step)
            for part in range(2):
                out, start, stride = self.targets[self.units[unit][0]][part]
                col_at = pl.ds(pl.multiple_of(start + stride * col.start, 128), col.size)
                out[row, col_at] = self.buf(unit, 6)[(step, part) + self.inner(unit)]
        self.swap(unit).wait_send()
        for slot in range(2):
            self.first(unit, slot).wait_send()
        self.second(unit).wait_send()
        for k in range(1, p.chips):
            self.third(unit, k).wait_send()
        for step in range(1, p.streams):
            self.fourth(unit, step).wait_send()

    def steps(self):
        count = len(self.units)
        ahead = REDUCE_AHEAD
        steps = [functools.partial(self.begin, u) for u in range(min(ahead, count))]
        lags = (
            (0, self.add_first), (3, self.add_second), (6, self.add_third), (7, self.spread),
            (10, self.finish),
        )
        for t in range(count + 10):
            for lag, act in lags:
                if 0 <= t - lag < count:
                    steps.append(functools.partial(act, t - lag))
                if lag == 0 and t + ahead < count:
                    steps.append(functools.partial(self.begin, t + ahead))
        return steps


def split_columns(out, width):
    return [(out, 0, 1), (out, width, 1)]


def reduce_kernel(streams, spans, *refs):
    grads, outs, rest = refs[:5], refs[5:8], refs[8:]
    half = grads[0].shape[2]
    targets = [split_columns(outs[0], half)]
    targets += [
        [(outs[1], 2 * i * half, 2), (outs[1], 2 * i * half + 128, 2)] for i in range(3)
    ]
    targets += [split_columns(outs[2], grads[4].shape[2])]
    bufs = [rest[9 * w : 9 * w + 9] for w in range(5)]
    work = Reduce(Place(streams, spans), grads, targets, bufs, rest[45:], 0.3)
    greet(work.neighbours())
    for step in work.steps():
        step()


def reduce_call(grads, collective_id):
    streams, spans = lax.axis_size("stream"), lax.axis_size("span")
    shapes = [grad.shape for grad in grads]
    vmem = pl.BlockSpec(memory_space=pltpu.VMEM)
    rows, width = shapes[0][1:]
    small_rows, small_width = shapes[4][1:]
    return pl.pallas_call(
        functools.partial(reduce_kernel, streams, spans),
        in_specs=[vmem] * len(grads),
        out_specs=[vmem] * 3,
        out_shape=[
            jax.ShapeDtypeStruct((rows, 2 * width), BF16),
            jax.ShapeDtypeStruct((rows, 6 * width), BF16),
            jax.ShapeDtypeStruct((small_rows, 2 * small_width), F32),
        ],
        scratch_shapes=Reduce.scratch(shapes, [g.dtype for g in grads], streams),
        compiler_params=pltpu.CompilerParams(
            collective_id=collective_id, has_side_effects=True, vmem_limit_bytes=VMEM_LIMIT
        ),
        name="reduce_grads",
    )(*grads)


def chain_body(p, backward, source, maps, state_ref, scratch):
    p_low, p_high, p_chip = maps
    swap, carry, outgo, sent = scratch[:4]
    swap_sem, hop_sem, back_sem = scratch[-3:]
    s_chip = None if backward else scratch[4]
    heads, size = source.shape[0], source.shape[2]
    half = heads // 2
    mine = p.core * half
    theirs = (1 - p.core) * half
    ahead, behind = (-1, 1) if backward else (1, -1)
    edge_in = p.chips - 1 if backward else 0
    edge_out = 0 if backward else p.chips - 1
    swap_copy = copy_to(
        source.at[pl.ds(theirs, half)], swap, swap_sem.at[0], swap_sem.at[1], p.other()
    )
    swap_copy.start()
    swap_copy.wait_recv()
    low_core = p.core == 0
    for h in range(half):
        own, got = source[mine + h], swap[h]
        low = jnp.where(low_core, own, got)
        high = jnp.where(low_core, got, own)
        if backward:
            outgo[h] = low.astype(F32) + nt(high, p_low[h])
        else:
            joined = nn(low, high[size:])
            s_chip[h] = joined[:size] + high[:size].astype(F32)
            p_chip[h] = joined[size:].astype(BF16)
            p_low[h] = low[size:]
            p_high[h] = high[size:]
            outgo[h] = low[:size].astype(F32)

    def hop(h):
        return copy_to(
            sent.at[h], carry.at[h], hop_sem.at[h, 0], hop_sem.at[h, 1], p.along(ahead)
        )

    @pl.when(p.chip == edge_in)
    def _():
        carry[...] = jnp.zeros(carry.shape, BF16)

    for h in range(half):

        @pl.when(p.chip != edge_in)
        def _():
            hop(h).wait_recv()

        moved = nt(carry[h], p_chip[h]) + outgo[h] if backward else nn(carry[h], p_chip[h]) + s_chip[h]
        sent[h] = moved.astype(BF16)

        @pl.when(p.chip != edge_out)
        def _():
            hop(h).start()

    for h in range(half):
        state = carry[h]
        if backward:
            low_state = (nt(state, p_high[h]) + jnp.where(low_core, swap[h], source[mine + h]).astype(F32)).astype(BF16)
            keep = jnp.where(low_core, low_state, state)
            give = jnp.where(low_core, state, low_state)
        else:
            high_state = (nn(state, p_low[h]) + outgo[h]).astype(BF16)
            keep = jnp.where(low_core, state, high_state)
            give = jnp.where(low_core, high_state, state)
        state_ref[mine + h] = keep
        sent[half + h] = give
    back = copy_to(
        sent.at[pl.ds(half, half)], state_ref.at[pl.ds(mine, half)],
        back_sem.at[0], back_sem.at[1], p.other(),
    )
    back.start()
    copy_to(
        sent.at[pl.ds(half, half)], state_ref.at[pl.ds(theirs, half)],
        back_sem.at[0], back_sem.at[1], p.other(),
    ).wait_recv()
    back.wait_send()
    swap_copy.wait_send()

    @pl.when(p.chip != edge_out)
    def _():
        for h in range(half):
            hop(h).wait_send()


def chain_scratch(heads, size, rows, backward):
    half = heads // 2
    dma = pltpu.SemaphoreType.DMA
    scratch = [
        pltpu.VMEM((half, rows, size), BF16),
        pltpu.VMEM((half, size, size), BF16),
        pltpu.VMEM((half, size, size), F32),
        pltpu.VMEM((heads, size, size), BF16),
    ]
    if not backward:
        scratch.append(pltpu.VMEM((half, size, size), F32))
    return scratch + [dma((2,)), dma((half, 2)), dma((2,))]


def readout_body(readout, gain):
    inv = lax.rsqrt(jnp.mean(readout * readout, -1, keepdims=True) + EPSILON)
    return (readout * inv * gain).astype(BF16)


def spread_steps(steps, first, slots, index):
    if index == 0:
        return steps[:first]
    rest = steps[first:]
    count = len(rest)
    return rest[count * (index - 1) // slots : count * index // slots]


def forward_kernel(streams, spans, heads, weights, *refs):
    ins, refs = refs[:11], refs[11:]
    shards, refs = refs[:weights], refs[weights:]
    outs, refs = refs[:15], refs[15:]
    fulls, refs = refs[:weights], refs[weights:]
    gather_sems, refs = refs[:3], refs[3:]
    map_buf, read_buf, rmap_buf, state_buf = refs[:4]
    chain_bufs = refs[4:]
    gain_ref = ins[10]
    (ext_ref, q_ref, k_ref, v_ref, inv_ref, wk_ref, pre_ref, nv_ref, np_ref,
     state_ref, p_low, p_high, p_chip, out_ref, normal_ref) = outs
    step_id = pl.program_id(0)
    place = Place(streams, spans)
    work = Gather(place, shards, fulls, gather_sems)
    steps = work.steps()

    @pl.when(step_id == 0)
    def _():
        greet(work.neighbours())

    for index in range(heads + 1):

        @pl.when(step_id == index)
        def _():
            for step in spread_steps(steps, GATHER_AHEAD, FORWARD_SLOTS, index):
                step()

    @pl.when(step_id < heads)
    def _():
        local_kernel(
            *ins[:10], ext_ref, q_ref, k_ref, v_ref, inv_ref, wk_ref, pre_ref, map_buf.at[pl.ds(step_id, 1)],
            read_buf.at[step_id], rmap_buf.at[step_id], nv_ref, np_ref,
        )

    @pl.when(step_id == heads)
    def _():
        chain_body(
            place, False, map_buf, (p_low, p_high, p_chip), state_buf, chain_bufs,
        )
        state_ref[...] = state_buf[...]
        size = gain_ref.shape[1]
        for h in range(heads):
            cols = slice(h * size, (h + 1) * size)
            readout = read_buf[h] + nt(rmap_buf[h], state_buf[h])
            out_ref[:, cols] = readout
            normal_ref[:, cols] = readout_body(readout, gain_ref[...])
        for index in range(heads + 1, 20):
            for step in spread_steps(steps, GATHER_AHEAD, FORWARD_SLOTS, index):
                step()


def forward_call(
    keep, normed, w_qkv, conv, rate, allow, gain, shards, heads, collective_id
):
    streams, spans = lax.axis_size("stream"), lax.axis_size("span")
    tok = rate.shape[0]
    rows, width = normed.shape
    size = width // heads
    count = tok // STRETCH
    taps = conv.shape[0]
    half = heads // 2
    hbm = pl.BlockSpec(memory_space=pl.ANY)

    def at(i):
        return jnp.minimum(i, heads - 1)

    def third(i, r):
        return pl.BlockSpec((r, size), lambda h: (0, at(h) + i * heads))

    def token_block():
        return pl.BlockSpec((tok, size), lambda h: (0, at(h)))

    def whole(*shape):
        return pl.BlockSpec(shape, lambda h: (0,) * len(shape))

    token_shape = jax.ShapeDtypeStruct((tok, width), BF16)
    square = jax.ShapeDtypeStruct((half, size, size), BF16)
    shapes = [s.shape for s in shards]
    outs = pl.pallas_call(
        functools.partial(forward_kernel, streams, spans, heads, len(shards)),
        grid=(heads + 1,),
        in_specs=[
            pl.BlockSpec(memory_space=pltpu.SMEM),
            whole(rows, width),
            third(0, width), third(1, width), third(2, width),
            third(0, taps), third(1, taps), third(2, taps),
            whole(tok, heads), whole(tok, taps), whole(1, size),
        ]
        + [pl.BlockSpec(memory_space=pltpu.VMEM)] * len(shards),
        out_specs=[
            pl.BlockSpec((3, rows, size), lambda h: (0, 0, at(h))),
            token_block(), token_block(), token_block(),
            pl.BlockSpec((1, tok, STRETCH), lambda h: (at(h), 0, 0)),
            token_block(),
            pl.BlockSpec((1, count, 2 * size, size), lambda h: (at(h), 0, 0, 0)),
            token_block(), token_block(),
            whole(heads, size, size),
            whole(half, size, size), whole(half, size, size), whole(half, size, size),
            whole(tok, width), whole(tok, width),
        ]
        + [hbm] * len(shards),
        out_shape=[
            jax.ShapeDtypeStruct((3, rows, width), BF16),
            token_shape, token_shape, token_shape,
            jax.ShapeDtypeStruct((heads, tok, STRETCH), BF16),
            token_shape,
            jax.ShapeDtypeStruct((heads, count, 2 * size, size), BF16),
            token_shape, token_shape,
            jax.ShapeDtypeStruct((heads, size, size), BF16),
            square, square, square,
            jax.ShapeDtypeStruct((tok, width), F32),
            token_shape,
        ]
        + [jax.ShapeDtypeStruct((spans,) + s.shape, s.dtype) for s in shards],
        scratch_shapes=Gather.sem_shapes(shapes, streams, spans)
        + [
            pltpu.VMEM((heads, 2 * size, size), BF16),
            pltpu.VMEM((heads, tok, size), F32),
            pltpu.VMEM((heads, tok, size), BF16),
            pltpu.VMEM((heads, size, size), BF16),
        ]
        + chain_scratch(heads, size, 2 * size, False),
        compiler_params=pltpu.CompilerParams(
            collective_id=collective_id, has_side_effects=True, vmem_limit_bytes=VMEM_LIMIT
        ),
        name="delta_forward",
    )(keep, normed, w_qkv, w_qkv, w_qkv, conv, conv, conv, rate, allow, gain, *shards)
    return outs[:15], outs[15:]


def backward_kernel(streams, spans, heads, weights, *refs):
    (keep_ref, gn_ref, read_ref, gain_ref, q_ref, k_ref, v_ref, wk_ref, inv_ref, min_ref, pre_ref,
     nv_ref, np_ref, rate_ref, allow_ref, eq_ref, ek_ref, ev_ref, cq_ref, ck_ref, cv_ref,
     p_low, p_high, p_chip, pair_ref, wq_ref, wkey_ref, wv_ref, heads_ref, attn_ref) = refs[:30]
    refs = refs[30:]
    grads, refs = refs[:weights], refs[weights:]
    gconv_ref, grate_ref, gain_grad_ref, gnormed_ref = refs[:4]
    halves, edge_ref, out_grad_ref, sums, refs = refs[4:7], refs[7], refs[8], refs[9:12], refs[12:]
    bufs, refs = [refs[9 * w : 9 * w + 9] for w in range(weights)], refs[9 * weights :]
    reduce_sems, refs = refs[:3], refs[3:]
    go_buf, adj_buf, din_buf = refs[:3]
    pair_buf, own_buf, got_buf, pair_sem = refs[3:7]
    edge_buf, edge_got, attn_give, attn_got, edge_sem = refs[7:12]
    row_bufs, chain_bufs = refs[12:15], refs[15:]
    step_id = pl.program_id(0)
    turns = heads // GROUP
    place = Place(streams, spans)
    targets = [
        split_columns(sums[0], grads[0].shape[2]),
        [(sums[1], 0, 1), (sums[2], 0, 1)],
    ]
    work = Reduce(place, grads, targets, bufs, reduce_sems, 0.1)
    steps = work.steps()
    slots = BACKWARD_SLOTS
    size = gain_ref.shape[1]

    def hand_over(turn):
        return copy_to(
            own_buf.at[GROUP * turn + 1 - place.core], got_buf.at[turn],
            pair_sem.at[turn, 0], pair_sem.at[turn, 1], place.other(),
        )

    def weigh(turn):
        hand_over(turn).wait_recv()
        both = jnp.concatenate([own_buf[GROUP * turn + place.core], got_buf[turn]], 0)
        grad = nn(pair_buf[...], both).astype(BF16)
        lanes = pl.ds(pl.multiple_of(turn * size, size), size)
        for i in range(3):
            rows = halves[i].shape[1]
            halves[i][:, :, lanes] = grad[:, lanes_of(i, size)].reshape(-1, rows, size)
        hand_over(turn).wait_send()

    half = attn_got.shape[1]

    def columns(core):
        return attn_ref[:, pl.ds(pl.multiple_of(core * half, half), half)]

    attn_copy = copy_to(attn_give, attn_got, edge_sem.at[0], edge_sem.at[1], place.other())
    edge_copy = copy_to(edge_buf, edge_got, edge_sem.at[2], edge_sem.at[3], place.span_at(-1))

    @pl.when(step_id == 0)
    def _():
        greet(work.neighbours() + place.either_side())
        attn_give[...] = columns(1 - place.core)
        attn_copy.start()
        pair_buf[...] = pair_ref[...].T

    @pl.when(step_id == 1)
    def _():
        attn_copy.wait()
        both = jnp.concatenate([columns(place.core), attn_got[...]], 0)
        out_grad_ref[...] = tn(heads_ref[...], both).astype(BF16).reshape(out_grad_ref.shape)

    for index in range(2 * turns + 1):

        @pl.when(step_id == index)
        def _():
            for step in spread_steps(steps, REDUCE_AHEAD, slots, index):
                step()

    @pl.when(step_id < turns)
    def _():
        adjoint_body(
            keep_ref, gn_ref, read_ref, gain_ref, q_ref, k_ref, wk_ref,
            go_buf.at[step_id], adj_buf.at[pl.ds(GROUP * step_id, GROUP)], gain_grad_ref,
        )

    @pl.when(step_id == turns)
    def _():
        chain_body(place, True, adj_buf, (p_low, p_high, p_chip), din_buf, chain_bufs)

    @pl.when(step_id > turns + 1)
    def _():
        weigh(step_id - turns - 2)

    @pl.when(step_id > turns)
    def _():
        turn = step_id - turns - 1
        pair = pl.ds(GROUP * turn, GROUP)
        own = own_buf.at[pair]
        backward_body(
            turn, keep_ref, din_buf.at[pair], min_ref, pre_ref, go_buf.at[turn],
            q_ref, k_ref, v_ref, inv_ref, wk_ref, nv_ref, np_ref, rate_ref, allow_ref,
            eq_ref, ek_ref, ev_ref, cq_ref, ck_ref, cv_ref,
            own, gconv_ref, grate_ref, *row_bufs,
        )
        hand_over(turn).start()
        part = None
        for i, weight in enumerate((wq_ref, wkey_ref, wv_ref)):
            grad = jnp.concatenate([own[g, :, lanes_of(i, size)] for g in range(GROUP)], 1)
            term = nt(grad, weight[...])
            part = term if part is None else part + term
        before = jnp.where(turn == 0, jnp.zeros_like(part), gnormed_ref[...])
        gnormed_ref[...] = before + part

    @pl.when(step_id == 2 * turns)
    def _():
        edge_buf[...] = gnormed_ref[:HALO, :].astype(BF16)
        edge_copy.start()
        weigh(turns - 1)
        for index in range(2 * turns + 1, slots + 1):
            for step in spread_steps(steps, REDUCE_AHEAD, slots, index):
                step()
        edge_copy.wait()
        edge_ref[...] = edge_got[...]


def backward_call(
    keep, grad_normal, readout, gain, queries, keys, values, wkeys, invs, state, prefix,
    new_v, new_p, rate, allow, ext, conv, maps, pair_normed, w_qkv,
    pair_heads, grad_attn, grads, heads, collective_id,
):
    streams, spans = lax.axis_size("stream"), lax.axis_size("span")
    tok, width = queries.shape
    size = width // heads
    count = tok // STRETCH
    taps = conv.shape[0]
    rows = ext.shape[1]
    half = heads // 2

    turns = heads // GROUP
    wide = GROUP * size

    def first(i):
        return jnp.minimum(i, turns - 1)

    def second(i):
        return jnp.maximum(i - turns - 1, 0)

    def both(i):
        return jnp.where(i < turns, i, second(i))

    def block(at):
        return pl.BlockSpec((tok, wide), lambda h: (0, at(h)))

    def third(i, r):
        return pl.BlockSpec((r, wide), lambda h: (0, second(h) + i * turns))

    def part(i):
        return pl.BlockSpec((1, rows, wide), lambda h: (i, 0, second(h)))

    def whole(*shape):
        return pl.BlockSpec(shape, lambda h: (0,) * len(shape))

    vmem = pl.BlockSpec(memory_space=pltpu.VMEM)
    shapes = [g.shape for g in grads]
    outs = pl.pallas_call(
        functools.partial(backward_kernel, streams, spans, heads, len(grads)),
        grid=(2 * turns + 1,),
        in_specs=[
            pl.BlockSpec(memory_space=pltpu.SMEM),
            block(first), block(first), whole(1, size),
            block(both), block(both), block(second), block(both),
            pl.BlockSpec((GROUP, tok, STRETCH), lambda h: (second(h), 0, 0)),
            pl.BlockSpec((GROUP, size, size), lambda h: (second(h), 0, 0)),
            pl.BlockSpec((GROUP, count, 2 * size, size), lambda h: (second(h), 0, 0, 0)),
            block(second), block(second),
            whole(tok, heads), whole(tok, taps),
            part(0), part(1), part(2),
            third(0, taps), third(1, taps), third(2, taps),
            whole(half, size, size), whole(half, size, size), whole(half, size, size),
            vmem, third(0, width), third(1, width), third(2, width), vmem, vmem,
        ]
        + [vmem] * len(grads),
        out_specs=[
            pl.BlockSpec((3, taps, wide), lambda h: (0, 0, second(h))),
            whole(tok, heads),
            pl.BlockSpec((GROUP, 1, size), lambda h: (first(h), 0, 0)),
            whole(rows, width),
        ]
        + [vmem] * 8,
        out_shape=[
            jax.ShapeDtypeStruct((3, taps, width), F32),
            jax.ShapeDtypeStruct((tok, heads), F32),
            jax.ShapeDtypeStruct((heads, 1, size), F32),
            jax.ShapeDtypeStruct((rows, width), F32),
        ]
        + [jax.ShapeDtypeStruct((spans, width // spans, width // 2), BF16)] * 3
        + [
            jax.ShapeDtypeStruct((HALO, width), BF16),
            jax.ShapeDtypeStruct((spans, width // spans, width // 2), BF16),
        ]
        + [
            jax.ShapeDtypeStruct((shapes[0][1], 2 * shapes[0][2]), BF16),
            jax.ShapeDtypeStruct(shapes[1][1:], BF16),
            jax.ShapeDtypeStruct(shapes[1][1:], BF16),
        ],
        scratch_shapes=Reduce.scratch(shapes, [g.dtype for g in grads], streams)
        + [
            pltpu.VMEM((turns, tok, wide), BF16),
            pltpu.VMEM((heads, size, size), BF16),
            pltpu.VMEM((heads, size, size), BF16),
            pltpu.VMEM((width, 2 * rows), BF16),
            pltpu.VMEM((heads, rows, 3 * size), BF16),
            pltpu.VMEM((turns, rows, 3 * size), BF16),
            pltpu.SemaphoreType.DMA((turns, 2)),
            pltpu.VMEM((HALO, width), BF16),
            pltpu.VMEM((HALO, width), BF16),
            pltpu.VMEM((tok, width // 2), BF16),
            pltpu.VMEM((tok, width // 2), BF16),
            pltpu.SemaphoreType.DMA((4,)),
        ]
        + [pltpu.VMEM((tok, wide), F32)] * 3
        + chain_scratch(heads, size, size, True),
        compiler_params=pltpu.CompilerParams(
            collective_id=collective_id, has_side_effects=True, vmem_limit_bytes=VMEM_LIMIT
        ),
        name="delta_backward",
    )(
        keep, grad_normal, readout, gain, queries, keys, values, wkeys, invs, state, prefix,
        new_v, new_p, rate, allow, ext, ext, ext, conv, conv, conv, *maps, pair_normed,
        w_qkv, w_qkv, w_qkv, pair_heads, grad_attn, *grads,
    )
    return outs[:4], outs[4:9], outs[9:]


def feed_kernel(
    streams, spans,
    heads_ref, tok_ref, cot_ref, out_w_ref, gain_ref, gate_ref, up_ref, down_ref,
    result_ref, gmid_ref, gattn_ref, gnormal_ref, ggain_ref, ffn_grad_ref, down_grad_ref,
    mid_buf, grad_buf, res_buf, normed_buf, turned_buf, cot_buf, hid_buf, mine_buf, give_buf,
    hid_got, mine_got, row_sem, unit_sem,
):
    step_id = pl.program_id(0)
    last = pl.num_programs(0) - 1
    place = Place(streams, spans)
    width = cot_ref.shape[1]
    half = width // 2
    tok = cot_ref.shape[0]

    def exchange(source, target, sems):
        return copy_to(source, target, sems.at[0], sems.at[1], place.other())

    def rows(which):
        buf = normed_buf if which == 0 else cot_buf
        return exchange(buf.at[0 if which == 0 else 2], buf.at[1], row_sem.at[which])

    def units(step, which):
        source, target = (hid_buf, hid_got) if which == 0 else (give_buf, mine_got)
        return exchange(source.at[step], target.at[step], unit_sem.at[step, which])

    @pl.when(step_id == 0)
    def _():
        greet([place.other()])
        for own in range(2):
            which = place.core if own else 1 - place.core
            lanes = pl.ds(pl.multiple_of(which * half, half), half)
            cot_buf[0 if own else 2] = cot_ref[:, lanes]
        rows(1).start()
        middle = tok_ref[...].astype(F32) + nn(heads_ref[...], out_w_ref[...])
        inv = lax.rsqrt(jnp.mean(middle * middle, -1, keepdims=True) + EPSILON)
        mid_buf[...] = middle
        normed_buf[0] = (middle * inv * gain_ref[...]).astype(BF16)
        rows(0).start()
        grad_buf[...] = jnp.zeros(grad_buf.shape, F32)
        res_buf[...] = middle

    @pl.when(step_id == 1)
    def _():
        rows(0).wait_recv()
        rows(1).wait_recv()
        turned_buf[:, :tok] = normed_buf[0].T
        turned_buf[:, tok:] = normed_buf[1].T

    @pl.when(step_id < last)
    def _():
        normed = normed_buf[0]
        gate_w, up_w, down_w = gate_ref[...], up_ref[...], down_ref[...]
        gate = nn(normed, gate_w)
        up = nn(normed, up_w)
        grad_hidden = nt(cot_ref[...], down_w)
        sig = jax.nn.sigmoid(gate)
        act = gate * sig
        hidden = (act * up).astype(BF16)
        grad_gate = (grad_hidden * up * (sig * (1.0 + gate * (1.0 - sig)))).astype(BF16)
        grad_up = (grad_hidden * act).astype(BF16)
        low = place.core == 0
        hid_buf[step_id] = hidden
        mine_buf[step_id] = jnp.where(low, grad_gate, grad_up)
        give_buf[step_id] = jnp.where(low, grad_up, grad_gate)
        units(step_id, 0).start()
        units(step_id, 1).start()
        grad_buf[...] += nt(grad_gate, gate_w) + nt(grad_up, up_w)
        res_buf[...] += nn(hidden, down_w)

    @pl.when(step_id == last)
    def _():
        result_ref[...] = res_buf[...].astype(BF16)
        middle, grad = mid_buf[...], grad_buf[...]
        inv = lax.rsqrt(jnp.mean(middle * middle, -1, keepdims=True) + EPSILON)
        ggain_ref[...] = jnp.sum(grad * middle * inv, 0, keepdims=True)
        scaled = grad * gain_ref[...]
        total = cot_ref[...].astype(F32) + inv * scaled - middle * (inv * inv * inv) * jnp.mean(
            scaled * middle, -1, keepdims=True
        )
        gmid_ref[...] = total
        low_total = total.astype(BF16)
        gattn_ref[...] = low_total
        gnormal_ref[...] = nt(low_total, out_w_ref[...])

    @pl.when(step_id > 0)
    def _():
        before = step_id - 1
        units(before, 0).wait_recv()
        units(before, 1).wait_recv()
        mine = jnp.concatenate([mine_buf[before], mine_got[before]], 0)
        grad = nn(turned_buf[...], mine).astype(BF16)
        ffn_grad_ref[...] = grad.reshape(ffn_grad_ref.shape)
        both = jnp.concatenate([hid_buf[before], hid_got[before]], 0)
        cot = jnp.concatenate([cot_buf[0], cot_buf[1]], 0)
        down_grad_ref[...] = tn(both, cot).astype(BF16)

    @pl.when(step_id == last)
    def _():
        for which in range(2):
            rows(which).wait_send()
            for step in range(hid_buf.shape[0]):
                units(step, which).wait_send()


def feed_call(normal_heads, tokens, cotangent, w_out, gain, w_gate, w_up, w_down, collective_id):
    streams, spans = lax.axis_size("stream"), lax.axis_size("span")
    tok, width = tokens.shape
    units = w_gate.shape[1]
    step = 256
    count = units // step
    dma = pltpu.SemaphoreType.DMA

    def now(f):
        return jnp.minimum(f, count - 1)

    def before(f):
        return jnp.maximum(f - 1, 0)

    def whole(*shape):
        return pl.BlockSpec(shape, lambda f: (0,) * len(shape))

    rows = whole(tok, width)
    square = pltpu.VMEM((count, tok, step), BF16)
    return pl.pallas_call(
        functools.partial(feed_kernel, streams, spans),
        grid=(count + 1,),
        in_specs=[
            rows, rows, rows, whole(width, width), whole(1, width),
            pl.BlockSpec((width, step), lambda f: (0, now(f))),
            pl.BlockSpec((width, step), lambda f: (0, now(f))),
            pl.BlockSpec((step, width), lambda f: (now(f), 0)),
        ],
        out_specs=[
            rows, rows, rows, rows, whole(1, width),
            pl.BlockSpec((spans, width // spans, step), lambda f: (0, 0, before(f))),
            pl.BlockSpec((step, width // 2), lambda f: (before(f), 0)),
        ],
        out_shape=[
            jax.ShapeDtypeStruct((tok, width), BF16),
            jax.ShapeDtypeStruct((tok, width), F32),
            jax.ShapeDtypeStruct((tok, width), BF16),
            jax.ShapeDtypeStruct((tok, width), F32),
            jax.ShapeDtypeStruct((1, width), F32),
            jax.ShapeDtypeStruct((spans, width // spans, units), BF16),
            jax.ShapeDtypeStruct((units, width // 2), BF16),
        ],
        scratch_shapes=[pltpu.VMEM((tok, width), F32)] * 3
        + [
            pltpu.VMEM((2, tok, width), BF16),
            pltpu.VMEM((width, 2 * tok), BF16),
            pltpu.VMEM((3, tok, width // 2), BF16),
            square, square, square, square, square,
            dma((2, 2)), dma((count, 2, 2)),
        ],
        compiler_params=pltpu.CompilerParams(
            collective_id=collective_id, has_side_effects=True, vmem_limit_bytes=VMEM_LIMIT
        ),
        name="feed_forward",
    )(normal_heads, tokens, cotangent, w_out, gain, w_gate, w_up, w_down)


def local(
    tokens, cotangent, doc_stretches, w_qkv, conv_weight, w_beta, beta_bias, norm_attn, norm_head,
    w_out, norm_ffn, w_gate, w_up, w_down,
):
    tok_rows, model_width = tokens.shape[1:]
    heads = beta_bias.shape[0]
    size = model_width // heads
    count = tok_rows // STRETCH
    span_count = lax.axis_size("span")
    place = lax.axis_index("span")
    taps = conv_weight.shape[0]

    small = jnp.concatenate(
        [x.reshape(-1) for x in (conv_weight, w_beta, norm_attn, norm_ffn, norm_head)]
    )
    small_len = small.shape[0]
    small = jnp.pad(small, (0, 16 * 512 - small_len)).reshape(16, 512)
    full_qkv, smalls, before = gather_call([w_qkv, small], tokens[0], 1)
    full_qkv = full_qkv.reshape(-1, full_qkv.shape[2])
    smalls = smalls.reshape(span_count, -1)

    def small_part(shape, start):
        length = 1
        for dim in shape:
            length *= dim
        return smalls[:, start : start + length].reshape((span_count,) + shape), start + length

    at = 0
    full_conv, at = small_part(conv_weight.shape, at)
    full_beta, at = small_part(w_beta.shape, at)
    gain_attn, at = small_part(norm_attn.shape, at)
    gain_ffn, at = small_part(norm_ffn.shape, at)
    gain_head, at = small_part(norm_head.shape, at)
    full_conv = jnp.swapaxes(full_conv, 0, 1).reshape(taps, -1)
    full_beta = full_beta.reshape(-1, heads)
    attn_gain = gain_attn.reshape(-1).astype(F32)
    ffn_gain = gain_ffn.reshape(-1).astype(F32)
    head_gain = gain_head.reshape(1, -1).astype(F32)

    stretch_ids = place * count + jnp.arange(count, dtype=jnp.int32)
    doc_lengths = doc_stretches[0]
    doc_begins = jnp.cumsum(doc_lengths) - doc_lengths
    stretch_start = jnp.any(stretch_ids[:, None] == doc_begins[None, :], axis=1).astype(F32)
    stretch_keep = 1.0 - stretch_start
    token_start = jnp.repeat(stretch_start, STRETCH)
    token_offset = jnp.arange(tok_rows, dtype=jnp.int32) % STRETCH
    allow = jnp.stack(
        [1.0 - token_start * (token_offset < tap).astype(F32) for tap in range(taps)], 1
    )

    inputs_ext = jnp.concatenate([before, tokens[0]], 0).astype(F32)
    inv_ext = lax.rsqrt(jnp.mean(inputs_ext * inputs_ext, -1, keepdims=True) + EPSILON)
    normed_ext = (inputs_ext * inv_ext * attn_gain).astype(BF16)
    inputs_f, inv_first, normed = inputs_ext[HALO:], inv_ext[HALO:], normed_ext[HALO:]
    strength = jax.nn.sigmoid(
        jnp.dot(normed, full_beta, preferred_element_type=F32) + beta_bias
    )
    (
        projected, queries, keys, values, invs, wkeys, prefix, new_v, new_p,
        state_in, p_low, p_high, p_chip, readout, normal_heads,
    ), rest = forward_call(
        stretch_keep, normed_ext, full_qkv, full_conv, strength, allow, head_gain,
        [w_out, w_gate, w_up, w_down], heads, 2,
    )
    full_out, full_gate, full_up, full_down = (w.reshape(-1, w.shape[2]) for w in rest)

    (
        result, grad_middle, grad_attn_in, grad_normal, grad_norm_ffn, half_ffn, half_down
    ) = feed_call(
        normal_heads, tokens[0], cotangent[0], full_out, ffn_gain[None], full_gate, full_up,
        full_down, 3,
    )
    half_down = half_down.reshape(span_count, -1, half_down.shape[1])
    (
        (grad_conv, grad_strength, head_grads, grad_normed_ext),
        (half_q, half_k, half_v, halo_back, half_out),
        ffn_parts,
    ) = backward_call(
        stretch_keep, grad_normal, readout, head_gain, queries, keys, values, wkeys, invs,
        state_in, prefix, new_v, new_p, strength, allow, projected, full_conv,
        (p_low, p_high, p_chip), pair_tokens(normed_ext), full_qkv, pair_tokens(normal_heads),
        grad_attn_in, [half_down, half_ffn], heads, 4,
    )
    grad_logit = grad_strength * strength * (1.0 - strength)
    grad_logit_low = grad_logit.astype(BF16)
    grad_w_beta = product("td,th->dh", normed, grad_logit_low)
    grad_normed = (
        grad_normed_ext[HALO:]
        + product("th,dh->td", grad_logit_low, full_beta)
        + jnp.pad(halo_back.astype(F32), ((tok_rows - HALO, 0), (0, 0)))
    )
    grad_norm_attn = jnp.sum(grad_normed * inputs_f * inv_first, 0)
    grad_tokens = grad_middle + norm_back(grad_normed, inputs_f, inv_first, attn_gain)

    def by_span(array):
        return array.reshape(span_count, -1)

    grad_conv = jnp.swapaxes(grad_conv, 0, 1).reshape(taps, span_count, -1)
    packed = jnp.concatenate(
        [
            by_span(jnp.swapaxes(grad_conv, 0, 1)),
            by_span(grad_w_beta),
            by_span(grad_norm_attn),
            by_span(grad_norm_ffn),
            by_span(jnp.sum(head_grads, (0, 1))),
            jnp.broadcast_to(jnp.sum(grad_logit, 0)[None], (span_count, heads)),
        ],
        1,
    )
    packed = jnp.pad(packed, ((0, 0), (0, 16 * 1024 - packed.shape[1])))
    packed = packed.reshape(span_count, 16, 2, 512)
    core = place % 2
    half_small = lax.dynamic_index_in_dim(packed, core, 2, keepdims=False) + swap_core(
        lax.dynamic_index_in_dim(packed, 1 - core, 2, keepdims=False)
    )
    parts = reduce_call([half_out, half_q, half_k, half_v, half_small], 5)
    part_down, part_gate, part_up = (x.astype(F32) for x in ffn_parts)
    part_out, part_qkv = parts[0].astype(F32), parts[1].astype(F32)
    part_small = parts[2].reshape(-1)
    sums = []
    at = 0
    for like in (conv_weight, w_beta, norm_attn, norm_ffn, norm_head, beta_bias):
        sums.append(part_small[at : at + like.size].reshape(like.shape))
        at += like.size

    return (
        result[None],
        grad_tokens[None],
        part_qkv,
        sums[0],
        sums[1],
        sums[5],
        sums[2],
        sums[4],
        part_out,
        sums[3],
        part_gate,
        part_up,
        part_down,
    )


def solution(mesh):
    in_specs = (
        P("stream", "span", None),
        P("stream", "span", None),
        P("stream", None),
        P("span", None),
        P(None, "span"),
        P("span", None),
        P(),
        P("span"),
        P("span"),
        P("span", None),
        P("span"),
        P("span", None),
        P("span", None),
        P("span", None),
    )
    out_specs = (
        P("stream", "span", None),
        P("stream", "span", None),
        P("span", None),
        P(None, "span"),
        P("span", None),
        P(),
        P("span"),
        P("span"),
        P("span", None),
        P("span"),
        P("span", None),
        P("span", None),
        P("span", None),
    )
    return jax.shard_map(local, mesh=mesh, in_specs=in_specs, out_specs=out_specs, check_vma=False)
```

```python
import functools

import jax
import jax.numpy as jnp
from jax import lax
from jax.experimental import pallas as pl
from jax.experimental.pallas import tpu as pltpu
from jax.sharding import PartitionSpec as P

STRETCH = 64
HALO = 16
GROUP = 2
EPSILON = 1e-06
F32 = jnp.float32
BF16 = jnp.bfloat16
AXES = ("stream", "span")
VMEM_LIMIT = 60 * 2**20
GATHER_PIECE = 24 * 1024
GATHER_AHEAD = 3
GATHER_LAG = 2
REDUCE_PIECE = 100 * 1024
REDUCE_AHEAD = 5
FORWARD_SLOTS = 10
BACKWARD_SLOTS = 13


def nn(a, b):
    return lax.dot_general(a, b, (((1,), (0,)), ((), ())), preferred_element_type=F32)


def nt(a, b):
    return lax.dot_general(a, b, (((1,), (1,)), ((), ())), preferred_element_type=F32)


def tn(a, b):
    return lax.dot_general(a, b, (((0,), (0,)), ((), ())), preferred_element_type=F32)


def fine(a, b):
    a_hi = a.astype(BF16)
    a_lo = (a - a_hi.astype(F32)).astype(BF16)
    b_hi = b.astype(BF16)
    b_lo = (b - b_hi.astype(F32)).astype(BF16)
    return nn(jnp.concatenate([a_hi, a_hi, a_lo], 1), jnp.concatenate([b_hi, b_lo, b_hi], 0))


def grid_ids(size):
    return (
        lax.broadcasted_iota(jnp.int32, (size, size), 0),
        lax.broadcasted_iota(jnp.int32, (size, size), 1),
    )


def unit_inverse(lower_list):
    rows, cols = grid_ids(STRETCH)
    eye = (rows == cols).astype(F32)
    out = [eye - jnp.where((rows // 2) == (cols // 2), low, 0.0) for low in lower_list]
    half = 2
    while half < STRETCH:
        cross = ((rows // (2 * half)) == (cols // (2 * half))) & ((rows // half) != (cols // half))
        inner = [fine(jnp.where(cross, low, 0.0), inv) for low, inv in zip(lower_list, out)]
        out = [inv - fine(inv, mid) for inv, mid in zip(out, inner)]
        half *= 2
    return out


def column_of(table, index):
    lanes = lax.broadcasted_iota(jnp.int32, table.shape, 1)
    return jnp.sum(jnp.where(lanes == index, table, 0.0), -1, keepdims=True)


def mix_rows(ext, conv_ref, allow):
    ext = ext.astype(F32)
    conv = conv_ref.astype(F32)
    shifted = [
        (ext if tap == 0 else pltpu.roll(ext, tap, 0))[HALO:] * allow[tap]
        for tap in range(conv.shape[0])
    ]
    mixed = sum(conv[tap : tap + 1] * shifted[tap] for tap in range(conv.shape[0]))
    return shifted, mixed, conv


def local_kernel(
    keep_ref, normed_ref, wq_ref, wkey_ref, wv_ref, cq_ref, ck_ref, cv_ref, rate_ref, allow_ref,
    ext_ref, q_ref, k_ref, v_ref, inv_ref, wk_ref, pre_ref, end_ref, read_ref, rmap_ref, nv_ref, np_ref,
):
    head = pl.program_id(0)
    allow_all = allow_ref[...]
    allow = [allow_all[:, tap : tap + 1] for tap in range(cq_ref.shape[0])]
    rate = column_of(rate_ref[...], head)

    normed = normed_ref[...]

    def activation(index, weight_ref, conv_ref):
        ext = nn(normed, weight_ref[...]).astype(BF16)
        ext_ref[index] = ext
        _, mixed, _ = mix_rows(ext, conv_ref[...], allow)
        return mixed * jax.nn.sigmoid(mixed)

    act_q = activation(0, wq_ref, cq_ref)
    act_k = activation(1, wkey_ref, ck_ref)
    act_v = activation(2, wv_ref, cv_ref)
    queries = (act_q * lax.rsqrt(jnp.sum(act_q * act_q, -1, keepdims=True) + EPSILON)).astype(BF16)
    keys = (act_k * lax.rsqrt(jnp.sum(act_k * act_k, -1, keepdims=True) + EPSILON)).astype(BF16)
    values = act_v.astype(BF16)
    q_ref[...] = queries
    k_ref[...] = keys
    v_ref[...] = values
    count = queries.shape[0] // STRETCH
    rows, cols = grid_ids(STRETCH)
    parts = [slice(n * STRETCH, (n + 1) * STRETCH) for n in range(count)]
    lows = []
    for part in parts:
        gram = nt(keys[part], keys[part])
        lows.append(jnp.where(rows > cols, gram * rate[part], 0.0))
    invs = unit_inverse(lows)
    size = keys.shape[1]
    drows, dcols = grid_ids(size)
    running = jnp.concatenate(
        [jnp.zeros((size, size), F32), (drows == dcols).astype(F32)], 0
    )
    for n, part in enumerate(parts):
        key, query = keys[part], queries[part]
        inv = invs[n].astype(BF16)
        inv_ref[0, part, :] = inv
        scaled = jnp.concatenate(
            [key.astype(F32) * rate[part], values[part].astype(F32) * rate[part]], 1
        ).astype(BF16)
        weighted = nn(inv, scaled)
        wkey = weighted[:, :size].astype(BF16)
        wk_ref[part, :] = wkey
        running = running * keep_ref[n]
        low_state = running.astype(BF16)
        pre_ref[0, n] = low_state
        back = nt(jnp.concatenate([wkey, query], 0), low_state)
        new = jnp.concatenate(
            [weighted[:, size:] - back[:STRETCH, :size], -back[:STRETCH, size:]], 1
        ).astype(BF16)
        nv_ref[part, :] = new[:, :size]
        np_ref[part, :] = new[:, size:]
        scores = jnp.where(rows >= cols, nt(query, key), 0.0).astype(BF16)
        out = back[STRETCH:] + nn(scores, new)
        read_ref[part, :] = out[:, :size]
        rmap_ref[part, :] = out[:, size:].astype(BF16)
        running = running + tn(new, key)
    end_ref[0] = running.astype(BF16)


def lanes_of(index, size):
    return slice(index * size, (index + 1) * size)


def adjoint_body(
    keep_ref, gn_ref, read_ref, gain_ref, q_ref, k_ref, wk_ref, go_ref, adj_ref, gain_grad_ref
):
    size = gain_ref.shape[1]
    tok = gn_ref.shape[0]
    grads = []
    for g in range(GROUP):
        grad, readout = gn_ref[:, lanes_of(g, size)], read_ref[:, lanes_of(g, size)]
        inv = lax.rsqrt(jnp.mean(readout * readout, -1, keepdims=True) + EPSILON)
        scaled = grad * gain_ref[...]
        grad_read = inv * scaled - readout * (inv * inv * inv) * jnp.mean(
            scaled * readout, -1, keepdims=True
        )
        gain_grad_ref[g] = jnp.sum(grad * readout * inv, 0, keepdims=True)
        grads.append(grad_read.astype(BF16))
        go_ref[:, lanes_of(g, size)] = grads[g]
    rows, cols = grid_ids(STRETCH)
    adj = [jnp.zeros((size, size), F32)] * GROUP
    for n in range(tok // STRETCH - 1, -1, -1):
        part = slice(n * STRETCH, (n + 1) * STRETCH)
        for g in range(GROUP):
            lanes = lanes_of(g, size)
            key, query, out = k_ref[part, lanes], q_ref[part, lanes], grads[g][part]
            scores = jnp.where(rows >= cols, nt(query, key), 0.0).astype(BF16)
            new_grad = tn(scores, out) + nt(key, adj[g].astype(BF16))
            adj[g] = (
                adj[g]
                + tn(
                    jnp.concatenate([out, (-new_grad).astype(BF16)], 0),
                    jnp.concatenate([query, wk_ref[part, lanes]], 0),
                )
            ) * keep_ref[n]
    for g in range(GROUP):
        adj_ref[g] = adj[g].astype(BF16)


def backward_body(
    turn, keep_ref, din_ref, min_ref, pre_ref, go_ref, q_ref, k_ref, v_ref, inv_ref, wk_ref,
    nv_ref, np_ref, rate_ref, allow_ref,
    eq_ref, ek_ref, ev_ref, cq_ref, ck_ref, cv_ref,
    gext_ref, gconv_ref, grate_ref,
    gq_buf, gk_buf, gv_buf,
):
    size = min_ref.shape[1]
    tok = q_ref.shape[0]
    count = tok // STRETCH
    rows, cols = grid_ids(STRETCH)
    rates = [column_of(rate_ref[...], GROUP * turn + g) for g in range(GROUP)]
    low_in = [min_ref[g] for g in range(GROUP)]
    adj = [din_ref[g].astype(F32) for g in range(GROUP)]
    grate_parts = [[None] * count for _ in range(GROUP)]
    for n in range(count - 1, -1, -1):
        part = slice(n * STRETCH, (n + 1) * STRETCH)
        for g in range(GROUP):
            lanes = lanes_of(g, size)
            key, query, value = k_ref[part, lanes], q_ref[part, lanes], v_ref[part, lanes]
            out = go_ref[part, lanes]
            beta = rates[g][part]
            pre = pre_ref[g, n]
            state = (nn(low_in[g], pre[size:]) + pre[:size].astype(F32)).astype(BF16)
            new = (nt(np_ref[part, lanes], low_in[g]) + nv_ref[part, lanes].astype(F32)).astype(BF16)
            low_adj = adj[g].astype(BF16)
            gram_both = nt(jnp.concatenate([key, query], 0), key)
            gram = gram_both[:STRETCH]
            scores = jnp.where(rows >= cols, gram_both[STRETCH:], 0.0).astype(BF16)
            new_grad = tn(scores, out) + nt(key, low_adj)
            low_new_grad = new_grad.astype(BF16)
            adj[g] = (
                adj[g]
                + tn(
                    jnp.concatenate([out, -low_new_grad], 0),
                    jnp.concatenate([query, wk_ref[part, lanes]], 0),
                )
            ) * keep_ref[n]
            grad_b = tn(inv_ref[g, part, :], low_new_grad)
            both = nt(jnp.concatenate([out, grad_b.astype(BF16)], 0), new)
            grad_scores = jnp.where(rows >= cols, both[:STRETCH], 0.0).astype(BF16)
            grad_low = jnp.where(rows > cols, -both[STRETCH:], 0.0)
            left = value.astype(F32) - nt(key, state)
            grate_parts[g][n] = jnp.sum(grad_low * gram, -1, keepdims=True) + jnp.sum(
                grad_b * left, -1, keepdims=True
            )
            grad_v = beta * grad_b
            grad_gram = beta * grad_low
            symmetric = (grad_gram + grad_gram.T).astype(BF16)
            by_state = nn(jnp.concatenate([out, -grad_v.astype(BF16)], 0), state)
            gq_buf[part, lanes] = by_state[:STRETCH] + nn(grad_scores, key)
            gk_buf[part, lanes] = (
                by_state[STRETCH:]
                + tn(grad_scores, query)
                + nn(jnp.concatenate([new, symmetric], 1), jnp.concatenate([low_adj, key], 0))
            )
            gv_buf[part, lanes] = grad_v
    heads_at = lax.broadcasted_iota(jnp.int32, grate_ref.shape, 1)
    grate = jnp.where(turn == 0, jnp.zeros(grate_ref.shape, F32), grate_ref[...])
    for g in range(GROUP):
        grate = jnp.where(
            heads_at == GROUP * turn + g, jnp.concatenate(grate_parts[g], 0), grate
        )
    grate_ref[...] = grate
    allow_all = allow_ref[...]
    allow = [allow_all[:, tap : tap + 1] for tap in range(cq_ref.shape[0])]
    zeros = jnp.zeros((HALO, size), F32)
    for i, (ext, conv_ref, buf) in enumerate(
        ((eq_ref, cq_ref, gq_buf), (ek_ref, ck_ref, gk_buf), (ev_ref, cv_ref, gv_buf))
    ):
        for g in range(GROUP):
            lanes = lanes_of(g, size)
            shifted, mixed, conv = mix_rows(ext[0, :, lanes], conv_ref[:, lanes], allow)
            sig = jax.nn.sigmoid(mixed)
            grad = buf[:, lanes]
            if i < 2:
                raw = mixed * sig
                inv = lax.rsqrt(jnp.sum(raw * raw, -1, keepdims=True) + EPSILON)
                grad = inv * grad - raw * (inv * inv * inv) * jnp.sum(grad * raw, -1, keepdims=True)
            grad = grad * (sig * (1.0 + mixed * (1.0 - sig)))
            total = None
            for tap in range(conv.shape[0]):
                gconv_ref[i, tap : tap + 1, lanes] = jnp.sum(grad * shifted[tap], 0, keepdims=True)
                term = jnp.concatenate([zeros, grad * (conv[tap : tap + 1] * allow[tap])], 0)
                if tap:
                    term = pltpu.roll(term, tok + HALO - tap, 0)
                total = term if total is None else total + term
            gext_ref[g, :, lanes_of(i, size)] = total.astype(BF16)


def norm_back(grad_in, values, inv_rms, gain_vec):
    scaled = grad_in * gain_vec
    return inv_rms * scaled - values * inv_rms**3 * jnp.mean(scaled * values, -1, keepdims=True)


def product(pattern, first, second, kind=F32):
    return jnp.einsum(pattern, first, second, preferred_element_type=F32).astype(kind)


def swap_core(block):
    streams, spans = lax.axis_size("stream"), lax.axis_size("span")
    pairs = [
        (s * spans + p, s * spans + (p ^ 1)) for s in range(streams) for p in range(spans)
    ]
    return lax.ppermute(block, AXES, pairs)


def pair_tokens(block):
    return jnp.concatenate([block, swap_core(block)], 0)


def pair_half(block):
    width = block.shape[1] // 2
    core = lax.axis_index("span") % 2
    mine = lax.dynamic_slice_in_dim(block, core * width, width, 1)
    theirs = lax.dynamic_slice_in_dim(block, (1 - core) * width, width, 1)
    return jnp.concatenate([mine, swap_core(theirs)], 0)


def weight_grad(left, right, spans):
    grad = product("td,te->de", left, right, BF16)
    return grad.reshape(spans, -1, grad.shape[1])


MESH = pl.DeviceIdType.MESH


class Place:
    def __init__(self, streams, spans):
        self.streams, self.spans, self.chips = streams, spans, spans // 2
        self.stream = lax.axis_index("stream")
        self.span = lax.axis_index("span")
        self.chip = lax.div(self.span, 2)
        self.core = lax.rem(self.span, 2)

    def beside(self, step):
        return (self.stream ^ step, self.span)

    def along(self, step):
        return (self.stream, 2 * self.shifted(step) + self.core)

    def shifted(self, step):
        return lax.rem(self.chip + step + self.chips, self.chips)

    def other(self):
        return (self.stream, 2 * self.chip + 1 - self.core)

    def span_at(self, step):
        return (self.stream, lax.rem(self.span + step + self.spans, self.spans))

    def either_side(self):
        return [self.span_at(1), self.span_at(-1)]


def greet(places):
    barrier = pltpu.get_barrier_semaphore()
    for target in places:
        pl.semaphore_signal(barrier, inc=1, device_id=target, device_id_type=MESH)
    pl.semaphore_wait(barrier, len(places))


def quarter_of(rows, width, streams):
    if (width // 128) % streams == 0:
        return 1, streams
    return 2, streams // 2


def pieces_of(rows, width, streams, most):
    down, across = quarter_of(rows, width, streams)
    r, c = rows // down, width // across
    best = (1, 1)
    for cut_r in range(1, max(r // 16, 1) + 1):
        for cut_c in range(1, c // 128 + 1):
            if (cut_r > 1 and r % (16 * cut_r)) or c % (128 * cut_c):
                continue
            small = r * c <= most * cut_r * cut_c
            best_small = r * c <= most * best[0] * best[1]
            fewer = (cut_r * cut_c, cut_c) < (best[0] * best[1], best[1])
            if (small and (not best_small or fewer)) or (not best_small and not fewer):
                best = (cut_r, cut_c)
    return best


def units_of(shapes, streams, most):
    units = []
    for w, (rows, width) in enumerate(shapes):
        cut_r, cut_c = pieces_of(rows, width, streams, most)
        units += [(w, i, j, cut_r, cut_c) for i in range(cut_r) for j in range(cut_c)]
    return units


def quarter_index(rows, width, streams, at, unit):
    _, i, j, cut_r, cut_c = unit
    down, across = quarter_of(rows, width, streams)
    r, c = rows // down, width // across
    pr, pc = r // cut_r, c // cut_c
    if down == 1:
        row = pl.ds(i * pr, pr)
    else:
        row = pl.ds(pl.multiple_of(lax.div(at, across) * r + i * pr, pr), pr)
    start = lax.rem(at, across) * c + j * pc
    return row, pl.ds(pl.multiple_of(start, 128), pc)


def copy_to(source, target, send_sem, recv_sem, device):
    return pltpu.make_async_remote_copy(
        src_ref=source, dst_ref=target, send_sem=send_sem, recv_sem=recv_sem,
        device_id=device, device_id_type=MESH,
    )


class Gather:
    def __init__(self, place, shards, fulls, sems, depth):
        self.depth = depth
        self.place, self.shards, self.fulls = place, shards, fulls
        self.sems = sems
        self.units = units_of([x.shape for x in shards], place.streams, GATHER_PIECE)

    @staticmethod
    def sem_shapes(shapes, streams, spans):
        units = len(units_of(shapes, streams, GATHER_PIECE))
        slots = spans // 2
        dma = pltpu.SemaphoreType.DMA
        return [dma((units, slots, 4, 2)), dma((len(shapes), slots, 2)), dma((len(shapes),))]

    def part(self, unit, at, span=None):
        w = self.units[unit][0]
        rows, width = self.shards[w].shape
        index = quarter_index(rows, width, self.place.streams, at, self.units[unit])
        if span is None:
            return self.shards[w].at[index]
        return self.fulls[w].at[(span,) + index]

    def source_span(self, k):
        return 2 * self.place.shifted(-k) + self.place.core

    def wire(self, unit, k, kind, span, at, device, source=None):
        region = self.part(unit, at, span)
        return copy_to(
            region if source is None else source, region,
            self.sems[0].at[unit, k, kind, 0], self.sems[0].at[unit, k, kind, 1], device,
        )

    def along(self, unit, k):
        p = self.place
        return self.wire(
            unit, k, 0, p.span, p.stream, p.along(k), self.part(unit, p.stream)
        )

    def along_wait(self, unit, k):
        p = self.place
        self.wire(unit, k, 0, self.source_span(k), p.stream, p.along(k)).wait_recv()

    def sideways(self, unit, k, step):
        p = self.place
        return self.wire(unit, k, step, self.source_span(k), p.stream, p.beside(step))

    def sideways_wait(self, unit, k, step):
        p = self.place
        self.wire(
            unit, k, step, self.source_span(k), p.stream ^ step, p.beside(step)
        ).wait_recv()

    @staticmethod
    def turns(unit, k):
        return (1, 2) if (unit + k) % 2 == 0 else (2, 1)

    def corner(self, unit, k):
        p = self.place
        first, second = self.turns(unit, k)
        return self.wire(
            unit, k, 3, self.source_span(k), p.stream ^ first, p.beside(second)
        )

    def corner_wait(self, unit, k):
        p = self.place
        self.wire(unit, k, 3, self.source_span(k), p.stream ^ 3, p.beside(1)).wait_recv()

    def across(self, w, k):
        p = self.place
        span = p.span if k == 0 else self.source_span(k)
        region = self.fulls[w].at[span]
        return copy_to(
            self.shards[w] if k == 0 else region, region,
            self.sems[1].at[w, k, 0], self.sems[1].at[w, k, 1], p.other(),
        )

    def across_wait(self, w, k):
        p = self.place
        span = 2 * p.shifted(-k) + 1 - p.core
        region = self.fulls[w].at[span]
        copy_to(
            region, region, self.sems[1].at[w, k, 0], self.sems[1].at[w, k, 1], p.other()
        ).wait_recv()

    def own(self, w):
        return pltpu.make_async_copy(
            self.shards[w], self.fulls[w].at[self.place.span], self.sems[2].at[w]
        )

    def neighbours(self):
        p = self.place
        return (
            [p.along(k) for k in range(1, p.chips)] + [p.beside(1), p.beside(2), p.other()]
        )

    def steps(self):
        p = self.place
        slots = range(1, p.chips)
        count = len(self.units)
        owner = [unit[0] for unit in self.units]
        ends = {u: w for u, w in enumerate(owner) if u + 1 == count or owner[u + 1] != w}
        starts = {u for u, w in enumerate(owner) if u == 0 or owner[u - 1] != w}
        steps = []

        def begin(unit):
            for k in slots:
                self.along(unit, k).start()

        def hand_over(w):
            self.across(w, 0).start()
            self.own(w).start()

        def beside(unit, k):
            self.along_wait(unit, k)
            self.sideways(unit, k, 1).start()
            self.sideways(unit, k, 2).start()

        def turn(unit, k):
            self.sideways_wait(unit, k, self.turns(unit, k)[0])
            self.corner(unit, k).start()

        def close(w, k):
            for unit in range(count):
                if owner[unit] == w:
                    self.sideways_wait(unit, k, self.turns(unit, k)[1])
                    self.corner_wait(unit, k)
            self.across(w, k).start()

        def finish(w):
            for k in range(p.chips):
                self.across_wait(w, k)
                self.across(w, k).wait_send()
            self.own(w).wait()
            for unit in range(count):
                if owner[unit] == w:
                    for k in slots:
                        self.along(unit, k).wait_send()
                        self.sideways(unit, k, 1).wait_send()
                        self.sideways(unit, k, 2).wait_send()
                        self.corner(unit, k).wait_send()

        ahead, lag = self.depth
        for unit in range(min(ahead, count)):
            steps.append(functools.partial(begin, unit))
        for t in range(count + 2 * lag):
            if t < count:
                steps += [functools.partial(beside, t, k) for k in slots]
                if t in starts:
                    steps.append(functools.partial(hand_over, owner[t]))
            if t + ahead < count:
                steps.append(functools.partial(begin, t + ahead))
            if 0 <= t - lag < count:
                steps += [functools.partial(turn, t - lag, k) for k in slots]
            if t - 2 * lag in ends:
                steps += [functools.partial(close, ends[t - 2 * lag], k) for k in slots]
        steps += [functools.partial(finish, w) for w in range(len(self.shards))]
        return steps


def gather_kernel(streams, spans, count, *refs):
    shards, tok_ref, fulls = refs[:count], refs[count], refs[count + 1 : 2 * count + 1]
    halo_ref, sems, halo_sem = refs[2 * count + 1], refs[2 * count + 2 : -1], refs[-1]
    place = Place(streams, spans)
    work = Gather(place, shards, fulls, sems, (2, 1))
    greet(work.neighbours() + place.either_side())
    halo = copy_to(
        tok_ref.at[pl.ds(tok_ref.shape[0] - HALO, HALO)], halo_ref, halo_sem.at[0], halo_sem.at[1],
        place.span_at(1),
    )
    halo.start()
    for step in work.steps():
        step()
    halo.wait()


def gather_call(shards, tokens, collective_id):
    streams, spans = lax.axis_size("stream"), lax.axis_size("span")
    shapes = [shard.shape for shard in shards]
    hbm = pl.BlockSpec(memory_space=pl.ANY)
    return pl.pallas_call(
        functools.partial(gather_kernel, streams, spans, len(shards)),
        in_specs=[pl.BlockSpec(memory_space=pltpu.VMEM)] * len(shards) + [hbm],
        out_specs=[hbm] * (len(shards) + 1),
        out_shape=[jax.ShapeDtypeStruct((spans,) + s.shape, s.dtype) for s in shards]
        + [jax.ShapeDtypeStruct((HALO, tokens.shape[1]), tokens.dtype)],
        scratch_shapes=Gather.sem_shapes(shapes, streams, spans) + [pltpu.SemaphoreType.DMA((2,))],
        compiler_params=pltpu.CompilerParams(
            collective_id=collective_id, has_side_effects=True, vmem_limit_bytes=VMEM_LIMIT
        ),
        name="gather_weights",
    )(*shards, tokens)


class Reduce:
    def __init__(self, place, grads, targets, bufs, sems, share):
        self.place, self.grads, self.bufs, self.sems = place, grads, bufs, sems
        self.targets = targets
        self.units = self.cut([g.shape for g in grads], place.streams)
        self.modes = self.plan(self.units, [g.shape for g in grads], place.streams, share)

    @staticmethod
    def cut(shapes, streams):
        return units_of([s[1:] for s in shapes], streams, REDUCE_PIECE // shapes[0][0])

    @staticmethod
    def plan(units, shapes, streams, share):
        whole = part = 0
        modes = []
        loads = [[0, 0], [0, 0]]
        for w, _, _, cut_r, cut_c in units:
            _, rows, width = shapes[w]
            size = rows * width // (cut_r * cut_c)
            plain = quarter_of(rows, width, streams)[0] == 1 and cut_c == 1 and rows > 16
            whole += size
            first = plain and part + size <= share * whole
            part += size if first else 0
            load = loads[first]
            way = load.index(min(load))
            load[way] += size
            modes.append((first, (1, 2) if way == 0 else (2, 1)))
        return modes

    @staticmethod
    def block(shape, streams):
        _, rows, width = shape
        down, across = quarter_of(rows, width, streams)
        return rows // down, width // across

    @staticmethod
    def scratch(shapes, kinds, streams):
        out = []
        dma = pltpu.SemaphoreType.DMA
        spans = shapes[0][0]
        for shape, kind in zip(shapes, kinds):
            r, c = Reduce.block(shape, streams)
            out += [
                pltpu.VMEM((2, spans, r, c), kind),
                pltpu.VMEM((2, spans, r, c), kind),
                pltpu.VMEM((spans, r, c), kind),
                pltpu.VMEM((spans, r, c), kind),
                pltpu.VMEM((spans, r, c), kind),
                pltpu.VMEM((r, c), kind),
                pltpu.VMEM((streams, 2, r, c), kind),
            ]
            across = quarter_of(*shape[1:], streams)[1]
            out += [
                pltpu.VMEM((spans, r, c * across) if across == streams else (2, 16, 128), kind),
                pltpu.VMEM((2, r, c * across) if across == streams else (2, 16, 128), kind),
            ]
        n = len(Reduce.cut(shapes, streams))
        out += [dma((n, 3, 2)), dma((n, spans // 2, 2)), dma((n, streams, 2))]
        return out

    def turn(self, unit):
        return self.modes[unit][1]

    def chips_first(self, unit):
        return self.modes[unit][0]

    def inner(self, unit):
        w, i, j, cut_r, cut_c = self.units[unit]
        r, c = self.block(self.grads[w].shape, self.place.streams)
        r, c = r // cut_r, c // cut_c
        return pl.ds(i * r, r), pl.ds(j * c, c)

    def outer(self, unit, at):
        _, rows, width = self.grads[self.units[unit][0]].shape
        return quarter_index(rows, width, self.place.streams, at, self.units[unit])

    def buf(self, unit, which):
        return self.bufs[self.units[unit][0]][which]

    def count(self, unit):
        return 2 if self.chips_first(unit) else self.place.spans

    def first(self, unit, slot):
        p = self.place
        a, b = self.turn(unit)
        spans = pl.ds(0, self.count(unit))
        at = p.stream ^ a if slot == 0 else p.stream ^ a ^ b
        source = self.buf(unit, 8) if self.chips_first(unit) else self.grads[self.units[unit][0]]
        return copy_to(
            source.at[(spans,) + self.outer(unit, at)],
            self.buf(unit, 0).at[(slot, spans) + self.inner(unit)],
            self.sems[0].at[unit, slot, 0], self.sems[0].at[unit, slot, 1], p.beside(a),
        )

    def second(self, unit):
        p = self.place
        _, b = self.turn(unit)
        spans = pl.ds(0, self.count(unit))
        return copy_to(
            self.buf(unit, 1).at[(1, spans) + self.inner(unit)],
            self.buf(unit, 2).at[(spans,) + self.inner(unit)],
            self.sems[0].at[unit, 2, 0], self.sems[0].at[unit, 2, 1], p.beside(b),
        )

    def third(self, unit, k):
        p = self.place
        if self.chips_first(unit):
            rows, _ = self.inner(unit)
            return copy_to(
                self.grads[self.units[unit][0]].at[pl.ds(2 * p.shifted(k), 2), rows],
                self.buf(unit, 7).at[pl.ds(2 * k, 2), rows],
                self.sems[1].at[unit, k, 0], self.sems[1].at[unit, k, 1], p.along(k),
            )
        return copy_to(
            self.buf(unit, 3).at[(pl.ds(2 * p.shifted(k), 2),) + self.inner(unit)],
            self.buf(unit, 4).at[(pl.ds(2 * k, 2),) + self.inner(unit)],
            self.sems[1].at[unit, k, 0], self.sems[1].at[unit, k, 1], p.along(k),
        )

    def swap(self, unit):
        p = self.place
        return copy_to(
            self.buf(unit, 5).at[self.inner(unit)],
            self.buf(unit, 6).at[(0, p.core) + self.inner(unit)],
            self.sems[2].at[unit, 0, 0], self.sems[2].at[unit, 0, 1], p.other(),
        )

    def fourth(self, unit, step):
        p = self.place
        return copy_to(
            self.buf(unit, 6).at[(0, pl.ds(0, 2)) + self.inner(unit)],
            self.buf(unit, 6).at[(step, pl.ds(0, 2)) + self.inner(unit)],
            self.sems[2].at[unit, step, 0], self.sems[2].at[unit, step, 1], p.beside(step),
        )

    def neighbours(self):
        p = self.place
        return [p.along(k) for k in range(1, p.chips)] + [
            p.beside(s) for s in range(1, p.streams)
        ] + [p.other()]

    def begin(self, unit):
        if self.chips_first(unit):
            for k in range(1, self.place.chips):
                self.third(unit, k).start()
            return
        for slot in (1, 0):
            self.first(unit, slot).start()

    def add_first(self, unit):
        if self.chips_first(unit):
            self.sum_chips(unit)
            for slot in (1, 0):
                self.first(unit, slot).start()
            return
        self.sum_first(unit, self.grads[self.units[unit][0]])

    def sum_chips(self, unit):
        p = self.place
        grad = self.grads[self.units[unit][0]]
        rows, _ = self.inner(unit)
        for k in range(1, p.chips):
            self.third(unit, k).wait_recv()
        for part in range(2):
            total = grad[2 * p.chip + part, rows, :].astype(F32)
            for k in range(1, p.chips):
                total = total + self.buf(unit, 7)[2 * k + part, rows, :].astype(F32)
            self.buf(unit, 8)[part, rows, :] = total.astype(grad.dtype)

    def sum_first(self, unit, grad):
        p = self.place
        _, b = self.turn(unit)
        inner = self.inner(unit)
        for slot in (1, 0):
            self.first(unit, slot).wait_recv()
            outer = self.outer(unit, p.stream ^ b if slot else p.stream)
            for span in range(self.count(unit)):
                self.buf(unit, 1)[(slot, span) + inner] = (
                    grad[(span,) + outer].astype(F32)
                    + self.buf(unit, 0)[(slot, span) + inner].astype(F32)
                ).astype(grad.dtype)
            if slot:
                self.second(unit).start()

    def add_second(self, unit):
        p = self.place
        if self.chips_first(unit):
            self.sum_first(unit, self.buf(unit, 8))
            return
        inner = self.inner(unit)
        self.second(unit).wait_recv()
        for span in range(p.spans):
            self.buf(unit, 3)[(span,) + inner] = (
                self.buf(unit, 1)[(0, span) + inner].astype(F32)
                + self.buf(unit, 2)[(span,) + inner].astype(F32)
            ).astype(self.buf(unit, 3).dtype)
        for k in range(1, p.chips):
            self.third(unit, k).start()

    def add_third(self, unit):
        p = self.place
        inner = self.inner(unit)
        kind = self.buf(unit, 5).dtype
        if self.chips_first(unit):
            self.second(unit).wait_recv()
        else:
            for k in range(1, p.chips):
                self.third(unit, k).wait_recv()
        for mine in (False, True):
            core = p.core if mine else 1 - p.core
            if self.chips_first(unit):
                total = self.buf(unit, 1)[(0, core) + inner].astype(F32)
                total = total + self.buf(unit, 2)[(core,) + inner].astype(F32)
            else:
                total = self.buf(unit, 3)[(2 * p.chip + core,) + inner].astype(F32)
                for k in range(1, p.chips):
                    total = total + self.buf(unit, 4)[(2 * k + core,) + inner].astype(F32)
            if mine:
                self.buf(unit, 6)[(0, p.core) + inner] = total.astype(kind)
            else:
                self.buf(unit, 5)[inner] = total.astype(kind)
                self.swap(unit).start()

    def spread(self, unit):
        self.swap(unit).wait_recv()
        for step in range(1, self.place.streams):
            self.fourth(unit, step).start()

    def finish(self, unit):
        p = self.place
        for step in range(p.streams):
            if step:
                self.fourth(unit, step).wait_recv()
            row, col = self.outer(unit, p.stream ^ step)
            for part in range(2):
                out, start, stride = self.targets[self.units[unit][0]][part]
                col_at = pl.ds(pl.multiple_of(start + stride * col.start, 128), col.size)
                out[row, col_at] = self.buf(unit, 6)[(step, part) + self.inner(unit)]
        self.swap(unit).wait_send()
        for slot in range(2):
            self.first(unit, slot).wait_send()
        self.second(unit).wait_send()
        for k in range(1, p.chips):
            self.third(unit, k).wait_send()
        for step in range(1, p.streams):
            self.fourth(unit, step).wait_send()

    def steps(self):
        count = len(self.units)
        ahead = REDUCE_AHEAD
        steps = [functools.partial(self.begin, u) for u in range(min(ahead, count))]
        lags = (
            (0, self.add_first), (3, self.add_second), (6, self.add_third), (7, self.spread),
            (10, self.finish),
        )
        for t in range(count + 10):
            for lag, act in lags:
                if 0 <= t - lag < count:
                    steps.append(functools.partial(act, t - lag))
                if lag == 0 and t + ahead < count:
                    steps.append(functools.partial(self.begin, t + ahead))
        return steps


def split_columns(out, width):
    return [(out, 0, 1), (out, width, 1)]


def reduce_kernel(streams, spans, *refs):
    grads, outs, rest = refs[:5], refs[5:8], refs[8:]
    half = grads[0].shape[2]
    targets = [split_columns(outs[0], half)]
    targets += [
        [(outs[1], 2 * i * half, 2), (outs[1], 2 * i * half + 128, 2)] for i in range(3)
    ]
    targets += [split_columns(outs[2], grads[4].shape[2])]
    bufs = [rest[9 * w : 9 * w + 9] for w in range(5)]
    work = Reduce(Place(streams, spans), grads, targets, bufs, rest[45:], 0.3)
    greet(work.neighbours())
    for step in work.steps():
        step()


def reduce_call(grads, collective_id):
    streams, spans = lax.axis_size("stream"), lax.axis_size("span")
    shapes = [grad.shape for grad in grads]
    vmem = pl.BlockSpec(memory_space=pltpu.VMEM)
    rows, width = shapes[0][1:]
    small_rows, small_width = shapes[4][1:]
    return pl.pallas_call(
        functools.partial(reduce_kernel, streams, spans),
        in_specs=[vmem] * len(grads),
        out_specs=[vmem] * 3,
        out_shape=[
            jax.ShapeDtypeStruct((rows, 2 * width), BF16),
            jax.ShapeDtypeStruct((rows, 6 * width), BF16),
            jax.ShapeDtypeStruct((small_rows, 2 * small_width), F32),
        ],
        scratch_shapes=Reduce.scratch(shapes, [g.dtype for g in grads], streams),
        compiler_params=pltpu.CompilerParams(
            collective_id=collective_id, has_side_effects=True, vmem_limit_bytes=VMEM_LIMIT
        ),
        name="reduce_grads",
    )(*grads)


def chain_body(p, backward, source, maps, state_ref, scratch):
    p_low, p_high, p_chip = maps
    swap, carry, outgo, sent = scratch[:4]
    swap_sem, hop_sem, back_sem = scratch[-3:]
    s_chip = None if backward else scratch[4]
    heads, size = source.shape[0], source.shape[2]
    half = heads // 2
    mine = p.core * half
    theirs = (1 - p.core) * half
    ahead, behind = (-1, 1) if backward else (1, -1)
    edge_in = p.chips - 1 if backward else 0
    edge_out = 0 if backward else p.chips - 1
    swap_copy = copy_to(
        source.at[pl.ds(theirs, half)], swap, swap_sem.at[0], swap_sem.at[1], p.other()
    )
    swap_copy.start()
    swap_copy.wait_recv()
    low_core = p.core == 0
    for h in range(half):
        own, got = source[mine + h], swap[h]
        low = jnp.where(low_core, own, got)
        high = jnp.where(low_core, got, own)
        if backward:
            outgo[h] = low.astype(F32) + nt(high, p_low[h])
        else:
            joined = nn(low, high[size:])
            s_chip[h] = joined[:size] + high[:size].astype(F32)
            p_chip[h] = joined[size:].astype(BF16)
            p_low[h] = low[size:]
            p_high[h] = high[size:]
            outgo[h] = low[:size].astype(F32)

    def hop(h):
        return copy_to(
            sent.at[h], carry.at[h], hop_sem.at[h, 0], hop_sem.at[h, 1], p.along(ahead)
        )

    @pl.when(p.chip == edge_in)
    def _():
        carry[...] = jnp.zeros(carry.shape, BF16)

    for h in range(half):

        @pl.when(p.chip != edge_in)
        def _():
            hop(h).wait_recv()

        moved = nt(carry[h], p_chip[h]) + outgo[h] if backward else nn(carry[h], p_chip[h]) + s_chip[h]
        sent[h] = moved.astype(BF16)

        @pl.when(p.chip != edge_out)
        def _():
            hop(h).start()

    for h in range(half):
        state = carry[h]
        if backward:
            low_state = (nt(state, p_high[h]) + jnp.where(low_core, swap[h], source[mine + h]).astype(F32)).astype(BF16)
            keep = jnp.where(low_core, low_state, state)
            give = jnp.where(low_core, state, low_state)
        else:
            high_state = (nn(state, p_low[h]) + outgo[h]).astype(BF16)
            keep = jnp.where(low_core, state, high_state)
            give = jnp.where(low_core, high_state, state)
        state_ref[mine + h] = keep
        sent[half + h] = give
    back = copy_to(
        sent.at[pl.ds(half, half)], state_ref.at[pl.ds(mine, half)],
        back_sem.at[0], back_sem.at[1], p.other(),
    )
    back.start()
    copy_to(
        sent.at[pl.ds(half, half)], state_ref.at[pl.ds(theirs, half)],
        back_sem.at[0], back_sem.at[1], p.other(),
    ).wait_recv()
    back.wait_send()
    swap_copy.wait_send()

    @pl.when(p.chip != edge_out)
    def _():
        for h in range(half):
            hop(h).wait_send()


def chain_scratch(heads, size, rows, backward):
    half = heads // 2
    dma = pltpu.SemaphoreType.DMA
    scratch = [
        pltpu.VMEM((half, rows, size), BF16),
        pltpu.VMEM((half, size, size), BF16),
        pltpu.VMEM((half, size, size), F32),
        pltpu.VMEM((heads, size, size), BF16),
    ]
    if not backward:
        scratch.append(pltpu.VMEM((half, size, size), F32))
    return scratch + [dma((2,)), dma((half, 2)), dma((2,))]


def readout_body(readout, gain):
    inv = lax.rsqrt(jnp.mean(readout * readout, -1, keepdims=True) + EPSILON)
    return (readout * inv * gain).astype(BF16)


def spread_steps(steps, first, slots, index):
    if index == 0:
        return steps[:first]
    rest = steps[first:]
    count = len(rest)
    return rest[count * (index - 1) // slots : count * index // slots]


def forward_kernel(streams, spans, heads, weights, *refs):
    ins, refs = refs[:11], refs[11:]
    shards, refs = refs[:weights], refs[weights:]
    outs, refs = refs[:15], refs[15:]
    fulls, refs = refs[:weights], refs[weights:]
    gather_sems, refs = refs[:3], refs[3:]
    map_buf, read_buf, rmap_buf, state_buf = refs[:4]
    chain_bufs = refs[4:]
    gain_ref = ins[10]
    (ext_ref, q_ref, k_ref, v_ref, inv_ref, wk_ref, pre_ref, nv_ref, np_ref,
     state_ref, p_low, p_high, p_chip, out_ref, normal_ref) = outs
    step_id = pl.program_id(0)
    place = Place(streams, spans)
    work = Gather(place, shards, fulls, gather_sems, (GATHER_AHEAD, GATHER_LAG))
    steps = work.steps()

    @pl.when(step_id == 0)
    def _():
        greet(work.neighbours())

    for index in range(heads + 1):

        @pl.when(step_id == index)
        def _():
            for step in spread_steps(steps, GATHER_AHEAD, FORWARD_SLOTS, index):
                step()

    @pl.when(step_id < heads)
    def _():
        local_kernel(
            *ins[:10], ext_ref, q_ref, k_ref, v_ref, inv_ref, wk_ref, pre_ref, map_buf.at[pl.ds(step_id, 1)],
            read_buf.at[step_id], rmap_buf.at[step_id], nv_ref, np_ref,
        )

    @pl.when(step_id == heads)
    def _():
        chain_body(
            place, False, map_buf, (p_low, p_high, p_chip), state_buf, chain_bufs,
        )
        state_ref[...] = state_buf[...]
        size = gain_ref.shape[1]
        for h in range(heads):
            cols = slice(h * size, (h + 1) * size)
            readout = read_buf[h] + nt(rmap_buf[h], state_buf[h])
            out_ref[:, cols] = readout
            normal_ref[:, cols] = readout_body(readout, gain_ref[...])
        for index in range(heads + 1, 20):
            for step in spread_steps(steps, GATHER_AHEAD, FORWARD_SLOTS, index):
                step()


def forward_call(
    keep, normed, w_qkv, conv, rate, allow, gain, shards, heads, collective_id
):
    streams, spans = lax.axis_size("stream"), lax.axis_size("span")
    tok = rate.shape[0]
    rows, width = normed.shape
    size = width // heads
    count = tok // STRETCH
    taps = conv.shape[0]
    half = heads // 2
    hbm = pl.BlockSpec(memory_space=pl.ANY)

    def at(i):
        return jnp.minimum(i, heads - 1)

    def third(i, r):
        return pl.BlockSpec((r, size), lambda h: (0, at(h) + i * heads))

    def token_block():
        return pl.BlockSpec((tok, size), lambda h: (0, at(h)))

    def whole(*shape):
        return pl.BlockSpec(shape, lambda h: (0,) * len(shape))

    token_shape = jax.ShapeDtypeStruct((tok, width), BF16)
    square = jax.ShapeDtypeStruct((half, size, size), BF16)
    shapes = [s.shape for s in shards]
    outs = pl.pallas_call(
        functools.partial(forward_kernel, streams, spans, heads, len(shards)),
        grid=(heads + 1,),
        in_specs=[
            pl.BlockSpec(memory_space=pltpu.SMEM),
            whole(rows, width),
            third(0, width), third(1, width), third(2, width),
            third(0, taps), third(1, taps), third(2, taps),
            whole(tok, heads), whole(tok, taps), whole(1, size),
        ]
        + [pl.BlockSpec(memory_space=pltpu.VMEM)] * len(shards),
        out_specs=[
            pl.BlockSpec((3, rows, size), lambda h: (0, 0, at(h))),
            token_block(), token_block(), token_block(),
            pl.BlockSpec((1, tok, STRETCH), lambda h: (at(h), 0, 0)),
            token_block(),
            pl.BlockSpec((1, count, 2 * size, size), lambda h: (at(h), 0, 0, 0)),
            token_block(), token_block(),
            whole(heads, size, size),
            whole(half, size, size), whole(half, size, size), whole(half, size, size),
            whole(tok, width), whole(tok, width),
        ]
        + [hbm] * len(shards),
        out_shape=[
            jax.ShapeDtypeStruct((3, rows, width), BF16),
            token_shape, token_shape, token_shape,
            jax.ShapeDtypeStruct((heads, tok, STRETCH), BF16),
            token_shape,
            jax.ShapeDtypeStruct((heads, count, 2 * size, size), BF16),
            token_shape, token_shape,
            jax.ShapeDtypeStruct((heads, size, size), BF16),
            square, square, square,
            jax.ShapeDtypeStruct((tok, width), F32),
            token_shape,
        ]
        + [jax.ShapeDtypeStruct((spans,) + s.shape, s.dtype) for s in shards],
        scratch_shapes=Gather.sem_shapes(shapes, streams, spans)
        + [
            pltpu.VMEM((heads, 2 * size, size), BF16),
            pltpu.VMEM((heads, tok, size), F32),
            pltpu.VMEM((heads, tok, size), BF16),
            pltpu.VMEM((heads, size, size), BF16),
        ]
        + chain_scratch(heads, size, 2 * size, False),
        compiler_params=pltpu.CompilerParams(
            collective_id=collective_id, has_side_effects=True, vmem_limit_bytes=VMEM_LIMIT
        ),
        name="delta_forward",
    )(keep, normed, w_qkv, w_qkv, w_qkv, conv, conv, conv, rate, allow, gain, *shards)
    return outs[:15], outs[15:]


def backward_kernel(streams, spans, heads, weights, *refs):
    (keep_ref, gn_ref, read_ref, gain_ref, q_ref, k_ref, v_ref, wk_ref, inv_ref, min_ref, pre_ref,
     nv_ref, np_ref, rate_ref, allow_ref, eq_ref, ek_ref, ev_ref, cq_ref, ck_ref, cv_ref,
     p_low, p_high, p_chip, pair_ref, wq_ref, wkey_ref, wv_ref, heads_ref, attn_ref) = refs[:30]
    refs = refs[30:]
    grads, refs = refs[:weights], refs[weights:]
    gconv_ref, grate_ref, gain_grad_ref, gnormed_ref = refs[:4]
    halves, edge_ref, out_grad_ref, sums, refs = refs[4:7], refs[7], refs[8], refs[9:12], refs[12:]
    bufs, refs = [refs[9 * w : 9 * w + 9] for w in range(weights)], refs[9 * weights :]
    reduce_sems, refs = refs[:3], refs[3:]
    go_buf, adj_buf, din_buf = refs[:3]
    pair_buf, own_buf, got_buf, pair_sem = refs[3:7]
    edge_buf, edge_got, attn_give, attn_got, edge_sem = refs[7:12]
    row_bufs, chain_bufs = refs[12:15], refs[15:]
    step_id = pl.program_id(0)
    turns = heads // GROUP
    place = Place(streams, spans)
    targets = [
        split_columns(sums[0], grads[0].shape[2]),
        [(sums[1], 0, 1), (sums[2], 0, 1)],
    ]
    work = Reduce(place, grads, targets, bufs, reduce_sems, 0.1)
    steps = work.steps()
    slots = BACKWARD_SLOTS
    size = gain_ref.shape[1]

    def hand_over(turn):
        return copy_to(
            own_buf.at[GROUP * turn + 1 - place.core], got_buf.at[turn],
            pair_sem.at[turn, 0], pair_sem.at[turn, 1], place.other(),
        )

    def weigh(turn):
        hand_over(turn).wait_recv()
        both = jnp.concatenate([own_buf[GROUP * turn + place.core], got_buf[turn]], 0)
        grad = nn(pair_buf[...], both).astype(BF16)
        lanes = pl.ds(pl.multiple_of(turn * size, size), size)
        for i in range(3):
            rows = halves[i].shape[1]
            halves[i][:, :, lanes] = grad[:, lanes_of(i, size)].reshape(-1, rows, size)
        hand_over(turn).wait_send()

    half = attn_got.shape[1]

    def columns(core):
        return attn_ref[:, pl.ds(pl.multiple_of(core * half, half), half)]

    attn_copy = copy_to(attn_give, attn_got, edge_sem.at[0], edge_sem.at[1], place.other())
    edge_copy = copy_to(edge_buf, edge_got, edge_sem.at[2], edge_sem.at[3], place.span_at(-1))

    @pl.when(step_id == 0)
    def _():
        greet(work.neighbours() + place.either_side())
        attn_give[...] = columns(1 - place.core)
        attn_copy.start()
        pair_buf[...] = pair_ref[...].T

    @pl.when(step_id == 1)
    def _():
        attn_copy.wait()
        both = jnp.concatenate([columns(place.core), attn_got[...]], 0)
        out_grad_ref[...] = tn(heads_ref[...], both).astype(BF16).reshape(out_grad_ref.shape)

    for index in range(2 * turns + 1):

        @pl.when(step_id == index)
        def _():
            for step in spread_steps(steps, REDUCE_AHEAD, slots, index):
                step()

    @pl.when(step_id < turns)
    def _():
        adjoint_body(
            keep_ref, gn_ref, read_ref, gain_ref, q_ref, k_ref, wk_ref,
            go_buf.at[step_id], adj_buf.at[pl.ds(GROUP * step_id, GROUP)], gain_grad_ref,
        )

    @pl.when(step_id == turns)
    def _():
        chain_body(place, True, adj_buf, (p_low, p_high, p_chip), din_buf, chain_bufs)

    @pl.when(step_id > turns + 1)
    def _():
        weigh(step_id - turns - 2)

    @pl.when(step_id > turns)
    def _():
        turn = step_id - turns - 1
        pair = pl.ds(GROUP * turn, GROUP)
        own = own_buf.at[pair]
        backward_body(
            turn, keep_ref, din_buf.at[pair], min_ref, pre_ref, go_buf.at[turn],
            q_ref, k_ref, v_ref, inv_ref, wk_ref, nv_ref, np_ref, rate_ref, allow_ref,
            eq_ref, ek_ref, ev_ref, cq_ref, ck_ref, cv_ref,
            own, gconv_ref, grate_ref, *row_bufs,
        )
        hand_over(turn).start()
        part = None
        for i, weight in enumerate((wq_ref, wkey_ref, wv_ref)):
            grad = jnp.concatenate([own[g, :, lanes_of(i, size)] for g in range(GROUP)], 1)
            term = nt(grad, weight[...])
            part = term if part is None else part + term
        before = jnp.where(turn == 0, jnp.zeros_like(part), gnormed_ref[...])
        gnormed_ref[...] = before + part

    @pl.when(step_id == 2 * turns)
    def _():
        edge_buf[...] = gnormed_ref[:HALO, :].astype(BF16)
        edge_copy.start()
        weigh(turns - 1)
        for index in range(2 * turns + 1, slots + 1):
            for step in spread_steps(steps, REDUCE_AHEAD, slots, index):
                step()
        edge_copy.wait()
        edge_ref[...] = edge_got[...]


def backward_call(
    keep, grad_normal, readout, gain, queries, keys, values, wkeys, invs, state, prefix,
    new_v, new_p, rate, allow, ext, conv, maps, pair_normed, w_qkv,
    pair_heads, grad_attn, grads, heads, collective_id,
):
    streams, spans = lax.axis_size("stream"), lax.axis_size("span")
    tok, width = queries.shape
    size = width // heads
    count = tok // STRETCH
    taps = conv.shape[0]
    rows = ext.shape[1]
    half = heads // 2

    turns = heads // GROUP
    wide = GROUP * size

    def first(i):
        return jnp.minimum(i, turns - 1)

    def second(i):
        return jnp.maximum(i - turns - 1, 0)

    def both(i):
        return jnp.where(i < turns, i, second(i))

    def block(at):
        return pl.BlockSpec((tok, wide), lambda h: (0, at(h)))

    def third(i, r):
        return pl.BlockSpec((r, wide), lambda h: (0, second(h) + i * turns))

    def part(i):
        return pl.BlockSpec((1, rows, wide), lambda h: (i, 0, second(h)))

    def whole(*shape):
        return pl.BlockSpec(shape, lambda h: (0,) * len(shape))

    vmem = pl.BlockSpec(memory_space=pltpu.VMEM)
    shapes = [g.shape for g in grads]
    outs = pl.pallas_call(
        functools.partial(backward_kernel, streams, spans, heads, len(grads)),
        grid=(2 * turns + 1,),
        in_specs=[
            pl.BlockSpec(memory_space=pltpu.SMEM),
            block(first), block(first), whole(1, size),
            block(both), block(both), block(second), block(both),
            pl.BlockSpec((GROUP, tok, STRETCH), lambda h: (second(h), 0, 0)),
            pl.BlockSpec((GROUP, size, size), lambda h: (second(h), 0, 0)),
            pl.BlockSpec((GROUP, count, 2 * size, size), lambda h: (second(h), 0, 0, 0)),
            block(second), block(second),
            whole(tok, heads), whole(tok, taps),
            part(0), part(1), part(2),
            third(0, taps), third(1, taps), third(2, taps),
            whole(half, size, size), whole(half, size, size), whole(half, size, size),
            vmem, third(0, width), third(1, width), third(2, width), vmem, vmem,
        ]
        + [vmem] * len(grads),
        out_specs=[
            pl.BlockSpec((3, taps, wide), lambda h: (0, 0, second(h))),
            whole(tok, heads),
            pl.BlockSpec((GROUP, 1, size), lambda h: (first(h), 0, 0)),
            whole(rows, width),
        ]
        + [vmem] * 8,
        out_shape=[
            jax.ShapeDtypeStruct((3, taps, width), F32),
            jax.ShapeDtypeStruct((tok, heads), F32),
            jax.ShapeDtypeStruct((heads, 1, size), F32),
            jax.ShapeDtypeStruct((rows, width), F32),
        ]
        + [jax.ShapeDtypeStruct((spans, width // spans, width // 2), BF16)] * 3
        + [
            jax.ShapeDtypeStruct((HALO, width), BF16),
            jax.ShapeDtypeStruct((spans, width // spans, width // 2), BF16),
        ]
        + [
            jax.ShapeDtypeStruct((shapes[0][1], 2 * shapes[0][2]), BF16),
            jax.ShapeDtypeStruct(shapes[1][1:], BF16),
            jax.ShapeDtypeStruct(shapes[1][1:], BF16),
        ],
        scratch_shapes=Reduce.scratch(shapes, [g.dtype for g in grads], streams)
        + [
            pltpu.VMEM((turns, tok, wide), BF16),
            pltpu.VMEM((heads, size, size), BF16),
            pltpu.VMEM((heads, size, size), BF16),
            pltpu.VMEM((width, 2 * rows), BF16),
            pltpu.VMEM((heads, rows, 3 * size), BF16),
            pltpu.VMEM((turns, rows, 3 * size), BF16),
            pltpu.SemaphoreType.DMA((turns, 2)),
            pltpu.VMEM((HALO, width), BF16),
            pltpu.VMEM((HALO, width), BF16),
            pltpu.VMEM((tok, width // 2), BF16),
            pltpu.VMEM((tok, width // 2), BF16),
            pltpu.SemaphoreType.DMA((4,)),
        ]
        + [pltpu.VMEM((tok, wide), F32)] * 3
        + chain_scratch(heads, size, size, True),
        compiler_params=pltpu.CompilerParams(
            collective_id=collective_id, has_side_effects=True, vmem_limit_bytes=VMEM_LIMIT
        ),
        name="delta_backward",
    )(
        keep, grad_normal, readout, gain, queries, keys, values, wkeys, invs, state, prefix,
        new_v, new_p, rate, allow, ext, ext, ext, conv, conv, conv, *maps, pair_normed,
        w_qkv, w_qkv, w_qkv, pair_heads, grad_attn, *grads,
    )
    return outs[:4], outs[4:9], outs[9:]


def feed_kernel(
    streams, spans,
    heads_ref, tok_ref, cot_ref, out_w_ref, gain_ref, gate_ref, up_ref, down_ref,
    result_ref, gmid_ref, gattn_ref, gnormal_ref, ggain_ref, ffn_grad_ref, down_grad_ref,
    mid_buf, grad_buf, res_buf, normed_buf, turned_buf, cot_buf, hid_buf, mine_buf, give_buf,
    hid_got, mine_got, row_sem, unit_sem,
):
    step_id = pl.program_id(0)
    last = pl.num_programs(0) - 1
    place = Place(streams, spans)
    width = cot_ref.shape[1]
    half = width // 2
    tok = cot_ref.shape[0]

    def exchange(source, target, sems):
        return copy_to(source, target, sems.at[0], sems.at[1], place.other())

    def rows(which):
        buf = normed_buf if which == 0 else cot_buf
        return exchange(buf.at[0 if which == 0 else 2], buf.at[1], row_sem.at[which])

    def units(step, which):
        source, target = (hid_buf, hid_got) if which == 0 else (give_buf, mine_got)
        return exchange(source.at[step], target.at[step], unit_sem.at[step, which])

    @pl.when(step_id == 0)
    def _():
        greet([place.other()])
        for own in range(2):
            which = place.core if own else 1 - place.core
            lanes = pl.ds(pl.multiple_of(which * half, half), half)
            cot_buf[0 if own else 2] = cot_ref[:, lanes]
        rows(1).start()
        middle = tok_ref[...].astype(F32) + nn(heads_ref[...], out_w_ref[...])
        inv = lax.rsqrt(jnp.mean(middle * middle, -1, keepdims=True) + EPSILON)
        mid_buf[...] = middle
        normed_buf[0] = (middle * inv * gain_ref[...]).astype(BF16)
        rows(0).start()
        grad_buf[...] = jnp.zeros(grad_buf.shape, F32)
        res_buf[...] = middle

    @pl.when(step_id == 1)
    def _():
        rows(0).wait_recv()
        rows(1).wait_recv()
        turned_buf[:, :tok] = normed_buf[0].T
        turned_buf[:, tok:] = normed_buf[1].T

    @pl.when(step_id < last)
    def _():
        normed = normed_buf[0]
        gate_w, up_w, down_w = gate_ref[...], up_ref[...], down_ref[...]
        gate = nn(normed, gate_w)
        up = nn(normed, up_w)
        grad_hidden = nt(cot_ref[...], down_w)
        sig = jax.nn.sigmoid(gate)
        act = gate * sig
        hidden = (act * up).astype(BF16)
        grad_gate = (grad_hidden * up * (sig * (1.0 + gate * (1.0 - sig)))).astype(BF16)
        grad_up = (grad_hidden * act).astype(BF16)
        low = place.core == 0
        hid_buf[step_id] = hidden
        mine_buf[step_id] = jnp.where(low, grad_gate, grad_up)
        give_buf[step_id] = jnp.where(low, grad_up, grad_gate)
        units(step_id, 0).start()
        units(step_id, 1).start()
        grad_buf[...] += nt(grad_gate, gate_w) + nt(grad_up, up_w)
        res_buf[...] += nn(hidden, down_w)

    @pl.when(step_id == last)
    def _():
        result_ref[...] = res_buf[...].astype(BF16)
        middle, grad = mid_buf[...], grad_buf[...]
        inv = lax.rsqrt(jnp.mean(middle * middle, -1, keepdims=True) + EPSILON)
        ggain_ref[...] = jnp.sum(grad * middle * inv, 0, keepdims=True)
        scaled = grad * gain_ref[...]
        total = cot_ref[...].astype(F32) + inv * scaled - middle * (inv * inv * inv) * jnp.mean(
            scaled * middle, -1, keepdims=True
        )
        gmid_ref[...] = total
        low_total = total.astype(BF16)
        gattn_ref[...] = low_total
        gnormal_ref[...] = nt(low_total, out_w_ref[...])

    @pl.when(step_id > 0)
    def _():
        before = step_id - 1
        units(before, 0).wait_recv()
        units(before, 1).wait_recv()
        mine = jnp.concatenate([mine_buf[before], mine_got[before]], 0)
        grad = nn(turned_buf[...], mine).astype(BF16)
        ffn_grad_ref[...] = grad.reshape(ffn_grad_ref.shape)
        both = jnp.concatenate([hid_buf[before], hid_got[before]], 0)
        cot = jnp.concatenate([cot_buf[0], cot_buf[1]], 0)
        down_grad_ref[...] = tn(both, cot).astype(BF16)

    @pl.when(step_id == last)
    def _():
        for which in range(2):
            rows(which).wait_send()
            for step in range(hid_buf.shape[0]):
                units(step, which).wait_send()


def feed_call(normal_heads, tokens, cotangent, w_out, gain, w_gate, w_up, w_down, collective_id):
    streams, spans = lax.axis_size("stream"), lax.axis_size("span")
    tok, width = tokens.shape
    units = w_gate.shape[1]
    step = 256
    count = units // step
    dma = pltpu.SemaphoreType.DMA

    def now(f):
        return jnp.minimum(f, count - 1)

    def before(f):
        return jnp.maximum(f - 1, 0)

    def whole(*shape):
        return pl.BlockSpec(shape, lambda f: (0,) * len(shape))

    rows = whole(tok, width)
    square = pltpu.VMEM((count, tok, step), BF16)
    return pl.pallas_call(
        functools.partial(feed_kernel, streams, spans),
        grid=(count + 1,),
        in_specs=[
            rows, rows, rows, whole(width, width), whole(1, width),
            pl.BlockSpec((width, step), lambda f: (0, now(f))),
            pl.BlockSpec((width, step), lambda f: (0, now(f))),
            pl.BlockSpec((step, width), lambda f: (now(f), 0)),
        ],
        out_specs=[
            rows, rows, rows, rows, whole(1, width),
            pl.BlockSpec((spans, width // spans, step), lambda f: (0, 0, before(f))),
            pl.BlockSpec((step, width // 2), lambda f: (before(f), 0)),
        ],
        out_shape=[
            jax.ShapeDtypeStruct((tok, width), BF16),
            jax.ShapeDtypeStruct((tok, width), F32),
            jax.ShapeDtypeStruct((tok, width), BF16),
            jax.ShapeDtypeStruct((tok, width), F32),
            jax.ShapeDtypeStruct((1, width), F32),
            jax.ShapeDtypeStruct((spans, width // spans, units), BF16),
            jax.ShapeDtypeStruct((units, width // 2), BF16),
        ],
        scratch_shapes=[pltpu.VMEM((tok, width), F32)] * 3
        + [
            pltpu.VMEM((2, tok, width), BF16),
            pltpu.VMEM((width, 2 * tok), BF16),
            pltpu.VMEM((3, tok, width // 2), BF16),
            square, square, square, square, square,
            dma((2, 2)), dma((count, 2, 2)),
        ],
        compiler_params=pltpu.CompilerParams(
            collective_id=collective_id, has_side_effects=True, vmem_limit_bytes=VMEM_LIMIT
        ),
        name="feed_forward",
    )(normal_heads, tokens, cotangent, w_out, gain, w_gate, w_up, w_down)


def local(
    tokens, cotangent, doc_stretches, w_qkv, conv_weight, w_beta, beta_bias, norm_attn, norm_head,
    w_out, norm_ffn, w_gate, w_up, w_down,
):
    tok_rows, model_width = tokens.shape[1:]
    heads = beta_bias.shape[0]
    size = model_width // heads
    count = tok_rows // STRETCH
    span_count = lax.axis_size("span")
    place = lax.axis_index("span")
    taps = conv_weight.shape[0]

    small = jnp.concatenate(
        [x.reshape(-1) for x in (conv_weight, w_beta, norm_attn, norm_ffn, norm_head)]
    )
    small_len = small.shape[0]
    small = jnp.pad(small, (0, 16 * 512 - small_len)).reshape(16, 512)
    full_qkv, smalls, before = gather_call([w_qkv, small], tokens[0], 1)
    full_qkv = full_qkv.reshape(-1, full_qkv.shape[2])
    smalls = smalls.reshape(span_count, -1)

    def small_part(shape, start):
        length = 1
        for dim in shape:
            length *= dim
        return smalls[:, start : start + length].reshape((span_count,) + shape), start + length

    at = 0
    full_conv, at = small_part(conv_weight.shape, at)
    full_beta, at = small_part(w_beta.shape, at)
    gain_attn, at = small_part(norm_attn.shape, at)
    gain_ffn, at = small_part(norm_ffn.shape, at)
    gain_head, at = small_part(norm_head.shape, at)
    full_conv = jnp.swapaxes(full_conv, 0, 1).reshape(taps, -1)
    full_beta = full_beta.reshape(-1, heads)
    attn_gain = gain_attn.reshape(-1).astype(F32)
    ffn_gain = gain_ffn.reshape(-1).astype(F32)
    head_gain = gain_head.reshape(1, -1).astype(F32)

    stretch_ids = place * count + jnp.arange(count, dtype=jnp.int32)
    doc_lengths = doc_stretches[0]
    doc_begins = jnp.cumsum(doc_lengths) - doc_lengths
    stretch_start = jnp.any(stretch_ids[:, None] == doc_begins[None, :], axis=1).astype(F32)
    stretch_keep = 1.0 - stretch_start
    token_start = jnp.repeat(stretch_start, STRETCH)
    token_offset = jnp.arange(tok_rows, dtype=jnp.int32) % STRETCH
    allow = jnp.stack(
        [1.0 - token_start * (token_offset < tap).astype(F32) for tap in range(taps)], 1
    )

    inputs_ext = jnp.concatenate([before, tokens[0]], 0).astype(F32)
    inv_ext = lax.rsqrt(jnp.mean(inputs_ext * inputs_ext, -1, keepdims=True) + EPSILON)
    normed_ext = (inputs_ext * inv_ext * attn_gain).astype(BF16)
    inputs_f, inv_first, normed = inputs_ext[HALO:], inv_ext[HALO:], normed_ext[HALO:]
    strength = jax.nn.sigmoid(
        jnp.dot(normed, full_beta, preferred_element_type=F32) + beta_bias
    )
    (
        projected, queries, keys, values, invs, wkeys, prefix, new_v, new_p,
        state_in, p_low, p_high, p_chip, readout, normal_heads,
    ), rest = forward_call(
        stretch_keep, normed_ext, full_qkv, full_conv, strength, allow, head_gain,
        [w_out, w_gate, w_up, w_down], heads, 2,
    )
    full_out, full_gate, full_up, full_down = (w.reshape(-1, w.shape[2]) for w in rest)

    (
        result, grad_middle, grad_attn_in, grad_normal, grad_norm_ffn, half_ffn, half_down
    ) = feed_call(
        normal_heads, tokens[0], cotangent[0], full_out, ffn_gain[None], full_gate, full_up,
        full_down, 3,
    )
    half_down = half_down.reshape(span_count, -1, half_down.shape[1])
    (
        (grad_conv, grad_strength, head_grads, grad_normed_ext),
        (half_q, half_k, half_v, halo_back, half_out),
        ffn_parts,
    ) = backward_call(
        stretch_keep, grad_normal, readout, head_gain, queries, keys, values, wkeys, invs,
        state_in, prefix, new_v, new_p, strength, allow, projected, full_conv,
        (p_low, p_high, p_chip), pair_tokens(normed_ext), full_qkv, pair_tokens(normal_heads),
        grad_attn_in, [half_down, half_ffn], heads, 4,
    )
    grad_logit = grad_strength * strength * (1.0 - strength)
    grad_logit_low = grad_logit.astype(BF16)
    grad_w_beta = product("td,th->dh", normed, grad_logit_low)
    grad_normed = (
        grad_normed_ext[HALO:]
        + product("th,dh->td", grad_logit_low, full_beta)
        + jnp.pad(halo_back.astype(F32), ((tok_rows - HALO, 0), (0, 0)))
    )
    grad_norm_attn = jnp.sum(grad_normed * inputs_f * inv_first, 0)
    grad_tokens = grad_middle + norm_back(grad_normed, inputs_f, inv_first, attn_gain)

    def by_span(array):
        return array.reshape(span_count, -1)

    grad_conv = jnp.swapaxes(grad_conv, 0, 1).reshape(taps, span_count, -1)
    packed = jnp.concatenate(
        [
            by_span(jnp.swapaxes(grad_conv, 0, 1)),
            by_span(grad_w_beta),
            by_span(grad_norm_attn),
            by_span(grad_norm_ffn),
            by_span(jnp.sum(head_grads, (0, 1))),
            jnp.broadcast_to(jnp.sum(grad_logit, 0)[None], (span_count, heads)),
        ],
        1,
    )
    packed = jnp.pad(packed, ((0, 0), (0, 16 * 1024 - packed.shape[1])))
    packed = packed.reshape(span_count, 16, 2, 512)
    core = place % 2
    half_small = lax.dynamic_index_in_dim(packed, core, 2, keepdims=False) + swap_core(
        lax.dynamic_index_in_dim(packed, 1 - core, 2, keepdims=False)
    )
    parts = reduce_call([half_out, half_q, half_k, half_v, half_small], 5)
    part_down, part_gate, part_up = (x.astype(F32) for x in ffn_parts)
    part_out, part_qkv = parts[0].astype(F32), parts[1].astype(F32)
    part_small = parts[2].reshape(-1)
    sums = []
    at = 0
    for like in (conv_weight, w_beta, norm_attn, norm_ffn, norm_head, beta_bias):
        sums.append(part_small[at : at + like.size].reshape(like.shape))
        at += like.size

    return (
        result[None],
        grad_tokens[None],
        part_qkv,
        sums[0],
        sums[1],
        sums[5],
        sums[2],
        sums[4],
        part_out,
        sums[3],
        part_gate,
        part_up,
        part_down,
    )


def solution(mesh):
    in_specs = (
        P("stream", "span", None),
        P("stream", "span", None),
        P("stream", None),
        P("span", None),
        P(None, "span"),
        P("span", None),
        P(),
        P("span"),
        P("span"),
        P("span", None),
        P("span"),
        P("span", None),
        P("span", None),
        P("span", None),
    )
    out_specs = (
        P("stream", "span", None),
        P("stream", "span", None),
        P("span", None),
        P(None, "span"),
        P("span", None),
        P(),
        P("span"),
        P("span"),
        P("span", None),
        P("span"),
        P("span", None),
        P("span", None),
        P("span", None),
    )
    return jax.shard_map(local, mesh=mesh, in_specs=in_specs, out_specs=out_specs, check_vma=False)
```
